32 devices in a mesh: dp: 8 (over z, y), ctx: 4 (over x, core).
Axes of the slice: x: 2, y: 2, z: 4, core: 2. Of those that a mesh axis runs over, the one named last changes fastest.
Arguments:
- tokens: bfloat16 [12288, 768], P(('dp', 'ctx')), may hold values from -6 to 6
- first_gain: bfloat16 [768], P('dp'), may hold values from 0.25 to 1.75
- first_shift: bfloat16 [768], P('dp'), may hold values from -1.75 to 1.75
- in_weight: bfloat16 [768, 2304], P('dp'), may hold values from -0.21875 to 0.21875
- in_bias: bfloat16 [2, 768], P(None, 'dp'), may hold values from -1.75 to 1.75
- out_weight: bfloat16 [768, 768], P('dp'), may hold values from -2 to 2
- out_bias: bfloat16 [768], P('dp'), may hold values from -1.75 to 1.75
- second_gain: bfloat16 [768], P('dp'), may hold values from 0.25 to 1.75
- second_shift: bfloat16 [768], P('dp'), may hold values from -1.75 to 1.75
- up_weight: bfloat16 [768, 3072], P('dp'), may hold values from -0.21875 to 0.21875
- up_bias: bfloat16 [3072], P('dp'), may hold values from -3 to 3
- down_weight: bfloat16 [3072, 768], P('dp'), may hold values from -0.109375 to 0.109375
- down_bias: bfloat16 [768], P('dp'), may hold values from -1.75 to 1.75
- cotangent: bfloat16 [12288, 768], P(('dp', 'ctx')), may hold values from -6 to 6
Outputs:
- layer_out: bfloat16 [12288, 768], P(('dp', 'ctx'))
- tokens_grad: bfloat16 [12288, 768], P(('dp', 'ctx'))
- first_gain_grad: float32 [768], P('dp')
- first_shift_grad: float32 [768], P('dp')
- in_weight_grad: float32 [768, 2304], P('dp')
- in_bias_grad: float32 [2, 768], P(None, 'dp')
- out_weight_grad: float32 [768, 768], P('dp')
- out_bias_grad: float32 [768], P('dp')
- second_gain_grad: float32 [768], P('dp')
- second_shift_grad: float32 [768], P('dp')
- up_weight_grad: float32 [768, 3072], P('dp')
- up_bias_grad: float32 [3072], P('dp')
- down_weight_grad: float32 [3072, 768], P('dp')
- down_bias_grad: float32 [768], P('dp')
The draws below stay inside these ranges and needn't reach their ends.
All inputs are finite; a program needn't handle non-finite values.
Results may differ from the reference program's by a relative error of at most 0.018.
Values may be sent and summed in bfloat16 or wider, within the bound.
No kernel may reach another device: no remote copies, remote signals or barrier semaphores. Data moves between devices by JAX's collectives and lax.ppermute only.
A program may use at most 192 MiB of HBM per device.

```python
import math
import jax
import jax.numpy as jnp
from jax import lax

D = 768
HEADS = 12
HEAD_DIM = 64
FF = 3072
SEQ = 1536
TOKENS = 12288
N_DP = 8


def spiked(drawn, key, source, target, shards_of, factor):
    def block_of(dim):
        return (jnp.arange(drawn.shape[dim]) // (drawn.shape[dim] // shards_of)).reshape((-1,) + (1,) * (drawn.ndim - 1 - dim))

    one_side = jax.random.permutation(key, shards_of)[block_of(target)]
    other_side = (block_of(target) + shards_of // 2) % shards_of
    return jnp.where((block_of(source) == one_side) | (block_of(source) == other_side), factor * drawn, drawn)


def block_scale(stream_key, dims, shards, smallest, high):
    level, own = 1.0, jax.random.fold_in(stream_key, 6)
    for dim, blocks in shards:
        steps = jnp.exp(jax.random.uniform(jax.random.fold_in(own, dim), (blocks,), jnp.float32, smallest / len(shards), high / len(shards)))
        level = level * jnp.repeat(steps, dims[dim] // blocks).reshape([-1 if axis == dim else 1 for axis in range(len(dims))])
    return level


def normal_values(own_key, dims, scale, most, shards=(), kind=jnp.bfloat16):
    values = jax.random.normal(own_key, dims, jnp.float32) * scale
    if len(shards) > 0:
        values = block_scale(own_key, dims, shards, -0.22, 0.18) * values
    return jnp.clip(values, min=-most, max=most).astype(kind)


def heavy_noise(stream_key, dims, scale, limit, cuts, heavy, kind=jnp.bfloat16):
    entries = scale * jax.random.normal(stream_key, dims, jnp.float32)
    if cuts:
        entries = entries * block_scale(stream_key, dims, cuts, -0.22, 0.18)
    return jnp.clip(spiked(entries, jax.random.fold_in(stream_key, 3), *heavy), -limit, limit).astype(kind)


def setup_inputs(seed: int = 0) -> dict:
    key_list = jax.random.split(jax.random.key(seed), 15)
    tokens = heavy_noise(key_list[0], (TOKENS, D), 1.0, 6.0, ((0, 32),), (0, 1, 32, 2.75))
    first_gain = jnp.clip(1.0 + 0.15 * jax.random.normal(key_list[1], (D,), jnp.float32), 0.25, 1.75).astype(jnp.bfloat16)
    first_shift = normal_values(key_list[2], (D,), 0.3, 1.75, ((0, 8),))
    in_weight = normal_values(key_list[3], (D, 3 * D), D ** -0.5, 0.21875, ((0, 8),))
    in_bias = normal_values(key_list[4], (2, D), 0.3, 1.75, ((1, 8),))
    out_weight = normal_values(key_list[5], (D, D), 8 ** -0.5, 2.0, ((0, 8),))
    out_bias = normal_values(key_list[6], (D,), 0.3, 1.75, ((0, 8),))
    second_gain = jnp.clip(1.0 + 0.15 * jax.random.normal(key_list[7], (D,), jnp.float32), 0.25, 1.75).astype(jnp.bfloat16)
    second_shift = normal_values(key_list[8], (D,), 0.3, 1.75, ((0, 8),))
    up_weight = normal_values(key_list[9], (D, FF), D ** -0.5, 0.21875, ((0, 8),))
    up_bias = normal_values(key_list[10], (FF,), 0.5, 3.0, ((0, 8),))
    down_weight = normal_values(key_list[11], (FF, D), FF ** -0.5, 0.109375, ((0, 8),))
    down_bias = normal_values(key_list[12], (D,), 0.3, 1.75, ((0, 8),))
    cotangent = normal_values(key_list[13], (TOKENS, D), 1.0, 6.0, ((0, 32),))
    return dict(tokens=tokens, first_gain=first_gain, first_shift=first_shift, in_weight=in_weight, in_bias=in_bias, out_weight=out_weight, out_bias=out_bias, second_gain=second_gain, second_shift=second_shift, up_weight=up_weight, up_bias=up_bias, down_weight=down_weight, down_bias=down_bias, cotangent=cotangent)


epsilon = 1e-05
highest = lax.Precision.HIGHEST

@jax.custom_vjp
def low(v):
    return lax.optimization_barrier(v.astype(jnp.bfloat16)).astype(jnp.float32)

@jax.custom_vjp
def low_back(v):
    return v

def low_keep(v):
    return (low(v), None)

def low_pass(kept, grad):
    return (grad,)

def back_keep(v):
    return (v, None)

def back_low(kept, grad):
    return (low(grad),)
low.defvjp(low_keep, low_pass)
low_back.defvjp(back_keep, back_low)

def layer_norm(values, gain, shift):
    center = values - lax.optimization_barrier(jnp.mean(values, axis=-1, keepdims=True))
    spread = lax.optimization_barrier(jnp.mean(center * center, axis=-1, keepdims=True))
    return center * lax.rsqrt(spread + epsilon) * gain + shift

def smooth_gate(values):
    return jax.nn.gelu(values, approximate=True)

def matmul(left, right):
    return jnp.dot(left, right, precision=highest, preferred_element_type=jnp.float32)

def attend(queries, key_rows, value_rows):
    stride = math.gcd(SEQ, 512)
    key_heads = key_rows.reshape(SEQ, HEADS, HEAD_DIM)
    value_heads = value_rows.reshape(SEQ, HEADS, HEAD_DIM)
    positions = jnp.arange(SEQ, dtype=jnp.int32)
    factor = 1.0 / math.sqrt(HEAD_DIM)

    def one_block(operands):
        block_rows, offset = operands
        query_heads = block_rows.reshape(stride, HEADS, HEAD_DIM)
        scores = jnp.einsum('qhd,khd->hqk', query_heads, key_heads, precision=highest) * factor
        scores = low_back(scores)
        allowed = (offset + jnp.arange(stride, dtype=jnp.int32))[:, None] >= positions[None, :]
        scores = jnp.where(allowed[None], scores, -1e+30)
        stats = jax.nn.logsumexp(scores, axis=-1, keepdims=True)
        weights = low(jnp.exp(scores - stats))
        context = jnp.einsum('hqk,khd->qhd', weights, value_heads, precision=highest)
        return context.reshape(stride, D)
    blocks = queries.reshape(SEQ // stride, stride, D)
    offsets = jnp.arange(SEQ // stride, dtype=jnp.int32) * stride
    return lax.map(jax.checkpoint(one_block), (blocks, offsets)).reshape(SEQ, D)

def forward(tokens, first_gain, first_shift, in_weight, in_bias, out_weight, out_bias, second_gain, second_shift, up_weight, up_bias, down_weight, down_bias):
    bias_full = jnp.concatenate([in_bias[0], jnp.zeros((D,), in_bias.dtype), in_bias[1]])

    def one_sequence(rows):
        normed = layer_norm(rows, first_gain, first_shift)
        mixture = low(low_back(matmul(low(normed), in_weight) + bias_full))
        context = low_back(attend(mixture[:, :D], mixture[:, D:2 * D], mixture[:, 2 * D:]))
        residual = rows + low_back(matmul(low(context), out_weight) + out_bias)
        hidden = low_back(matmul(low(layer_norm(residual, second_gain, second_shift)), up_weight) + up_bias)
        branch = low_back(matmul(low(smooth_gate(hidden)), down_weight) + down_bias)
        return residual + branch
    sequences = tokens.reshape(N_DP, SEQ, D)
    return lax.map(jax.checkpoint(one_sequence), sequences).reshape(TOKENS, D)

def reference(tokens, first_gain, first_shift, in_weight, in_bias, out_weight, out_bias, second_gain, second_shift, up_weight, up_bias, down_weight, down_bias, cotangent):
    params = [array.astype(jnp.float32) for array in (tokens, first_gain, first_shift, in_weight, in_bias, out_weight, out_bias, second_gain, second_shift, up_weight, up_bias, down_weight, down_bias)]
    output, pullback = jax.vjp(forward, *params)
    gradients = pullback(cotangent.astype(jnp.float32))
    return (output.astype(jnp.bfloat16), gradients[0].astype(jnp.bfloat16), gradients[1], gradients[2], gradients[3], gradients[4], gradients[5], gradients[6], gradients[7], gradients[8], gradients[9], gradients[10], gradients[11], gradients[12])
```

```python
import math

import jax
import jax.numpy as jnp
from jax import lax
from jax.experimental import pallas as pl
from jax.experimental.pallas import tpu as pltpu
from jax.sharding import PartitionSpec as P

HEAD_DIM = 64


epsilon = 1e-05
neg_large = -1e30


def layer_norm(values, gain, shift):
    center = values - jnp.mean(values, axis=-1, keepdims=True)
    spread = jnp.mean(center * center, axis=-1, keepdims=True)
    return center * lax.rsqrt(spread + epsilon) * gain + shift


def norm_back(values, gain, shift, upstream):
    result, pullback = jax.vjp(layer_norm, values, gain, shift)
    return pullback(upstream)


def smooth_gate(values):
    return jax.nn.gelu(values, approximate=True)


def forward_block(state, query_heads, query_pos, key_blk, value_blk, key_pos, factor):
    row_max, row_total, accumulated = state
    scores = (
        jnp.einsum("qhd,khd->hqk", query_heads, key_blk, preferred_element_type=jnp.float32)
        * factor
    )
    allowed = (query_pos[:, None] >= key_pos[None, :])[None]
    scores = jnp.where(allowed, scores, neg_large)
    new_max = jnp.maximum(row_max, jnp.max(scores, axis=-1))
    rescale = jnp.exp(row_max - new_max)
    weights = jnp.where(allowed, jnp.exp(scores - new_max[:, :, None]), 0.0)
    row_total = row_total * rescale + jnp.sum(weights, axis=-1)
    update = jnp.einsum(
        "hqk,khd->qhd", weights.astype(jnp.bfloat16), value_blk, preferred_element_type=jnp.float32
    )
    accumulated = accumulated * rescale.T[:, :, None] + update
    return (new_max, row_total, accumulated)


def pair_grads(
    query_heads, grad_heads, stats, deltas, query_pos, key_blk, value_blk, key_pos, factor
):
    scores = (
        jnp.einsum("qhd,khd->hqk", query_heads, key_blk, preferred_element_type=jnp.float32)
        * factor
    )
    allowed = (query_pos[:, None] >= key_pos[None, :])[None]
    probs = jnp.where(allowed, jnp.exp(scores - stats[:, :, None]), 0.0)
    grad_probs = jnp.einsum(
        "qhd,khd->hqk", grad_heads, value_blk, preferred_element_type=jnp.float32
    )
    grad_scores = (probs * (grad_probs - deltas[:, :, None])).astype(jnp.bfloat16)
    grad_query = (
        jnp.einsum("hqk,khd->qhd", grad_scores, key_blk, preferred_element_type=jnp.float32)
        * factor
    )
    grad_key = (
        jnp.einsum("hqk,qhd->khd", grad_scores, query_heads, preferred_element_type=jnp.float32)
        * factor
    )
    grad_value = jnp.einsum(
        "hqk,qhd->khd", probs.astype(jnp.bfloat16), grad_heads, preferred_element_type=jnp.float32
    )
    return (grad_query, grad_key, grad_value)


def over_keys(state, key_part, value_part, begin_row, top_query, place, block_fn):
    amount, head_count, head_dim = key_part.shape
    stride = math.gcd(amount, 512)
    key_blocks = key_part.reshape(amount // stride, stride, head_count, head_dim)
    value_blocks = value_part.reshape(amount // stride, stride, head_count, head_dim)
    offsets = begin_row + jnp.arange(amount // stride, dtype=jnp.int32) * stride

    def over_step_fn(inner, operands):
        key_blk, value_blk, offset = operands
        key_pos = place(offset + jnp.arange(stride, dtype=jnp.int32))

        def over_compute(current):
            return block_fn(current, key_blk, value_blk, key_pos)

        def keep(current):
            return current

        return (lax.cond(jnp.min(key_pos) <= top_query, over_compute, keep, inner), None)

    state, unused = lax.scan(over_step_fn, state, (key_blocks, value_blocks, offsets))
    return state


def gathered_body(
    tokens,
    first_gain,
    first_shift,
    in_weight,
    in_bias,
    out_weight,
    out_bias,
    second_gain,
    second_shift,
    up_weight,
    up_bias,
    down_weight,
    down_bias,
    cotangent,
):
    (
        first_gain,
        first_shift,
        in_weight,
        in_bias,
        out_weight,
        out_bias,
        second_gain,
        second_shift,
        up_weight,
        up_bias,
        down_weight,
        down_bias,
    ) = (
        lax.all_gather(first_gain, "dp", axis=0, tiled=True),
        lax.all_gather(first_shift, "dp", axis=0, tiled=True),
        lax.all_gather(in_weight, "dp", axis=0, tiled=True),
        lax.all_gather(in_bias, "dp", axis=1, tiled=True),
        lax.all_gather(out_weight, "dp", axis=0, tiled=True),
        lax.all_gather(out_bias, "dp", axis=0, tiled=True),
        lax.all_gather(second_gain, "dp", axis=0, tiled=True),
        lax.all_gather(second_shift, "dp", axis=0, tiled=True),
        lax.all_gather(up_weight, "dp", axis=0, tiled=True),
        lax.all_gather(up_bias, "dp", axis=0, tiled=True),
        lax.all_gather(down_weight, "dp", axis=0, tiled=True),
        lax.all_gather(down_bias, "dp", axis=0, tiled=True),
    )
    rows_dev = tokens.shape[0]
    width = tokens.shape[1]
    head_dim = HEAD_DIM
    head_count = width // head_dim
    factor = 1.0 / math.sqrt(head_dim)
    my_index = lax.axis_index("ctx")

    def place(rows):
        return rows

    query_pos = place(my_index * rows_dev + jnp.arange(rows_dev, dtype=jnp.int32))
    top_query = jnp.max(query_pos)
    inputs = tokens.astype(jnp.float32)
    gain_one = first_gain.astype(jnp.float32)
    shift_one = first_shift.astype(jnp.float32)
    first_low = layer_norm(inputs, gain_one, shift_one).astype(jnp.bfloat16)
    bias_full = jnp.concatenate([in_bias[0], jnp.zeros((width,), jnp.bfloat16), in_bias[1]]).astype(
        jnp.float32
    )
    mixture = (
        jnp.dot(first_low, in_weight, preferred_element_type=jnp.float32) + bias_full
    ).astype(jnp.bfloat16)
    query_rows = mixture[:, :width]
    key_rows = mixture[:, width : 2 * width]
    value_rows = mixture[:, 2 * width :]
    query_heads = query_rows.reshape(rows_dev, head_count, head_dim)

    def forward_fold(state, portion, begin_row):
        key_part, value_part = portion
        amount = key_part.shape[0]

        def block_fn(inner, key_blk, value_blk, key_pos):
            return forward_block(inner, query_heads, query_pos, key_blk, value_blk, key_pos, factor)

        return over_keys(
            state,
            key_part.reshape(amount, head_count, head_dim),
            value_part.reshape(amount, head_count, head_dim),
            begin_row,
            top_query,
            place,
            block_fn,
        )

    start_state = (
        jnp.full((head_count, rows_dev), neg_large, jnp.float32),
        jnp.zeros((head_count, rows_dev), jnp.float32),
        jnp.zeros((rows_dev, head_count, head_dim), jnp.float32),
    )
    row_max, row_total, accumulated = forward_fold(
        start_state,
        (
            lax.all_gather(key_rows, "ctx", axis=0, tiled=True),
            lax.all_gather(value_rows, "ctx", axis=0, tiled=True),
        ),
        jnp.int32(0),
    )
    stats = row_max + jnp.log(row_total)
    context_heads = accumulated / row_total.T[:, :, None]
    context_low = context_heads.reshape(rows_dev, width).astype(jnp.bfloat16)
    residual = (
        inputs
        + jnp.dot(context_low, out_weight, preferred_element_type=jnp.float32)
        + out_bias.astype(jnp.float32)
    )
    gain_two = second_gain.astype(jnp.float32)
    shift_two = second_shift.astype(jnp.float32)
    second_low = layer_norm(residual, gain_two, shift_two).astype(jnp.bfloat16)
    hidden = jnp.dot(second_low, up_weight, preferred_element_type=jnp.float32) + up_bias.astype(
        jnp.float32
    )
    activated, gate_back = jax.vjp(smooth_gate, hidden)
    active_low = activated.astype(jnp.bfloat16)
    layer_out = (
        residual
        + jnp.dot(active_low, down_weight, preferred_element_type=jnp.float32)
        + down_bias.astype(jnp.float32)
    ).astype(jnp.bfloat16)
    upstream = cotangent.astype(jnp.float32)
    down_bias_grad = jnp.sum(upstream, axis=0)
    down_weight_grad = jnp.einsum(
        "tf,td->fd", active_low, cotangent, preferred_element_type=jnp.float32
    )
    (grad_hidden,) = gate_back(
        jnp.einsum("td,fd->tf", cotangent, down_weight, preferred_element_type=jnp.float32)
    )
    grad_hidden = grad_hidden.astype(jnp.bfloat16)
    up_weight_grad = jnp.einsum(
        "td,tf->df", second_low, grad_hidden, preferred_element_type=jnp.float32
    )
    up_bias_grad = jnp.sum(grad_hidden.astype(jnp.float32), axis=0)
    grad_second = jnp.einsum(
        "tf,df->td", grad_hidden, up_weight, preferred_element_type=jnp.float32
    )
    grad_residual, second_gain_grad, second_shift_grad = norm_back(
        residual, gain_two, shift_two, grad_second
    )
    grad_residual = grad_residual + upstream
    grad_attn = grad_residual.astype(jnp.bfloat16)
    out_bias_grad = jnp.sum(grad_attn.astype(jnp.float32), axis=0)
    out_weight_grad = jnp.einsum(
        "td,te->de", context_low, grad_attn, preferred_element_type=jnp.float32
    )
    grad_context = jnp.einsum(
        "te,de->td", grad_attn, out_weight, preferred_element_type=jnp.float32
    ).astype(jnp.bfloat16)
    grad_heads = grad_context.reshape(rows_dev, head_count, head_dim)
    deltas = jnp.sum(grad_heads.astype(jnp.float32) * context_heads, axis=-1).T

    def query_fold(state, portion, begin_row):
        key_part, value_part = portion
        amount = key_part.shape[0]

        def block_fn(inner, key_blk, value_blk, key_pos):
            grad_query, grad_key, grad_value = pair_grads(
                query_heads,
                grad_heads,
                stats,
                deltas,
                query_pos,
                key_blk,
                value_blk,
                key_pos,
                factor,
            )
            return inner + grad_query

        return over_keys(
            state,
            key_part.reshape(amount, head_count, head_dim),
            value_part.reshape(amount, head_count, head_dim),
            begin_row,
            top_query,
            place,
            block_fn,
        )

    zero_heads = jnp.zeros((rows_dev, head_count, head_dim), jnp.float32)
    key_all, value_all = (
        lax.all_gather(key_rows, "ctx", axis=0, tiled=True),
        lax.all_gather(value_rows, "ctx", axis=0, tiled=True),
    )
    grad_query = query_fold(zero_heads, (key_all, value_all), 0)
    amount = lax.axis_size("ctx") * rows_dev
    stride = math.gcd(amount, 512)
    key_part = key_all.reshape(amount // stride, stride, head_count, head_dim)
    value_part = value_all.reshape(amount // stride, stride, head_count, head_dim)
    offsets = jnp.arange(amount // stride, dtype=jnp.int32) * stride

    def key_step_fn(unused, operands):
        key_blk, value_blk, offset = operands
        key_pos = place(offset + jnp.arange(stride, dtype=jnp.int32))

        def key_compute(blocks_in):
            grad_query_part, grad_key, grad_value = pair_grads(
                query_heads,
                grad_heads,
                stats,
                deltas,
                query_pos,
                blocks_in[0],
                blocks_in[1],
                key_pos,
                factor,
            )
            return jnp.concatenate(
                [grad_key.reshape(stride, width), grad_value.reshape(stride, width)], axis=1
            )

        def nothing(blocks_in):
            return jnp.zeros((stride, 2 * width), jnp.float32)

        return (
            unused,
            lax.cond(jnp.min(key_pos) <= top_query, key_compute, nothing, (key_blk, value_blk)),
        )

    unused, stacked = lax.scan(key_step_fn, 0, (key_part, value_part, offsets))
    grad_pairs = lax.psum_scatter(
        stacked.reshape(amount, 2 * width).astype(jnp.bfloat16),
        "ctx",
        scatter_dimension=0,
        tiled=True,
    ).astype(jnp.float32)
    grad_key = grad_pairs[:, :width]
    grad_value = grad_pairs[:, width:]
    grad_mixture = jnp.concatenate(
        [grad_query.reshape(rows_dev, width), grad_key, grad_value], axis=1
    ).astype(jnp.bfloat16)
    in_weight_grad = jnp.einsum(
        "td,te->de", first_low, grad_mixture, preferred_element_type=jnp.float32
    )
    in_bias_grad = jnp.stack(
        [
            jnp.sum(grad_mixture[:, :width].astype(jnp.float32), axis=0),
            jnp.sum(grad_mixture[:, 2 * width :].astype(jnp.float32), axis=0),
        ]
    )
    grad_first = jnp.einsum(
        "te,de->td", grad_mixture, in_weight, preferred_element_type=jnp.float32
    )
    grad_inputs, first_gain_grad, first_shift_grad = norm_back(
        inputs, gain_one, shift_one, grad_first
    )
    tokens_grad = (grad_inputs + grad_residual).astype(jnp.bfloat16)
    (
        first_gain_grad,
        first_shift_grad,
        in_weight_grad,
        in_bias_grad,
        out_weight_grad,
        out_bias_grad,
        second_gain_grad,
        second_shift_grad,
        up_weight_grad,
        up_bias_grad,
        down_weight_grad,
        down_bias_grad,
    ) = (
        lax.psum_scatter(
            first_gain_grad.astype(jnp.bfloat16), "dp", scatter_dimension=0, tiled=True
        ).astype(jnp.float32),
        lax.psum_scatter(
            first_shift_grad.astype(jnp.bfloat16), "dp", scatter_dimension=0, tiled=True
        ).astype(jnp.float32),
        lax.psum_scatter(
            in_weight_grad.astype(jnp.bfloat16), "dp", scatter_dimension=0, tiled=True
        ).astype(jnp.float32),
        lax.psum_scatter(
            in_bias_grad.astype(jnp.bfloat16), "dp", scatter_dimension=1, tiled=True
        ).astype(jnp.float32),
        lax.psum_scatter(
            out_weight_grad.astype(jnp.bfloat16), "dp", scatter_dimension=0, tiled=True
        ).astype(jnp.float32),
        lax.psum_scatter(
            out_bias_grad.astype(jnp.bfloat16), "dp", scatter_dimension=0, tiled=True
        ).astype(jnp.float32),
        lax.psum_scatter(
            second_gain_grad.astype(jnp.bfloat16), "dp", scatter_dimension=0, tiled=True
        ).astype(jnp.float32),
        lax.psum_scatter(
            second_shift_grad.astype(jnp.bfloat16), "dp", scatter_dimension=0, tiled=True
        ).astype(jnp.float32),
        lax.psum_scatter(
            up_weight_grad.astype(jnp.bfloat16), "dp", scatter_dimension=0, tiled=True
        ).astype(jnp.float32),
        lax.psum_scatter(
            up_bias_grad.astype(jnp.bfloat16), "dp", scatter_dimension=0, tiled=True
        ).astype(jnp.float32),
        lax.psum_scatter(
            down_weight_grad.astype(jnp.bfloat16), "dp", scatter_dimension=0, tiled=True
        ).astype(jnp.float32),
        lax.psum_scatter(
            down_bias_grad.astype(jnp.bfloat16), "dp", scatter_dimension=0, tiled=True
        ).astype(jnp.float32),
    )
    (
        first_gain_grad,
        first_shift_grad,
        in_weight_grad,
        in_bias_grad,
        out_weight_grad,
        out_bias_grad,
        second_gain_grad,
        second_shift_grad,
        up_weight_grad,
        up_bias_grad,
        down_weight_grad,
        down_bias_grad,
    ) = (
        lax.psum(first_gain_grad.astype(jnp.bfloat16), "ctx").astype(jnp.float32),
        lax.psum(first_shift_grad.astype(jnp.bfloat16), "ctx").astype(jnp.float32),
        lax.psum(in_weight_grad.astype(jnp.bfloat16), "ctx").astype(jnp.float32),
        lax.psum(in_bias_grad.astype(jnp.bfloat16), "ctx").astype(jnp.float32),
        lax.psum(out_weight_grad.astype(jnp.bfloat16), "ctx").astype(jnp.float32),
        lax.psum(out_bias_grad.astype(jnp.bfloat16), "ctx").astype(jnp.float32),
        lax.psum(second_gain_grad.astype(jnp.bfloat16), "ctx").astype(jnp.float32),
        lax.psum(second_shift_grad.astype(jnp.bfloat16), "ctx").astype(jnp.float32),
        lax.psum(up_weight_grad.astype(jnp.bfloat16), "ctx").astype(jnp.float32),
        lax.psum(up_bias_grad.astype(jnp.bfloat16), "ctx").astype(jnp.float32),
        lax.psum(down_weight_grad.astype(jnp.bfloat16), "ctx").astype(jnp.float32),
        lax.psum(down_bias_grad.astype(jnp.bfloat16), "ctx").astype(jnp.float32),
    )
    return (
        layer_out,
        tokens_grad,
        first_gain_grad,
        first_shift_grad,
        in_weight_grad,
        in_bias_grad,
        out_weight_grad,
        out_bias_grad,
        second_gain_grad,
        second_shift_grad,
        up_weight_grad,
        up_bias_grad,
        down_weight_grad,
        down_bias_grad,
    )


masks = (0, 2, 1, 3)
tile = 256
lanes = 256


def heads_split(mesh):
    return mesh.shape["ctx"] == 4 and mesh.shape["dp"] == 8


def swap(values, axis, bit):
    count = lax.axis_size(axis)
    return lax.ppermute(values, axis, [(i, i ^ bit) for i in range(count)])


def gather_rows(values):
    pair = jnp.concatenate([values, swap(values, "ctx", 2)], axis=0)
    return jnp.concatenate([pair, swap(pair, "ctx", 1)], axis=0)


def scatter_rows(partial):
    half = partial.shape[0] // 2
    quarter = half // 2
    pair = partial[:half] + swap(partial[half:].astype(jnp.bfloat16), "ctx", 1).astype(jnp.float32)
    return pair[:quarter] + swap(pair[quarter:].astype(jnp.bfloat16), "ctx", 2).astype(jnp.float32)


def bit_of(index, bit):
    return (index // bit) % 2 == 1


def dp_gather(values):
    index = lax.axis_index("dp")
    values = values[None, None, None]
    for axis, bit in ((0, 4), (1, 2), (2, 1)):
        other = swap(values, "dp", bit)
        upper = bit_of(index, bit)
        values = jnp.concatenate(
            [jnp.where(upper, other, values), jnp.where(upper, values, other)], axis=axis
        )
    return values.reshape((8,) + values.shape[3:])


def dp_scatter(partial):
    index = lax.axis_index("dp")
    values = partial.reshape((2, 2, 2) + partial.shape[1:])
    for axis, bit in ((2, 1), (1, 2), (0, 4)):
        upper = bit_of(index, bit)
        low = lax.index_in_dim(values, 0, axis, keepdims=False)
        high = lax.index_in_dim(values, 1, axis, keepdims=False)
        sent = jnp.where(upper, low, high).astype(jnp.bfloat16)
        values = jnp.where(upper, high, low) + swap(sent, "dp", bit).astype(jnp.float32)
    return values


def ctx_parts(values):
    index = lax.axis_index("ctx")
    for bit in (2, 1):
        other = swap(values, "ctx", bit)
        values = jnp.stack([values, other]) if bit == 2 else jnp.concatenate([values, other])
    order = [0, 2, 1, 3]
    out = []
    for place in range(4):
        mask = index ^ place
        spot = (mask % 2) * 2 + mask // 2
        out.append(lax.dynamic_index_in_dim(values, spot, 0, keepdims=False))
    return out


def to_heads(own):
    count = own.shape[0] // 4
    blocks = own.reshape(4, count, own.shape[1])
    far = swap(jnp.concatenate([blocks[1], blocks[3]], axis=1), "ctx", 2)
    rows = own.shape[1]
    near = swap(jnp.concatenate([blocks[2], far[:, rows:]], axis=1), "ctx", 1)
    return jnp.concatenate([blocks[0], far[:, :rows], near], axis=1)


def to_rows(mine):
    rows = mine.shape[1] // 4
    part = [mine[:, i * rows : (i + 1) * rows] for i in range(4)]
    far = swap(jnp.concatenate([part[1], part[3]], axis=1), "ctx", 2)
    near = swap(jnp.concatenate([part[2], far[:, rows:]], axis=1), "ctx", 1)
    return jnp.concatenate([part[0], far[:, :rows], near[:, :rows], near[:, rows:]], axis=0)


def dot_nt(left, right):
    return lax.dot_general(left, right, (((1,), (1,)), ((), ())), preferred_element_type=jnp.float32)


def dot_nn(left, right):
    return jnp.dot(left, right, preferred_element_type=jnp.float32)


def dot_tn(left, right):
    return lax.dot_general(left, right, (((0,), (0,)), ((), ())), preferred_element_type=jnp.float32)


def place_of(index, spot, rows):
    return pl.multiple_of((index ^ masks[spot]) * rows, 128)


def diagonal():
    keys = lax.broadcasted_iota(jnp.int32, (tile, tile), 0)
    queries = lax.broadcasted_iota(jnp.int32, (tile, tile), 1)
    return keys <= queries


def attend_kernel(index_ref, mix_ref, low_ref, full_ref, stats_ref, q_s, k_s, v_s, o_s):
    total = mix_ref.shape[0]
    rows = total // 4
    index = index_ref[0]
    for spot in range(4):
        here = pl.ds(spot * rows, rows)
        there = pl.ds(place_of(index, spot, rows), rows)
        q_s[there, :] = mix_ref[here, 0:64] * jnp.bfloat16(0.125)
        k_s[there, :] = mix_ref[here, 64:128]
        v_s[there, :] = mix_ref[here, 128:192]
    allowed = diagonal()
    flipped = v_s[...].astype(jnp.float32).T.astype(jnp.bfloat16)
    for i in range(total // tile):
        begin, end = i * tile, (i + 1) * tile
        queries = q_s[begin:end, :]
        near = jnp.where(allowed, dot_nt(k_s[begin:end, :], queries), neg_large)
        top = jnp.max(near, axis=0, keepdims=True)
        if i > 0:
            past = dot_nt(k_s[:begin, :], queries)
            top = jnp.maximum(top, jnp.max(past, axis=0, keepdims=True))
        near = jnp.exp(near - top)
        amount = jnp.sum(near, axis=0, keepdims=True)
        context = dot_nn(flipped[:, begin:end], near.astype(jnp.bfloat16))
        if i > 0:
            past = jnp.exp(past - top)
            amount = amount + jnp.sum(past, axis=0, keepdims=True)
            context = context + dot_nn(flipped[:, :begin], past.astype(jnp.bfloat16))
        o_s[:, begin:end] = context / amount
        stats_ref[0, :, begin:end] = top + jnp.log(amount)
    for spot in range(4):
        here = pl.ds(spot * rows, rows)
        there = pl.ds(place_of(index, spot, rows), rows)
        block = o_s[:, there]
        full_ref[:, here] = block
        low_ref[:, here] = block.astype(jnp.bfloat16)


def attend(index, mix):
    total = mix.shape[0]
    heads = mix.shape[1] // lanes
    grid_spec = pltpu.PrefetchScalarGridSpec(
        num_scalar_prefetch=1,
        grid=(heads,),
        in_specs=[pl.BlockSpec((total, lanes), lambda h, s: (0, h))],
        out_specs=[
            pl.BlockSpec((HEAD_DIM, total), lambda h, s: (h, 0)),
            pl.BlockSpec((HEAD_DIM, total), lambda h, s: (h, 0)),
            pl.BlockSpec((1, 1, total), lambda h, s: (h, 0, 0)),
        ],
        scratch_shapes=[pltpu.VMEM((total, HEAD_DIM), jnp.bfloat16)] * 3
        + [pltpu.VMEM((HEAD_DIM, total), jnp.float32)],
    )
    pairs = heads * total * total // 2
    return pl.pallas_call(
        attend_kernel,
        grid_spec=grid_spec,
        out_shape=[
            jax.ShapeDtypeStruct((heads * HEAD_DIM, total), jnp.bfloat16),
            jax.ShapeDtypeStruct((heads * HEAD_DIM, total), jnp.float32),
            jax.ShapeDtypeStruct((heads, 1, total), jnp.float32),
        ],
        compiler_params=pltpu.CompilerParams(vmem_limit_bytes=32 * 1024 * 1024),
        cost_estimate=pl.CostEstimate(
            flops=pairs * 4 * 256, bytes_accessed=total * lanes * heads * 4, transcendentals=pairs
        ),
        name="attend",
    )(index, mix)


def attend_back_kernel(
    index_ref, mix_ref, grad_ref, full_ref, stats_ref, out_ref, q_s, k_s, v_s, g_s, d_s, dq_s
):
    total = mix_ref.shape[0]
    rows = total // 4
    index = index_ref[0]
    for spot in range(4):
        here = pl.ds(spot * rows, rows)
        there = pl.ds(place_of(index, spot, rows), rows)
        q_s[there, :] = mix_ref[here, 0:64] * jnp.bfloat16(0.125)
        k_s[there, :] = mix_ref[here, 64:128]
        v_s[there, :] = mix_ref[here, 128:192]
        block = grad_ref[:, here]
        g_s[:, there] = block
        d_s[:, there] = jnp.sum(block.astype(jnp.float32) * full_ref[:, here], axis=0, keepdims=True)
    allowed = diagonal()
    turned = g_s[...].astype(jnp.float32).T.astype(jnp.bfloat16)
    flipped = k_s[...].astype(jnp.float32).T.astype(jnp.bfloat16)
    count = total // tile
    dkv = []
    for j in range(count):
        begin, end = j * tile, (j + 1) * tile
        keys, values = k_s[begin:end, :], v_s[begin:end, :]
        probs = jnp.exp(dot_nt(keys, q_s[begin:, :]) - stats_ref[0, :, begin:])
        near = jnp.where(allowed, probs[:, :tile], 0.0)
        probs = near if j == count - 1 else jnp.concatenate([near, probs[:, tile:]], axis=1)
        scores = (probs * (dot_nn(values, g_s[:, begin:]) - d_s[:, begin:])).astype(jnp.bfloat16)
        grad_value = dot_nn(probs.astype(jnp.bfloat16), turned[begin:, :])
        grad_key = dot_nn(scores, q_s[begin:, :])
        update = dot_nn(flipped[:, begin:end], scores)
        if j == 0:
            dq_s[...] = update
        else:
            dq_s[:, begin:] = dq_s[:, begin:] + update
        k_s[begin:end, :] = grad_key.astype(jnp.bfloat16)
        v_s[begin:end, :] = grad_value.astype(jnp.bfloat16)
    q_s[...] = (dq_s[...] * 0.125).T.astype(jnp.bfloat16)
    for spot in range(4):
        here = pl.ds(spot * rows, rows)
        there = pl.ds(place_of(index, spot, rows), rows)
        out_ref[here, 0:64] = q_s[there, :]
        out_ref[here, 64:128] = k_s[there, :]
        out_ref[here, 128:192] = v_s[there, :]
        out_ref[here, 192:256] = jnp.zeros((rows, 64), jnp.bfloat16)


def attend_back(index, mix, grad, full, stats):
    total = mix.shape[0]
    heads = mix.shape[1] // lanes
    grid_spec = pltpu.PrefetchScalarGridSpec(
        num_scalar_prefetch=1,
        grid=(heads,),
        in_specs=[
            pl.BlockSpec((total, lanes), lambda h, s: (0, h)),
            pl.BlockSpec((HEAD_DIM, total), lambda h, s: (h, 0)),
            pl.BlockSpec((HEAD_DIM, total), lambda h, s: (h, 0)),
            pl.BlockSpec((1, 1, total), lambda h, s: (h, 0, 0)),
        ],
        out_specs=pl.BlockSpec((total, lanes), lambda h, s: (0, h)),
        scratch_shapes=[pltpu.VMEM((total, HEAD_DIM), jnp.bfloat16)] * 3
        + [
            pltpu.VMEM((HEAD_DIM, total), jnp.bfloat16),
            pltpu.VMEM((1, total), jnp.float32),
            pltpu.VMEM((HEAD_DIM, total), jnp.float32),
        ],
    )
    pairs = heads * total * total // 2
    return pl.pallas_call(
        attend_back_kernel,
        grid_spec=grid_spec,
        out_shape=jax.ShapeDtypeStruct(mix.shape, jnp.bfloat16),
        compiler_params=pltpu.CompilerParams(vmem_limit_bytes=40 * 1024 * 1024),
        cost_estimate=pl.CostEstimate(
            flops=pairs * 10 * 256, bytes_accessed=total * lanes * heads * 8, transcendentals=pairs
        ),
        name="attend_back",
    )(index, mix, grad, full, stats)


def normalized(values):
    center = values - jnp.mean(values, axis=-1, keepdims=True)
    spread = jnp.mean(center * center, axis=-1, keepdims=True)
    scale = lax.rsqrt(spread + epsilon)
    return center * scale, scale


def norm_pull(unit, scale, gain, upstream):
    scaled = upstream * gain
    return scale * (
        scaled
        - jnp.mean(scaled, axis=-1, keepdims=True)
        - unit * jnp.mean(scaled * unit, axis=-1, keepdims=True)
    )


def split_body(
    tokens,
    first_gain,
    first_shift,
    in_weight,
    in_bias,
    out_weight,
    out_bias,
    second_gain,
    second_shift,
    up_weight,
    up_bias,
    down_weight,
    down_bias,
    cotangent,
):
    low, wide = jnp.bfloat16, jnp.float32
    width = tokens.shape[1]
    n_dp = lax.axis_size("dp")
    shard = width // n_dp
    ctx = lax.axis_index("ctx")
    heads = width // HEAD_DIM // 4
    own = heads * HEAD_DIM
    index = ctx.astype(jnp.int32).reshape(1)

    in_own = lax.dynamic_index_in_dim(
        in_weight.reshape(shard, 3, 4, heads, HEAD_DIM), ctx, 2, keepdims=False
    )
    in_own = in_own.transpose(0, 2, 1, 3).reshape(shard, 3 * own)
    vectors = jnp.concatenate(
        [first_gain, first_shift, in_bias[0], in_bias[1], out_bias, second_gain, second_shift]
        + [down_bias, up_bias]
    ).reshape(2, 3 * own)
    gathered = dp_gather(jnp.concatenate([in_own, vectors], axis=0))
    in_full = gathered[:, :shard].reshape(width, heads, 3 * HEAD_DIM)
    in_full = jnp.pad(in_full, ((0, 0), (0, 0), (0, lanes - 3 * HEAD_DIM))).reshape(
        width, heads * lanes
    )
    vectors = gathered[:, shard:].reshape(n_dp, 12, shard).astype(wide)
    gain_one, shift_one, query_bias, value_bias, out_bias, gain_two, shift_two, down_bias = [
        vectors[:, i].reshape(width) for i in range(8)
    ]
    up_bias = lax.dynamic_index_in_dim(vectors[:, 8:], ctx, 1, keepdims=False).reshape(width)
    bias_full = jnp.stack(
        [
            lax.dynamic_slice_in_dim(query_bias, ctx * own, own).reshape(heads, HEAD_DIM),
            jnp.zeros((heads, HEAD_DIM), wide),
            lax.dynamic_slice_in_dim(value_bias, ctx * own, own).reshape(heads, HEAD_DIM),
            jnp.zeros((heads, HEAD_DIM), wide),
        ],
        axis=1,
    ).reshape(heads * lanes)

    up_own = lax.dynamic_index_in_dim(
        up_weight.reshape(shard, n_dp, 4, shard), ctx, 2, keepdims=False
    ).reshape(shard, width)
    down_own = lax.dynamic_slice_in_dim(down_weight, ctx * shard, shard, 0)
    up_full = dp_gather(up_own).reshape(width, width)
    down_full = dp_gather(down_own).reshape(width, width)
    out_full = lax.all_gather(out_weight, "dp", axis=0, tiled=True)
    out_rel = jnp.concatenate(
        [lax.dynamic_slice_in_dim(out_full, (ctx ^ mask) * own, own, 0) for mask in masks], axis=0
    )

    unit_one, scale_one = normalized(gather_rows(tokens).astype(wide))
    first_low = (unit_one * gain_one + shift_one).astype(low)
    mix = (dot_nn(first_low, in_full) + bias_full).astype(low)
    context_mine, context_full, stats = attend(index, mix)
    context_low = to_rows(context_mine)
    inputs = tokens.astype(wide)
    residual = inputs + dot_tn(context_low, out_rel) + out_bias

    unit_two, scale_two = normalized(residual)
    second_low = gather_rows((unit_two * gain_two + shift_two).astype(low))
    upstream_all = gather_rows(cotangent)
    hidden = dot_nn(second_low, up_full) + up_bias
    root = math.sqrt(2.0 / math.pi)
    square = hidden * hidden
    bend = jnp.tanh(root * hidden * (1.0 + 0.044715 * square))
    active_low = (0.5 * hidden * (1.0 + bend)).astype(low)
    slope = 0.5 * (1.0 + bend) + 0.5 * hidden * (1.0 - bend * bend) * (
        root * (1.0 + 3 * 0.044715 * square)
    )
    grad_hidden = (slope * dot_nt(upstream_all, down_full)).astype(low)
    grad_second = scatter_rows(dot_nt(grad_hidden, up_full))
    branch = scatter_rows(dot_nn(active_low, down_full))
    layer_out = (residual + branch + down_bias).astype(low)

    down_weight_grad = dot_tn(active_low, upstream_all)
    up_weight_grad = dot_tn(second_low, grad_hidden)
    up_bias_grad = jnp.sum(grad_hidden.astype(wide), axis=0)
    upstream = cotangent.astype(wide)
    down_bias_grad = jnp.sum(upstream, axis=0)
    second_gain_grad = jnp.sum(grad_second * unit_two, axis=0)
    second_shift_grad = jnp.sum(grad_second, axis=0)
    grad_residual = upstream + norm_pull(unit_two, scale_two, gain_two, grad_second)
    grad_attn = grad_residual.astype(low)
    out_bias_grad = jnp.sum(grad_attn.astype(wide), axis=0)
    grad_context = to_heads(dot_nt(out_rel, grad_attn).astype(low))
    out_weight_rel = dot_nn(context_low, grad_attn).reshape(4, own, width)
    out_weight_grad = jnp.concatenate(
        [
            lax.dynamic_index_in_dim(
                out_weight_rel,
                ((ctx ^ place) % 2) * 2 + (ctx ^ place) // 2,
                0,
                keepdims=False,
            )
            for place in range(4)
        ],
        axis=0,
    )

    grad_mix = attend_back(index, mix, grad_context, context_full, stats)
    in_weight_grad = dot_tn(first_low, grad_mix).reshape(width, heads, lanes)
    in_weight_grad = in_weight_grad[:, :, : 3 * HEAD_DIM].reshape(n_dp, shard, 3 * own)
    sums = jnp.sum(grad_mix.astype(wide), axis=0).reshape(heads, 4, HEAD_DIM)
    own_bias = jnp.zeros((2, 4, own), wide)
    own_bias = lax.dynamic_update_slice(
        own_bias, jnp.stack([sums[:, 0].reshape(1, own), sums[:, 2].reshape(1, own)]), (0, ctx, 0)
    ).reshape(2, width)
    grad_first_part = dot_nt(grad_mix, in_full)
    first_gain_grad = jnp.sum(grad_first_part * unit_one, axis=0)
    first_shift_grad = jnp.sum(grad_first_part, axis=0)
    grad_first = scatter_rows(grad_first_part)
    rows = tokens.shape[0]
    tokens_grad = (
        grad_residual + norm_pull(unit_one[:rows], scale_one[:rows], gain_one, grad_first)
    ).astype(low)

    def rows_of(parts, columns):
        flat = jnp.concatenate([part.reshape(n_dp, shard) for part in parts], axis=1)
        return jnp.pad(flat, ((0, 0), (0, columns - flat.shape[1])))[:, None]

    late = [first_gain_grad, first_shift_grad, own_bias[0], own_bias[1]]
    early = [up_bias_grad, down_bias_grad, second_gain_grad, second_shift_grad, out_bias_grad]
    down_mine = dp_scatter(down_weight_grad.reshape(n_dp, shard, width))
    up_mine = dp_scatter(up_weight_grad.reshape(n_dp, shard, width))
    out_mine = dp_scatter(
        jnp.concatenate([out_weight_grad.reshape(n_dp, shard, width), rows_of(early, width)], 1)
    )
    in_mine = dp_scatter(jnp.concatenate([in_weight_grad, rows_of(late, 3 * own)], 1))
    first = ctx_parts(jnp.concatenate([down_mine, up_mine, out_mine]).astype(low))
    last = ctx_parts(in_mine.astype(low))
    first = [part.astype(wide) for part in first]
    last = [part.astype(wide) for part in last]
    down_weight_grad = jnp.concatenate([part[:shard] for part in first], axis=0)
    up_weight_grad = jnp.stack(
        [part[shard : 2 * shard].reshape(shard, n_dp, shard) for part in first], axis=2
    ).reshape(shard, 4 * width)
    summed = first[0][2 * shard :] + first[1][2 * shard :] + first[2][2 * shard :]
    summed = summed + first[3][2 * shard :]
    out_weight_grad = summed[:shard]
    up_bias_grad = jnp.concatenate([part[3 * shard, :shard] for part in first])
    down_bias_grad, second_gain_grad, second_shift_grad, out_bias_grad = [
        summed[shard, i * shard : (i + 1) * shard] for i in range(1, 5)
    ]
    in_weight_grad = jnp.stack(
        [
            part[:shard].reshape(shard, heads, 3, HEAD_DIM).transpose(0, 2, 1, 3)
            for part in last
        ],
        axis=2,
    ).reshape(shard, 3 * width)
    summed = last[0][shard] + last[1][shard] + last[2][shard] + last[3][shard]
    first_gain_grad = summed[:shard]
    first_shift_grad = summed[shard : 2 * shard]
    in_bias_grad = summed[2 * shard : 4 * shard].reshape(2, shard)
    return (
        layer_out,
        tokens_grad,
        first_gain_grad,
        first_shift_grad,
        in_weight_grad,
        in_bias_grad,
        out_weight_grad,
        out_bias_grad,
        second_gain_grad,
        second_shift_grad,
        up_weight_grad,
        up_bias_grad,
        down_weight_grad,
        down_bias_grad,
    )


def solution(mesh):
    in_specs = (
        P(("dp", "ctx"), None),
        P("dp"),
        P("dp"),
        P("dp", None),
        P(None, "dp"),
        P("dp", None),
        P("dp"),
        P("dp"),
        P("dp"),
        P("dp", None),
        P("dp"),
        P("dp", None),
        P("dp"),
        P(("dp", "ctx"), None),
    )
    out_specs = (
        P(("dp", "ctx"), None),
        P(("dp", "ctx"), None),
        P("dp"),
        P("dp"),
        P("dp", None),
        P(None, "dp"),
        P("dp", None),
        P("dp"),
        P("dp"),
        P("dp"),
        P("dp", None),
        P("dp"),
        P("dp", None),
        P("dp"),
    )
    chosen = split_body if heads_split(mesh) else gathered_body
    return jax.shard_map(chosen, mesh=mesh, in_specs=in_specs, out_specs=out_specs, check_vma=False)
```

```python
import math

import jax
import jax.numpy as jnp
from jax import lax
from jax.experimental import pallas as pl
from jax.experimental.pallas import tpu as pltpu
from jax.sharding import PartitionSpec as P

HEAD_DIM = 64


epsilon = 1e-05
neg_large = -1e30


def layer_norm(values, gain, shift):
    center = values - jnp.mean(values, axis=-1, keepdims=True)
    spread = jnp.mean(center * center, axis=-1, keepdims=True)
    return center * lax.rsqrt(spread + epsilon) * gain + shift


def norm_back(values, gain, shift, upstream):
    result, pullback = jax.vjp(layer_norm, values, gain, shift)
    return pullback(upstream)


def smooth_gate(values):
    return jax.nn.gelu(values, approximate=True)


def forward_block(state, query_heads, query_pos, key_blk, value_blk, key_pos, factor):
    row_max, row_total, accumulated = state
    scores = (
        jnp.einsum("qhd,khd->hqk", query_heads, key_blk, preferred_element_type=jnp.float32)
        * factor
    )
    allowed = (query_pos[:, None] >= key_pos[None, :])[None]
    scores = jnp.where(allowed, scores, neg_large)
    new_max = jnp.maximum(row_max, jnp.max(scores, axis=-1))
    rescale = jnp.exp(row_max - new_max)
    weights = jnp.where(allowed, jnp.exp(scores - new_max[:, :, None]), 0.0)
    row_total = row_total * rescale + jnp.sum(weights, axis=-1)
    update = jnp.einsum(
        "hqk,khd->qhd", weights.astype(jnp.bfloat16), value_blk, preferred_element_type=jnp.float32
    )
    accumulated = accumulated * rescale.T[:, :, None] + update
    return (new_max, row_total, accumulated)


def pair_grads(
    query_heads, grad_heads, stats, deltas, query_pos, key_blk, value_blk, key_pos, factor
):
    scores = (
        jnp.einsum("qhd,khd->hqk", query_heads, key_blk, preferred_element_type=jnp.float32)
        * factor
    )
    allowed = (query_pos[:, None] >= key_pos[None, :])[None]
    probs = jnp.where(allowed, jnp.exp(scores - stats[:, :, None]), 0.0)
    grad_probs = jnp.einsum(
        "qhd,khd->hqk", grad_heads, value_blk, preferred_element_type=jnp.float32
    )
    grad_scores = (probs * (grad_probs - deltas[:, :, None])).astype(jnp.bfloat16)
    grad_query = (
        jnp.einsum("hqk,khd->qhd", grad_scores, key_blk, preferred_element_type=jnp.float32)
        * factor
    )
    grad_key = (
        jnp.einsum("hqk,qhd->khd", grad_scores, query_heads, preferred_element_type=jnp.float32)
        * factor
    )
    grad_value = jnp.einsum(
        "hqk,qhd->khd", probs.astype(jnp.bfloat16), grad_heads, preferred_element_type=jnp.float32
    )
    return (grad_query, grad_key, grad_value)


def over_keys(state, key_part, value_part, begin_row, top_query, place, block_fn):
    amount, head_count, head_dim = key_part.shape
    stride = math.gcd(amount, 512)
    key_blocks = key_part.reshape(amount // stride, stride, head_count, head_dim)
    value_blocks = value_part.reshape(amount // stride, stride, head_count, head_dim)
    offsets = begin_row + jnp.arange(amount // stride, dtype=jnp.int32) * stride

    def over_step_fn(inner, operands):
        key_blk, value_blk, offset = operands
        key_pos = place(offset + jnp.arange(stride, dtype=jnp.int32))

        def over_compute(current):
            return block_fn(current, key_blk, value_blk, key_pos)

        def keep(current):
            return current

        return (lax.cond(jnp.min(key_pos) <= top_query, over_compute, keep, inner), None)

    state, unused = lax.scan(over_step_fn, state, (key_blocks, value_blocks, offsets))
    return state


def gathered_body(
    tokens,
    first_gain,
    first_shift,
    in_weight,
    in_bias,
    out_weight,
    out_bias,
    second_gain,
    second_shift,
    up_weight,
    up_bias,
    down_weight,
    down_bias,
    cotangent,
):
    (
        first_gain,
        first_shift,
        in_weight,
        in_bias,
        out_weight,
        out_bias,
        second_gain,
        second_shift,
        up_weight,
        up_bias,
        down_weight,
        down_bias,
    ) = (
        lax.all_gather(first_gain, "dp", axis=0, tiled=True),
        lax.all_gather(first_shift, "dp", axis=0, tiled=True),
        lax.all_gather(in_weight, "dp", axis=0, tiled=True),
        lax.all_gather(in_bias, "dp", axis=1, tiled=True),
        lax.all_gather(out_weight, "dp", axis=0, tiled=True),
        lax.all_gather(out_bias, "dp", axis=0, tiled=True),
        lax.all_gather(second_gain, "dp", axis=0, tiled=True),
        lax.all_gather(second_shift, "dp", axis=0, tiled=True),
        lax.all_gather(up_weight, "dp", axis=0, tiled=True),
        lax.all_gather(up_bias, "dp", axis=0, tiled=True),
        lax.all_gather(down_weight, "dp", axis=0, tiled=True),
        lax.all_gather(down_bias, "dp", axis=0, tiled=True),
    )
    rows_dev = tokens.shape[0]
    width = tokens.shape[1]
    head_dim = HEAD_DIM
    head_count = width // head_dim
    factor = 1.0 / math.sqrt(head_dim)
    my_index = lax.axis_index("ctx")

    def place(rows):
        return rows

    query_pos = place(my_index * rows_dev + jnp.arange(rows_dev, dtype=jnp.int32))
    top_query = jnp.max(query_pos)
    inputs = tokens.astype(jnp.float32)
    gain_one = first_gain.astype(jnp.float32)
    shift_one = first_shift.astype(jnp.float32)
    first_low = layer_norm(inputs, gain_one, shift_one).astype(jnp.bfloat16)
    bias_full = jnp.concatenate([in_bias[0], jnp.zeros((width,), jnp.bfloat16), in_bias[1]]).astype(
        jnp.float32
    )
    mixture = (
        jnp.dot(first_low, in_weight, preferred_element_type=jnp.float32) + bias_full
    ).astype(jnp.bfloat16)
    query_rows = mixture[:, :width]
    key_rows = mixture[:, width : 2 * width]
    value_rows = mixture[:, 2 * width :]
    query_heads = query_rows.reshape(rows_dev, head_count, head_dim)

    def forward_fold(state, portion, begin_row):
        key_part, value_part = portion
        amount = key_part.shape[0]

        def block_fn(inner, key_blk, value_blk, key_pos):
            return forward_block(inner, query_heads, query_pos, key_blk, value_blk, key_pos, factor)

        return over_keys(
            state,
            key_part.reshape(amount, head_count, head_dim),
            value_part.reshape(amount, head_count, head_dim),
            begin_row,
            top_query,
            place,
            block_fn,
        )

    start_state = (
        jnp.full((head_count, rows_dev), neg_large, jnp.float32),
        jnp.zeros((head_count, rows_dev), jnp.float32),
        jnp.zeros((rows_dev, head_count, head_dim), jnp.float32),
    )
    row_max, row_total, accumulated = forward_fold(
        start_state,
        (
            lax.all_gather(key_rows, "ctx", axis=0, tiled=True),
            lax.all_gather(value_rows, "ctx", axis=0, tiled=True),
        ),
        jnp.int32(0),
    )
    stats = row_max + jnp.log(row_total)
    context_heads = accumulated / row_total.T[:, :, None]
    context_low = context_heads.reshape(rows_dev, width).astype(jnp.bfloat16)
    residual = (
        inputs
        + jnp.dot(context_low, out_weight, preferred_element_type=jnp.float32)
        + out_bias.astype(jnp.float32)
    )
    gain_two = second_gain.astype(jnp.float32)
    shift_two = second_shift.astype(jnp.float32)
    second_low = layer_norm(residual, gain_two, shift_two).astype(jnp.bfloat16)
    hidden = jnp.dot(second_low, up_weight, preferred_element_type=jnp.float32) + up_bias.astype(
        jnp.float32
    )
    activated, gate_back = jax.vjp(smooth_gate, hidden)
    active_low = activated.astype(jnp.bfloat16)
    layer_out = (
        residual
        + jnp.dot(active_low, down_weight, preferred_element_type=jnp.float32)
        + down_bias.astype(jnp.float32)
    ).astype(jnp.bfloat16)
    upstream = cotangent.astype(jnp.float32)
    down_bias_grad = jnp.sum(upstream, axis=0)
    down_weight_grad = jnp.einsum(
        "tf,td->fd", active_low, cotangent, preferred_element_type=jnp.float32
    )
    (grad_hidden,) = gate_back(
        jnp.einsum("td,fd->tf", cotangent, down_weight, preferred_element_type=jnp.float32)
    )
    grad_hidden = grad_hidden.astype(jnp.bfloat16)
    up_weight_grad = jnp.einsum(
        "td,tf->df", second_low, grad_hidden, preferred_element_type=jnp.float32
    )
    up_bias_grad = jnp.sum(grad_hidden.astype(jnp.float32), axis=0)
    grad_second = jnp.einsum(
        "tf,df->td", grad_hidden, up_weight, preferred_element_type=jnp.float32
    )
    grad_residual, second_gain_grad, second_shift_grad = norm_back(
        residual, gain_two, shift_two, grad_second
    )
    grad_residual = grad_residual + upstream
    grad_attn = grad_residual.astype(jnp.bfloat16)
    out_bias_grad = jnp.sum(grad_attn.astype(jnp.float32), axis=0)
    out_weight_grad = jnp.einsum(
        "td,te->de", context_low, grad_attn, preferred_element_type=jnp.float32
    )
    grad_context = jnp.einsum(
        "te,de->td", grad_attn, out_weight, preferred_element_type=jnp.float32
    ).astype(jnp.bfloat16)
    grad_heads = grad_context.reshape(rows_dev, head_count, head_dim)
    deltas = jnp.sum(grad_heads.astype(jnp.float32) * context_heads, axis=-1).T

    def query_fold(state, portion, begin_row):
        key_part, value_part = portion
        amount = key_part.shape[0]

        def block_fn(inner, key_blk, value_blk, key_pos):
            grad_query, grad_key, grad_value = pair_grads(
                query_heads,
                grad_heads,
                stats,
                deltas,
                query_pos,
                key_blk,
                value_blk,
                key_pos,
                factor,
            )
            return inner + grad_query

        return over_keys(
            state,
            key_part.reshape(amount, head_count, head_dim),
            value_part.reshape(amount, head_count, head_dim),
            begin_row,
            top_query,
            place,
            block_fn,
        )

    zero_heads = jnp.zeros((rows_dev, head_count, head_dim), jnp.float32)
    key_all, value_all = (
        lax.all_gather(key_rows, "ctx", axis=0, tiled=True),
        lax.all_gather(value_rows, "ctx", axis=0, tiled=True),
    )
    grad_query = query_fold(zero_heads, (key_all, value_all), 0)
    amount = lax.axis_size("ctx") * rows_dev
    stride = math.gcd(amount, 512)
    key_part = key_all.reshape(amount // stride, stride, head_count, head_dim)
    value_part = value_all.reshape(amount // stride, stride, head_count, head_dim)
    offsets = jnp.arange(amount // stride, dtype=jnp.int32) * stride

    def key_step_fn(unused, operands):
        key_blk, value_blk, offset = operands
        key_pos = place(offset + jnp.arange(stride, dtype=jnp.int32))

        def key_compute(blocks_in):
            grad_query_part, grad_key, grad_value = pair_grads(
                query_heads,
                grad_heads,
                stats,
                deltas,
                query_pos,
                blocks_in[0],
                blocks_in[1],
                key_pos,
                factor,
            )
            return jnp.concatenate(
                [grad_key.reshape(stride, width), grad_value.reshape(stride, width)], axis=1
            )

        def nothing(blocks_in):
            return jnp.zeros((stride, 2 * width), jnp.float32)

        return (
            unused,
            lax.cond(jnp.min(key_pos) <= top_query, key_compute, nothing, (key_blk, value_blk)),
        )

    unused, stacked = lax.scan(key_step_fn, 0, (key_part, value_part, offsets))
    grad_pairs = lax.psum_scatter(
        stacked.reshape(amount, 2 * width).astype(jnp.bfloat16),
        "ctx",
        scatter_dimension=0,
        tiled=True,
    ).astype(jnp.float32)
    grad_key = grad_pairs[:, :width]
    grad_value = grad_pairs[:, width:]
    grad_mixture = jnp.concatenate(
        [grad_query.reshape(rows_dev, width), grad_key, grad_value], axis=1
    ).astype(jnp.bfloat16)
    in_weight_grad = jnp.einsum(
        "td,te->de", first_low, grad_mixture, preferred_element_type=jnp.float32
    )
    in_bias_grad = jnp.stack(
        [
            jnp.sum(grad_mixture[:, :width].astype(jnp.float32), axis=0),
            jnp.sum(grad_mixture[:, 2 * width :].astype(jnp.float32), axis=0),
        ]
    )
    grad_first = jnp.einsum(
        "te,de->td", grad_mixture, in_weight, preferred_element_type=jnp.float32
    )
    grad_inputs, first_gain_grad, first_shift_grad = norm_back(
        inputs, gain_one, shift_one, grad_first
    )
    tokens_grad = (grad_inputs + grad_residual).astype(jnp.bfloat16)
    (
        first_gain_grad,
        first_shift_grad,
        in_weight_grad,
        in_bias_grad,
        out_weight_grad,
        out_bias_grad,
        second_gain_grad,
        second_shift_grad,
        up_weight_grad,
        up_bias_grad,
        down_weight_grad,
        down_bias_grad,
    ) = (
        lax.psum_scatter(
            first_gain_grad.astype(jnp.bfloat16), "dp", scatter_dimension=0, tiled=True
        ).astype(jnp.float32),
        lax.psum_scatter(
            first_shift_grad.astype(jnp.bfloat16), "dp", scatter_dimension=0, tiled=True
        ).astype(jnp.float32),
        lax.psum_scatter(
            in_weight_grad.astype(jnp.bfloat16), "dp", scatter_dimension=0, tiled=True
        ).astype(jnp.float32),
        lax.psum_scatter(
            in_bias_grad.astype(jnp.bfloat16), "dp", scatter_dimension=1, tiled=True
        ).astype(jnp.float32),
        lax.psum_scatter(
            out_weight_grad.astype(jnp.bfloat16), "dp", scatter_dimension=0, tiled=True
        ).astype(jnp.float32),
        lax.psum_scatter(
            out_bias_grad.astype(jnp.bfloat16), "dp", scatter_dimension=0, tiled=True
        ).astype(jnp.float32),
        lax.psum_scatter(
            second_gain_grad.astype(jnp.bfloat16), "dp", scatter_dimension=0, tiled=True
        ).astype(jnp.float32),
        lax.psum_scatter(
            second_shift_grad.astype(jnp.bfloat16), "dp", scatter_dimension=0, tiled=True
        ).astype(jnp.float32),
        lax.psum_scatter(
            up_weight_grad.astype(jnp.bfloat16), "dp", scatter_dimension=0, tiled=True
        ).astype(jnp.float32),
        lax.psum_scatter(
            up_bias_grad.astype(jnp.bfloat16), "dp", scatter_dimension=0, tiled=True
        ).astype(jnp.float32),
        lax.psum_scatter(
            down_weight_grad.astype(jnp.bfloat16), "dp", scatter_dimension=0, tiled=True
        ).astype(jnp.float32),
        lax.psum_scatter(
            down_bias_grad.astype(jnp.bfloat16), "dp", scatter_dimension=0, tiled=True
        ).astype(jnp.float32),
    )
    (
        first_gain_grad,
        first_shift_grad,
        in_weight_grad,
        in_bias_grad,
        out_weight_grad,
        out_bias_grad,
        second_gain_grad,
        second_shift_grad,
        up_weight_grad,
        up_bias_grad,
        down_weight_grad,
        down_bias_grad,
    ) = (
        lax.psum(first_gain_grad.astype(jnp.bfloat16), "ctx").astype(jnp.float32),
        lax.psum(first_shift_grad.astype(jnp.bfloat16), "ctx").astype(jnp.float32),
        lax.psum(in_weight_grad.astype(jnp.bfloat16), "ctx").astype(jnp.float32),
        lax.psum(in_bias_grad.astype(jnp.bfloat16), "ctx").astype(jnp.float32),
        lax.psum(out_weight_grad.astype(jnp.bfloat16), "ctx").astype(jnp.float32),
        lax.psum(out_bias_grad.astype(jnp.bfloat16), "ctx").astype(jnp.float32),
        lax.psum(second_gain_grad.astype(jnp.bfloat16), "ctx").astype(jnp.float32),
        lax.psum(second_shift_grad.astype(jnp.bfloat16), "ctx").astype(jnp.float32),
        lax.psum(up_weight_grad.astype(jnp.bfloat16), "ctx").astype(jnp.float32),
        lax.psum(up_bias_grad.astype(jnp.bfloat16), "ctx").astype(jnp.float32),
        lax.psum(down_weight_grad.astype(jnp.bfloat16), "ctx").astype(jnp.float32),
        lax.psum(down_bias_grad.astype(jnp.bfloat16), "ctx").astype(jnp.float32),
    )
    return (
        layer_out,
        tokens_grad,
        first_gain_grad,
        first_shift_grad,
        in_weight_grad,
        in_bias_grad,
        out_weight_grad,
        out_bias_grad,
        second_gain_grad,
        second_shift_grad,
        up_weight_grad,
        up_bias_grad,
        down_weight_grad,
        down_bias_grad,
    )


masks = (0, 2, 1, 3)
dp_masks = (0, 4, 2, 6, 1, 5, 3, 7)
tile = 256
lanes = 256
part = 3 * HEAD_DIM
root = math.sqrt(2.0 / math.pi)
low, wide = jnp.bfloat16, jnp.float32


def heads_split(mesh):
    return mesh.shape["ctx"] == 4 and mesh.shape["dp"] == 8


def swap(values, axis, bit):
    count = lax.axis_size(axis)
    return lax.ppermute(values, axis, [(i, i ^ bit) for i in range(count)])


def dp_gather(values):
    index = lax.axis_index("dp")
    for bit in (1, 2, 4):
        other = swap(values, "dp", bit)
        upper = (index // bit) % 2 == 1
        values = jnp.concatenate(
            [jnp.where(upper, other, values), jnp.where(upper, values, other)], axis=0
        )
    return values


def dp_scatter(partial):
    index = lax.axis_index("dp")
    values = partial.reshape((2, 2, 2) + partial.shape[1:])
    for axis, bit in ((2, 1), (1, 2), (0, 4)):
        mine = (index // bit) % 2
        sent = lax.dynamic_index_in_dim(values, 1 - mine, axis, keepdims=False).astype(low)
        kept = lax.dynamic_index_in_dim(values, mine, axis, keepdims=False)
        values = kept + swap(sent, "dp", bit).astype(wide)
    return values


def sum_all(values):
    for axis, bit in (("dp", 1), ("dp", 2), ("dp", 4), ("ctx", 1), ("ctx", 2)):
        sent = values.astype(low)
        values = sent.astype(wide) + swap(sent, axis, bit).astype(wide)
    return values


def dot_nt(left, right):
    return lax.dot_general(left, right, (((1,), (1,)), ((), ())), preferred_element_type=wide)


def dot_nn(left, right):
    return jnp.dot(left, right, preferred_element_type=wide)


def dot_tn(left, right):
    return lax.dot_general(left, right, (((0,), (0,)), ((), ())), preferred_element_type=wide)


def flip(values):
    return values.astype(wide).T.astype(values.dtype)


def whole(array):
    rank = len(array.shape)
    return pl.BlockSpec(array.shape, lambda *_: (0,) * rank)


def third(place):
    return lambda array: pl.BlockSpec(
        (array.shape[0], array.shape[1] // 3, array.shape[2]), lambda *_: (0, place, 0)
    )


def kernel_call(kernel, name, index, inputs, outputs, flops, exps=0, grid=(1,), scratch=()):
    arrays = [item[0] if isinstance(item, tuple) else item for item in inputs]
    specs = [
        (item[1](item[0]) if callable(item[1]) else item[1]) if isinstance(item, tuple) else whole(item)
        for item in inputs
    ]
    shapes = [item[0] if isinstance(item, tuple) else item for item in outputs]
    out_specs = [item[1] if isinstance(item, tuple) else whole(item) for item in outputs]
    moved = sum(math.prod(a.shape) * a.dtype.itemsize for a in arrays + shapes)
    return pl.pallas_call(
        kernel,
        grid_spec=pltpu.PrefetchScalarGridSpec(
            num_scalar_prefetch=1,
            grid=grid,
            in_specs=specs,
            out_specs=out_specs,
            scratch_shapes=list(scratch),
        ),
        out_shape=shapes,
        compiler_params=pltpu.CompilerParams(vmem_limit_bytes=56 * 1024 * 1024),
        cost_estimate=pl.CostEstimate(flops=flops, bytes_accessed=moved, transcendentals=exps),
        name=name,
    )(index, *arrays)


def shape_of(shape, kind):
    return jax.ShapeDtypeStruct(shape, kind)


def place_of(index, spot, rows):
    return pl.ds(pl.multiple_of((index ^ masks[spot]) * rows, 128), rows)


def diagonal():
    keys = lax.broadcasted_iota(jnp.int32, (tile, tile), 0)
    queries = lax.broadcasted_iota(jnp.int32, (tile, tile), 1)
    return keys <= queries


def unit_of(values):
    center = values - jnp.mean(values, axis=-1, keepdims=True)
    spread = jnp.mean(center * center, axis=-1, keepdims=True)
    scale = lax.rsqrt(spread + epsilon)
    return center * scale, scale


def norm_pull(unit, scale, gain, upstream):
    scaled = upstream * gain
    return scale * (
        scaled
        - jnp.mean(scaled, axis=-1, keepdims=True)
        - unit * jnp.mean(scaled * unit, axis=-1, keepdims=True)
    )


def column_sum(values):
    return jnp.sum(values, axis=0, keepdims=True)


def pick_in_kernel(index_ref, in_ref, out_ref):
    width = in_ref.shape[1] // 3
    own = width // 4
    for ctx in range(4):

        @pl.when(index_ref[0] == ctx)
        def pick():
            for head in range(own // HEAD_DIM):
                for kind in range(3):
                    begin = kind * width + ctx * own + head * HEAD_DIM
                    target = head * part + kind * HEAD_DIM
                    out_ref[:, target : target + HEAD_DIM] = in_ref[:, begin : begin + HEAD_DIM]


def pick_rest_kernel(index_ref, out_weight_ref, up_ref, down_ref, out_ref):
    shard, width = out_weight_ref.shape
    out_ref[:shard, :] = out_weight_ref[...]
    for ctx in range(4):

        @pl.when(index_ref[0] == ctx)
        def pick():
            for owner in range(width // shard):
                begin = owner * 4 * shard + ctx * shard
                out_ref[shard : 2 * shard, owner * shard : (owner + 1) * shard] = up_ref[
                    :, begin : begin + shard
                ]
            out_ref[2 * shard :, :] = down_ref[ctx * shard : (ctx + 1) * shard, :]


def attend_kernel(
    index_ref,
    own_ref,
    far_ref,
    near_ref,
    low_half_ref,
    high_half_ref,
    vector_ref,
    bias_ref,
    first_ref,
    unit_ref,
    weight_ref,
    mix_ref,
    keep_ref,
    send_ref,
    full_ref,
    stats_ref,
    q_s,
    k_s,
    v_s,
    o_s,
):
    rows, width = own_ref.shape
    total = 4 * rows
    index = index_ref[0]
    heads = width // lanes

    @pl.when(pl.program_id(0) == 0)
    def begin_all():
        pieces = [own_ref[...], far_ref[...], near_ref[:rows, :], near_ref[rows:, :]]
        for spot in range(4):
            unit, scale = unit_of(pieces[spot].astype(wide))
            unit_ref[spot * rows : (spot + 1) * rows, :] = unit.astype(low)
            first_ref[spot * rows : (spot + 1) * rows, :] = (
                unit * vector_ref[0:1, :] + vector_ref[1:2, :]
            ).astype(low)
        shard = low_half_ref.shape[0] // 4
        for spot in range(8):
            source = low_half_ref if spot < 4 else high_half_ref
            block = source[(spot % 4) * shard : (spot % 4 + 1) * shard, :]
            there = pl.ds(pl.multiple_of((index_ref[1] ^ dp_masks[spot]) * shard, 32), shard)
            for head in range(heads):
                begin = head * lanes
                weight_ref[there, begin : begin + part] = block[:, head * part : (head + 1) * part]
                weight_ref[there, begin + part : begin + lanes] = jnp.zeros(
                    (shard, lanes - part), low
                )

    here = pl.ds(pl.multiple_of(pl.program_id(0) * lanes, lanes), lanes)
    mix_ref[...] = (dot_nn(first_ref[...], weight_ref[:, here]) + bias_ref[0]).astype(low)
    for spot in range(4):
        here = slice(spot * rows, (spot + 1) * rows)
        there = place_of(index, spot, rows)
        q_s[there, :] = mix_ref[here, 0:64] * jnp.bfloat16(0.125)
        k_s[there, :] = mix_ref[here, 64:128]
        v_s[there, :] = mix_ref[here, 128:192]
    allowed = diagonal()
    flipped = flip(v_s[...])
    for i in range(total // tile):
        begin, end = i * tile, (i + 1) * tile
        queries = q_s[begin:end, :]
        near = jnp.where(allowed, dot_nt(k_s[begin:end, :], queries), neg_large)
        top = jnp.max(near, axis=0, keepdims=True)
        if i > 0:
            past = dot_nt(k_s[:begin, :], queries)
            top = jnp.maximum(top, jnp.max(past, axis=0, keepdims=True))
        near = jnp.exp(near - top)
        amount = column_sum(near)
        context = dot_nn(flipped[:, begin:end], near.astype(low))
        if i > 0:
            past = jnp.exp(past - top)
            amount = amount + column_sum(past)
            context = context + dot_nn(flipped[:, :begin], past.astype(low))
        o_s[:, begin:end] = context / amount
        stats_ref[0, :, begin:end] = top + jnp.log(amount)
    for spot in range(4):
        block = o_s[:, place_of(index, spot, rows)]
        full_ref[:, spot * rows : (spot + 1) * rows] = block
        target = keep_ref if spot in (0, 2) else send_ref
        target[:, (spot // 2) * rows : (spot // 2 + 1) * rows] = block.astype(low)


def attend(index, tokens, far, near, low_half, high_half, vectors, bias):
    rows, width = tokens.shape
    total = 4 * rows
    heads = width // lanes
    features = heads * HEAD_DIM
    by_head = lambda h, s: (h, 0)
    pairs = heads * total * total // 2
    return kernel_call(
        attend_kernel,
        "attend",
        index,
        [tokens, far, near, low_half, high_half, vectors]
        + [(bias, pl.BlockSpec((1, 1, lanes), lambda h, s: (h, 0, 0)))],
        [
            shape_of((total, width), low),
            shape_of((total, width), low),
            shape_of((width, width), low),
            (shape_of((total, width), low), pl.BlockSpec((total, lanes), lambda h, s: (0, h))),
            (shape_of((features, 2 * rows), low), pl.BlockSpec((HEAD_DIM, 2 * rows), by_head)),
            (shape_of((features, 2 * rows), low), pl.BlockSpec((HEAD_DIM, 2 * rows), by_head)),
            (shape_of((features, total), wide), pl.BlockSpec((HEAD_DIM, total), by_head)),
            (
                shape_of((heads, 1, total), wide),
                pl.BlockSpec((1, 1, total), lambda h, s: (h, 0, 0)),
            ),
        ],
        pairs * 4 * 256 + 2 * total * width * width,
        pairs,
        (heads,),
        [pltpu.VMEM((total, HEAD_DIM), low)] * 3 + [pltpu.VMEM((HEAD_DIM, total), wide)],
    )


def project_kernel(
    index_ref,
    keep_ref,
    far_ref,
    near_ref,
    weight_ref,
    tokens_ref,
    vector_ref,
    residual_ref,
    second_ref,
    turned_ref,
):
    rows, width = tokens_ref.shape
    own = width // 4
    pieces = [keep_ref[:, :rows], far_ref[:, :rows], near_ref[:, :rows], near_ref[:, rows:]]
    residual = tokens_ref[...].astype(wide) + vector_ref[4:5, :]
    for spot in range(4):
        turned = flip(pieces[spot])
        group = index_ref[0] ^ masks[spot]
        weights = weight_ref[pl.ds(2 * group, 2)].reshape(own, width)
        residual = residual + dot_nn(turned, weights)
    residual_ref[...] = residual
    unit, scale = unit_of(residual)
    second_ref[...] = (unit * vector_ref[5:6, :] + vector_ref[6:7, :]).astype(low)
    for spot in range(4):
        turned_ref[spot * own : (spot + 1) * own, :] = pieces[spot]


def feed_kernel(
    index_ref,
    own_ref,
    far_ref,
    near_ref,
    up_own_ref,
    up_far_ref,
    up_near_ref,
    up_ref,
    down_ref,
    bias_ref,
    second_ref,
    upstream_ref,
    active_ref,
    hidden_ref,
    kept_ref,
    sent_ref,
    sum_ref,
):
    rows, width = own_ref.shape
    up = up_ref[...].reshape(width, width)
    down = down_ref[...].reshape(width, width)
    rests = [
        (own_ref, up_own_ref, 0),
        (far_ref, up_far_ref, 0),
        (near_ref, up_near_ref, 0),
        (near_ref, up_near_ref, rows),
    ]
    for spot in (2, 3, 0, 1):
        values_ref, grads_ref, begin = rests[spot]
        here = slice(spot * rows, (spot + 1) * rows)
        values = values_ref[begin : begin + rows, :]
        grads = grads_ref[begin : begin + rows, :]
        second_ref[here, :] = values
        upstream_ref[here, :] = grads
        hidden = dot_nn(values, up) + bias_ref[...]
        square = hidden * hidden
        bend = jnp.tanh(root * hidden * (1.0 + 0.044715 * square))
        active_ref[here, :] = (0.5 * hidden * (1.0 + bend)).astype(low)
        slope = 0.5 * (1.0 + bend) + 0.5 * hidden * (1.0 - bend * bend) * (
            root * (1.0 + 3 * 0.044715 * square)
        )
        grad = (slope * dot_nt(grads, down)).astype(low)
        hidden_ref[here, :] = grad
        sums = column_sum(grad.astype(wide))
        sum_ref[...] = sums if spot == 2 else sum_ref[...] + sums
        result = dot_nt(grad, up)
        if spot < 2:
            kept_ref[here, :] = result
        else:
            sent_ref[(spot - 2) * rows : (spot - 1) * rows, :] = result.astype(low)


def branch_kernel(index_ref, active_ref, down_ref, kept_ref, sent_ref):
    half = active_ref.shape[0] // 2
    width = active_ref.shape[1]
    down = down_ref[...].reshape(width, width)
    kept_ref[...] = dot_nn(active_ref[:half, :], down)
    sent_ref[...] = dot_nn(active_ref[half:, :], down).astype(low)


def turn_kernel(
    index_ref,
    kept_ref,
    core_ref,
    far_ref,
    residual_ref,
    cotangent_ref,
    weight_ref,
    vector_ref,
    grad_ref,
    attn_ref,
    keep_ref,
    send_ref,
    sum_ref,
):
    rows, width = residual_ref.shape
    own = width // 4
    grad = kept_ref[:rows, :] + core_ref[:rows, :].astype(wide) + far_ref[...].astype(wide)
    unit, scale = unit_of(residual_ref[...])
    upstream = cotangent_ref[...].astype(wide)
    result = upstream + norm_pull(unit, scale, vector_ref[5:6, :], grad)
    grad_ref[...] = result
    attn = result.astype(low)
    attn_ref[...] = attn
    for spot in range(4):
        group = index_ref[0] ^ masks[spot]
        weights = weight_ref[pl.ds(2 * group, 2)].reshape(own, width)
        block = dot_nt(weights, attn).astype(low)
        target = keep_ref if spot in (0, 2) else send_ref
        target[:, (spot // 2) * rows : (spot // 2 + 1) * rows] = block
    sum_ref[0:1, :] = column_sum(grad * unit)
    sum_ref[1:2, :] = column_sum(grad)
    sum_ref[2:3, :] = column_sum(attn.astype(wide))
    sum_ref[3:4, :] = column_sum(upstream)


def out_grad_kernel(index_ref, turned_ref, attn_ref, out_ref):
    width = turned_ref.shape[0]
    own = width // 4
    shard = own // 2
    for spot in range(4):
        group = index_ref[0] ^ masks[spot]
        block = dot_nn(turned_ref[spot * own : (spot + 1) * own, :], attn_ref[...])
        out_ref[pl.ds(2 * group, 2)] = block.reshape(2, shard, width)


def attend_back_kernel(
    index_ref,
    mix_ref,
    keep_ref,
    far_ref,
    near_ref,
    full_ref,
    stats_ref,
    out_ref,
    sum_ref,
    q_s,
    k_s,
    v_s,
    g_s,
    d_s,
    dq_s,
):
    total = mix_ref.shape[0]
    rows = total // 4
    index = index_ref[0]
    pieces = [keep_ref[:, :rows], far_ref[:, :rows], near_ref[:, :rows], near_ref[:, rows:]]
    for spot in range(4):
        here = slice(spot * rows, (spot + 1) * rows)
        there = place_of(index, spot, rows)
        q_s[there, :] = mix_ref[here, 0:64] * jnp.bfloat16(0.125)
        k_s[there, :] = mix_ref[here, 64:128]
        v_s[there, :] = mix_ref[here, 128:192]
        block = pieces[spot]
        g_s[:, there] = block
        d_s[:, there] = column_sum(block.astype(wide) * full_ref[:, here])
    allowed = diagonal()
    turned = flip(g_s[...])
    flipped = flip(k_s[...])
    count = total // tile
    for j in range(count):
        begin, end = j * tile, (j + 1) * tile
        keys, values = k_s[begin:end, :], v_s[begin:end, :]
        probs = jnp.exp(dot_nt(keys, q_s[begin:, :]) - stats_ref[0, :, begin:])
        near = jnp.where(allowed, probs[:, :tile], 0.0)
        probs = near if j == count - 1 else jnp.concatenate([near, probs[:, tile:]], axis=1)
        scores = (probs * (dot_nn(values, g_s[:, begin:]) - d_s[:, begin:])).astype(low)
        grad_value = dot_nn(probs.astype(low), turned[begin:, :])
        grad_key = dot_nn(scores, q_s[begin:, :])
        update = dot_nn(flipped[:, begin:end], scores)
        if j == 0:
            dq_s[...] = update
        else:
            dq_s[:, begin:] = dq_s[:, begin:] + update
        k_s[begin:end, :] = grad_key.astype(low)
        v_s[begin:end, :] = grad_value.astype(low)
    q_s[...] = (dq_s[...] * 0.125).T.astype(low)
    for spot in range(4):
        here = slice(spot * rows, (spot + 1) * rows)
        there = place_of(index, spot, rows)
        out_ref[here, 0:64] = q_s[there, :]
        out_ref[here, 64:128] = k_s[there, :]
        out_ref[here, 128:192] = v_s[there, :]
        out_ref[here, 192:256] = jnp.zeros((rows, 64), low)
    sum_ref[0] = column_sum(out_ref[...].astype(wide))


def attend_back(index, mix, keep, far, near, full, stats):
    total, width = mix.shape
    heads = width // lanes
    by_head = lambda h, s: (h, 0)
    half = pl.BlockSpec((HEAD_DIM, total // 2), by_head)
    slab = pl.BlockSpec((total, lanes), lambda h, s: (0, h))
    pairs = heads * total * total // 2
    return kernel_call(
        attend_back_kernel,
        "attend_back",
        index,
        [(mix, slab), (keep, half), (far, half), (near, half)]
        + [(full, pl.BlockSpec((HEAD_DIM, total), by_head))]
        + [(stats, pl.BlockSpec((1, 1, total), lambda h, s: (h, 0, 0)))],
        [
            (shape_of((total, width), low), slab),
            (
                shape_of((heads, 1, lanes), wide),
                pl.BlockSpec((1, 1, lanes), lambda h, s: (h, 0, 0)),
            ),
        ],
        pairs * 10 * 256,
        pairs,
        (heads,),
        [pltpu.VMEM((total, HEAD_DIM), low)] * 3
        + [
            pltpu.VMEM((HEAD_DIM, total), low),
            pltpu.VMEM((1, total), wide),
            pltpu.VMEM((HEAD_DIM, total), wide),
        ],
    )


def first_back_kernel(index_ref, mix_ref, weight_ref, unit_ref, kept_ref, sent_ref, sum_ref):
    total = mix_ref.shape[0]
    rows = total // 4
    for spot in (2, 3, 0, 1):
        here = slice(spot * rows, (spot + 1) * rows)
        grad = dot_nt(mix_ref[here, :], weight_ref[...])
        gain = column_sum(grad * unit_ref[here, :].astype(wide))
        shift = column_sum(grad)
        sums = jnp.concatenate([gain, shift], axis=0)
        sum_ref[...] = sums if spot == 2 else sum_ref[...] + sums
        if spot < 2:
            kept_ref[here, :] = grad
        else:
            sent_ref[(spot - 2) * rows : (spot - 1) * rows, :] = grad.astype(low)


def tokens_kernel(
    index_ref, kept_ref, core_ref, far_ref, tokens_ref, residual_ref, vector_ref, out_ref
):
    rows = tokens_ref.shape[0]
    grad = kept_ref[:rows, :] + core_ref[:rows, :].astype(wide) + far_ref[...].astype(wide)
    unit, scale = unit_of(tokens_ref[...].astype(wide))
    result = residual_ref[...] + norm_pull(unit, scale, vector_ref[0:1, :], grad)
    out_ref[...] = result.astype(low)


def spread_kernel(index_ref, own_ref, far_ref, near_ref, up_ref, down_ref, out_ref):
    width = own_ref.shape[1]
    shard = own_ref.shape[0] // 3
    total = None
    for ctx in range(4):
        for spot in range(4):

            @pl.when((index_ref[0] ^ ctx) == masks[spot])
            def put():
                source = [own_ref, far_ref, near_ref, near_ref][spot]
                base = 3 * shard if spot == 3 else 0
                block = source[base : base + shard, :].astype(wide)
                for owner in range(width // shard):
                    begin = (owner * 4 + ctx) * shard
                    up_ref[:, begin : begin + shard] = block[:, owner * shard : (owner + 1) * shard]
                down_ref[ctx * shard : (ctx + 1) * shard, :] = source[
                    base + shard : base + 2 * shard, :
                ].astype(wide)
                last = source[base + 2 * shard : base + 3 * shard, :].astype(wide)
                if ctx == 0:
                    out_ref[...] = last
                else:
                    out_ref[...] = out_ref[...] + last


def spread_in_kernel(index_ref, own_ref, far_ref, near_ref, in_ref):
    shard, width = own_ref.shape
    own = width // 4
    for ctx in range(4):
        for spot in range(4):

            @pl.when((index_ref[0] ^ ctx) == masks[spot])
            def put():
                source = [own_ref, far_ref, near_ref, near_ref][spot]
                base = shard if spot == 3 else 0
                block = source[base : base + shard, :].astype(wide)
                for head in range(own // HEAD_DIM):
                    for kind in range(3):
                        begin = kind * width + ctx * own + head * HEAD_DIM
                        target = head * lanes + kind * HEAD_DIM
                        in_ref[:, begin : begin + HEAD_DIM] = block[:, target : target + HEAD_DIM]


def pieces_of(values):
    far = swap(values, "ctx", 2)
    return values, far, swap(jnp.concatenate([values, far], axis=0), "ctx", 1)


def split_body(
    tokens,
    first_gain,
    first_shift,
    in_weight,
    in_bias,
    out_weight,
    out_bias,
    second_gain,
    second_shift,
    up_weight,
    up_bias,
    down_weight,
    down_bias,
    cotangent,
):
    rows, width = tokens.shape
    total = 4 * rows
    n_dp = lax.axis_size("dp")
    shard = width // n_dp
    ctx = lax.axis_index("ctx")
    owner = lax.axis_index("dp")
    heads = width // HEAD_DIM // 4
    own = heads * HEAD_DIM
    index = jnp.stack([ctx, owner]).astype(jnp.int32)

    (in_own,) = kernel_call(
        pick_in_kernel, "pick_in", index, [in_weight], [shape_of((shard, 3 * own), low)], 0
    )
    in_two = jnp.concatenate([in_own, swap(in_own, "dp", 4)], axis=0)
    low_half = jnp.concatenate([in_two, swap(in_two, "dp", 2)], axis=0)
    high_half = swap(low_half, "dp", 1)
    (rest,) = kernel_call(
        pick_rest_kernel,
        "pick_rest",
        index,
        [out_weight, up_weight, down_weight],
        [shape_of((3 * shard, width), low)],
        0,
    )
    rest = lax.all_gather(rest, "dp", axis=0, tiled=False)
    vectors = jnp.concatenate(
        [first_gain, first_shift, in_bias[0], in_bias[1], out_bias, second_gain, second_shift]
        + [down_bias, up_bias]
    ).reshape(1, 12 * shard)
    vectors = dp_gather(vectors).reshape(n_dp, 12, shard).transpose(1, 0, 2).reshape(12, width)
    vectors = vectors.astype(wide)
    hidden_bias = lax.dynamic_slice_in_dim(vectors, 8 + ctx, 1, 0)
    zeros = jnp.zeros((heads, HEAD_DIM), wide)
    mine = lax.dynamic_slice(vectors, (2, ctx * own), (2, own)).reshape(2, heads, HEAD_DIM)
    bias_full = jnp.concatenate([mine[0], zeros, mine[1], zeros], axis=1).reshape(heads, 1, lanes)

    tokens_own, tokens_far, tokens_near = pieces_of(tokens)
    first_low, unit_one, in_full, mix, keep, send, context_full, stats = attend(
        index, tokens_own, tokens_far, tokens_near, low_half, high_half, vectors, bias_full
    )

    def exchange(keep, send):
        far = swap(send, "ctx", 2)
        near = swap(jnp.concatenate([keep[:, rows:], far[:, rows:]], axis=1), "ctx", 1)
        return far, near

    far, near = exchange(keep, send)
    out_block = (rest, third(0))
    up_block = (rest, third(1))
    down_block = (rest, third(2))
    residual, second_low, turned = kernel_call(
        project_kernel,
        "project",
        index,
        [keep, far, near, out_block, tokens, vectors],
        [
            shape_of((rows, width), wide),
            shape_of((rows, width), low),
            shape_of((width, rows), low),
        ],
        2 * rows * width * width,
    )

    big = 2 * total * width * width
    second, upstream, active, grad_hidden, kept, sent, up_bias_grad = kernel_call(
        feed_kernel,
        "feed",
        index,
        [*pieces_of(second_low), *pieces_of(cotangent), up_block, down_block, hidden_bias],
        [shape_of((total, width), low)] * 4
        + [shape_of((total // 2, width), wide), shape_of((total // 2, width), low)]
        + [shape_of((1, width), wide)],
        3 * big,
        total * width,
    )
    core = swap(sent, "ctx", 1)
    far = swap((kept[rows:] + core[rows:].astype(wide)).astype(low), "ctx", 2)
    grad_residual, grad_attn, keep, send, sums_two = kernel_call(
        turn_kernel,
        "turn",
        index,
        [kept, core, far, residual, cotangent, out_block, vectors],
        [
            shape_of((rows, width), wide),
            shape_of((rows, width), low),
            shape_of((own, 2 * rows), low),
            shape_of((own, 2 * rows), low),
            shape_of((4, width), wide),
        ],
        2 * rows * width * width,
    )
    far, near = exchange(keep, send)
    grad_mix, bias_sums = attend_back(index, mix, keep, far, near, context_full, stats)

    up_weight_grad = dot_tn(second, grad_hidden).astype(low).reshape(n_dp, shard, width)
    down_weight_grad = dot_tn(active, upstream).astype(low).reshape(n_dp, shard, width)
    feed_mine = lax.psum_scatter(
        jnp.concatenate([up_weight_grad, down_weight_grad], axis=1),
        "dp",
        scatter_dimension=0,
        tiled=False,
    )
    kept, sent = kernel_call(
        branch_kernel,
        "branch",
        index,
        [active, down_block],
        [shape_of((total // 2, width), wide), shape_of((total // 2, width), low)],
        big,
    )
    core = swap(sent, "ctx", 1)
    far = swap((kept[rows:] + core[rows:].astype(wide)).astype(low), "ctx", 2)
    branch = kept[:rows] + core[:rows].astype(wide) + far.astype(wide)
    layer_out = (residual + branch + vectors[7]).astype(low)
    (out_weight_grad,) = kernel_call(
        out_grad_kernel,
        "out_grad",
        index,
        [turned, grad_attn],
        [shape_of((n_dp, shard, width), wide)],
        2 * rows * width * width,
    )
    out_mine = dp_scatter(out_weight_grad)

    kept, sent, sums_one = kernel_call(
        first_back_kernel,
        "first_back",
        index,
        [grad_mix, in_full, unit_one],
        [shape_of((total // 2, width), wide), shape_of((total // 2, width), low)]
        + [shape_of((2, width), wide)],
        big,
    )
    in_mine = dp_scatter(dot_tn(first_low, grad_mix).reshape(n_dp, shard, width))
    core = swap(sent, "ctx", 1)
    far = swap((kept[rows:] + core[rows:].astype(wide)).astype(low), "ctx", 2)
    (tokens_grad,) = kernel_call(
        tokens_kernel,
        "tokens",
        index,
        [kept, core, far, tokens, grad_residual, vectors],
        [shape_of((rows, width), low)],
        0,
    )

    bias_sums = bias_sums.reshape(heads, 4, HEAD_DIM)
    bias_sums = jnp.stack([bias_sums[:, 0].reshape(own), bias_sums[:, 2].reshape(own)])
    column = jnp.arange(width, dtype=jnp.int32)[None, :] // own == ctx
    in_rows = jnp.where(column, jnp.tile(bias_sums, (1, 4)), 0.0)
    up_rows = jnp.where(jnp.arange(4, dtype=jnp.int32)[:, None] == ctx, up_bias_grad, 0.0)
    sums = sum_all(jnp.concatenate([sums_one, in_rows, sums_two, up_rows], axis=0))
    sums = lax.dynamic_slice_in_dim(sums, owner * shard, shard, 1)

    feed = jnp.concatenate([feed_mine.reshape(2 * shard, width), out_mine.astype(low)], axis=0)
    up_weight_grad, down_weight_grad, out_weight_grad = kernel_call(
        spread_kernel,
        "spread",
        index,
        [*pieces_of(feed)],
        [
            shape_of((shard, 4 * width), wide),
            shape_of((4 * shard, width), wide),
            shape_of((shard, width), wide),
        ],
        0,
    )
    (in_weight_grad,) = kernel_call(
        spread_in_kernel,
        "spread_in",
        index,
        [*pieces_of(in_mine.astype(low))],
        [shape_of((shard, 3 * width), wide)],
        0,
    )
    return (
        layer_out,
        tokens_grad,
        sums[0],
        sums[1],
        in_weight_grad,
        sums[2:4],
        out_weight_grad,
        sums[6],
        sums[4],
        sums[5],
        up_weight_grad,
        sums[8:12].reshape(4 * shard),
        down_weight_grad,
        sums[7],
    )


def solution(mesh):
    in_specs = (
        P(("dp", "ctx"), None),
        P("dp"),
        P("dp"),
        P("dp", None),
        P(None, "dp"),
        P("dp", None),
        P("dp"),
        P("dp"),
        P("dp"),
        P("dp", None),
        P("dp"),
        P("dp", None),
        P("dp"),
        P(("dp", "ctx"), None),
    )
    out_specs = (
        P(("dp", "ctx"), None),
        P(("dp", "ctx"), None),
        P("dp"),
        P("dp"),
        P("dp", None),
        P(None, "dp"),
        P("dp", None),
        P("dp"),
        P("dp"),
        P("dp"),
        P("dp", None),
        P("dp"),
        P("dp", None),
        P("dp"),
    )
    chosen = split_body if heads_split(mesh) else gathered_body
    return jax.shard_map(chosen, mesh=mesh, in_specs=in_specs, out_specs=out_specs, check_vma=False)
```

```python
import math

import jax
import jax.numpy as jnp
from jax import lax
from jax.experimental import pallas as pl
from jax.experimental.pallas import tpu as pltpu
from jax.sharding import PartitionSpec as P

HEAD_DIM = 64


epsilon = 1e-05
neg_large = -1e30


def layer_norm(values, gain, shift):
    center = values - jnp.mean(values, axis=-1, keepdims=True)
    spread = jnp.mean(center * center, axis=-1, keepdims=True)
    return center * lax.rsqrt(spread + epsilon) * gain + shift


def norm_back(values, gain, shift, upstream):
    result, pullback = jax.vjp(layer_norm, values, gain, shift)
    return pullback(upstream)


def smooth_gate(values):
    return jax.nn.gelu(values, approximate=True)


def forward_block(state, query_heads, query_pos, key_blk, value_blk, key_pos, factor):
    row_max, row_total, accumulated = state
    scores = (
        jnp.einsum("qhd,khd->hqk", query_heads, key_blk, preferred_element_type=jnp.float32)
        * factor
    )
    allowed = (query_pos[:, None] >= key_pos[None, :])[None]
    scores = jnp.where(allowed, scores, neg_large)
    new_max = jnp.maximum(row_max, jnp.max(scores, axis=-1))
    rescale = jnp.exp(row_max - new_max)
    weights = jnp.where(allowed, jnp.exp(scores - new_max[:, :, None]), 0.0)
    row_total = row_total * rescale + jnp.sum(weights, axis=-1)
    update = jnp.einsum(
        "hqk,khd->qhd", weights.astype(jnp.bfloat16), value_blk, preferred_element_type=jnp.float32
    )
    accumulated = accumulated * rescale.T[:, :, None] + update
    return (new_max, row_total, accumulated)


def pair_grads(
    query_heads, grad_heads, stats, deltas, query_pos, key_blk, value_blk, key_pos, factor
):
    scores = (
        jnp.einsum("qhd,khd->hqk", query_heads, key_blk, preferred_element_type=jnp.float32)
        * factor
    )
    allowed = (query_pos[:, None] >= key_pos[None, :])[None]
    probs = jnp.where(allowed, jnp.exp(scores - stats[:, :, None]), 0.0)
    grad_probs = jnp.einsum(
        "qhd,khd->hqk", grad_heads, value_blk, preferred_element_type=jnp.float32
    )
    grad_scores = (probs * (grad_probs - deltas[:, :, None])).astype(jnp.bfloat16)
    grad_query = (
        jnp.einsum("hqk,khd->qhd", grad_scores, key_blk, preferred_element_type=jnp.float32)
        * factor
    )
    grad_key = (
        jnp.einsum("hqk,qhd->khd", grad_scores, query_heads, preferred_element_type=jnp.float32)
        * factor
    )
    grad_value = jnp.einsum(
        "hqk,qhd->khd", probs.astype(jnp.bfloat16), grad_heads, preferred_element_type=jnp.float32
    )
    return (grad_query, grad_key, grad_value)


def over_keys(state, key_part, value_part, begin_row, top_query, place, block_fn):
    amount, head_count, head_dim = key_part.shape
    stride = math.gcd(amount, 512)
    key_blocks = key_part.reshape(amount // stride, stride, head_count, head_dim)
    value_blocks = value_part.reshape(amount // stride, stride, head_count, head_dim)
    offsets = begin_row + jnp.arange(amount // stride, dtype=jnp.int32) * stride

    def over_step_fn(inner, operands):
        key_blk, value_blk, offset = operands
        key_pos = place(offset + jnp.arange(stride, dtype=jnp.int32))

        def over_compute(current):
            return block_fn(current, key_blk, value_blk, key_pos)

        def keep(current):
            return current

        return (lax.cond(jnp.min(key_pos) <= top_query, over_compute, keep, inner), None)

    state, unused = lax.scan(over_step_fn, state, (key_blocks, value_blocks, offsets))
    return state


def gathered_body(
    tokens,
    first_gain,
    first_shift,
    in_weight,
    in_bias,
    out_weight,
    out_bias,
    second_gain,
    second_shift,
    up_weight,
    up_bias,
    down_weight,
    down_bias,
    cotangent,
):
    (
        first_gain,
        first_shift,
        in_weight,
        in_bias,
        out_weight,
        out_bias,
        second_gain,
        second_shift,
        up_weight,
        up_bias,
        down_weight,
        down_bias,
    ) = (
        lax.all_gather(first_gain, "dp", axis=0, tiled=True),
        lax.all_gather(first_shift, "dp", axis=0, tiled=True),
        lax.all_gather(in_weight, "dp", axis=0, tiled=True),
        lax.all_gather(in_bias, "dp", axis=1, tiled=True),
        lax.all_gather(out_weight, "dp", axis=0, tiled=True),
        lax.all_gather(out_bias, "dp", axis=0, tiled=True),
        lax.all_gather(second_gain, "dp", axis=0, tiled=True),
        lax.all_gather(second_shift, "dp", axis=0, tiled=True),
        lax.all_gather(up_weight, "dp", axis=0, tiled=True),
        lax.all_gather(up_bias, "dp", axis=0, tiled=True),
        lax.all_gather(down_weight, "dp", axis=0, tiled=True),
        lax.all_gather(down_bias, "dp", axis=0, tiled=True),
    )
    rows_dev = tokens.shape[0]
    width = tokens.shape[1]
    head_dim = HEAD_DIM
    head_count = width // head_dim
    factor = 1.0 / math.sqrt(head_dim)
    my_index = lax.axis_index("ctx")

    def place(rows):
        return rows

    query_pos = place(my_index * rows_dev + jnp.arange(rows_dev, dtype=jnp.int32))
    top_query = jnp.max(query_pos)
    inputs = tokens.astype(jnp.float32)
    gain_one = first_gain.astype(jnp.float32)
    shift_one = first_shift.astype(jnp.float32)
    first_low = layer_norm(inputs, gain_one, shift_one).astype(jnp.bfloat16)
    bias_full = jnp.concatenate([in_bias[0], jnp.zeros((width,), jnp.bfloat16), in_bias[1]]).astype(
        jnp.float32
    )
    mixture = (
        jnp.dot(first_low, in_weight, preferred_element_type=jnp.float32) + bias_full
    ).astype(jnp.bfloat16)
    query_rows = mixture[:, :width]
    key_rows = mixture[:, width : 2 * width]
    value_rows = mixture[:, 2 * width :]
    query_heads = query_rows.reshape(rows_dev, head_count, head_dim)

    def forward_fold(state, portion, begin_row):
        key_part, value_part = portion
        amount = key_part.shape[0]

        def block_fn(inner, key_blk, value_blk, key_pos):
            return forward_block(inner, query_heads, query_pos, key_blk, value_blk, key_pos, factor)

        return over_keys(
            state,
            key_part.reshape(amount, head_count, head_dim),
            value_part.reshape(amount, head_count, head_dim),
            begin_row,
            top_query,
            place,
            block_fn,
        )

    start_state = (
        jnp.full((head_count, rows_dev), neg_large, jnp.float32),
        jnp.zeros((head_count, rows_dev), jnp.float32),
        jnp.zeros((rows_dev, head_count, head_dim), jnp.float32),
    )
    row_max, row_total, accumulated = forward_fold(
        start_state,
        (
            lax.all_gather(key_rows, "ctx", axis=0, tiled=True),
            lax.all_gather(value_rows, "ctx", axis=0, tiled=True),
        ),
        jnp.int32(0),
    )
    stats = row_max + jnp.log(row_total)
    context_heads = accumulated / row_total.T[:, :, None]
    context_low = context_heads.reshape(rows_dev, width).astype(jnp.bfloat16)
    residual = (
        inputs
        + jnp.dot(context_low, out_weight, preferred_element_type=jnp.float32)
        + out_bias.astype(jnp.float32)
    )
    gain_two = second_gain.astype(jnp.float32)
    shift_two = second_shift.astype(jnp.float32)
    second_low = layer_norm(residual, gain_two, shift_two).astype(jnp.bfloat16)
    hidden = jnp.dot(second_low, up_weight, preferred_element_type=jnp.float32) + up_bias.astype(
        jnp.float32
    )
    activated, gate_back = jax.vjp(smooth_gate, hidden)
    active_low = activated.astype(jnp.bfloat16)
    layer_out = (
        residual
        + jnp.dot(active_low, down_weight, preferred_element_type=jnp.float32)
        + down_bias.astype(jnp.float32)
    ).astype(jnp.bfloat16)
    upstream = cotangent.astype(jnp.float32)
    down_bias_grad = jnp.sum(upstream, axis=0)
    down_weight_grad = jnp.einsum(
        "tf,td->fd", active_low, cotangent, preferred_element_type=jnp.float32
    )
    (grad_hidden,) = gate_back(
        jnp.einsum("td,fd->tf", cotangent, down_weight, preferred_element_type=jnp.float32)
    )
    grad_hidden = grad_hidden.astype(jnp.bfloat16)
    up_weight_grad = jnp.einsum(
        "td,tf->df", second_low, grad_hidden, preferred_element_type=jnp.float32
    )
    up_bias_grad = jnp.sum(grad_hidden.astype(jnp.float32), axis=0)
    grad_second = jnp.einsum(
        "tf,df->td", grad_hidden, up_weight, preferred_element_type=jnp.float32
    )
    grad_residual, second_gain_grad, second_shift_grad = norm_back(
        residual, gain_two, shift_two, grad_second
    )
    grad_residual = grad_residual + upstream
    grad_attn = grad_residual.astype(jnp.bfloat16)
    out_bias_grad = jnp.sum(grad_attn.astype(jnp.float32), axis=0)
    out_weight_grad = jnp.einsum(
        "td,te->de", context_low, grad_attn, preferred_element_type=jnp.float32
    )
    grad_context = jnp.einsum(
        "te,de->td", grad_attn, out_weight, preferred_element_type=jnp.float32
    ).astype(jnp.bfloat16)
    grad_heads = grad_context.reshape(rows_dev, head_count, head_dim)
    deltas = jnp.sum(grad_heads.astype(jnp.float32) * context_heads, axis=-1).T

    def query_fold(state, portion, begin_row):
        key_part, value_part = portion
        amount = key_part.shape[0]

        def block_fn(inner, key_blk, value_blk, key_pos):
            grad_query, grad_key, grad_value = pair_grads(
                query_heads,
                grad_heads,
                stats,
                deltas,
                query_pos,
                key_blk,
                value_blk,
                key_pos,
                factor,
            )
            return inner + grad_query

        return over_keys(
            state,
            key_part.reshape(amount, head_count, head_dim),
            value_part.reshape(amount, head_count, head_dim),
            begin_row,
            top_query,
            place,
            block_fn,
        )

    zero_heads = jnp.zeros((rows_dev, head_count, head_dim), jnp.float32)
    key_all, value_all = (
        lax.all_gather(key_rows, "ctx", axis=0, tiled=True),
        lax.all_gather(value_rows, "ctx", axis=0, tiled=True),
    )
    grad_query = query_fold(zero_heads, (key_all, value_all), 0)
    amount = lax.axis_size("ctx") * rows_dev
    stride = math.gcd(amount, 512)
    key_part = key_all.reshape(amount // stride, stride, head_count, head_dim)
    value_part = value_all.reshape(amount // stride, stride, head_count, head_dim)
    offsets = jnp.arange(amount // stride, dtype=jnp.int32) * stride

    def key_step_fn(unused, operands):
        key_blk, value_blk, offset = operands
        key_pos = place(offset + jnp.arange(stride, dtype=jnp.int32))

        def key_compute(blocks_in):
            grad_query_part, grad_key, grad_value = pair_grads(
                query_heads,
                grad_heads,
                stats,
                deltas,
                query_pos,
                blocks_in[0],
                blocks_in[1],
                key_pos,
                factor,
            )
            return jnp.concatenate(
                [grad_key.reshape(stride, width), grad_value.reshape(stride, width)], axis=1
            )

        def nothing(blocks_in):
            return jnp.zeros((stride, 2 * width), jnp.float32)

        return (
            unused,
            lax.cond(jnp.min(key_pos) <= top_query, key_compute, nothing, (key_blk, value_blk)),
        )

    unused, stacked = lax.scan(key_step_fn, 0, (key_part, value_part, offsets))
    grad_pairs = lax.psum_scatter(
        stacked.reshape(amount, 2 * width).astype(jnp.bfloat16),
        "ctx",
        scatter_dimension=0,
        tiled=True,
    ).astype(jnp.float32)
    grad_key = grad_pairs[:, :width]
    grad_value = grad_pairs[:, width:]
    grad_mixture = jnp.concatenate(
        [grad_query.reshape(rows_dev, width), grad_key, grad_value], axis=1
    ).astype(jnp.bfloat16)
    in_weight_grad = jnp.einsum(
        "td,te->de", first_low, grad_mixture, preferred_element_type=jnp.float32
    )
    in_bias_grad = jnp.stack(
        [
            jnp.sum(grad_mixture[:, :width].astype(jnp.float32), axis=0),
            jnp.sum(grad_mixture[:, 2 * width :].astype(jnp.float32), axis=0),
        ]
    )
    grad_first = jnp.einsum(
        "te,de->td", grad_mixture, in_weight, preferred_element_type=jnp.float32
    )
    grad_inputs, first_gain_grad, first_shift_grad = norm_back(
        inputs, gain_one, shift_one, grad_first
    )
    tokens_grad = (grad_inputs + grad_residual).astype(jnp.bfloat16)
    (
        first_gain_grad,
        first_shift_grad,
        in_weight_grad,
        in_bias_grad,
        out_weight_grad,
        out_bias_grad,
        second_gain_grad,
        second_shift_grad,
        up_weight_grad,
        up_bias_grad,
        down_weight_grad,
        down_bias_grad,
    ) = (
        lax.psum_scatter(
            first_gain_grad.astype(jnp.bfloat16), "dp", scatter_dimension=0, tiled=True
        ).astype(jnp.float32),
        lax.psum_scatter(
            first_shift_grad.astype(jnp.bfloat16), "dp", scatter_dimension=0, tiled=True
        ).astype(jnp.float32),
        lax.psum_scatter(
            in_weight_grad.astype(jnp.bfloat16), "dp", scatter_dimension=0, tiled=True
        ).astype(jnp.float32),
        lax.psum_scatter(
            in_bias_grad.astype(jnp.bfloat16), "dp", scatter_dimension=1, tiled=True
        ).astype(jnp.float32),
        lax.psum_scatter(
            out_weight_grad.astype(jnp.bfloat16), "dp", scatter_dimension=0, tiled=True
        ).astype(jnp.float32),
        lax.psum_scatter(
            out_bias_grad.astype(jnp.bfloat16), "dp", scatter_dimension=0, tiled=True
        ).astype(jnp.float32),
        lax.psum_scatter(
            second_gain_grad.astype(jnp.bfloat16), "dp", scatter_dimension=0, tiled=True
        ).astype(jnp.float32),
        lax.psum_scatter(
            second_shift_grad.astype(jnp.bfloat16), "dp", scatter_dimension=0, tiled=True
        ).astype(jnp.float32),
        lax.psum_scatter(
            up_weight_grad.astype(jnp.bfloat16), "dp", scatter_dimension=0, tiled=True
        ).astype(jnp.float32),
        lax.psum_scatter(
            up_bias_grad.astype(jnp.bfloat16), "dp", scatter_dimension=0, tiled=True
        ).astype(jnp.float32),
        lax.psum_scatter(
            down_weight_grad.astype(jnp.bfloat16), "dp", scatter_dimension=0, tiled=True
        ).astype(jnp.float32),
        lax.psum_scatter(
            down_bias_grad.astype(jnp.bfloat16), "dp", scatter_dimension=0, tiled=True
        ).astype(jnp.float32),
    )
    (
        first_gain_grad,
        first_shift_grad,
        in_weight_grad,
        in_bias_grad,
        out_weight_grad,
        out_bias_grad,
        second_gain_grad,
        second_shift_grad,
        up_weight_grad,
        up_bias_grad,
        down_weight_grad,
        down_bias_grad,
    ) = (
        lax.psum(first_gain_grad.astype(jnp.bfloat16), "ctx").astype(jnp.float32),
        lax.psum(first_shift_grad.astype(jnp.bfloat16), "ctx").astype(jnp.float32),
        lax.psum(in_weight_grad.astype(jnp.bfloat16), "ctx").astype(jnp.float32),
        lax.psum(in_bias_grad.astype(jnp.bfloat16), "ctx").astype(jnp.float32),
        lax.psum(out_weight_grad.astype(jnp.bfloat16), "ctx").astype(jnp.float32),
        lax.psum(out_bias_grad.astype(jnp.bfloat16), "ctx").astype(jnp.float32),
        lax.psum(second_gain_grad.astype(jnp.bfloat16), "ctx").astype(jnp.float32),
        lax.psum(second_shift_grad.astype(jnp.bfloat16), "ctx").astype(jnp.float32),
        lax.psum(up_weight_grad.astype(jnp.bfloat16), "ctx").astype(jnp.float32),
        lax.psum(up_bias_grad.astype(jnp.bfloat16), "ctx").astype(jnp.float32),
        lax.psum(down_weight_grad.astype(jnp.bfloat16), "ctx").astype(jnp.float32),
        lax.psum(down_bias_grad.astype(jnp.bfloat16), "ctx").astype(jnp.float32),
    )
    return (
        layer_out,
        tokens_grad,
        first_gain_grad,
        first_shift_grad,
        in_weight_grad,
        in_bias_grad,
        out_weight_grad,
        out_bias_grad,
        second_gain_grad,
        second_shift_grad,
        up_weight_grad,
        up_bias_grad,
        down_weight_grad,
        down_bias_grad,
    )


masks = (0, 2, 1, 3)
dp_masks = (0, 4, 2, 6, 1, 5, 3, 7)
tile = 256
share = 20
lanes = 256
part = 3 * HEAD_DIM
root = math.sqrt(2.0 / math.pi)
low, wide = jnp.bfloat16, jnp.float32


def heads_split(mesh):
    return mesh.shape["ctx"] == 4 and mesh.shape["dp"] == 8


def swap(values, axis, bit):
    count = lax.axis_size(axis)
    return lax.ppermute(values, axis, [(i, i ^ bit) for i in range(count)])


def dp_gather(values):
    index = lax.axis_index("dp")
    for bit in (1, 2, 4):
        other = swap(values, "dp", bit)
        upper = (index // bit) % 2 == 1
        values = jnp.concatenate(
            [jnp.where(upper, other, values), jnp.where(upper, values, other)], axis=0
        )
    return values


def dp_scatter(kept, sent):
    index = lax.axis_index("dp")
    values = kept + swap(sent, "dp", 1).astype(wide)
    values = values.reshape((2, 2) + values.shape[1:])
    for axis, bit in ((1, 2), (0, 4)):
        mine = (index // bit) % 2
        sent = lax.dynamic_index_in_dim(values, 1 - mine, axis, keepdims=False).astype(low)
        kept = lax.dynamic_index_in_dim(values, mine, axis, keepdims=False)
        values = kept + swap(sent, "dp", bit).astype(wide)
    return values


def after(values, *others):
    return lax.optimization_barrier((values, *others))[0]


def sum_all(values):
    for axis, bit in (("dp", 1), ("dp", 2), ("dp", 4), ("ctx", 1), ("ctx", 2)):
        sent = values.astype(low)
        values = sent.astype(wide) + swap(sent, axis, bit).astype(wide)
    return values


def dot_nt(left, right):
    return lax.dot_general(left, right, (((1,), (1,)), ((), ())), preferred_element_type=wide)


def dot_nn(left, right):
    return jnp.dot(left, right, preferred_element_type=wide)


def dot_tn(left, right):
    return lax.dot_general(left, right, (((0,), (0,)), ((), ())), preferred_element_type=wide)


def flip(values):
    return values.astype(wide).T.astype(values.dtype)


def whole(array):
    rank = len(array.shape)
    return pl.BlockSpec(array.shape, lambda *_: (0,) * rank)


def third(place):
    return lambda array: pl.BlockSpec(
        (array.shape[0], array.shape[1] // 3, array.shape[2]), lambda *_: (0, place, 0)
    )


def kernel_call(kernel, name, index, inputs, outputs, flops, exps=0, grid=(1,), scratch=()):
    arrays = [item[0] if isinstance(item, tuple) else item for item in inputs]
    specs = [
        (item[1](item[0]) if callable(item[1]) else item[1]) if isinstance(item, tuple) else whole(item)
        for item in inputs
    ]
    shapes = [item[0] if isinstance(item, tuple) else item for item in outputs]
    out_specs = [item[1] if isinstance(item, tuple) else whole(item) for item in outputs]
    moved = sum(math.prod(a.shape) * a.dtype.itemsize for a in arrays + shapes)
    return pl.pallas_call(
        kernel,
        grid_spec=pltpu.PrefetchScalarGridSpec(
            num_scalar_prefetch=1,
            grid=grid,
            in_specs=specs,
            out_specs=out_specs,
            scratch_shapes=list(scratch),
        ),
        out_shape=shapes,
        compiler_params=pltpu.CompilerParams(vmem_limit_bytes=56 * 1024 * 1024),
        cost_estimate=pl.CostEstimate(
            flops=flops // share, bytes_accessed=moved // share, transcendentals=exps // share
        ),
        name=name,
    )(index, *arrays)


def shape_of(shape, kind):
    return jax.ShapeDtypeStruct(shape, kind)


def place_of(index, spot, rows):
    return pl.ds(pl.multiple_of((index ^ masks[spot]) * rows, 128), rows)


def diagonal():
    keys = lax.broadcasted_iota(jnp.int32, (tile, tile), 0)
    queries = lax.broadcasted_iota(jnp.int32, (tile, tile), 1)
    return keys <= queries


def unit_of(values):
    center = values - jnp.mean(values, axis=-1, keepdims=True)
    spread = jnp.mean(center * center, axis=-1, keepdims=True)
    scale = lax.rsqrt(spread + epsilon)
    return center * scale, scale


def norm_pull(unit, scale, gain, upstream):
    scaled = upstream * gain
    return scale * (
        scaled
        - jnp.mean(scaled, axis=-1, keepdims=True)
        - unit * jnp.mean(scaled * unit, axis=-1, keepdims=True)
    )


def column_sum(values):
    return jnp.sum(values, axis=0, keepdims=True)


def pick_in_kernel(index_ref, in_ref, out_ref):
    width = in_ref.shape[1] // 3
    own = width // 4
    for ctx in range(4):

        @pl.when(index_ref[0] == ctx)
        def pick():
            for head in range(own // HEAD_DIM):
                for kind in range(3):
                    begin = kind * width + ctx * own + head * HEAD_DIM
                    target = head * part + kind * HEAD_DIM
                    out_ref[:, target : target + HEAD_DIM] = in_ref[:, begin : begin + HEAD_DIM]


def pick_rest_kernel(index_ref, out_weight_ref, up_ref, down_ref, out_ref):
    shard, width = out_weight_ref.shape
    out_ref[:shard, :] = out_weight_ref[...]
    for ctx in range(4):

        @pl.when(index_ref[0] == ctx)
        def pick():
            for owner in range(width // shard):
                begin = owner * 4 * shard + ctx * shard
                out_ref[shard : 2 * shard, owner * shard : (owner + 1) * shard] = up_ref[
                    :, begin : begin + shard
                ]
            out_ref[2 * shard :, :] = down_ref[ctx * shard : (ctx + 1) * shard, :]


def norm_kernel(
    index_ref,
    own_ref,
    far_ref,
    near_ref,
    last_ref,
    vector_ref,
    first_ref,
    unit_ref,
    turned_ref,
):
    rows = own_ref.shape[0]
    for spot, piece in enumerate((own_ref, far_ref, near_ref, last_ref)):
        here = slice(spot * rows, (spot + 1) * rows)
        unit, scale = unit_of(piece[...].astype(wide))
        unit_ref[here, :] = unit.astype(low)
        normed = unit * vector_ref[0:1, :] + vector_ref[1:2, :]
        first_ref[here, :] = normed.astype(low)
        turned_ref[:, here] = normed.T.astype(low)


def attend_kernel(
    index_ref,
    first_ref,
    low_half_ref,
    high_half_ref,
    bias_ref,
    weight_ref,
    mix_ref,
    keep_ref,
    send_ref,
    full_ref,
    stats_ref,
    q_s,
    k_s,
    v_s,
    o_s,
):
    total, width = first_ref.shape
    rows = total // 4
    index = index_ref[0]
    heads = width // lanes

    @pl.when(pl.program_id(0) == 0)
    def begin_all():
        shard = low_half_ref.shape[0] // 4
        for spot in range(8):
            source = low_half_ref if spot < 4 else high_half_ref
            block = source[(spot % 4) * shard : (spot % 4 + 1) * shard, :]
            there = pl.ds(pl.multiple_of((index_ref[1] ^ dp_masks[spot]) * shard, 32), shard)
            for head in range(heads):
                begin = head * lanes
                weight_ref[there, begin : begin + part] = block[:, head * part : (head + 1) * part]
                weight_ref[there, begin + part : begin + lanes] = jnp.zeros(
                    (shard, lanes - part), low
                )

    here = pl.ds(pl.multiple_of(pl.program_id(0) * lanes, lanes), lanes)
    mix_ref[...] = (dot_nn(first_ref[...], weight_ref[:, here]) + bias_ref[0]).astype(low)
    for spot in range(4):
        here = slice(spot * rows, (spot + 1) * rows)
        there = place_of(index, spot, rows)
        q_s[there, :] = mix_ref[here, 0:64] * jnp.bfloat16(0.125)
        k_s[there, :] = mix_ref[here, 64:128]
        v_s[there, :] = mix_ref[here, 128:192]
    allowed = diagonal()
    flipped = flip(v_s[...])
    for i in range(total // tile):
        begin, end = i * tile, (i + 1) * tile
        queries = q_s[begin:end, :]
        near = jnp.where(allowed, dot_nt(k_s[begin:end, :], queries), neg_large)
        top = jnp.max(near, axis=0, keepdims=True)
        if i > 0:
            past = dot_nt(k_s[:begin, :], queries)
            top = jnp.maximum(top, jnp.max(past, axis=0, keepdims=True))
        near = jnp.exp(near - top)
        amount = column_sum(near)
        context = dot_nn(flipped[:, begin:end], near.astype(low))
        if i > 0:
            past = jnp.exp(past - top)
            amount = amount + column_sum(past)
            context = context + dot_nn(flipped[:, :begin], past.astype(low))
        o_s[:, begin:end] = context / amount
        stats_ref[0, :, begin:end] = top + jnp.log(amount)
    for spot in range(4):
        block = o_s[:, place_of(index, spot, rows)]
        full_ref[:, spot * rows : (spot + 1) * rows] = block
        target = keep_ref if spot in (0, 2) else send_ref
        target[:, (spot // 2) * rows : (spot // 2 + 1) * rows] = block.astype(low)


def attend(index, first_low, low_half, high_half, bias):
    total, width = first_low.shape
    rows = total // 4
    heads = width // lanes
    features = heads * HEAD_DIM
    by_head = lambda h, s: (h, 0)
    pairs = heads * total * total // 2
    return kernel_call(
        attend_kernel,
        "attend",
        index,
        [first_low, low_half, high_half]
        + [(bias, pl.BlockSpec((1, 1, lanes), lambda h, s: (h, 0, 0)))],
        [
            shape_of((width, width), low),
            (shape_of((total, width), low), pl.BlockSpec((total, lanes), lambda h, s: (0, h))),
            (shape_of((features, 2 * rows), low), pl.BlockSpec((HEAD_DIM, 2 * rows), by_head)),
            (shape_of((features, 2 * rows), low), pl.BlockSpec((HEAD_DIM, 2 * rows), by_head)),
            (shape_of((features, total), wide), pl.BlockSpec((HEAD_DIM, total), by_head)),
            (
                shape_of((heads, 1, total), wide),
                pl.BlockSpec((1, 1, total), lambda h, s: (h, 0, 0)),
            ),
        ],
        pairs * 4 * 256 + 2 * total * width * width,
        pairs,
        (heads,),
        [pltpu.VMEM((total, HEAD_DIM), low)] * 3 + [pltpu.VMEM((HEAD_DIM, total), wide)],
    )


def project_kernel(
    index_ref,
    keep_ref,
    far_ref,
    near_ref,
    weight_ref,
    tokens_ref,
    vector_ref,
    residual_ref,
    second_ref,
    turned_ref,
):
    rows, width = tokens_ref.shape
    own = width // 4
    pieces = [keep_ref[:, :rows], far_ref[:, :rows], near_ref[:, :rows], near_ref[:, rows:]]
    residual = tokens_ref[...].astype(wide) + vector_ref[4:5, :]
    for spot in range(4):
        turned = flip(pieces[spot])
        group = index_ref[0] ^ masks[spot]
        weights = weight_ref[pl.ds(2 * group, 2)].reshape(own, width)
        residual = residual + dot_nn(turned, weights)
    residual_ref[...] = residual
    unit, scale = unit_of(residual)
    second_ref[...] = (unit * vector_ref[5:6, :] + vector_ref[6:7, :]).astype(low)
    for spot in range(4):
        turned_ref[spot * own : (spot + 1) * own, :] = pieces[spot]


def feed_kernel(
    index_ref,
    one_ref,
    two_ref,
    up_one_ref,
    up_two_ref,
    up_ref,
    down_ref,
    bias_ref,
    active_ref,
    hidden_ref,
    kept_ref,
    sent_ref,
    sum_ref,
):
    rows, width = one_ref.shape
    up = up_ref[...].reshape(width, width)
    down = down_ref[...].reshape(width, width)
    for spot in (1, 0):
        here = slice(spot * rows, (spot + 1) * rows)
        values = two_ref[...] if spot else one_ref[...]
        grads = up_two_ref[...] if spot else up_one_ref[...]
        hidden = dot_nn(values, up) + bias_ref[...]
        square = hidden * hidden
        bend = jnp.tanh(root * hidden * (1.0 + 0.044715 * square))
        active_ref[here, :] = (0.5 * hidden * (1.0 + bend)).astype(low)
        slope = 0.5 * (1.0 + bend) + 0.5 * hidden * (1.0 - bend * bend) * (
            root * (1.0 + 3 * 0.044715 * square)
        )
        grad = (slope * dot_nt(grads, down)).astype(low)
        hidden_ref[here, :] = grad
        sums = column_sum(grad.astype(wide))
        sum_ref[...] = sums if spot else sum_ref[...] + sums
        result = dot_nt(grad, up)
        if spot:
            sent_ref[...] = result.astype(low)
        else:
            kept_ref[...] = result


def branch_kernel(index_ref, one_ref, two_ref, down_ref, kept_one_ref, sent_one_ref, kept_two_ref, sent_two_ref):
    width = one_ref.shape[1]
    rows = one_ref.shape[0] // 2
    down = down_ref[...].reshape(width, width)
    kept_one_ref[...] = dot_nn(one_ref[:rows, :], down)
    sent_one_ref[...] = dot_nn(one_ref[rows:, :], down).astype(low)
    kept_two_ref[...] = dot_nn(two_ref[:rows, :], down)
    sent_two_ref[...] = dot_nn(two_ref[rows:, :], down).astype(low)


def halves(index_ref, block, kept_ref, sent_ref, pair):
    upper = index_ref[1] % 2 == 1
    kept_ref[pair] = jnp.where(upper, block[1], block[0])
    sent_ref[pair] = jnp.where(upper, block[0], block[1]).astype(low)


def feed_grad_kernel(
    index_ref,
    own_ref,
    far_ref,
    near_ref,
    last_ref,
    up_own_ref,
    up_far_ref,
    up_near_ref,
    up_last_ref,
    hidden_one_ref,
    hidden_two_ref,
    active_one_ref,
    active_two_ref,
    out_ref,
):
    rows, width = own_ref.shape
    count, shard = out_ref.shape[0], out_ref.shape[1] // 2

    def halved(one, two):
        return (one[:rows, :], one[rows:, :], two[:rows, :], two[rows:, :])

    pairs = (
        ((own_ref, near_ref, far_ref, last_ref), halved(hidden_one_ref, hidden_two_ref)),
        (
            halved(active_one_ref, active_two_ref),
            (up_own_ref, up_near_ref, up_far_ref, up_last_ref),
        ),
    )
    for place, (lefts, rights) in enumerate(pairs):
        total = None
        for left, right in zip(lefts, rights):
            update = dot_tn(left[...], right[...])
            total = update if total is None else total + update
        total = total.astype(low).reshape(count, shard, width)
        out_ref[:, place * shard : (place + 1) * shard, :] = total


def in_grad_kernel(index_ref, turned_ref, mix_ref, kept_ref, sent_ref):
    pairs, shard, columns = kept_ref.shape
    upper = index_ref[1] % 2 == 1
    for pair in range(pairs):
        begin = 2 * pair * shard
        block = dot_nn(turned_ref[begin : begin + 2 * shard, :], mix_ref[...])
        kept = jnp.where(upper, block[shard:, :], block[:shard, :])
        sent = jnp.where(upper, block[:shard, :], block[shard:, :]).astype(low)
        for head in range(columns // part):
            here = slice(head * part, (head + 1) * part)
            there = slice(head * lanes, head * lanes + part)
            kept_ref[pair, :, here] = kept[:, there]
            sent_ref[pair, :, here] = sent[:, there]


def turn_kernel(
    index_ref,
    kept_ref,
    core_ref,
    far_ref,
    residual_ref,
    cotangent_ref,
    weight_ref,
    vector_ref,
    grad_ref,
    attn_ref,
    keep_ref,
    send_ref,
    sum_ref,
):
    rows, width = residual_ref.shape
    own = width // 4
    grad = kept_ref[...] + core_ref[...].astype(wide) + far_ref[...].astype(wide)
    unit, scale = unit_of(residual_ref[...])
    upstream = cotangent_ref[...].astype(wide)
    result = upstream + norm_pull(unit, scale, vector_ref[5:6, :], grad)
    grad_ref[...] = result
    attn = result.astype(low)
    attn_ref[...] = attn
    for spot in range(4):
        group = index_ref[0] ^ masks[spot]
        weights = weight_ref[pl.ds(2 * group, 2)].reshape(own, width)
        block = dot_nt(weights, attn).astype(low)
        target = keep_ref if spot in (0, 2) else send_ref
        target[:, (spot // 2) * rows : (spot // 2 + 1) * rows] = block
    sum_ref[0:1, :] = column_sum(grad * unit)
    sum_ref[1:2, :] = column_sum(grad)
    sum_ref[2:3, :] = column_sum(attn.astype(wide))
    sum_ref[3:4, :] = column_sum(upstream)


def out_grad_kernel(index_ref, turned_ref, attn_ref, kept_ref, sent_ref):
    width = turned_ref.shape[0]
    own = width // 4
    for spot in range(4):
        group = index_ref[0] ^ masks[spot]
        block = dot_nn(turned_ref[spot * own : (spot + 1) * own, :], attn_ref[...])
        halves(index_ref, block.reshape(2, own // 2, width), kept_ref, sent_ref, group)


def attend_back_kernel(
    index_ref,
    mix_ref,
    keep_ref,
    far_ref,
    near_ref,
    full_ref,
    stats_ref,
    out_ref,
    sum_ref,
    q_s,
    k_s,
    v_s,
    g_s,
    d_s,
    dq_s,
):
    total = mix_ref.shape[0]
    rows = total // 4
    index = index_ref[0]
    pieces = [keep_ref[:, :rows], far_ref[:, :rows], near_ref[:, :rows], near_ref[:, rows:]]
    for spot in range(4):
        here = slice(spot * rows, (spot + 1) * rows)
        there = place_of(index, spot, rows)
        q_s[there, :] = mix_ref[here, 0:64] * jnp.bfloat16(0.125)
        k_s[there, :] = mix_ref[here, 64:128]
        v_s[there, :] = mix_ref[here, 128:192]
        block = pieces[spot]
        g_s[:, there] = block
        d_s[:, there] = column_sum(block.astype(wide) * full_ref[:, here])
    allowed = diagonal()
    turned = flip(g_s[...])
    flipped = flip(k_s[...])
    count = total // tile
    for j in range(count):
        begin, end = j * tile, (j + 1) * tile
        keys, values = k_s[begin:end, :], v_s[begin:end, :]
        probs = jnp.exp(dot_nt(keys, q_s[begin:, :]) - stats_ref[0, :, begin:])
        near = jnp.where(allowed, probs[:, :tile], 0.0)
        probs = near if j == count - 1 else jnp.concatenate([near, probs[:, tile:]], axis=1)
        scores = (probs * (dot_nn(values, g_s[:, begin:]) - d_s[:, begin:])).astype(low)
        grad_value = dot_nn(probs.astype(low), turned[begin:, :])
        grad_key = dot_nn(scores, q_s[begin:, :])
        update = dot_nn(flipped[:, begin:end], scores)
        if j == 0:
            dq_s[...] = update
        else:
            dq_s[:, begin:] = dq_s[:, begin:] + update
        k_s[begin:end, :] = grad_key.astype(low)
        v_s[begin:end, :] = grad_value.astype(low)
    q_s[...] = (dq_s[...] * 0.125).T.astype(low)
    for spot in range(4):
        here = slice(spot * rows, (spot + 1) * rows)
        there = place_of(index, spot, rows)
        out_ref[here, 0:64] = q_s[there, :]
        out_ref[here, 64:128] = k_s[there, :]
        out_ref[here, 128:192] = v_s[there, :]
        out_ref[here, 192:256] = jnp.zeros((rows, 64), low)
    sum_ref[0] = column_sum(out_ref[...].astype(wide))


def attend_back(index, mix, keep, far, near, full, stats):
    total, width = mix.shape
    heads = width // lanes
    by_head = lambda h, s: (h, 0)
    half = pl.BlockSpec((HEAD_DIM, total // 2), by_head)
    slab = pl.BlockSpec((total, lanes), lambda h, s: (0, h))
    pairs = heads * total * total // 2
    return kernel_call(
        attend_back_kernel,
        "attend_back",
        index,
        [(mix, slab), (keep, half), (far, half), (near, half)]
        + [(full, pl.BlockSpec((HEAD_DIM, total), by_head))]
        + [(stats, pl.BlockSpec((1, 1, total), lambda h, s: (h, 0, 0)))],
        [
            (shape_of((total, width), low), slab),
            (
                shape_of((heads, 1, lanes), wide),
                pl.BlockSpec((1, 1, lanes), lambda h, s: (h, 0, 0)),
            ),
        ],
        pairs * 10 * 256,
        pairs,
        (heads,),
        [pltpu.VMEM((total, HEAD_DIM), low)] * 3
        + [
            pltpu.VMEM((HEAD_DIM, total), low),
            pltpu.VMEM((1, total), wide),
            pltpu.VMEM((HEAD_DIM, total), wide),
        ],
    )


def first_back_kernel(
    index_ref, mix_ref, weight_ref, unit_ref, kept_one_ref, sent_one_ref, kept_two_ref, sent_two_ref, sum_ref
):
    total = mix_ref.shape[0]
    rows = total // 4
    targets = (kept_one_ref, kept_two_ref, sent_one_ref, sent_two_ref)
    for spot in (3, 1, 2, 0):
        here = slice(spot * rows, (spot + 1) * rows)
        grad = dot_nt(mix_ref[here, :], weight_ref[...])
        gain = column_sum(grad * unit_ref[here, :].astype(wide))
        shift = column_sum(grad)
        sums = jnp.concatenate([gain, shift], axis=0)
        sum_ref[...] = sums if spot == 3 else sum_ref[...] + sums
        targets[spot][...] = grad.astype(targets[spot].dtype)


def vector_kernel(index_ref, one_ref, bias_ref, two_ref, up_one_ref, up_two_ref, out_ref):
    width = one_ref.shape[1]
    own = width // 4
    out_ref[...] = jnp.zeros(out_ref.shape, wide)
    out_ref[0:2, :] = one_ref[...]
    out_ref[4:8, :] = two_ref[...]
    for ctx in range(4):

        @pl.when(index_ref[0] == ctx)
        def put():
            out_ref[8 + ctx : 9 + ctx, :] = up_one_ref[...] + up_two_ref[...]
            for head in range(own // HEAD_DIM):
                begin = ctx * own + head * HEAD_DIM
                for row, kind in ((2, 0), (3, 2)):
                    out_ref[row : row + 1, begin : begin + HEAD_DIM] = bias_ref[
                        head, :, kind * HEAD_DIM : (kind + 1) * HEAD_DIM
                    ]


def tokens_kernel(
    index_ref, kept_ref, core_ref, far_ref, tokens_ref, residual_ref, vector_ref, out_ref
):
    rows = tokens_ref.shape[0]
    grad = kept_ref[...] + core_ref[...].astype(wide) + far_ref[...].astype(wide)
    unit, scale = unit_of(tokens_ref[...].astype(wide))
    result = residual_ref[...] + norm_pull(unit, scale, vector_ref[0:1, :], grad)
    out_ref[...] = result.astype(low)


def spread_kernel(index_ref, own_ref, far_ref, near_ref, up_ref, down_ref, out_ref):
    width = own_ref.shape[1]
    shard = own_ref.shape[0] // 3
    total = None
    for ctx in range(4):
        for spot in range(4):

            @pl.when((index_ref[0] ^ ctx) == masks[spot])
            def put():
                source = [own_ref, far_ref, near_ref, near_ref][spot]
                base = 3 * shard if spot == 3 else 0
                block = source[base : base + shard, :].astype(wide)
                for owner in range(width // shard):
                    begin = (owner * 4 + ctx) * shard
                    up_ref[:, begin : begin + shard] = block[:, owner * shard : (owner + 1) * shard]
                down_ref[ctx * shard : (ctx + 1) * shard, :] = source[
                    base + shard : base + 2 * shard, :
                ].astype(wide)
                last = source[base + 2 * shard : base + 3 * shard, :].astype(wide)
                if ctx == 0:
                    out_ref[...] = last
                else:
                    out_ref[...] = out_ref[...] + last


def spread_in_kernel(index_ref, own_ref, far_ref, near_ref, in_ref):
    shard, own = own_ref.shape[0], own_ref.shape[1] // 3
    width = 4 * own
    for ctx in range(4):
        for spot in range(4):

            @pl.when((index_ref[0] ^ ctx) == masks[spot])
            def put():
                source = [own_ref, far_ref, near_ref, near_ref][spot]
                base = shard if spot == 3 else 0
                block = source[base : base + shard, :].astype(wide)
                for head in range(own // HEAD_DIM):
                    for kind in range(3):
                        begin = kind * width + ctx * own + head * HEAD_DIM
                        target = head * part + kind * HEAD_DIM
                        in_ref[:, begin : begin + HEAD_DIM] = block[:, target : target + HEAD_DIM]


def pieces_of(values):
    far = swap(values, "ctx", 2)
    return values, far, swap(jnp.concatenate([values, far], axis=0), "ctx", 1)


def blocks_of(values):
    far = swap(values, "ctx", 2)
    near = swap(values, "ctx", 1)
    return values, far, near, swap(far, "ctx", 1)


def exchange(keep, send):
    rows = keep.shape[1] // 2
    far = swap(send, "ctx", 2)
    near = swap(jnp.concatenate([keep[:, rows:], far[:, rows:]], axis=1), "ctx", 1)
    return far, near


def split_body(
    tokens,
    first_gain,
    first_shift,
    in_weight,
    in_bias,
    out_weight,
    out_bias,
    second_gain,
    second_shift,
    up_weight,
    up_bias,
    down_weight,
    down_bias,
    cotangent,
):
    rows, width = tokens.shape
    total = 4 * rows
    n_dp = lax.axis_size("dp")
    shard = width // n_dp
    ctx = lax.axis_index("ctx")
    owner = lax.axis_index("dp")
    heads = width // HEAD_DIM // 4
    own = heads * HEAD_DIM
    index = jnp.stack([ctx, owner]).astype(jnp.int32)
    big = 2 * total * width * width
    small = 2 * rows * width * width
    row_wide, row_low = shape_of((rows, width), wide), shape_of((rows, width), low)

    (in_own,) = kernel_call(
        pick_in_kernel, "pick_in", index, [in_weight], [shape_of((shard, 3 * own), low)], 0
    )
    in_other = swap(in_own, "dp", 4)
    in_two = jnp.concatenate([in_own, in_other], axis=0)
    low_half = jnp.concatenate([in_two, swap(in_two, "dp", 2)], axis=0)
    high_half = swap(low_half, "dp", 1)
    (rest,) = kernel_call(
        pick_rest_kernel,
        "pick_rest",
        index,
        [out_weight, up_weight, after(down_weight, in_own)],
        [shape_of((3 * shard, width), low)],
        0,
    )
    rest = lax.all_gather(rest, "dp", axis=0, tiled=False)
    vectors = jnp.concatenate(
        [first_gain, first_shift, in_bias[0], in_bias[1], out_bias, second_gain, second_shift]
        + [down_bias, up_bias]
    ).reshape(1, 12 * shard)
    vectors = dp_gather(after(vectors, in_other)).reshape(n_dp, 12, shard).transpose(1, 0, 2).reshape(12, width)
    vectors = vectors.astype(wide)
    hidden_bias = lax.dynamic_slice_in_dim(vectors, 8 + ctx, 1, 0)
    zeros = jnp.zeros((heads, HEAD_DIM), wide)
    mine = lax.dynamic_slice(vectors, (2, ctx * own), (2, own)).reshape(2, heads, HEAD_DIM)
    bias_full = jnp.concatenate([mine[0], zeros, mine[1], zeros], axis=1).reshape(heads, 1, lanes)

    first_low, unit_one, first_turned = kernel_call(
        norm_kernel,
        "norm",
        index,
        [*blocks_of(tokens), vectors],
        [shape_of((total, width), low)] * 2 + [shape_of((width, total), low)],
        0,
    )
    upstream = blocks_of(cotangent)
    first_low, *upstream = lax.optimization_barrier((first_low, *upstream))
    in_full, mix, keep, send, context_full, stats = attend(
        index, first_low, low_half, high_half, bias_full
    )
    far, near = exchange(keep, send)
    out_block = (rest, third(0))
    up_block = (rest, third(1))
    down_block = (rest, third(2))
    residual, second_low, turned = kernel_call(
        project_kernel,
        "project",
        index,
        [keep, far, near, out_block, tokens, vectors],
        [row_wide, row_low, shape_of((width, rows), low)],
        small,
    )

    def feed(name, one, two, up_one, up_two):
        return kernel_call(
            feed_kernel,
            name,
            index,
            [one, two, up_one, up_two, up_block, down_block, hidden_bias],
            [shape_of((total // 2, width), low)] * 2
            + [row_wide, row_low, shape_of((1, width), wide)],
            3 * big // 2,
            total * width // 2,
        )

    far, near = swap(second_low, "ctx", 2), swap(second_low, "ctx", 1)
    active_one, hidden_one, kept_one, sent_one, up_sum_one = feed(
        "feed_one", second_low, near, upstream[0], upstream[2]
    )
    far = after(far, active_one)
    second = (second_low, far, near, swap(far, "ctx", 1))
    active_two, hidden_two, kept_two, sent_two, up_sum_two = feed(
        "feed_two", second[1], second[3], upstream[1], upstream[3]
    )
    core_one = swap(sent_one, "ctx", 1)
    passed = (kept_two + swap(sent_two, "ctx", 1).astype(wide)).astype(low)
    far = swap(passed, "ctx", 2)
    (feed_grad,) = kernel_call(
        feed_grad_kernel,
        "feed_grad",
        index,
        [after(second[0], passed), *second[1:], *upstream, hidden_one, hidden_two]
        + [active_one, active_two],
        [shape_of((n_dp, 2 * shard, width), low)],
        2 * big,
    )
    branch = kernel_call(
        branch_kernel,
        "branch",
        index,
        [after(active_one, feed_grad), active_two, down_block],
        [row_wide, row_low, row_wide, row_low],
        big,
    )
    far, feed_grad, *branch = lax.optimization_barrier((far, feed_grad, *branch))
    feed_mine = lax.psum_scatter(feed_grad, "dp", scatter_dimension=0, tiled=False)
    grad_residual, grad_attn, keep, send, sums_two = kernel_call(
        turn_kernel,
        "turn",
        index,
        [kept_one, core_one, far, residual, cotangent, out_block, vectors],
        [
            row_wide,
            row_low,
            shape_of((own, 2 * rows), low),
            shape_of((own, 2 * rows), low),
            shape_of((4, width), wide),
        ],
        small,
    )
    out_kept, out_sent = kernel_call(
        out_grad_kernel,
        "out_grad",
        index,
        [turned, grad_attn],
        [shape_of((n_dp // 2, shard, width), wide), shape_of((n_dp // 2, shard, width), low)],
        small,
    )
    far = swap(send, "ctx", 2)
    late = after(far, out_sent)
    near = swap(jnp.concatenate([keep[:, rows:], late[:, rows:]], axis=1), "ctx", 1)
    grad_mix, bias_sums = attend_back(index, mix, keep, far, near, context_full, stats)

    in_kept, in_sent = kernel_call(
        in_grad_kernel,
        "in_grad",
        index,
        [first_turned, grad_mix],
        [shape_of((n_dp // 2, shard, 3 * own), wide), shape_of((n_dp // 2, shard, 3 * own), low)],
        big,
    )
    kept_one, sent_one, kept_two, sent_two, sums_one = kernel_call(
        first_back_kernel,
        "first_back",
        index,
        [after(grad_mix, in_sent), in_full, unit_one],
        [row_wide, row_low, row_wide, row_low, shape_of((2, width), wide)],
        big,
    )
    out_mine = dp_scatter(out_kept, out_sent)
    in_mine = dp_scatter(in_kept, in_sent)
    core_one = swap(sent_one, "ctx", 1)
    far = swap((kept_two + swap(sent_two, "ctx", 1).astype(wide)).astype(low), "ctx", 2)
    (tokens_grad,) = kernel_call(
        tokens_kernel,
        "tokens",
        index,
        [kept_one, core_one, far, tokens, grad_residual, vectors],
        [row_low],
        0,
    )
    kept_one, sent_one, kept_two, sent_two = branch
    core_one = swap(sent_one, "ctx", 1)
    far = swap((kept_two + swap(sent_two, "ctx", 1).astype(wide)).astype(low), "ctx", 2)
    branch = kept_one + core_one.astype(wide) + far.astype(wide)
    layer_out = (residual + branch + vectors[7]).astype(low)

    (sums,) = kernel_call(
        vector_kernel,
        "vectors",
        index,
        [sums_one, bias_sums, sums_two, up_sum_one, up_sum_two],
        [shape_of((16, width), wide)],
        0,
    )
    sums = lax.dynamic_slice_in_dim(sum_all(sums), owner * shard, shard, 1)

    feed_mine = jnp.concatenate([feed_mine, out_mine.astype(low)], axis=0)
    up_weight_grad, down_weight_grad, out_weight_grad = kernel_call(
        spread_kernel,
        "spread",
        index,
        [*pieces_of(feed_mine)],
        [
            shape_of((shard, 4 * width), wide),
            shape_of((4 * shard, width), wide),
            shape_of((shard, width), wide),
        ],
        0,
    )
    (in_weight_grad,) = kernel_call(
        spread_in_kernel,
        "spread_in",
        index,
        [*pieces_of(in_mine.astype(low))],
        [shape_of((shard, 3 * width), wide)],
        0,
    )
    return (
        layer_out,
        tokens_grad,
        sums[0],
        sums[1],
        in_weight_grad,
        sums[2:4],
        out_weight_grad,
        sums[6],
        sums[4],
        sums[5],
        up_weight_grad,
        sums[8:12].reshape(4 * shard),
        down_weight_grad,
        sums[7],
    )


def solution(mesh):
    in_specs = (
        P(("dp", "ctx"), None),
        P("dp"),
        P("dp"),
        P("dp", None),
        P(None, "dp"),
        P("dp", None),
        P("dp"),
        P("dp"),
        P("dp"),
        P("dp", None),
        P("dp"),
        P("dp", None),
        P("dp"),
        P(("dp", "ctx"), None),
    )
    out_specs = (
        P(("dp", "ctx"), None),
        P(("dp", "ctx"), None),
        P("dp"),
        P("dp"),
        P("dp", None),
        P(None, "dp"),
        P("dp", None),
        P("dp"),
        P("dp"),
        P("dp"),
        P("dp", None),
        P("dp"),
        P("dp", None),
        P("dp"),
    )
    chosen = split_body if heads_split(mesh) else gathered_body
    return jax.shard_map(chosen, mesh=mesh, in_specs=in_specs, out_specs=out_specs, check_vma=False)
```

```python
import functools
import math

import jax
import jax.numpy as jnp
from jax import lax
from jax.experimental import pallas as pl
from jax.experimental.pallas import tpu as pltpu
from jax.sharding import PartitionSpec as P

HEAD_DIM = 64


epsilon = 1e-05
neg_large = -1e30


def layer_norm(values, gain, shift):
    center = values - jnp.mean(values, axis=-1, keepdims=True)
    spread = jnp.mean(center * center, axis=-1, keepdims=True)
    return center * lax.rsqrt(spread + epsilon) * gain + shift


def norm_back(values, gain, shift, upstream):
    result, pullback = jax.vjp(layer_norm, values, gain, shift)
    return pullback(upstream)


def smooth_gate(values):
    return jax.nn.gelu(values, approximate=True)


def forward_block(state, query_heads, query_pos, key_blk, value_blk, key_pos, factor):
    row_max, row_total, accumulated = state
    scores = (
        jnp.einsum("qhd,khd->hqk", query_heads, key_blk, preferred_element_type=jnp.float32)
        * factor
    )
    allowed = (query_pos[:, None] >= key_pos[None, :])[None]
    scores = jnp.where(allowed, scores, neg_large)
    new_max = jnp.maximum(row_max, jnp.max(scores, axis=-1))
    rescale = jnp.exp(row_max - new_max)
    weights = jnp.where(allowed, jnp.exp(scores - new_max[:, :, None]), 0.0)
    row_total = row_total * rescale + jnp.sum(weights, axis=-1)
    update = jnp.einsum(
        "hqk,khd->qhd", weights.astype(jnp.bfloat16), value_blk, preferred_element_type=jnp.float32
    )
    accumulated = accumulated * rescale.T[:, :, None] + update
    return (new_max, row_total, accumulated)


def pair_grads(
    query_heads, grad_heads, stats, deltas, query_pos, key_blk, value_blk, key_pos, factor
):
    scores = (
        jnp.einsum("qhd,khd->hqk", query_heads, key_blk, preferred_element_type=jnp.float32)
        * factor
    )
    allowed = (query_pos[:, None] >= key_pos[None, :])[None]
    probs = jnp.where(allowed, jnp.exp(scores - stats[:, :, None]), 0.0)
    grad_probs = jnp.einsum(
        "qhd,khd->hqk", grad_heads, value_blk, preferred_element_type=jnp.float32
    )
    grad_scores = (probs * (grad_probs - deltas[:, :, None])).astype(jnp.bfloat16)
    grad_query = (
        jnp.einsum("hqk,khd->qhd", grad_scores, key_blk, preferred_element_type=jnp.float32)
        * factor
    )
    grad_key = (
        jnp.einsum("hqk,qhd->khd", grad_scores, query_heads, preferred_element_type=jnp.float32)
        * factor
    )
    grad_value = jnp.einsum(
        "hqk,qhd->khd", probs.astype(jnp.bfloat16), grad_heads, preferred_element_type=jnp.float32
    )
    return (grad_query, grad_key, grad_value)


def over_keys(state, key_part, value_part, begin_row, top_query, place, block_fn):
    amount, head_count, head_dim = key_part.shape
    stride = math.gcd(amount, 512)
    key_blocks = key_part.reshape(amount // stride, stride, head_count, head_dim)
    value_blocks = value_part.reshape(amount // stride, stride, head_count, head_dim)
    offsets = begin_row + jnp.arange(amount // stride, dtype=jnp.int32) * stride

    def over_step_fn(inner, operands):
        key_blk, value_blk, offset = operands
        key_pos = place(offset + jnp.arange(stride, dtype=jnp.int32))

        def over_compute(current):
            return block_fn(current, key_blk, value_blk, key_pos)

        def keep(current):
            return current

        return (lax.cond(jnp.min(key_pos) <= top_query, over_compute, keep, inner), None)

    state, unused = lax.scan(over_step_fn, state, (key_blocks, value_blocks, offsets))
    return state


def gathered_body(
    tokens,
    first_gain,
    first_shift,
    in_weight,
    in_bias,
    out_weight,
    out_bias,
    second_gain,
    second_shift,
    up_weight,
    up_bias,
    down_weight,
    down_bias,
    cotangent,
):
    (
        first_gain,
        first_shift,
        in_weight,
        in_bias,
        out_weight,
        out_bias,
        second_gain,
        second_shift,
        up_weight,
        up_bias,
        down_weight,
        down_bias,
    ) = (
        lax.all_gather(first_gain, "dp", axis=0, tiled=True),
        lax.all_gather(first_shift, "dp", axis=0, tiled=True),
        lax.all_gather(in_weight, "dp", axis=0, tiled=True),
        lax.all_gather(in_bias, "dp", axis=1, tiled=True),
        lax.all_gather(out_weight, "dp", axis=0, tiled=True),
        lax.all_gather(out_bias, "dp", axis=0, tiled=True),
        lax.all_gather(second_gain, "dp", axis=0, tiled=True),
        lax.all_gather(second_shift, "dp", axis=0, tiled=True),
        lax.all_gather(up_weight, "dp", axis=0, tiled=True),
        lax.all_gather(up_bias, "dp", axis=0, tiled=True),
        lax.all_gather(down_weight, "dp", axis=0, tiled=True),
        lax.all_gather(down_bias, "dp", axis=0, tiled=True),
    )
    rows_dev = tokens.shape[0]
    width = tokens.shape[1]
    head_dim = HEAD_DIM
    head_count = width // head_dim
    factor = 1.0 / math.sqrt(head_dim)
    my_index = lax.axis_index("ctx")

    def place(rows):
        return rows

    query_pos = place(my_index * rows_dev + jnp.arange(rows_dev, dtype=jnp.int32))
    top_query = jnp.max(query_pos)
    inputs = tokens.astype(jnp.float32)
    gain_one = first_gain.astype(jnp.float32)
    shift_one = first_shift.astype(jnp.float32)
    first_low = layer_norm(inputs, gain_one, shift_one).astype(jnp.bfloat16)
    bias_full = jnp.concatenate([in_bias[0], jnp.zeros((width,), jnp.bfloat16), in_bias[1]]).astype(
        jnp.float32
    )
    mixture = (
        jnp.dot(first_low, in_weight, preferred_element_type=jnp.float32) + bias_full
    ).astype(jnp.bfloat16)
    query_rows = mixture[:, :width]
    key_rows = mixture[:, width : 2 * width]
    value_rows = mixture[:, 2 * width :]
    query_heads = query_rows.reshape(rows_dev, head_count, head_dim)

    def forward_fold(state, portion, begin_row):
        key_part, value_part = portion
        amount = key_part.shape[0]

        def block_fn(inner, key_blk, value_blk, key_pos):
            return forward_block(inner, query_heads, query_pos, key_blk, value_blk, key_pos, factor)

        return over_keys(
            state,
            key_part.reshape(amount, head_count, head_dim),
            value_part.reshape(amount, head_count, head_dim),
            begin_row,
            top_query,
            place,
            block_fn,
        )

    start_state = (
        jnp.full((head_count, rows_dev), neg_large, jnp.float32),
        jnp.zeros((head_count, rows_dev), jnp.float32),
        jnp.zeros((rows_dev, head_count, head_dim), jnp.float32),
    )
    row_max, row_total, accumulated = forward_fold(
        start_state,
        (
            lax.all_gather(key_rows, "ctx", axis=0, tiled=True),
            lax.all_gather(value_rows, "ctx", axis=0, tiled=True),
        ),
        jnp.int32(0),
    )
    stats = row_max + jnp.log(row_total)
    context_heads = accumulated / row_total.T[:, :, None]
    context_low = context_heads.reshape(rows_dev, width).astype(jnp.bfloat16)
    residual = (
        inputs
        + jnp.dot(context_low, out_weight, preferred_element_type=jnp.float32)
        + out_bias.astype(jnp.float32)
    )
    gain_two = second_gain.astype(jnp.float32)
    shift_two = second_shift.astype(jnp.float32)
    second_low = layer_norm(residual, gain_two, shift_two).astype(jnp.bfloat16)
    hidden = jnp.dot(second_low, up_weight, preferred_element_type=jnp.float32) + up_bias.astype(
        jnp.float32
    )
    activated, gate_back = jax.vjp(smooth_gate, hidden)
    active_low = activated.astype(jnp.bfloat16)
    layer_out = (
        residual
        + jnp.dot(active_low, down_weight, preferred_element_type=jnp.float32)
        + down_bias.astype(jnp.float32)
    ).astype(jnp.bfloat16)
    upstream = cotangent.astype(jnp.float32)
    down_bias_grad = jnp.sum(upstream, axis=0)
    down_weight_grad = jnp.einsum(
        "tf,td->fd", active_low, cotangent, preferred_element_type=jnp.float32
    )
    (grad_hidden,) = gate_back(
        jnp.einsum("td,fd->tf", cotangent, down_weight, preferred_element_type=jnp.float32)
    )
    grad_hidden = grad_hidden.astype(jnp.bfloat16)
    up_weight_grad = jnp.einsum(
        "td,tf->df", second_low, grad_hidden, preferred_element_type=jnp.float32
    )
    up_bias_grad = jnp.sum(grad_hidden.astype(jnp.float32), axis=0)
    grad_second = jnp.einsum(
        "tf,df->td", grad_hidden, up_weight, preferred_element_type=jnp.float32
    )
    grad_residual, second_gain_grad, second_shift_grad = norm_back(
        residual, gain_two, shift_two, grad_second
    )
    grad_residual = grad_residual + upstream
    grad_attn = grad_residual.astype(jnp.bfloat16)
    out_bias_grad = jnp.sum(grad_attn.astype(jnp.float32), axis=0)
    out_weight_grad = jnp.einsum(
        "td,te->de", context_low, grad_attn, preferred_element_type=jnp.float32
    )
    grad_context = jnp.einsum(
        "te,de->td", grad_attn, out_weight, preferred_element_type=jnp.float32
    ).astype(jnp.bfloat16)
    grad_heads = grad_context.reshape(rows_dev, head_count, head_dim)
    deltas = jnp.sum(grad_heads.astype(jnp.float32) * context_heads, axis=-1).T

    def query_fold(state, portion, begin_row):
        key_part, value_part = portion
        amount = key_part.shape[0]

        def block_fn(inner, key_blk, value_blk, key_pos):
            grad_query, grad_key, grad_value = pair_grads(
                query_heads,
                grad_heads,
                stats,
                deltas,
                query_pos,
                key_blk,
                value_blk,
                key_pos,
                factor,
            )
            return inner + grad_query

        return over_keys(
            state,
            key_part.reshape(amount, head_count, head_dim),
            value_part.reshape(amount, head_count, head_dim),
            begin_row,
            top_query,
            place,
            block_fn,
        )

    zero_heads = jnp.zeros((rows_dev, head_count, head_dim), jnp.float32)
    key_all, value_all = (
        lax.all_gather(key_rows, "ctx", axis=0, tiled=True),
        lax.all_gather(value_rows, "ctx", axis=0, tiled=True),
    )
    grad_query = query_fold(zero_heads, (key_all, value_all), 0)
    amount = lax.axis_size("ctx") * rows_dev
    stride = math.gcd(amount, 512)
    key_part = key_all.reshape(amount // stride, stride, head_count, head_dim)
    value_part = value_all.reshape(amount // stride, stride, head_count, head_dim)
    offsets = jnp.arange(amount // stride, dtype=jnp.int32) * stride

    def key_step_fn(unused, operands):
        key_blk, value_blk, offset = operands
        key_pos = place(offset + jnp.arange(stride, dtype=jnp.int32))

        def key_compute(blocks_in):
            grad_query_part, grad_key, grad_value = pair_grads(
                query_heads,
                grad_heads,
                stats,
                deltas,
                query_pos,
                blocks_in[0],
                blocks_in[1],
                key_pos,
                factor,
            )
            return jnp.concatenate(
                [grad_key.reshape(stride, width), grad_value.reshape(stride, width)], axis=1
            )

        def nothing(blocks_in):
            return jnp.zeros((stride, 2 * width), jnp.float32)

        return (
            unused,
            lax.cond(jnp.min(key_pos) <= top_query, key_compute, nothing, (key_blk, value_blk)),
        )

    unused, stacked = lax.scan(key_step_fn, 0, (key_part, value_part, offsets))
    grad_pairs = lax.psum_scatter(
        stacked.reshape(amount, 2 * width).astype(jnp.bfloat16),
        "ctx",
        scatter_dimension=0,
        tiled=True,
    ).astype(jnp.float32)
    grad_key = grad_pairs[:, :width]
    grad_value = grad_pairs[:, width:]
    grad_mixture = jnp.concatenate(
        [grad_query.reshape(rows_dev, width), grad_key, grad_value], axis=1
    ).astype(jnp.bfloat16)
    in_weight_grad = jnp.einsum(
        "td,te->de", first_low, grad_mixture, preferred_element_type=jnp.float32
    )
    in_bias_grad = jnp.stack(
        [
            jnp.sum(grad_mixture[:, :width].astype(jnp.float32), axis=0),
            jnp.sum(grad_mixture[:, 2 * width :].astype(jnp.float32), axis=0),
        ]
    )
    grad_first = jnp.einsum(
        "te,de->td", grad_mixture, in_weight, preferred_element_type=jnp.float32
    )
    grad_inputs, first_gain_grad, first_shift_grad = norm_back(
        inputs, gain_one, shift_one, grad_first
    )
    tokens_grad = (grad_inputs + grad_residual).astype(jnp.bfloat16)
    (
        first_gain_grad,
        first_shift_grad,
        in_weight_grad,
        in_bias_grad,
        out_weight_grad,
        out_bias_grad,
        second_gain_grad,
        second_shift_grad,
        up_weight_grad,
        up_bias_grad,
        down_weight_grad,
        down_bias_grad,
    ) = (
        lax.psum_scatter(
            first_gain_grad.astype(jnp.bfloat16), "dp", scatter_dimension=0, tiled=True
        ).astype(jnp.float32),
        lax.psum_scatter(
            first_shift_grad.astype(jnp.bfloat16), "dp", scatter_dimension=0, tiled=True
        ).astype(jnp.float32),
        lax.psum_scatter(
            in_weight_grad.astype(jnp.bfloat16), "dp", scatter_dimension=0, tiled=True
        ).astype(jnp.float32),
        lax.psum_scatter(
            in_bias_grad.astype(jnp.bfloat16), "dp", scatter_dimension=1, tiled=True
        ).astype(jnp.float32),
        lax.psum_scatter(
            out_weight_grad.astype(jnp.bfloat16), "dp", scatter_dimension=0, tiled=True
        ).astype(jnp.float32),
        lax.psum_scatter(
            out_bias_grad.astype(jnp.bfloat16), "dp", scatter_dimension=0, tiled=True
        ).astype(jnp.float32),
        lax.psum_scatter(
            second_gain_grad.astype(jnp.bfloat16), "dp", scatter_dimension=0, tiled=True
        ).astype(jnp.float32),
        lax.psum_scatter(
            second_shift_grad.astype(jnp.bfloat16), "dp", scatter_dimension=0, tiled=True
        ).astype(jnp.float32),
        lax.psum_scatter(
            up_weight_grad.astype(jnp.bfloat16), "dp", scatter_dimension=0, tiled=True
        ).astype(jnp.float32),
        lax.psum_scatter(
            up_bias_grad.astype(jnp.bfloat16), "dp", scatter_dimension=0, tiled=True
        ).astype(jnp.float32),
        lax.psum_scatter(
            down_weight_grad.astype(jnp.bfloat16), "dp", scatter_dimension=0, tiled=True
        ).astype(jnp.float32),
        lax.psum_scatter(
            down_bias_grad.astype(jnp.bfloat16), "dp", scatter_dimension=0, tiled=True
        ).astype(jnp.float32),
    )
    (
        first_gain_grad,
        first_shift_grad,
        in_weight_grad,
        in_bias_grad,
        out_weight_grad,
        out_bias_grad,
        second_gain_grad,
        second_shift_grad,
        up_weight_grad,
        up_bias_grad,
        down_weight_grad,
        down_bias_grad,
    ) = (
        lax.psum(first_gain_grad.astype(jnp.bfloat16), "ctx").astype(jnp.float32),
        lax.psum(first_shift_grad.astype(jnp.bfloat16), "ctx").astype(jnp.float32),
        lax.psum(in_weight_grad.astype(jnp.bfloat16), "ctx").astype(jnp.float32),
        lax.psum(in_bias_grad.astype(jnp.bfloat16), "ctx").astype(jnp.float32),
        lax.psum(out_weight_grad.astype(jnp.bfloat16), "ctx").astype(jnp.float32),
        lax.psum(out_bias_grad.astype(jnp.bfloat16), "ctx").astype(jnp.float32),
        lax.psum(second_gain_grad.astype(jnp.bfloat16), "ctx").astype(jnp.float32),
        lax.psum(second_shift_grad.astype(jnp.bfloat16), "ctx").astype(jnp.float32),
        lax.psum(up_weight_grad.astype(jnp.bfloat16), "ctx").astype(jnp.float32),
        lax.psum(up_bias_grad.astype(jnp.bfloat16), "ctx").astype(jnp.float32),
        lax.psum(down_weight_grad.astype(jnp.bfloat16), "ctx").astype(jnp.float32),
        lax.psum(down_bias_grad.astype(jnp.bfloat16), "ctx").astype(jnp.float32),
    )
    return (
        layer_out,
        tokens_grad,
        first_gain_grad,
        first_shift_grad,
        in_weight_grad,
        in_bias_grad,
        out_weight_grad,
        out_bias_grad,
        second_gain_grad,
        second_shift_grad,
        up_weight_grad,
        up_bias_grad,
        down_weight_grad,
        down_bias_grad,
    )


masks = (0, 2, 1, 3)
dp_masks = (0, 4, 2, 6, 1, 5, 3, 7)
tile = 256
share = 20
lanes = 256
part = 3 * HEAD_DIM
root = math.sqrt(2.0 / math.pi)
low, wide = jnp.bfloat16, jnp.float32


def heads_split(mesh):
    return mesh.shape["ctx"] == 4 and mesh.shape["dp"] == 8


def swap(values, axis, bit):
    count = lax.axis_size(axis)
    return lax.ppermute(values, axis, [(i, i ^ bit) for i in range(count)])


def dp_gather(values, waits):
    index = lax.axis_index("dp")
    for bit in (1, 2, 4):
        if bit > 1:
            values = after(values, waits[bit // 2 - 1])
        other = swap(values, "dp", bit)
        upper = (index // bit) % 2 == 1
        values = jnp.concatenate(
            [jnp.where(upper, other, values), jnp.where(upper, values, other)], axis=0
        )
    return values


def dp_scatter_one(kept, sent):
    values = kept + swap(sent, "dp", 1).astype(wide)
    return values.reshape((2, 2) + values.shape[1:])


def dp_parts(values, axis, bit):
    mine = (lax.axis_index("dp") // bit) % 2
    sent = lax.dynamic_index_in_dim(values, 1 - mine, axis, keepdims=False).astype(low)
    return lax.dynamic_index_in_dim(values, mine, axis, keepdims=False), sent


def after(values, *others):
    return lax.optimization_barrier((values, *others))[0]


def dot_nt(left, right):
    return lax.dot_general(left, right, (((1,), (1,)), ((), ())), preferred_element_type=wide)


def dot_nn(left, right):
    return jnp.dot(left, right, preferred_element_type=wide)


def dot_tn(left, right):
    return lax.dot_general(left, right, (((0,), (0,)), ((), ())), preferred_element_type=wide)


def flip(values):
    return values.astype(wide).T.astype(values.dtype)


def whole(array):
    rank = len(array.shape)
    return pl.BlockSpec(array.shape, lambda *_: (0,) * rank)


def third(place):
    return lambda array: pl.BlockSpec(
        (array.shape[0], array.shape[1] // 3, array.shape[2]), lambda *_: (0, place, 0)
    )


def kernel_call(kernel, name, index, inputs, outputs, flops, exps=0, grid=(1,), scratch=()):
    arrays = [item[0] if isinstance(item, tuple) else item for item in inputs]
    specs = [
        (item[1](item[0]) if callable(item[1]) else item[1]) if isinstance(item, tuple) else whole(item)
        for item in inputs
    ]
    shapes = [item[0] if isinstance(item, tuple) else item for item in outputs]
    out_specs = [item[1] if isinstance(item, tuple) else whole(item) for item in outputs]
    moved = sum(math.prod(a.shape) * a.dtype.itemsize for a in arrays + shapes)
    return pl.pallas_call(
        kernel,
        grid_spec=pltpu.PrefetchScalarGridSpec(
            num_scalar_prefetch=1,
            grid=grid,
            in_specs=specs,
            out_specs=out_specs,
            scratch_shapes=list(scratch),
        ),
        out_shape=shapes,
        compiler_params=pltpu.CompilerParams(vmem_limit_bytes=56 * 1024 * 1024),
        cost_estimate=pl.CostEstimate(
            flops=flops // share, bytes_accessed=moved // share, transcendentals=exps // share
        ),
        name=name,
    )(index, *arrays)


def shape_of(shape, kind):
    return jax.ShapeDtypeStruct(shape, kind)


def place_of(index, spot, rows):
    return pl.ds(pl.multiple_of((index ^ masks[spot]) * rows, 128), rows)


def diagonal():
    keys = lax.broadcasted_iota(jnp.int32, (tile, tile), 0)
    queries = lax.broadcasted_iota(jnp.int32, (tile, tile), 1)
    return keys <= queries


def unit_of(values):
    center = values - jnp.mean(values, axis=-1, keepdims=True)
    spread = jnp.mean(center * center, axis=-1, keepdims=True)
    scale = lax.rsqrt(spread + epsilon)
    return center * scale, scale


def norm_pull(unit, scale, gain, upstream):
    scaled = upstream * gain
    return scale * (
        scaled
        - jnp.mean(scaled, axis=-1, keepdims=True)
        - unit * jnp.mean(scaled * unit, axis=-1, keepdims=True)
    )


def column_sum(values):
    return jnp.sum(values, axis=0, keepdims=True)


def pick_in_kernel(index_ref, in_ref, out_ref):
    width = in_ref.shape[1] // 3
    own = width // 4
    for ctx in range(4):

        @pl.when(index_ref[0] == ctx)
        def pick():
            for head in range(own // HEAD_DIM):
                for kind in range(3):
                    begin = kind * width + ctx * own + head * HEAD_DIM
                    target = head * part + kind * HEAD_DIM
                    out_ref[:, target : target + HEAD_DIM] = in_ref[:, begin : begin + HEAD_DIM]


def pick_rest_kernel(index_ref, out_weight_ref, up_ref, down_ref, out_ref):
    shard, width = out_weight_ref.shape
    out_ref[:shard, :] = out_weight_ref[...]
    for ctx in range(4):

        @pl.when(index_ref[0] == ctx)
        def pick():
            for owner in range(width // shard):
                begin = owner * 4 * shard + ctx * shard
                out_ref[shard : 2 * shard, owner * shard : (owner + 1) * shard] = up_ref[
                    :, begin : begin + shard
                ]
            out_ref[2 * shard :, :] = down_ref[ctx * shard : (ctx + 1) * shard, :]


def norm_kernel(
    index_ref,
    own_ref,
    far_ref,
    near_ref,
    last_ref,
    vector_ref,
    first_ref,
    turned_ref,
    unit_ref,
):
    rows = own_ref.shape[0]
    for spot, piece in enumerate((own_ref, far_ref, near_ref, last_ref)):
        here = slice(spot * rows, (spot + 1) * rows)
        unit, scale = unit_of(piece[...].astype(wide))
        unit_ref[:, here] = unit.T.astype(low)
        normed = unit * vector_ref[0:1, :] + vector_ref[1:2, :]
        first_ref[here, :] = normed.astype(low)
        turned_ref[:, here] = normed.T.astype(low)


def attend_kernel(
    index_ref,
    first_ref,
    low_half_ref,
    high_half_ref,
    bias_ref,
    weight_ref,
    mix_ref,
    keep_ref,
    send_ref,
    full_ref,
    stats_ref,
    q_s,
    k_s,
    v_s,
    o_s,
):
    total, width = first_ref.shape
    rows = total // 4
    index = index_ref[0]
    heads = width // lanes

    @pl.when(pl.program_id(0) == 0)
    def begin_all():
        shard = low_half_ref.shape[0] // 4
        for spot in range(8):
            source = low_half_ref if spot < 4 else high_half_ref
            block = source[(spot % 4) * shard : (spot % 4 + 1) * shard, :]
            there = pl.ds(pl.multiple_of((index_ref[1] ^ dp_masks[spot]) * shard, 32), shard)
            for head in range(heads):
                begin = head * lanes
                weight_ref[there, begin : begin + part] = block[:, head * part : (head + 1) * part]
                weight_ref[there, begin + part : begin + lanes] = jnp.zeros(
                    (shard, lanes - part), low
                )

    here = pl.ds(pl.multiple_of(pl.program_id(0) * lanes, lanes), lanes)
    mix_ref[...] = (dot_nn(first_ref[...], weight_ref[:, here]) + bias_ref[0]).astype(low)
    for spot in range(4):
        here = slice(spot * rows, (spot + 1) * rows)
        there = place_of(index, spot, rows)
        q_s[there, :] = mix_ref[here, 0:64] * jnp.bfloat16(0.125)
        k_s[there, :] = mix_ref[here, 64:128]
        v_s[there, :] = mix_ref[here, 128:192]
    allowed = diagonal()
    flipped = flip(v_s[...])
    for i in range(total // tile):
        begin, end = i * tile, (i + 1) * tile
        queries = q_s[begin:end, :]
        near = jnp.where(allowed, dot_nt(k_s[begin:end, :], queries), neg_large)
        top = jnp.max(near, axis=0, keepdims=True)
        if i > 0:
            past = dot_nt(k_s[:begin, :], queries)
            top = jnp.maximum(top, jnp.max(past, axis=0, keepdims=True))
        near = jnp.exp(near - top)
        amount = column_sum(near)
        context = dot_nn(flipped[:, begin:end], near.astype(low))
        if i > 0:
            past = jnp.exp(past - top)
            amount = amount + column_sum(past)
            context = context + dot_nn(flipped[:, :begin], past.astype(low))
        o_s[:, begin:end] = context / amount
        stats_ref[0, :, begin:end] = top + jnp.log(amount)
    for spot in range(4):
        block = o_s[:, place_of(index, spot, rows)]
        full_ref[:, spot * rows : (spot + 1) * rows] = block
        target = keep_ref if spot in (0, 2) else send_ref
        target[:, (spot // 2) * rows : (spot // 2 + 1) * rows] = block.astype(low)


def attend(index, first_low, low_half, high_half, bias):
    total, width = first_low.shape
    rows = total // 4
    heads = width // lanes
    features = heads * HEAD_DIM
    by_head = lambda h, s: (h, 0)
    pairs = heads * total * total // 2
    return kernel_call(
        attend_kernel,
        "attend",
        index,
        [first_low, low_half, high_half]
        + [(bias, pl.BlockSpec((1, 1, lanes), lambda h, s: (h, 0, 0)))],
        [
            shape_of((width, width), low),
            (shape_of((total, width), low), pl.BlockSpec((total, lanes), lambda h, s: (0, h))),
            (shape_of((features, 2 * rows), low), pl.BlockSpec((HEAD_DIM, 2 * rows), by_head)),
            (shape_of((features, 2 * rows), low), pl.BlockSpec((HEAD_DIM, 2 * rows), by_head)),
            (shape_of((features, total), wide), pl.BlockSpec((HEAD_DIM, total), by_head)),
            (
                shape_of((heads, 1, total), wide),
                pl.BlockSpec((1, 1, total), lambda h, s: (h, 0, 0)),
            ),
        ],
        pairs * 4 * 256 + 2 * total * width * width,
        pairs,
        (heads,),
        [pltpu.VMEM((total, HEAD_DIM), low)] * 3 + [pltpu.VMEM((HEAD_DIM, total), wide)],
    )


def project_kernel(
    index_ref,
    keep_ref,
    far_ref,
    near_ref,
    weight_ref,
    tokens_ref,
    vector_ref,
    residual_ref,
    second_ref,
    turned_ref,
):
    rows, width = tokens_ref.shape
    own = width // 4
    pieces = [keep_ref[:, :rows], far_ref[:, :rows], near_ref[:, :rows], near_ref[:, rows:]]
    residual = tokens_ref[...].astype(wide) + vector_ref[4:5, :]
    for spot in range(4):
        turned = flip(pieces[spot])
        group = index_ref[0] ^ masks[spot]
        weights = weight_ref[pl.ds(2 * group, 2)].reshape(own, width)
        residual = residual + dot_nn(turned, weights)
    residual_ref[...] = residual
    unit, scale = unit_of(residual)
    second_ref[...] = (unit * vector_ref[5:6, :] + vector_ref[6:7, :]).astype(low)
    for spot in range(4):
        turned_ref[spot * own : (spot + 1) * own, :] = pieces[spot]


def feed_kernel(
    index_ref,
    one_ref,
    two_ref,
    up_one_ref,
    up_two_ref,
    up_ref,
    down_ref,
    bias_ref,
    active_ref,
    hidden_ref,
    kept_ref,
    sent_ref,
    sum_ref,
):
    rows, width = one_ref.shape
    up = up_ref[...].reshape(width, width)
    down = down_ref[...].reshape(width, width)
    for spot in (1, 0):
        here = slice(spot * rows, (spot + 1) * rows)
        values = two_ref[...] if spot else one_ref[...]
        grads = up_two_ref[...] if spot else up_one_ref[...]
        hidden = dot_nn(values, up) + bias_ref[...]
        square = hidden * hidden
        bend = jnp.tanh(root * hidden * (1.0 + 0.044715 * square))
        active_ref[here, :] = (0.5 * hidden * (1.0 + bend)).astype(low)
        slope = 0.5 * (1.0 + bend) + 0.5 * hidden * (1.0 - bend * bend) * (
            root * (1.0 + 3 * 0.044715 * square)
        )
        grad = (slope * dot_nt(grads, down)).astype(low)
        hidden_ref[here, :] = grad
        sums = column_sum(grad.astype(wide))
        sum_ref[...] = sums if spot else sum_ref[...] + sums
        result = dot_nt(grad, up)
        if spot:
            sent_ref[...] = result.astype(low)
        else:
            kept_ref[...] = result


def halves(index_ref, block, kept_ref, sent_ref, pair):
    upper = index_ref[1] % 2 == 1
    kept_ref[pair] = jnp.where(upper, block[1], block[0])
    sent_ref[pair] = jnp.where(upper, block[0], block[1]).astype(low)


def feed_grad_kernel(
    index_ref,
    own_ref,
    far_ref,
    near_ref,
    last_ref,
    up_own_ref,
    up_far_ref,
    up_near_ref,
    up_last_ref,
    hidden_one_ref,
    hidden_two_ref,
    active_one_ref,
    active_two_ref,
    down_ref,
    out_ref,
    kept_one_ref,
    sent_one_ref,
    kept_two_ref,
    sent_two_ref,
):
    rows, width = own_ref.shape
    count, shard = out_ref.shape[0], out_ref.shape[1] // 2

    def halved(one, two):
        return (one[:rows, :], one[rows:, :], two[:rows, :], two[rows:, :])

    pairs = (
        ((own_ref, near_ref, far_ref, last_ref), halved(hidden_one_ref, hidden_two_ref)),
        (
            halved(active_one_ref, active_two_ref),
            (up_own_ref, up_near_ref, up_far_ref, up_last_ref),
        ),
    )
    for place, (lefts, rights) in enumerate(pairs):
        total = None
        for left, right in zip(lefts, rights):
            update = dot_tn(left[...], right[...])
            total = update if total is None else total + update
        total = total.astype(low).reshape(count, shard, width)
        out_ref[:, place * shard : (place + 1) * shard, :] = total
    down = down_ref[...].reshape(width, width)
    kept_one_ref[...] = dot_nn(active_one_ref[:rows, :], down)
    sent_one_ref[...] = dot_nn(active_one_ref[rows:, :], down).astype(low)
    kept_two_ref[...] = dot_nn(active_two_ref[:rows, :], down)
    sent_two_ref[...] = dot_nn(active_two_ref[rows:, :], down).astype(low)


def in_grad_kernel(
    index_ref,
    turned_ref,
    unit_ref,
    mix_ref,
    weight_ref,
    bias_ref,
    two_ref,
    up_one_ref,
    up_two_ref,
    kept_ref,
    sent_ref,
    rows_s,
):
    pairs, high, columns = kept_ref.shape
    width = mix_ref.shape[1]
    shard = width // (2 * pairs)
    own = columns // 3
    upper = index_ref[1] % 2 == 1
    rows_s[...] = jnp.zeros(rows_s.shape, wide)
    rows_s[4:8, :] = two_ref[...]
    sums = jnp.concatenate([bias_ref[head] for head in range(width // lanes)], axis=1)
    for ctx in range(4):

        @pl.when(index_ref[0] == ctx)
        def put():
            rows_s[8 + ctx : 9 + ctx, :] = up_one_ref[...] + up_two_ref[...]
            for head in range(own // HEAD_DIM):
                begin = ctx * own + head * HEAD_DIM
                for row, kind in ((2, 0), (3, 2)):
                    rows_s[row : row + 1, begin : begin + HEAD_DIM] = bias_ref[
                        head, :, kind * HEAD_DIM : (kind + 1) * HEAD_DIM
                    ]

    column = lax.broadcasted_iota(jnp.int32, (2 * shard, 128), 1)
    for pair in range(pairs):
        here = slice(2 * pair * shard, 2 * (pair + 1) * shard)
        weights = weight_ref[here, :].astype(wide)
        gain = jnp.sum(weights * dot_nn(unit_ref[here, :], mix_ref[...]), axis=1, keepdims=True)
        shift = jnp.sum(weights * sums, axis=1, keepdims=True)
        both = jnp.where(column == 0, gain, jnp.where(column == 1, shift, 0.0)).T
        rows_s[0:2, here] = both[0:2, :]
    for pair in range(pairs):
        begin = 2 * pair * shard
        block = dot_nn(turned_ref[begin : begin + 2 * shard, :], mix_ref[...])
        kept = jnp.where(upper, block[shard:, :], block[:shard, :])
        sent = jnp.where(upper, block[:shard, :], block[shard:, :]).astype(low)
        for head in range(columns // part):
            here = slice(head * part, (head + 1) * part)
            there = slice(head * lanes, head * lanes + part)
            kept_ref[pair, :shard, here] = kept[:, there]
            sent_ref[pair, :shard, here] = sent[:, there]
        one = rows_s[0:12, begin : begin + shard]
        two = rows_s[0:12, begin + shard : begin + 2 * shard]
        kept = jnp.where(upper, two, one)
        sent = jnp.where(upper, one, two)

        def lines(values):
            return jnp.concatenate(
                [
                    jnp.concatenate([values[6 * r + i : 6 * r + i + 1] for i in range(6)], axis=1)
                    for r in range(2)
                ],
                axis=0,
            )

        kept_ref[pair, shard : shard + 2, :] = lines(kept)
        sent_ref[pair, shard:, :] = jnp.concatenate(
            [lines(sent), jnp.zeros((high - shard - 2, columns), wide)], axis=0
        ).astype(low)
        kept_ref[pair, shard + 2 :, :] = jnp.zeros((high - shard - 2, columns), wide)


def turn_kernel(
    index_ref,
    kept_ref,
    core_ref,
    far_ref,
    residual_ref,
    cotangent_ref,
    weight_ref,
    vector_ref,
    grad_ref,
    attn_ref,
    keep_ref,
    send_ref,
    sum_ref,
):
    rows, width = residual_ref.shape
    own = width // 4
    grad = kept_ref[...] + core_ref[...].astype(wide) + far_ref[...].astype(wide)
    unit, scale = unit_of(residual_ref[...])
    upstream = cotangent_ref[...].astype(wide)
    result = upstream + norm_pull(unit, scale, vector_ref[5:6, :], grad)
    grad_ref[...] = result
    attn = result.astype(low)
    attn_ref[...] = attn
    for spot in range(4):
        group = index_ref[0] ^ masks[spot]
        weights = weight_ref[pl.ds(2 * group, 2)].reshape(own, width)
        block = dot_nt(weights, attn).astype(low)
        target = keep_ref if spot in (0, 2) else send_ref
        target[:, (spot // 2) * rows : (spot // 2 + 1) * rows] = block
    sum_ref[0:1, :] = column_sum(grad * unit)
    sum_ref[1:2, :] = column_sum(grad)
    sum_ref[2:3, :] = column_sum(attn.astype(wide))
    sum_ref[3:4, :] = column_sum(upstream)


def out_grad_kernel(index_ref, turned_ref, attn_ref, kept_ref, sent_ref):
    width = turned_ref.shape[0]
    own = width // 4
    for spot in range(4):
        group = index_ref[0] ^ masks[spot]
        block = dot_nn(turned_ref[spot * own : (spot + 1) * own, :], attn_ref[...])
        halves(index_ref, block.reshape(2, own // 2, width), kept_ref, sent_ref, group)


def attend_back_kernel(
    index_ref,
    mix_ref,
    keep_ref,
    far_ref,
    near_ref,
    full_ref,
    stats_ref,
    out_ref,
    sum_ref,
    q_s,
    k_s,
    v_s,
    g_s,
    d_s,
    dq_s,
):
    total = mix_ref.shape[0]
    rows = total // 4
    index = index_ref[0]
    pieces = [keep_ref[:, :rows], far_ref[:, :rows], near_ref[:, :rows], near_ref[:, rows:]]
    for spot in range(4):
        here = slice(spot * rows, (spot + 1) * rows)
        there = place_of(index, spot, rows)
        q_s[there, :] = mix_ref[here, 0:64] * jnp.bfloat16(0.125)
        k_s[there, :] = mix_ref[here, 64:128]
        v_s[there, :] = mix_ref[here, 128:192]
        block = pieces[spot]
        g_s[:, there] = block
        d_s[:, there] = column_sum(block.astype(wide) * full_ref[:, here])
    allowed = diagonal()
    turned = flip(g_s[...])
    flipped = flip(k_s[...])
    count = total // tile
    for j in range(count):
        begin, end = j * tile, (j + 1) * tile
        keys, values = k_s[begin:end, :], v_s[begin:end, :]
        probs = jnp.exp(dot_nt(keys, q_s[begin:, :]) - stats_ref[0, :, begin:])
        near = jnp.where(allowed, probs[:, :tile], 0.0)
        probs = near if j == count - 1 else jnp.concatenate([near, probs[:, tile:]], axis=1)
        scores = (probs * (dot_nn(values, g_s[:, begin:]) - d_s[:, begin:])).astype(low)
        grad_value = dot_nn(probs.astype(low), turned[begin:, :])
        grad_key = dot_nn(scores, q_s[begin:, :])
        update = dot_nn(flipped[:, begin:end], scores)
        if j == 0:
            dq_s[...] = update
        else:
            dq_s[:, begin:] = dq_s[:, begin:] + update
        k_s[begin:end, :] = grad_key.astype(low)
        v_s[begin:end, :] = grad_value.astype(low)
    q_s[...] = (dq_s[...] * 0.125).T.astype(low)
    for spot in range(4):
        here = slice(spot * rows, (spot + 1) * rows)
        there = place_of(index, spot, rows)
        out_ref[here, 0:64] = q_s[there, :]
        out_ref[here, 64:128] = k_s[there, :]
        out_ref[here, 128:192] = v_s[there, :]
        out_ref[here, 192:256] = jnp.zeros((rows, 64), low)
    sum_ref[0] = column_sum(out_ref[...].astype(wide))


def attend_back(index, mix, keep, far, near, full, stats):
    total, width = mix.shape
    heads = width // lanes
    by_head = lambda h, s: (h, 0)
    half = pl.BlockSpec((HEAD_DIM, total // 2), by_head)
    slab = pl.BlockSpec((total, lanes), lambda h, s: (0, h))
    pairs = heads * total * total // 2
    return kernel_call(
        attend_back_kernel,
        "attend_back",
        index,
        [(mix, slab), (keep, half), (far, half), (near, half)]
        + [(full, pl.BlockSpec((HEAD_DIM, total), by_head))]
        + [(stats, pl.BlockSpec((1, 1, total), lambda h, s: (h, 0, 0)))],
        [
            (shape_of((total, width), low), slab),
            (
                shape_of((heads, 1, lanes), wide),
                pl.BlockSpec((1, 1, lanes), lambda h, s: (h, 0, 0)),
            ),
        ],
        pairs * 10 * 256,
        pairs,
        (heads,),
        [pltpu.VMEM((total, HEAD_DIM), low)] * 3
        + [
            pltpu.VMEM((HEAD_DIM, total), low),
            pltpu.VMEM((1, total), wide),
            pltpu.VMEM((HEAD_DIM, total), wide),
        ],
    )


def first_back_kernel(
    index_ref, mix_ref, weight_ref, kept_one_ref, sent_one_ref, kept_two_ref, sent_two_ref
):
    rows = kept_one_ref.shape[0]
    targets = (kept_one_ref, kept_two_ref, sent_one_ref, sent_two_ref)
    for spot in range(4):
        grad = dot_nt(mix_ref[spot * rows : (spot + 1) * rows, :], weight_ref[...])
        targets[spot][...] = grad.astype(targets[spot].dtype)


def tokens_kernel(
    index_ref, kept_ref, core_ref, far_ref, tokens_ref, residual_ref, vector_ref, out_ref
):
    rows = tokens_ref.shape[0]
    grad = kept_ref[...] + core_ref[...].astype(wide) + far_ref[...].astype(wide)
    unit, scale = unit_of(tokens_ref[...].astype(wide))
    result = residual_ref[...] + norm_pull(unit, scale, vector_ref[0:1, :], grad)
    out_ref[...] = result.astype(low)


def spread_kernel(index_ref, own_ref, far_ref, near_ref, up_ref, down_ref):
    width = own_ref.shape[1]
    shard = own_ref.shape[0] // 2
    for ctx in range(4):
        for spot in range(4):

            @pl.when((index_ref[0] ^ ctx) == masks[spot])
            def put():
                source = [own_ref, far_ref, near_ref, near_ref][spot]
                base = 2 * shard if spot == 3 else 0
                block = source[base : base + shard, :].astype(wide)
                for owner in range(width // shard):
                    begin = (owner * 4 + ctx) * shard
                    up_ref[:, begin : begin + shard] = block[:, owner * shard : (owner + 1) * shard]
                down_ref[ctx * shard : (ctx + 1) * shard, :] = source[
                    base + shard : base + 2 * shard, :
                ].astype(wide)


def spread_in_kernel(index_ref, own_ref, far_ref, near_ref, in_ref, sum_ref):
    shard, width = in_ref.shape[0], in_ref.shape[1] // 3
    high, own = own_ref.shape[0], width // 4
    for ctx in range(4):
        for spot in range(4):

            @pl.when((index_ref[0] ^ ctx) == masks[spot])
            def put():
                source = [own_ref, far_ref, near_ref, near_ref][spot]
                base = high if spot == 3 else 0
                block = source[base : base + shard, :].astype(wide)
                for head in range(own // HEAD_DIM):
                    for kind in range(3):
                        begin = kind * width + ctx * own + head * HEAD_DIM
                        target = head * part + kind * HEAD_DIM
                        in_ref[:, begin : begin + HEAD_DIM] = block[:, target : target + HEAD_DIM]
                extra = source[base + shard : base + high, :].astype(wide)
                sum_ref[...] = extra if ctx == 0 else sum_ref[...] + extra


def pieces_of(values):
    far = swap(values, "ctx", 2)
    return values, far, swap(jnp.concatenate([values, far], axis=0), "ctx", 1)


def blocks_of(values):
    far = swap(values, "ctx", 2)
    near = swap(values, "ctx", 1)
    return values, far, near, swap(far, "ctx", 1)


def exchange(keep, send):
    rows = keep.shape[1] // 2
    far = swap(send, "ctx", 2)
    near = swap(jnp.concatenate([keep[:, rows:], far[:, rows:]], axis=1), "ctx", 1)
    return far, near


def split_body(
    tokens,
    first_gain,
    first_shift,
    in_weight,
    in_bias,
    out_weight,
    out_bias,
    second_gain,
    second_shift,
    up_weight,
    up_bias,
    down_weight,
    down_bias,
    cotangent,
):
    rows, width = tokens.shape
    total = 4 * rows
    n_dp = lax.axis_size("dp")
    shard = width // n_dp
    ctx = lax.axis_index("ctx")
    owner = lax.axis_index("dp")
    heads = width // HEAD_DIM // 4
    own = heads * HEAD_DIM
    index = jnp.stack([ctx, owner]).astype(jnp.int32)
    big = 2 * total * width * width
    small = 2 * rows * width * width
    row_wide, row_low = shape_of((rows, width), wide), shape_of((rows, width), low)

    (in_own,) = kernel_call(
        pick_in_kernel, "pick_in", index, [in_weight], [shape_of((shard, 3 * own), low)], 0
    )
    in_other = swap(in_own, "dp", 4)
    in_two = jnp.concatenate([in_own, in_other], axis=0)
    low_half = jnp.concatenate([in_two, swap(in_two, "dp", 2)], axis=0)
    high_half = swap(low_half, "dp", 1)
    (rest,) = kernel_call(
        pick_rest_kernel,
        "pick_rest",
        index,
        [out_weight, up_weight, after(down_weight, in_own)],
        [shape_of((3 * shard, width), low)],
        0,
    )
    rest = lax.all_gather(rest, "dp", axis=0, tiled=False)
    vectors = jnp.concatenate(
        [first_gain, first_shift, in_bias[0], in_bias[1], out_bias, second_gain, second_shift]
        + [down_bias, up_bias]
    ).reshape(1, 12 * shard)
    vectors = dp_gather(vectors, (in_two, low_half)).reshape(n_dp, 12, shard).transpose(1, 0, 2).reshape(12, width)
    vectors = vectors.astype(wide)
    hidden_bias = lax.dynamic_slice_in_dim(vectors, 8 + ctx, 1, 0)
    zeros = jnp.zeros((heads, HEAD_DIM), wide)
    mine = lax.dynamic_slice(vectors, (2, ctx * own), (2, own)).reshape(2, heads, HEAD_DIM)
    bias_full = jnp.concatenate([mine[0], zeros, mine[1], zeros], axis=1).reshape(heads, 1, lanes)

    first_low, first_turned, unit_turned = kernel_call(
        norm_kernel,
        "norm",
        index,
        [*blocks_of(tokens), vectors],
        [shape_of((total, width), low)] + [shape_of((width, total), low)] * 2,
        0,
    )
    upstream = blocks_of(cotangent)
    first_low, *upstream = lax.optimization_barrier((first_low, *upstream))
    in_full, mix, keep, send, context_full, stats = attend(
        index, first_low, low_half, high_half, bias_full
    )
    far, near = exchange(keep, send)
    out_block = (rest, third(0))
    up_block = (rest, third(1))
    down_block = (rest, third(2))
    residual, second_low, turned = kernel_call(
        project_kernel,
        "project",
        index,
        [keep, far, near, out_block, tokens, vectors],
        [row_wide, row_low, shape_of((width, rows), low)],
        small,
    )

    def feed(name, one, two, up_one, up_two):
        return kernel_call(
            feed_kernel,
            name,
            index,
            [one, two, up_one, up_two, up_block, down_block, hidden_bias],
            [shape_of((total // 2, width), low)] * 2
            + [row_wide, row_low, shape_of((1, width), wide)],
            3 * big // 2,
            total * width // 2,
        )

    far, near = swap(second_low, "ctx", 2), swap(second_low, "ctx", 1)
    active_one, hidden_one, kept_one, sent_one, up_sum_one = feed(
        "feed_one", second_low, near, upstream[0], upstream[2]
    )
    far = after(far, active_one)
    second = (second_low, far, near, swap(far, "ctx", 1))
    active_two, hidden_two, kept_two, sent_two, up_sum_two = feed(
        "feed_two", second[1], second[3], upstream[1], upstream[3]
    )
    core_one = swap(sent_one, "ctx", 1)
    passed = (kept_two + swap(sent_two, "ctx", 1).astype(wide)).astype(low)
    far = swap(passed, "ctx", 2)
    feed_grad, *branch = kernel_call(
        feed_grad_kernel,
        "feed_grad",
        index,
        [after(second[0], passed), *second[1:], *upstream, hidden_one, hidden_two]
        + [active_one, active_two, down_block],
        [shape_of((n_dp, 2 * shard, width), low), row_wide, row_low, row_wide, row_low],
        3 * big,
    )
    far, feed_grad, *branch = lax.optimization_barrier((far, feed_grad, *branch))
    feed_mine = lax.psum_scatter(feed_grad, "dp", scatter_dimension=0, tiled=False)
    grad_residual, grad_attn, keep, send, sums_two = kernel_call(
        turn_kernel,
        "turn",
        index,
        [kept_one, core_one, far, residual, cotangent, out_block, vectors],
        [
            row_wide,
            row_low,
            shape_of((own, 2 * rows), low),
            shape_of((own, 2 * rows), low),
            shape_of((4, width), wide),
        ],
        small,
    )
    out_kept, out_sent = kernel_call(
        out_grad_kernel,
        "out_grad",
        index,
        [turned, grad_attn],
        [shape_of((n_dp // 2, shard, width), wide), shape_of((n_dp // 2, shard, width), low)],
        small,
    )
    far = swap(send, "ctx", 2)
    late = after(far, out_sent)
    near = swap(jnp.concatenate([keep[:, rows:], late[:, rows:]], axis=1), "ctx", 1)
    branch_kept, branch_sent, kept_two, sent_two = branch
    branch_core = swap(branch_sent, "ctx", 1)
    passed = (kept_two + swap(sent_two, "ctx", 1).astype(wide)).astype(low)
    branch_far = swap(passed, "ctx", 2)
    grad_mix, bias_sums = attend_back(
        index, mix, after(keep, passed), far, near, context_full, stats
    )

    high = shard + 16
    out_half = dp_scatter_one(out_kept, out_sent)
    out_next, out_sent = dp_parts(out_half, 1, 2)
    kept_one, sent_one, kept_two, sent_two = kernel_call(
        first_back_kernel,
        "first_back",
        index,
        [after(grad_mix, out_half, branch_far), in_full],
        [row_wide, row_low, row_wide, row_low],
        big,
    )
    core_one = swap(sent_one, "ctx", 1)
    passed = (kept_two + swap(sent_two, "ctx", 1).astype(wide)).astype(low)
    far = swap(passed, "ctx", 2)
    out_sent = after(out_sent, passed)
    out_next = out_next + swap(out_sent, "dp", 2).astype(wide)
    in_kept, in_sent = kernel_call(
        in_grad_kernel,
        "in_grad",
        index,
        [after(first_turned, passed, out_sent), unit_turned, grad_mix, in_full]
        + [bias_sums, sums_two, up_sum_one, up_sum_two],
        [shape_of((n_dp // 2, high, 3 * own), wide), shape_of((n_dp // 2, high, 3 * own), low)],
        2 * big,
        scratch=[pltpu.VMEM((16, width), wide)],
    )
    out_next, out_sent = dp_parts(after(out_next, in_sent), 0, 4)
    (tokens_grad,) = kernel_call(
        tokens_kernel,
        "tokens",
        index,
        [kept_one, core_one, after(far, in_sent, out_sent), tokens, grad_residual, vectors],
        [row_low],
        0,
    )
    in_half = dp_scatter_one(after(in_kept, tokens_grad), in_sent)
    in_next, in_sent = dp_parts(in_half, 1, 2)
    feed_mine = after(feed_mine.reshape(2 * shard, width), in_sent)
    feed_far = swap(feed_mine, "ctx", 2)
    out_mine = (after(out_next, feed_mine) + swap(out_sent, "dp", 4).astype(wide)).astype(low)
    out_far = swap(out_mine, "ctx", 2)
    in_next = after(in_next, out_mine) + swap(in_sent, "dp", 2).astype(wide)
    in_next, in_sent = dp_parts(in_next, 0, 4)
    feed_near = jnp.concatenate([after(feed_mine, in_sent), feed_far], axis=0)
    feed_near = swap(feed_near, "ctx", 1)
    out_mine = (after(out_mine, in_sent).astype(wide) + out_far.astype(wide)).astype(low)
    out_weight_grad = out_mine.astype(wide) + swap(out_mine, "ctx", 1).astype(wide)
    in_mine = (after(in_next, out_mine) + swap(in_sent, "dp", 4).astype(wide)).astype(low)
    branch = branch_kept + branch_core.astype(wide) + branch_far.astype(wide)
    layer_out = (residual + branch + vectors[7]).astype(low)
    up_weight_grad, down_weight_grad = kernel_call(
        spread_kernel,
        "spread",
        index,
        [after(feed_mine, in_mine), feed_far, feed_near],
        [shape_of((shard, 4 * width), wide), shape_of((4 * shard, width), wide)],
        0,
    )
    in_far = swap(in_mine, "ctx", 2)
    in_near = jnp.concatenate([after(in_mine, up_weight_grad, layer_out), in_far], axis=0)
    in_near = swap(in_near, "ctx", 1)
    in_weight_grad, sums = kernel_call(
        spread_in_kernel,
        "spread_in",
        index,
        [in_mine, in_far, in_near],
        [shape_of((shard, 3 * width), wide), shape_of((high - shard, 3 * own), wide)],
        0,
    )
    sums = sums[:2].reshape(12, shard)
    return (
        layer_out,
        tokens_grad,
        sums[0],
        sums[1],
        in_weight_grad,
        sums[2:4],
        out_weight_grad,
        sums[6],
        sums[4],
        sums[5],
        up_weight_grad,
        sums[8:12].reshape(4 * shard),
        down_weight_grad,
        sums[7],
    )


def solution(mesh):
    in_specs = (
        P(("dp", "ctx"), None),
        P("dp"),
        P("dp"),
        P("dp", None),
        P(None, "dp"),
        P("dp", None),
        P("dp"),
        P("dp"),
        P("dp"),
        P("dp", None),
        P("dp"),
        P("dp", None),
        P("dp"),
        P(("dp", "ctx"), None),
    )
    out_specs = (
        P(("dp", "ctx"), None),
        P(("dp", "ctx"), None),
        P("dp"),
        P("dp"),
        P("dp", None),
        P(None, "dp"),
        P("dp", None),
        P("dp"),
        P("dp"),
        P("dp"),
        P("dp", None),
        P("dp"),
        P("dp", None),
        P("dp"),
    )
    chosen = split_body if heads_split(mesh) else gathered_body
    return jax.shard_map(chosen, mesh=mesh, in_specs=in_specs, out_specs=out_specs, check_vma=False)
```

```python
import functools
import math

import jax
import jax.numpy as jnp
from jax import lax
from jax.experimental import pallas as pl
from jax.experimental.pallas import tpu as pltpu
from jax.sharding import PartitionSpec as P

HEAD_DIM = 64


epsilon = 1e-05
neg_large = -1e30


def layer_norm(values, gain, shift):
    center = values - jnp.mean(values, axis=-1, keepdims=True)
    spread = jnp.mean(center * center, axis=-1, keepdims=True)
    return center * lax.rsqrt(spread + epsilon) * gain + shift


def norm_back(values, gain, shift, upstream):
    result, pullback = jax.vjp(layer_norm, values, gain, shift)
    return pullback(upstream)


def smooth_gate(values):
    return jax.nn.gelu(values, approximate=True)


def forward_block(state, query_heads, query_pos, key_blk, value_blk, key_pos, factor):
    row_max, row_total, accumulated = state
    scores = (
        jnp.einsum("qhd,khd->hqk", query_heads, key_blk, preferred_element_type=jnp.float32)
        * factor
    )
    allowed = (query_pos[:, None] >= key_pos[None, :])[None]
    scores = jnp.where(allowed, scores, neg_large)
    new_max = jnp.maximum(row_max, jnp.max(scores, axis=-1))
    rescale = jnp.exp(row_max - new_max)
    weights = jnp.where(allowed, jnp.exp(scores - new_max[:, :, None]), 0.0)
    row_total = row_total * rescale + jnp.sum(weights, axis=-1)
    update = jnp.einsum(
        "hqk,khd->qhd", weights.astype(jnp.bfloat16), value_blk, preferred_element_type=jnp.float32
    )
    accumulated = accumulated * rescale.T[:, :, None] + update
    return (new_max, row_total, accumulated)


def pair_grads(
    query_heads, grad_heads, stats, deltas, query_pos, key_blk, value_blk, key_pos, factor
):
    scores = (
        jnp.einsum("qhd,khd->hqk", query_heads, key_blk, preferred_element_type=jnp.float32)
        * factor
    )
    allowed = (query_pos[:, None] >= key_pos[None, :])[None]
    probs = jnp.where(allowed, jnp.exp(scores - stats[:, :, None]), 0.0)
    grad_probs = jnp.einsum(
        "qhd,khd->hqk", grad_heads, value_blk, preferred_element_type=jnp.float32
    )
    grad_scores = (probs * (grad_probs - deltas[:, :, None])).astype(jnp.bfloat16)
    grad_query = (
        jnp.einsum("hqk,khd->qhd", grad_scores, key_blk, preferred_element_type=jnp.float32)
        * factor
    )
    grad_key = (
        jnp.einsum("hqk,qhd->khd", grad_scores, query_heads, preferred_element_type=jnp.float32)
        * factor
    )
    grad_value = jnp.einsum(
        "hqk,qhd->khd", probs.astype(jnp.bfloat16), grad_heads, preferred_element_type=jnp.float32
    )
    return (grad_query, grad_key, grad_value)


def over_keys(state, key_part, value_part, begin_row, top_query, place, block_fn):
    amount, head_count, head_dim = key_part.shape
    stride = math.gcd(amount, 512)
    key_blocks = key_part.reshape(amount // stride, stride, head_count, head_dim)
    value_blocks = value_part.reshape(amount // stride, stride, head_count, head_dim)
    offsets = begin_row + jnp.arange(amount // stride, dtype=jnp.int32) * stride

    def over_step_fn(inner, operands):
        key_blk, value_blk, offset = operands
        key_pos = place(offset + jnp.arange(stride, dtype=jnp.int32))

        def over_compute(current):
            return block_fn(current, key_blk, value_blk, key_pos)

        def keep(current):
            return current

        return (lax.cond(jnp.min(key_pos) <= top_query, over_compute, keep, inner), None)

    state, unused = lax.scan(over_step_fn, state, (key_blocks, value_blocks, offsets))
    return state


def gathered_body(
    tokens,
    first_gain,
    first_shift,
    in_weight,
    in_bias,
    out_weight,
    out_bias,
    second_gain,
    second_shift,
    up_weight,
    up_bias,
    down_weight,
    down_bias,
    cotangent,
):
    (
        first_gain,
        first_shift,
        in_weight,
        in_bias,
        out_weight,
        out_bias,
        second_gain,
        second_shift,
        up_weight,
        up_bias,
        down_weight,
        down_bias,
    ) = (
        lax.all_gather(first_gain, "dp", axis=0, tiled=True),
        lax.all_gather(first_shift, "dp", axis=0, tiled=True),
        lax.all_gather(in_weight, "dp", axis=0, tiled=True),
        lax.all_gather(in_bias, "dp", axis=1, tiled=True),
        lax.all_gather(out_weight, "dp", axis=0, tiled=True),
        lax.all_gather(out_bias, "dp", axis=0, tiled=True),
        lax.all_gather(second_gain, "dp", axis=0, tiled=True),
        lax.all_gather(second_shift, "dp", axis=0, tiled=True),
        lax.all_gather(up_weight, "dp", axis=0, tiled=True),
        lax.all_gather(up_bias, "dp", axis=0, tiled=True),
        lax.all_gather(down_weight, "dp", axis=0, tiled=True),
        lax.all_gather(down_bias, "dp", axis=0, tiled=True),
    )
    rows_dev = tokens.shape[0]
    width = tokens.shape[1]
    head_dim = HEAD_DIM
    head_count = width // head_dim
    factor = 1.0 / math.sqrt(head_dim)
    my_index = lax.axis_index("ctx")

    def place(rows):
        return rows

    query_pos = place(my_index * rows_dev + jnp.arange(rows_dev, dtype=jnp.int32))
    top_query = jnp.max(query_pos)
    inputs = tokens.astype(jnp.float32)
    gain_one = first_gain.astype(jnp.float32)
    shift_one = first_shift.astype(jnp.float32)
    first_low = layer_norm(inputs, gain_one, shift_one).astype(jnp.bfloat16)
    bias_full = jnp.concatenate([in_bias[0], jnp.zeros((width,), jnp.bfloat16), in_bias[1]]).astype(
        jnp.float32
    )
    mixture = (
        jnp.dot(first_low, in_weight, preferred_element_type=jnp.float32) + bias_full
    ).astype(jnp.bfloat16)
    query_rows = mixture[:, :width]
    key_rows = mixture[:, width : 2 * width]
    value_rows = mixture[:, 2 * width :]
    query_heads = query_rows.reshape(rows_dev, head_count, head_dim)

    def forward_fold(state, portion, begin_row):
        key_part, value_part = portion
        amount = key_part.shape[0]

        def block_fn(inner, key_blk, value_blk, key_pos):
            return forward_block(inner, query_heads, query_pos, key_blk, value_blk, key_pos, factor)

        return over_keys(
            state,
            key_part.reshape(amount, head_count, head_dim),
            value_part.reshape(amount, head_count, head_dim),
            begin_row,
            top_query,
            place,
            block_fn,
        )

    start_state = (
        jnp.full((head_count, rows_dev), neg_large, jnp.float32),
        jnp.zeros((head_count, rows_dev), jnp.float32),
        jnp.zeros((rows_dev, head_count, head_dim), jnp.float32),
    )
    row_max, row_total, accumulated = forward_fold(
        start_state,
        (
            lax.all_gather(key_rows, "ctx", axis=0, tiled=True),
            lax.all_gather(value_rows, "ctx", axis=0, tiled=True),
        ),
        jnp.int32(0),
    )
    stats = row_max + jnp.log(row_total)
    context_heads = accumulated / row_total.T[:, :, None]
    context_low = context_heads.reshape(rows_dev, width).astype(jnp.bfloat16)
    residual = (
        inputs
        + jnp.dot(context_low, out_weight, preferred_element_type=jnp.float32)
        + out_bias.astype(jnp.float32)
    )
    gain_two = second_gain.astype(jnp.float32)
    shift_two = second_shift.astype(jnp.float32)
    second_low = layer_norm(residual, gain_two, shift_two).astype(jnp.bfloat16)
    hidden = jnp.dot(second_low, up_weight, preferred_element_type=jnp.float32) + up_bias.astype(
        jnp.float32
    )
    activated, gate_back = jax.vjp(smooth_gate, hidden)
    active_low = activated.astype(jnp.bfloat16)
    layer_out = (
        residual
        + jnp.dot(active_low, down_weight, preferred_element_type=jnp.float32)
        + down_bias.astype(jnp.float32)
    ).astype(jnp.bfloat16)
    upstream = cotangent.astype(jnp.float32)
    down_bias_grad = jnp.sum(upstream, axis=0)
    down_weight_grad = jnp.einsum(
        "tf,td->fd", active_low, cotangent, preferred_element_type=jnp.float32
    )
    (grad_hidden,) = gate_back(
        jnp.einsum("td,fd->tf", cotangent, down_weight, preferred_element_type=jnp.float32)
    )
    grad_hidden = grad_hidden.astype(jnp.bfloat16)
    up_weight_grad = jnp.einsum(
        "td,tf->df", second_low, grad_hidden, preferred_element_type=jnp.float32
    )
    up_bias_grad = jnp.sum(grad_hidden.astype(jnp.float32), axis=0)
    grad_second = jnp.einsum(
        "tf,df->td", grad_hidden, up_weight, preferred_element_type=jnp.float32
    )
    grad_residual, second_gain_grad, second_shift_grad = norm_back(
        residual, gain_two, shift_two, grad_second
    )
    grad_residual = grad_residual + upstream
    grad_attn = grad_residual.astype(jnp.bfloat16)
    out_bias_grad = jnp.sum(grad_attn.astype(jnp.float32), axis=0)
    out_weight_grad = jnp.einsum(
        "td,te->de", context_low, grad_attn, preferred_element_type=jnp.float32
    )
    grad_context = jnp.einsum(
        "te,de->td", grad_attn, out_weight, preferred_element_type=jnp.float32
    ).astype(jnp.bfloat16)
    grad_heads = grad_context.reshape(rows_dev, head_count, head_dim)
    deltas = jnp.sum(grad_heads.astype(jnp.float32) * context_heads, axis=-1).T

    def query_fold(state, portion, begin_row):
        key_part, value_part = portion
        amount = key_part.shape[0]

        def block_fn(inner, key_blk, value_blk, key_pos):
            grad_query, grad_key, grad_value = pair_grads(
                query_heads,
                grad_heads,
                stats,
                deltas,
                query_pos,
                key_blk,
                value_blk,
                key_pos,
                factor,
            )
            return inner + grad_query

        return over_keys(
            state,
            key_part.reshape(amount, head_count, head_dim),
            value_part.reshape(amount, head_count, head_dim),
            begin_row,
            top_query,
            place,
            block_fn,
        )

    zero_heads = jnp.zeros((rows_dev, head_count, head_dim), jnp.float32)
    key_all, value_all = (
        lax.all_gather(key_rows, "ctx", axis=0, tiled=True),
        lax.all_gather(value_rows, "ctx", axis=0, tiled=True),
    )
    grad_query = query_fold(zero_heads, (key_all, value_all), 0)
    amount = lax.axis_size("ctx") * rows_dev
    stride = math.gcd(amount, 512)
    key_part = key_all.reshape(amount // stride, stride, head_count, head_dim)
    value_part = value_all.reshape(amount // stride, stride, head_count, head_dim)
    offsets = jnp.arange(amount // stride, dtype=jnp.int32) * stride

    def key_step_fn(unused, operands):
        key_blk, value_blk, offset = operands
        key_pos = place(offset + jnp.arange(stride, dtype=jnp.int32))

        def key_compute(blocks_in):
            grad_query_part, grad_key, grad_value = pair_grads(
                query_heads,
                grad_heads,
                stats,
                deltas,
                query_pos,
                blocks_in[0],
                blocks_in[1],
                key_pos,
                factor,
            )
            return jnp.concatenate(
                [grad_key.reshape(stride, width), grad_value.reshape(stride, width)], axis=1
            )

        def nothing(blocks_in):
            return jnp.zeros((stride, 2 * width), jnp.float32)

        return (
            unused,
            lax.cond(jnp.min(key_pos) <= top_query, key_compute, nothing, (key_blk, value_blk)),
        )

    unused, stacked = lax.scan(key_step_fn, 0, (key_part, value_part, offsets))
    grad_pairs = lax.psum_scatter(
        stacked.reshape(amount, 2 * width).astype(jnp.bfloat16),
        "ctx",
        scatter_dimension=0,
        tiled=True,
    ).astype(jnp.float32)
    grad_key = grad_pairs[:, :width]
    grad_value = grad_pairs[:, width:]
    grad_mixture = jnp.concatenate(
        [grad_query.reshape(rows_dev, width), grad_key, grad_value], axis=1
    ).astype(jnp.bfloat16)
    in_weight_grad = jnp.einsum(
        "td,te->de", first_low, grad_mixture, preferred_element_type=jnp.float32
    )
    in_bias_grad = jnp.stack(
        [
            jnp.sum(grad_mixture[:, :width].astype(jnp.float32), axis=0),
            jnp.sum(grad_mixture[:, 2 * width :].astype(jnp.float32), axis=0),
        ]
    )
    grad_first = jnp.einsum(
        "te,de->td", grad_mixture, in_weight, preferred_element_type=jnp.float32
    )
    grad_inputs, first_gain_grad, first_shift_grad = norm_back(
        inputs, gain_one, shift_one, grad_first
    )
    tokens_grad = (grad_inputs + grad_residual).astype(jnp.bfloat16)
    (
        first_gain_grad,
        first_shift_grad,
        in_weight_grad,
        in_bias_grad,
        out_weight_grad,
        out_bias_grad,
        second_gain_grad,
        second_shift_grad,
        up_weight_grad,
        up_bias_grad,
        down_weight_grad,
        down_bias_grad,
    ) = (
        lax.psum_scatter(
            first_gain_grad.astype(jnp.bfloat16), "dp", scatter_dimension=0, tiled=True
        ).astype(jnp.float32),
        lax.psum_scatter(
            first_shift_grad.astype(jnp.bfloat16), "dp", scatter_dimension=0, tiled=True
        ).astype(jnp.float32),
        lax.psum_scatter(
            in_weight_grad.astype(jnp.bfloat16), "dp", scatter_dimension=0, tiled=True
        ).astype(jnp.float32),
        lax.psum_scatter(
            in_bias_grad.astype(jnp.bfloat16), "dp", scatter_dimension=1, tiled=True
        ).astype(jnp.float32),
        lax.psum_scatter(
            out_weight_grad.astype(jnp.bfloat16), "dp", scatter_dimension=0, tiled=True
        ).astype(jnp.float32),
        lax.psum_scatter(
            out_bias_grad.astype(jnp.bfloat16), "dp", scatter_dimension=0, tiled=True
        ).astype(jnp.float32),
        lax.psum_scatter(
            second_gain_grad.astype(jnp.bfloat16), "dp", scatter_dimension=0, tiled=True
        ).astype(jnp.float32),
        lax.psum_scatter(
            second_shift_grad.astype(jnp.bfloat16), "dp", scatter_dimension=0, tiled=True
        ).astype(jnp.float32),
        lax.psum_scatter(
            up_weight_grad.astype(jnp.bfloat16), "dp", scatter_dimension=0, tiled=True
        ).astype(jnp.float32),
        lax.psum_scatter(
            up_bias_grad.astype(jnp.bfloat16), "dp", scatter_dimension=0, tiled=True
        ).astype(jnp.float32),
        lax.psum_scatter(
            down_weight_grad.astype(jnp.bfloat16), "dp", scatter_dimension=0, tiled=True
        ).astype(jnp.float32),
        lax.psum_scatter(
            down_bias_grad.astype(jnp.bfloat16), "dp", scatter_dimension=0, tiled=True
        ).astype(jnp.float32),
    )
    (
        first_gain_grad,
        first_shift_grad,
        in_weight_grad,
        in_bias_grad,
        out_weight_grad,
        out_bias_grad,
        second_gain_grad,
        second_shift_grad,
        up_weight_grad,
        up_bias_grad,
        down_weight_grad,
        down_bias_grad,
    ) = (
        lax.psum(first_gain_grad.astype(jnp.bfloat16), "ctx").astype(jnp.float32),
        lax.psum(first_shift_grad.astype(jnp.bfloat16), "ctx").astype(jnp.float32),
        lax.psum(in_weight_grad.astype(jnp.bfloat16), "ctx").astype(jnp.float32),
        lax.psum(in_bias_grad.astype(jnp.bfloat16), "ctx").astype(jnp.float32),
        lax.psum(out_weight_grad.astype(jnp.bfloat16), "ctx").astype(jnp.float32),
        lax.psum(out_bias_grad.astype(jnp.bfloat16), "ctx").astype(jnp.float32),
        lax.psum(second_gain_grad.astype(jnp.bfloat16), "ctx").astype(jnp.float32),
        lax.psum(second_shift_grad.astype(jnp.bfloat16), "ctx").astype(jnp.float32),
        lax.psum(up_weight_grad.astype(jnp.bfloat16), "ctx").astype(jnp.float32),
        lax.psum(up_bias_grad.astype(jnp.bfloat16), "ctx").astype(jnp.float32),
        lax.psum(down_weight_grad.astype(jnp.bfloat16), "ctx").astype(jnp.float32),
        lax.psum(down_bias_grad.astype(jnp.bfloat16), "ctx").astype(jnp.float32),
    )
    return (
        layer_out,
        tokens_grad,
        first_gain_grad,
        first_shift_grad,
        in_weight_grad,
        in_bias_grad,
        out_weight_grad,
        out_bias_grad,
        second_gain_grad,
        second_shift_grad,
        up_weight_grad,
        up_bias_grad,
        down_weight_grad,
        down_bias_grad,
    )


masks = (0, 2, 1, 3)
dp_masks = (0, 4, 2, 6, 1, 5, 3, 7)
tile = 256
share = 20
lanes = 256
part = 3 * HEAD_DIM
root = math.sqrt(2.0 / math.pi)
low, wide = jnp.bfloat16, jnp.float32


def heads_split(mesh):
    return mesh.shape["ctx"] == 4 and mesh.shape["dp"] == 8


def swap(values, axis, bit):
    count = lax.axis_size(axis)
    return lax.ppermute(values, axis, [(i, i ^ bit) for i in range(count)])


def dp_gather(values, waits):
    index = lax.axis_index("dp")
    for bit in (1, 2, 4):
        if bit > 1:
            values = after(values, waits[bit // 2 - 1])
        other = swap(values, "dp", bit)
        upper = (index // bit) % 2 == 1
        values = jnp.concatenate(
            [jnp.where(upper, other, values), jnp.where(upper, values, other)], axis=0
        )
    return values


def dp_scatter_one(kept, sent):
    values = kept + swap(sent, "dp", 1).astype(wide)
    return values.reshape((2, 2) + values.shape[1:])


def dp_parts(values, axis, bit):
    mine = (lax.axis_index("dp") // bit) % 2
    sent = lax.dynamic_index_in_dim(values, 1 - mine, axis, keepdims=False).astype(low)
    return lax.dynamic_index_in_dim(values, mine, axis, keepdims=False), sent


def after(values, *others):
    return lax.optimization_barrier((values, *others))[0]


def dot_nt(left, right):
    return lax.dot_general(left, right, (((1,), (1,)), ((), ())), preferred_element_type=wide)


def dot_nn(left, right):
    return jnp.dot(left, right, preferred_element_type=wide)


def dot_tn(left, right):
    return lax.dot_general(left, right, (((0,), (0,)), ((), ())), preferred_element_type=wide)


def flip(values):
    return values.astype(wide).T.astype(values.dtype)


def third_of(rest_ref, place):
    count, high, width = rest_ref.shape
    shard = high // 3
    return rest_ref[:, place * shard : (place + 1) * shard, :].reshape(count * shard, width)


def kernel_call(kernel, name, index, inputs, outputs, flops, exps=0, grid=(1,), scratch=()):
    arrays, shapes = list(inputs), list(outputs)
    held = pl.BlockSpec(memory_space=pltpu.VMEM)
    specs, out_specs = [held] * len(arrays), [held] * len(shapes)
    moved = sum(math.prod(a.shape) * a.dtype.itemsize for a in arrays + shapes)
    return pl.pallas_call(
        kernel,
        grid_spec=pltpu.PrefetchScalarGridSpec(
            num_scalar_prefetch=1,
            grid=grid,
            in_specs=specs,
            out_specs=out_specs,
            scratch_shapes=list(scratch),
        ),
        out_shape=shapes,
        compiler_params=pltpu.CompilerParams(vmem_limit_bytes=24 * 1024 * 1024),
        cost_estimate=pl.CostEstimate(
            flops=flops // share, bytes_accessed=moved // share, transcendentals=exps // share
        ),
        name=name,
    )(index, *arrays)


def shape_of(shape, kind):
    return jax.ShapeDtypeStruct(shape, kind)


def place_of(index, spot, rows):
    return pl.ds(pl.multiple_of((index ^ masks[spot]) * rows, 128), rows)


def diagonal():
    keys = lax.broadcasted_iota(jnp.int32, (tile, tile), 0)
    queries = lax.broadcasted_iota(jnp.int32, (tile, tile), 1)
    return keys <= queries


def unit_of(values):
    center = values - jnp.mean(values, axis=-1, keepdims=True)
    spread = jnp.mean(center * center, axis=-1, keepdims=True)
    scale = lax.rsqrt(spread + epsilon)
    return center * scale, scale


def norm_pull(unit, scale, gain, upstream):
    scaled = upstream * gain
    return scale * (
        scaled
        - jnp.mean(scaled, axis=-1, keepdims=True)
        - unit * jnp.mean(scaled * unit, axis=-1, keepdims=True)
    )


def column_sum(values):
    return jnp.sum(values, axis=0, keepdims=True)


def pick_in_kernel(index_ref, in_ref, out_ref):
    width = in_ref.shape[1] // 3
    own = width // 4
    for ctx in range(4):

        @pl.when(index_ref[0] == ctx)
        def pick():
            for head in range(own // HEAD_DIM):
                for kind in range(3):
                    begin = kind * width + ctx * own + head * HEAD_DIM
                    target = head * part + kind * HEAD_DIM
                    out_ref[:, target : target + HEAD_DIM] = in_ref[:, begin : begin + HEAD_DIM]


def pick_rest_kernel(index_ref, out_weight_ref, up_ref, down_ref, out_ref):
    shard, width = out_weight_ref.shape
    out_ref[:shard, :] = out_weight_ref[...]
    for ctx in range(4):

        @pl.when(index_ref[0] == ctx)
        def pick():
            for owner in range(width // shard):
                begin = owner * 4 * shard + ctx * shard
                out_ref[shard : 2 * shard, owner * shard : (owner + 1) * shard] = up_ref[
                    :, begin : begin + shard
                ]
            out_ref[2 * shard :, :] = down_ref[ctx * shard : (ctx + 1) * shard, :]


def norm_kernel(
    index_ref,
    own_ref,
    far_ref,
    near_ref,
    last_ref,
    vector_ref,
    first_ref,
    turned_ref,
    unit_ref,
):
    rows = own_ref.shape[0]
    for spot, piece in enumerate((own_ref, far_ref, near_ref, last_ref)):
        here = slice(spot * rows, (spot + 1) * rows)
        unit, scale = unit_of(piece[...].astype(wide))
        unit_ref[:, here] = unit.T.astype(low)
        normed = unit * vector_ref[0:1, :] + vector_ref[1:2, :]
        first_ref[here, :] = normed.astype(low)
        turned_ref[:, here] = normed.T.astype(low)


def attend_kernel(
    index_ref,
    first_ref,
    low_half_ref,
    high_half_ref,
    bias_ref,
    weight_ref,
    mix_ref,
    keep_ref,
    send_ref,
    full_ref,
    stats_ref,
    q_s,
    k_s,
    v_s,
    o_s,
):
    total, width = first_ref.shape
    rows = total // 4
    index = index_ref[0]
    heads = width // lanes

    @pl.when(pl.program_id(0) == 0)
    def begin_all():
        shard = low_half_ref.shape[0] // 4
        for spot in range(8):
            source = low_half_ref if spot < 4 else high_half_ref
            block = source[(spot % 4) * shard : (spot % 4 + 1) * shard, :]
            there = pl.ds(pl.multiple_of((index_ref[1] ^ dp_masks[spot]) * shard, 32), shard)
            for head in range(heads):
                begin = head * lanes
                weight_ref[there, begin : begin + part] = block[:, head * part : (head + 1) * part]
                weight_ref[there, begin + part : begin + lanes] = jnp.zeros(
                    (shard, lanes - part), low
                )

    head = pl.program_id(0)
    slab = pl.ds(pl.multiple_of(head * lanes, lanes), lanes)
    lines = pl.ds(pl.multiple_of(head * HEAD_DIM, HEAD_DIM), HEAD_DIM)
    for spot in range(4):
        here = slice(spot * rows, (spot + 1) * rows)
        there = place_of(index, spot, rows)
        block = (dot_nn(first_ref[here, :], weight_ref[:, slab]) + bias_ref[head]).astype(low)
        mix_ref[here, slab] = block
        q_s[there, :] = block[:, 0:64] * jnp.bfloat16(0.125)
        k_s[there, :] = block[:, 64:128]
        v_s[there, :] = block[:, 128:192]
    allowed = diagonal()
    flipped = flip(v_s[...])
    for i in range(total // tile):
        begin, end = i * tile, (i + 1) * tile
        queries = q_s[begin:end, :]
        near = jnp.where(allowed, dot_nt(k_s[begin:end, :], queries), neg_large)
        top = jnp.max(near, axis=0, keepdims=True)
        if i > 0:
            past = dot_nt(k_s[:begin, :], queries)
            top = jnp.maximum(top, jnp.max(past, axis=0, keepdims=True))
        near = jnp.exp(near - top)
        amount = column_sum(near)
        context = dot_nn(flipped[:, begin:end], near.astype(low))
        if i > 0:
            past = jnp.exp(past - top)
            amount = amount + column_sum(past)
            context = context + dot_nn(flipped[:, :begin], past.astype(low))
        o_s[:, begin:end] = context / amount
        stats_ref[head, :, begin:end] = top + jnp.log(amount)
    for spot in range(4):
        block = o_s[:, place_of(index, spot, rows)]
        full_ref[lines, spot * rows : (spot + 1) * rows] = block
        target = keep_ref if spot in (0, 2) else send_ref
        target[lines, (spot // 2) * rows : (spot // 2 + 1) * rows] = block.astype(low)


def attend(index, first_low, low_half, high_half, bias):
    total, width = first_low.shape
    rows = total // 4
    heads = width // lanes
    features = heads * HEAD_DIM
    pairs = heads * total * total // 2
    return kernel_call(
        attend_kernel,
        "attend",
        index,
        [first_low, low_half, high_half, bias],
        [
            shape_of((width, width), low),
            shape_of((total, width), low),
            shape_of((features, 2 * rows), low),
            shape_of((features, 2 * rows), low),
            shape_of((features, total), wide),
            shape_of((heads, 1, total), wide),
        ],
        pairs * 4 * 256 + 2 * total * width * width,
        pairs,
        (heads,),
        [pltpu.VMEM((total, HEAD_DIM), low)] * 3 + [pltpu.VMEM((HEAD_DIM, total), wide)],
    )


def project_kernel(
    index_ref,
    keep_ref,
    far_ref,
    near_ref,
    weight_ref,
    tokens_ref,
    vector_ref,
    residual_ref,
    second_ref,
    turned_ref,
):
    rows, width = tokens_ref.shape
    own = width // 4
    pieces = [keep_ref[:, :rows], far_ref[:, :rows], near_ref[:, :rows], near_ref[:, rows:]]
    residual = tokens_ref[...].astype(wide) + vector_ref[4:5, :]
    for spot in range(4):
        turned = flip(pieces[spot])
        group = index_ref[0] ^ masks[spot]
        weights = weight_ref[pl.ds(2 * group, 2), : own // 2, :].reshape(own, width)
        residual = residual + dot_nn(turned, weights)
    residual_ref[...] = residual
    unit, scale = unit_of(residual)
    second_ref[...] = (unit * vector_ref[5:6, :] + vector_ref[6:7, :]).astype(low)
    for spot in range(4):
        turned_ref[spot * own : (spot + 1) * own, :] = pieces[spot]


def feed_kernel(
    index_ref,
    one_ref,
    two_ref,
    up_one_ref,
    up_two_ref,
    rest_ref,
    bias_ref,
    active_ref,
    hidden_ref,
    kept_ref,
    sent_ref,
    sum_ref,
):
    rows, width = one_ref.shape
    up, down = third_of(rest_ref, 1), third_of(rest_ref, 2)
    for spot in (1, 0):
        here = slice(spot * rows, (spot + 1) * rows)
        values = two_ref[...] if spot else one_ref[...]
        grads = up_two_ref[...] if spot else up_one_ref[...]
        hidden = dot_nn(values, up) + bias_ref[...]
        square = hidden * hidden
        bend = jnp.tanh(root * hidden * (1.0 + 0.044715 * square))
        active_ref[here, :] = (0.5 * hidden * (1.0 + bend)).astype(low)
        slope = 0.5 * (1.0 + bend) + 0.5 * hidden * (1.0 - bend * bend) * (
            root * (1.0 + 3 * 0.044715 * square)
        )
        grad = (slope * dot_nt(grads, down)).astype(low)
        hidden_ref[here, :] = grad
        sums = column_sum(grad.astype(wide))
        sum_ref[...] = sums if spot else sum_ref[...] + sums
        result = dot_nt(grad, up)
        if spot:
            sent_ref[...] = result.astype(low)
        else:
            kept_ref[...] = result


def halves(index_ref, block, kept_ref, sent_ref, pair):
    upper = index_ref[1] % 2 == 1
    kept_ref[pair] = jnp.where(upper, block[1], block[0])
    sent_ref[pair] = jnp.where(upper, block[0], block[1]).astype(low)


def feed_grad_kernel(
    index_ref,
    own_ref,
    far_ref,
    near_ref,
    last_ref,
    up_own_ref,
    up_far_ref,
    up_near_ref,
    up_last_ref,
    hidden_one_ref,
    hidden_two_ref,
    active_one_ref,
    active_two_ref,
    rest_ref,
    out_ref,
    kept_one_ref,
    sent_one_ref,
    kept_two_ref,
    sent_two_ref,
):
    rows, width = own_ref.shape
    count, shard = out_ref.shape[0], out_ref.shape[1] // 2

    def halved(one, two):
        return (one[:rows, :], one[rows:, :], two[:rows, :], two[rows:, :])

    pairs = (
        ((own_ref, near_ref, far_ref, last_ref), halved(hidden_one_ref, hidden_two_ref)),
        (
            halved(active_one_ref, active_two_ref),
            (up_own_ref, up_near_ref, up_far_ref, up_last_ref),
        ),
    )
    for place, (lefts, rights) in enumerate(pairs):
        total = None
        for left, right in zip(lefts, rights):
            update = dot_tn(left[...], right[...])
            total = update if total is None else total + update
        total = total.astype(low).reshape(count, shard, width)
        out_ref[:, place * shard : (place + 1) * shard, :] = total
    down = third_of(rest_ref, 2)
    kept_one_ref[...] = dot_nn(active_one_ref[:rows, :], down)
    sent_one_ref[...] = dot_nn(active_one_ref[rows:, :], down).astype(low)
    kept_two_ref[...] = dot_nn(active_two_ref[:rows, :], down)
    sent_two_ref[...] = dot_nn(active_two_ref[rows:, :], down).astype(low)


def in_grad_kernel(
    index_ref,
    turned_ref,
    unit_ref,
    mix_ref,
    weight_ref,
    bias_ref,
    two_ref,
    up_one_ref,
    up_two_ref,
    kept_ref,
    sent_ref,
    rows_s,
):
    pairs, high, columns = kept_ref.shape
    width = mix_ref.shape[1]
    shard = width // (2 * pairs)
    own = columns // 3
    upper = index_ref[1] % 2 == 1
    rows_s[...] = jnp.zeros(rows_s.shape, wide)
    rows_s[4:8, :] = two_ref[...]
    sums = jnp.concatenate([bias_ref[head] for head in range(width // lanes)], axis=1)
    for ctx in range(4):

        @pl.when(index_ref[0] == ctx)
        def put():
            rows_s[8 + ctx : 9 + ctx, :] = up_one_ref[...] + up_two_ref[...]
            for head in range(own // HEAD_DIM):
                begin = ctx * own + head * HEAD_DIM
                for row, kind in ((2, 0), (3, 2)):
                    rows_s[row : row + 1, begin : begin + HEAD_DIM] = bias_ref[
                        head, :, kind * HEAD_DIM : (kind + 1) * HEAD_DIM
                    ]

    column = lax.broadcasted_iota(jnp.int32, (2 * shard, 128), 1)
    for pair in range(pairs):
        here = slice(2 * pair * shard, 2 * (pair + 1) * shard)
        weights = weight_ref[here, :].astype(wide)
        gain = jnp.sum(weights * dot_nn(unit_ref[here, :], mix_ref[...]), axis=1, keepdims=True)
        shift = jnp.sum(weights * sums, axis=1, keepdims=True)
        both = jnp.where(column == 0, gain, jnp.where(column == 1, shift, 0.0)).T
        rows_s[0:2, here] = both[0:2, :]
    for pair in range(pairs):
        begin = 2 * pair * shard
        block = dot_nn(turned_ref[begin : begin + 2 * shard, :], mix_ref[...])
        kept = jnp.where(upper, block[shard:, :], block[:shard, :])
        sent = jnp.where(upper, block[:shard, :], block[shard:, :]).astype(low)
        for head in range(columns // part):
            here = slice(head * part, (head + 1) * part)
            there = slice(head * lanes, head * lanes + part)
            kept_ref[pair, :shard, here] = kept[:, there]
            sent_ref[pair, :shard, here] = sent[:, there]
        one = rows_s[0:12, begin : begin + shard]
        two = rows_s[0:12, begin + shard : begin + 2 * shard]
        kept = jnp.where(upper, two, one)
        sent = jnp.where(upper, one, two)

        def lines(values):
            return jnp.concatenate(
                [
                    jnp.concatenate([values[6 * r + i : 6 * r + i + 1] for i in range(6)], axis=1)
                    for r in range(2)
                ],
                axis=0,
            )

        kept_ref[pair, shard : shard + 2, :] = lines(kept)
        sent_ref[pair, shard:, :] = jnp.concatenate(
            [lines(sent), jnp.zeros((high - shard - 2, columns), wide)], axis=0
        ).astype(low)
        kept_ref[pair, shard + 2 :, :] = jnp.zeros((high - shard - 2, columns), wide)


def turn_kernel(
    index_ref,
    kept_ref,
    core_ref,
    far_ref,
    residual_ref,
    cotangent_ref,
    weight_ref,
    vector_ref,
    grad_ref,
    attn_ref,
    keep_ref,
    send_ref,
    sum_ref,
):
    rows, width = residual_ref.shape
    own = width // 4
    grad = kept_ref[...] + core_ref[...].astype(wide) + far_ref[...].astype(wide)
    unit, scale = unit_of(residual_ref[...])
    upstream = cotangent_ref[...].astype(wide)
    result = upstream + norm_pull(unit, scale, vector_ref[5:6, :], grad)
    grad_ref[...] = result
    attn = result.astype(low)
    attn_ref[...] = attn
    for spot in range(4):
        group = index_ref[0] ^ masks[spot]
        weights = weight_ref[pl.ds(2 * group, 2), : own // 2, :].reshape(own, width)
        block = dot_nt(weights, attn).astype(low)
        target = keep_ref if spot in (0, 2) else send_ref
        target[:, (spot // 2) * rows : (spot // 2 + 1) * rows] = block
    sum_ref[0:1, :] = column_sum(grad * unit)
    sum_ref[1:2, :] = column_sum(grad)
    sum_ref[2:3, :] = column_sum(attn.astype(wide))
    sum_ref[3:4, :] = column_sum(upstream)


def out_grad_kernel(index_ref, turned_ref, attn_ref, kept_ref, sent_ref):
    width = turned_ref.shape[0]
    own = width // 4
    for spot in range(4):
        group = index_ref[0] ^ masks[spot]
        block = dot_nn(turned_ref[spot * own : (spot + 1) * own, :], attn_ref[...])
        halves(index_ref, block.reshape(2, own // 2, width), kept_ref, sent_ref, group)


def attend_back_kernel(
    index_ref,
    mix_ref,
    keep_ref,
    far_ref,
    near_ref,
    full_ref,
    stats_ref,
    out_ref,
    sum_ref,
    q_s,
    k_s,
    v_s,
    g_s,
    d_s,
    dq_s,
):
    total = mix_ref.shape[0]
    rows = total // 4
    index = index_ref[0]
    head = pl.program_id(0)
    slab = pl.ds(pl.multiple_of(head * lanes, lanes), lanes)
    lines = pl.ds(pl.multiple_of(head * HEAD_DIM, HEAD_DIM), HEAD_DIM)
    pieces = [keep_ref[lines, :rows], far_ref[lines, :rows]]
    pieces = pieces + [near_ref[lines, :rows], near_ref[lines, rows:]]
    for spot in range(4):
        here = slice(spot * rows, (spot + 1) * rows)
        there = place_of(index, spot, rows)
        block = mix_ref[here, slab]
        q_s[there, :] = block[:, 0:64] * jnp.bfloat16(0.125)
        k_s[there, :] = block[:, 64:128]
        v_s[there, :] = block[:, 128:192]
        block = pieces[spot]
        g_s[:, there] = block
        d_s[:, there] = column_sum(block.astype(wide) * full_ref[lines, here])
    allowed = diagonal()
    turned = flip(g_s[...])
    flipped = flip(k_s[...])
    count = total // tile
    for j in range(count):
        begin, end = j * tile, (j + 1) * tile
        keys, values = k_s[begin:end, :], v_s[begin:end, :]
        probs = jnp.exp(dot_nt(keys, q_s[begin:, :]) - stats_ref[head, :, begin:])
        near = jnp.where(allowed, probs[:, :tile], 0.0)
        probs = near if j == count - 1 else jnp.concatenate([near, probs[:, tile:]], axis=1)
        scores = (probs * (dot_nn(values, g_s[:, begin:]) - d_s[:, begin:])).astype(low)
        grad_value = dot_nn(probs.astype(low), turned[begin:, :])
        grad_key = dot_nn(scores, q_s[begin:, :])
        update = dot_nn(flipped[:, begin:end], scores)
        if j == 0:
            dq_s[...] = update
        else:
            dq_s[:, begin:] = dq_s[:, begin:] + update
        k_s[begin:end, :] = grad_key.astype(low)
        v_s[begin:end, :] = grad_value.astype(low)
    q_s[...] = (dq_s[...] * 0.125).T.astype(low)
    for spot in range(4):
        here = slice(spot * rows, (spot + 1) * rows)
        there = place_of(index, spot, rows)
        block = jnp.concatenate(
            [q_s[there, :], k_s[there, :], v_s[there, :], jnp.zeros((rows, 64), low)], axis=1
        )
        out_ref[here, slab] = block
        sums = column_sum(block.astype(wide))
        sum_ref[head] = sums if spot == 0 else sum_ref[head] + sums


def attend_back(index, mix, keep, far, near, full, stats):
    total, width = mix.shape
    heads = width // lanes
    pairs = heads * total * total // 2
    return kernel_call(
        attend_back_kernel,
        "attend_back",
        index,
        [mix, keep, far, near, full, stats],
        [shape_of((total, width), low), shape_of((heads, 1, lanes), wide)],
        pairs * 10 * 256,
        pairs,
        (heads,),
        [pltpu.VMEM((total, HEAD_DIM), low)] * 3
        + [
            pltpu.VMEM((HEAD_DIM, total), low),
            pltpu.VMEM((1, total), wide),
            pltpu.VMEM((HEAD_DIM, total), wide),
        ],
    )


def first_back_kernel(
    index_ref, mix_ref, weight_ref, kept_one_ref, sent_one_ref, kept_two_ref, sent_two_ref
):
    rows = kept_one_ref.shape[0]
    targets = (kept_one_ref, kept_two_ref, sent_one_ref, sent_two_ref)
    for spot in range(4):
        grad = dot_nt(mix_ref[spot * rows : (spot + 1) * rows, :], weight_ref[...])
        targets[spot][...] = grad.astype(targets[spot].dtype)


def tokens_kernel(
    index_ref, kept_ref, core_ref, far_ref, tokens_ref, residual_ref, vector_ref, out_ref
):
    rows = tokens_ref.shape[0]
    grad = kept_ref[...] + core_ref[...].astype(wide) + far_ref[...].astype(wide)
    unit, scale = unit_of(tokens_ref[...].astype(wide))
    result = residual_ref[...] + norm_pull(unit, scale, vector_ref[0:1, :], grad)
    out_ref[...] = result.astype(low)


def spread_kernel(index_ref, own_ref, far_ref, near_ref, up_ref, down_ref):
    width = own_ref.shape[1]
    shard = own_ref.shape[0] // 2
    for ctx in range(4):
        for spot in range(4):

            @pl.when((index_ref[0] ^ ctx) == masks[spot])
            def put():
                source = [own_ref, far_ref, near_ref, near_ref][spot]
                base = 2 * shard if spot == 3 else 0
                block = source[base : base + shard, :].astype(wide)
                for owner in range(width // shard):
                    begin = (owner * 4 + ctx) * shard
                    up_ref[:, begin : begin + shard] = block[:, owner * shard : (owner + 1) * shard]
                down_ref[ctx * shard : (ctx + 1) * shard, :] = source[
                    base + shard : base + 2 * shard, :
                ].astype(wide)


def spread_in_kernel(index_ref, own_ref, far_ref, near_ref, in_ref, sum_ref):
    shard, width = in_ref.shape[0], in_ref.shape[1] // 3
    high, own = own_ref.shape[0], width // 4
    for ctx in range(4):
        for spot in range(4):

            @pl.when((index_ref[0] ^ ctx) == masks[spot])
            def put():
                source = [own_ref, far_ref, near_ref, near_ref][spot]
                base = high if spot == 3 else 0
                block = source[base : base + shard, :].astype(wide)
                for head in range(own // HEAD_DIM):
                    for kind in range(3):
                        begin = kind * width + ctx * own + head * HEAD_DIM
                        target = head * part + kind * HEAD_DIM
                        in_ref[:, begin : begin + HEAD_DIM] = block[:, target : target + HEAD_DIM]
                extra = source[base + shard : base + high, :].astype(wide)
                sum_ref[...] = extra if ctx == 0 else sum_ref[...] + extra


def pieces_of(values):
    far = swap(values, "ctx", 2)
    return values, far, swap(jnp.concatenate([values, far], axis=0), "ctx", 1)


def blocks_of(values):
    far = swap(values, "ctx", 2)
    near = swap(values, "ctx", 1)
    return values, far, near, swap(far, "ctx", 1)


def exchange(keep, send):
    rows = keep.shape[1] // 2
    far = swap(send, "ctx", 2)
    near = swap(jnp.concatenate([keep[:, rows:], far[:, rows:]], axis=1), "ctx", 1)
    return far, near


def split_body(
    tokens,
    first_gain,
    first_shift,
    in_weight,
    in_bias,
    out_weight,
    out_bias,
    second_gain,
    second_shift,
    up_weight,
    up_bias,
    down_weight,
    down_bias,
    cotangent,
):
    rows, width = tokens.shape
    total = 4 * rows
    n_dp = lax.axis_size("dp")
    shard = width // n_dp
    ctx = lax.axis_index("ctx")
    owner = lax.axis_index("dp")
    heads = width // HEAD_DIM // 4
    own = heads * HEAD_DIM
    index = jnp.stack([ctx, owner]).astype(jnp.int32)
    big = 2 * total * width * width
    small = 2 * rows * width * width
    row_wide, row_low = shape_of((rows, width), wide), shape_of((rows, width), low)

    (in_own,) = kernel_call(
        pick_in_kernel, "pick_in", index, [in_weight], [shape_of((shard, 3 * own), low)], 0
    )
    in_other = swap(in_own, "dp", 4)
    in_two = jnp.concatenate([in_own, in_other], axis=0)
    low_half = jnp.concatenate([in_two, swap(in_two, "dp", 2)], axis=0)
    high_half = swap(low_half, "dp", 1)
    (rest,) = kernel_call(
        pick_rest_kernel,
        "pick_rest",
        index,
        [out_weight, up_weight, after(down_weight, in_own)],
        [shape_of((3 * shard, width), low)],
        0,
    )
    rest = lax.all_gather(rest, "dp", axis=0, tiled=False)
    vectors = jnp.concatenate(
        [first_gain, first_shift, in_bias[0], in_bias[1], out_bias, second_gain, second_shift]
        + [down_bias, up_bias]
    ).reshape(1, 12 * shard)
    vectors = dp_gather(vectors, (in_two, low_half)).reshape(n_dp, 12, shard).transpose(1, 0, 2).reshape(12, width)
    vectors = vectors.astype(wide)
    hidden_bias = lax.dynamic_slice_in_dim(vectors, 8 + ctx, 1, 0)
    zeros = jnp.zeros((heads, HEAD_DIM), wide)
    mine = lax.dynamic_slice(vectors, (2, ctx * own), (2, own)).reshape(2, heads, HEAD_DIM)
    bias_full = jnp.concatenate([mine[0], zeros, mine[1], zeros], axis=1).reshape(heads, 1, lanes)

    first_low, first_turned, unit_turned = kernel_call(
        norm_kernel,
        "norm",
        index,
        [*blocks_of(tokens), vectors],
        [shape_of((total, width), low)] + [shape_of((width, total), low)] * 2,
        0,
    )
    upstream = blocks_of(cotangent)
    first_low, *upstream = lax.optimization_barrier((first_low, *upstream))
    in_full, mix, keep, send, context_full, stats = attend(
        index, first_low, low_half, high_half, bias_full
    )
    far, near = exchange(keep, send)
    residual, second_low, turned = kernel_call(
        project_kernel,
        "project",
        index,
        [keep, far, near, rest, tokens, vectors],
        [row_wide, row_low, shape_of((width, rows), low)],
        small,
    )

    def feed(name, one, two, up_one, up_two):
        return kernel_call(
            feed_kernel,
            name,
            index,
            [one, two, up_one, up_two, rest, hidden_bias],
            [shape_of((total // 2, width), low)] * 2
            + [row_wide, row_low, shape_of((1, width), wide)],
            3 * big // 2,
            total * width // 2,
        )

    far, near = swap(second_low, "ctx", 2), swap(second_low, "ctx", 1)
    active_one, hidden_one, kept_one, sent_one, up_sum_one = feed(
        "feed_one", second_low, near, upstream[0], upstream[2]
    )
    far = after(far, active_one)
    second = (second_low, far, near, swap(far, "ctx", 1))
    active_two, hidden_two, kept_two, sent_two, up_sum_two = feed(
        "feed_two", second[1], second[3], upstream[1], upstream[3]
    )
    core_one = swap(sent_one, "ctx", 1)
    passed = (kept_two + swap(sent_two, "ctx", 1).astype(wide)).astype(low)
    far = swap(passed, "ctx", 2)
    feed_grad, *branch = kernel_call(
        feed_grad_kernel,
        "feed_grad",
        index,
        [after(second[0], passed), *second[1:], *upstream, hidden_one, hidden_two]
        + [active_one, active_two, rest],
        [shape_of((n_dp, 2 * shard, width), low), row_wide, row_low, row_wide, row_low],
        3 * big,
    )
    far, feed_grad, *branch = lax.optimization_barrier((far, feed_grad, *branch))
    feed_mine = lax.psum_scatter(feed_grad, "dp", scatter_dimension=0, tiled=False)
    grad_residual, grad_attn, keep, send, sums_two = kernel_call(
        turn_kernel,
        "turn",
        index,
        [kept_one, core_one, far, residual, cotangent, rest, vectors],
        [
            row_wide,
            row_low,
            shape_of((own, 2 * rows), low),
            shape_of((own, 2 * rows), low),
            shape_of((4, width), wide),
        ],
        small,
    )
    out_kept, out_sent = kernel_call(
        out_grad_kernel,
        "out_grad",
        index,
        [turned, grad_attn],
        [shape_of((n_dp // 2, shard, width), wide), shape_of((n_dp // 2, shard, width), low)],
        small,
    )
    far = swap(send, "ctx", 2)
    late = after(far, out_sent)
    near = swap(jnp.concatenate([keep[:, rows:], late[:, rows:]], axis=1), "ctx", 1)
    branch_kept, branch_sent, kept_two, sent_two = branch
    branch_core = swap(branch_sent, "ctx", 1)
    passed = (kept_two + swap(sent_two, "ctx", 1).astype(wide)).astype(low)
    branch_far = swap(passed, "ctx", 2)
    grad_mix, bias_sums = attend_back(
        index, mix, after(keep, passed), far, near, context_full, stats
    )

    high = shard + 16
    out_half = dp_scatter_one(out_kept, out_sent)
    out_next, out_sent = dp_parts(out_half, 1, 2)
    kept_one, sent_one, kept_two, sent_two = kernel_call(
        first_back_kernel,
        "first_back",
        index,
        [after(grad_mix, out_half, branch_far), in_full],
        [row_wide, row_low, row_wide, row_low],
        big,
    )
    core_one = swap(sent_one, "ctx", 1)
    passed = (kept_two + swap(sent_two, "ctx", 1).astype(wide)).astype(low)
    far = swap(passed, "ctx", 2)
    out_sent = after(out_sent, passed)
    out_next = out_next + swap(out_sent, "dp", 2).astype(wide)
    in_kept, in_sent = kernel_call(
        in_grad_kernel,
        "in_grad",
        index,
        [after(first_turned, passed, out_sent), unit_turned, grad_mix, in_full]
        + [bias_sums, sums_two, up_sum_one, up_sum_two],
        [shape_of((n_dp // 2, high, 3 * own), wide), shape_of((n_dp // 2, high, 3 * own), low)],
        2 * big,
        scratch=[pltpu.VMEM((16, width), wide)],
    )
    out_next, out_sent = dp_parts(after(out_next, in_sent), 0, 4)
    (tokens_grad,) = kernel_call(
        tokens_kernel,
        "tokens",
        index,
        [kept_one, core_one, after(far, in_sent, out_sent), tokens, grad_residual, vectors],
        [row_low],
        0,
    )
    in_half = dp_scatter_one(after(in_kept, tokens_grad), in_sent)
    in_next, in_sent = dp_parts(in_half, 1, 2)
    feed_mine = after(feed_mine.reshape(2 * shard, width), in_sent)
    feed_far = swap(feed_mine, "ctx", 2)
    out_mine = (after(out_next, feed_mine) + swap(out_sent, "dp", 4).astype(wide)).astype(low)
    out_far = swap(out_mine, "ctx", 2)
    in_next = after(in_next, out_mine) + swap(in_sent, "dp", 2).astype(wide)
    in_next, in_sent = dp_parts(in_next, 0, 4)
    feed_near = jnp.concatenate([after(feed_mine, in_sent), feed_far], axis=0)
    feed_near = swap(feed_near, "ctx", 1)
    out_mine = (after(out_mine, in_sent).astype(wide) + out_far.astype(wide)).astype(low)
    out_weight_grad = out_mine.astype(wide) + swap(out_mine, "ctx", 1).astype(wide)
    in_mine = (after(in_next, out_mine) + swap(in_sent, "dp", 4).astype(wide)).astype(low)
    branch = branch_kept + branch_core.astype(wide) + branch_far.astype(wide)
    layer_out = (residual + branch + vectors[7]).astype(low)
    up_weight_grad, down_weight_grad = kernel_call(
        spread_kernel,
        "spread",
        index,
        [after(feed_mine, in_mine), feed_far, feed_near],
        [shape_of((shard, 4 * width), wide), shape_of((4 * shard, width), wide)],
        0,
    )
    in_far = swap(in_mine, "ctx", 2)
    in_near = jnp.concatenate([after(in_mine, up_weight_grad, layer_out), in_far], axis=0)
    in_near = swap(in_near, "ctx", 1)
    in_weight_grad, sums = kernel_call(
        spread_in_kernel,
        "spread_in",
        index,
        [in_mine, in_far, in_near],
        [shape_of((shard, 3 * width), wide), shape_of((high - shard, 3 * own), wide)],
        0,
    )
    sums = sums[:2].reshape(12, shard)
    return (
        layer_out,
        tokens_grad,
        sums[0],
        sums[1],
        in_weight_grad,
        sums[2:4],
        out_weight_grad,
        sums[6],
        sums[4],
        sums[5],
        up_weight_grad,
        sums[8:12].reshape(4 * shard),
        down_weight_grad,
        sums[7],
    )


def solution(mesh):
    in_specs = (
        P(("dp", "ctx"), None),
        P("dp"),
        P("dp"),
        P("dp", None),
        P(None, "dp"),
        P("dp", None),
        P("dp"),
        P("dp"),
        P("dp"),
        P("dp", None),
        P("dp"),
        P("dp", None),
        P("dp"),
        P(("dp", "ctx"), None),
    )
    out_specs = (
        P(("dp", "ctx"), None),
        P(("dp", "ctx"), None),
        P("dp"),
        P("dp"),
        P("dp", None),
        P(None, "dp"),
        P("dp", None),
        P("dp"),
        P("dp"),
        P("dp"),
        P("dp", None),
        P("dp"),
        P("dp", None),
        P("dp"),
    )
    chosen = split_body if heads_split(mesh) else gathered_body
    return jax.shard_map(chosen, mesh=mesh, in_specs=in_specs, out_specs=out_specs, check_vma=False)
```

```python
import functools
import math

import jax
import jax.numpy as jnp
from jax import lax
from jax.experimental import pallas as pl
from jax.experimental.pallas import tpu as pltpu
from jax.sharding import PartitionSpec as P

HEAD_DIM = 64


epsilon = 1e-05
neg_large = -1e30


def layer_norm(values, gain, shift):
    center = values - jnp.mean(values, axis=-1, keepdims=True)
    spread = jnp.mean(center * center, axis=-1, keepdims=True)
    return center * lax.rsqrt(spread + epsilon) * gain + shift


def norm_back(values, gain, shift, upstream):
    result, pullback = jax.vjp(layer_norm, values, gain, shift)
    return pullback(upstream)


def smooth_gate(values):
    return jax.nn.gelu(values, approximate=True)


def forward_block(state, query_heads, query_pos, key_blk, value_blk, key_pos, factor):
    row_max, row_total, accumulated = state
    scores = (
        jnp.einsum("qhd,khd->hqk", query_heads, key_blk, preferred_element_type=jnp.float32)
        * factor
    )
    allowed = (query_pos[:, None] >= key_pos[None, :])[None]
    scores = jnp.where(allowed, scores, neg_large)
    new_max = jnp.maximum(row_max, jnp.max(scores, axis=-1))
    rescale = jnp.exp(row_max - new_max)
    weights = jnp.where(allowed, jnp.exp(scores - new_max[:, :, None]), 0.0)
    row_total = row_total * rescale + jnp.sum(weights, axis=-1)
    update = jnp.einsum(
        "hqk,khd->qhd", weights.astype(jnp.bfloat16), value_blk, preferred_element_type=jnp.float32
    )
    accumulated = accumulated * rescale.T[:, :, None] + update
    return (new_max, row_total, accumulated)


def pair_grads(
    query_heads, grad_heads, stats, deltas, query_pos, key_blk, value_blk, key_pos, factor
):
    scores = (
        jnp.einsum("qhd,khd->hqk", query_heads, key_blk, preferred_element_type=jnp.float32)
        * factor
    )
    allowed = (query_pos[:, None] >= key_pos[None, :])[None]
    probs = jnp.where(allowed, jnp.exp(scores - stats[:, :, None]), 0.0)
    grad_probs = jnp.einsum(
        "qhd,khd->hqk", grad_heads, value_blk, preferred_element_type=jnp.float32
    )
    grad_scores = (probs * (grad_probs - deltas[:, :, None])).astype(jnp.bfloat16)
    grad_query = (
        jnp.einsum("hqk,khd->qhd", grad_scores, key_blk, preferred_element_type=jnp.float32)
        * factor
    )
    grad_key = (
        jnp.einsum("hqk,qhd->khd", grad_scores, query_heads, preferred_element_type=jnp.float32)
        * factor
    )
    grad_value = jnp.einsum(
        "hqk,qhd->khd", probs.astype(jnp.bfloat16), grad_heads, preferred_element_type=jnp.float32
    )
    return (grad_query, grad_key, grad_value)


def over_keys(state, key_part, value_part, begin_row, top_query, place, block_fn):
    amount, head_count, head_dim = key_part.shape
    stride = math.gcd(amount, 512)
    key_blocks = key_part.reshape(amount // stride, stride, head_count, head_dim)
    value_blocks = value_part.reshape(amount // stride, stride, head_count, head_dim)
    offsets = begin_row + jnp.arange(amount // stride, dtype=jnp.int32) * stride

    def over_step_fn(inner, operands):
        key_blk, value_blk, offset = operands
        key_pos = place(offset + jnp.arange(stride, dtype=jnp.int32))

        def over_compute(current):
            return block_fn(current, key_blk, value_blk, key_pos)

        def keep(current):
            return current

        return (lax.cond(jnp.min(key_pos) <= top_query, over_compute, keep, inner), None)

    state, unused = lax.scan(over_step_fn, state, (key_blocks, value_blocks, offsets))
    return state


def gathered_body(
    tokens,
    first_gain,
    first_shift,
    in_weight,
    in_bias,
    out_weight,
    out_bias,
    second_gain,
    second_shift,
    up_weight,
    up_bias,
    down_weight,
    down_bias,
    cotangent,
):
    (
        first_gain,
        first_shift,
        in_weight,
        in_bias,
        out_weight,
        out_bias,
        second_gain,
        second_shift,
        up_weight,
        up_bias,
        down_weight,
        down_bias,
    ) = (
        lax.all_gather(first_gain, "dp", axis=0, tiled=True),
        lax.all_gather(first_shift, "dp", axis=0, tiled=True),
        lax.all_gather(in_weight, "dp", axis=0, tiled=True),
        lax.all_gather(in_bias, "dp", axis=1, tiled=True),
        lax.all_gather(out_weight, "dp", axis=0, tiled=True),
        lax.all_gather(out_bias, "dp", axis=0, tiled=True),
        lax.all_gather(second_gain, "dp", axis=0, tiled=True),
        lax.all_gather(second_shift, "dp", axis=0, tiled=True),
        lax.all_gather(up_weight, "dp", axis=0, tiled=True),
        lax.all_gather(up_bias, "dp", axis=0, tiled=True),
        lax.all_gather(down_weight, "dp", axis=0, tiled=True),
        lax.all_gather(down_bias, "dp", axis=0, tiled=True),
    )
    rows_dev = tokens.shape[0]
    width = tokens.shape[1]
    head_dim = HEAD_DIM
    head_count = width // head_dim
    factor = 1.0 / math.sqrt(head_dim)
    my_index = lax.axis_index("ctx")

    def place(rows):
        return rows

    query_pos = place(my_index * rows_dev + jnp.arange(rows_dev, dtype=jnp.int32))
    top_query = jnp.max(query_pos)
    inputs = tokens.astype(jnp.float32)
    gain_one = first_gain.astype(jnp.float32)
    shift_one = first_shift.astype(jnp.float32)
    first_low = layer_norm(inputs, gain_one, shift_one).astype(jnp.bfloat16)
    bias_full = jnp.concatenate([in_bias[0], jnp.zeros((width,), jnp.bfloat16), in_bias[1]]).astype(
        jnp.float32
    )
    mixture = (
        jnp.dot(first_low, in_weight, preferred_element_type=jnp.float32) + bias_full
    ).astype(jnp.bfloat16)
    query_rows = mixture[:, :width]
    key_rows = mixture[:, width : 2 * width]
    value_rows = mixture[:, 2 * width :]
    query_heads = query_rows.reshape(rows_dev, head_count, head_dim)

    def forward_fold(state, portion, begin_row):
        key_part, value_part = portion
        amount = key_part.shape[0]

        def block_fn(inner, key_blk, value_blk, key_pos):
            return forward_block(inner, query_heads, query_pos, key_blk, value_blk, key_pos, factor)

        return over_keys(
            state,
            key_part.reshape(amount, head_count, head_dim),
            value_part.reshape(amount, head_count, head_dim),
            begin_row,
            top_query,
            place,
            block_fn,
        )

    start_state = (
        jnp.full((head_count, rows_dev), neg_large, jnp.float32),
        jnp.zeros((head_count, rows_dev), jnp.float32),
        jnp.zeros((rows_dev, head_count, head_dim), jnp.float32),
    )
    row_max, row_total, accumulated = forward_fold(
        start_state,
        (
            lax.all_gather(key_rows, "ctx", axis=0, tiled=True),
            lax.all_gather(value_rows, "ctx", axis=0, tiled=True),
        ),
        jnp.int32(0),
    )
    stats = row_max + jnp.log(row_total)
    context_heads = accumulated / row_total.T[:, :, None]
    context_low = context_heads.reshape(rows_dev, width).astype(jnp.bfloat16)
    residual = (
        inputs
        + jnp.dot(context_low, out_weight, preferred_element_type=jnp.float32)
        + out_bias.astype(jnp.float32)
    )
    gain_two = second_gain.astype(jnp.float32)
    shift_two = second_shift.astype(jnp.float32)
    second_low = layer_norm(residual, gain_two, shift_two).astype(jnp.bfloat16)
    hidden = jnp.dot(second_low, up_weight, preferred_element_type=jnp.float32) + up_bias.astype(
        jnp.float32
    )
    activated, gate_back = jax.vjp(smooth_gate, hidden)
    active_low = activated.astype(jnp.bfloat16)
    layer_out = (
        residual
        + jnp.dot(active_low, down_weight, preferred_element_type=jnp.float32)
        + down_bias.astype(jnp.float32)
    ).astype(jnp.bfloat16)
    upstream = cotangent.astype(jnp.float32)
    down_bias_grad = jnp.sum(upstream, axis=0)
    down_weight_grad = jnp.einsum(
        "tf,td->fd", active_low, cotangent, preferred_element_type=jnp.float32
    )
    (grad_hidden,) = gate_back(
        jnp.einsum("td,fd->tf", cotangent, down_weight, preferred_element_type=jnp.float32)
    )
    grad_hidden = grad_hidden.astype(jnp.bfloat16)
    up_weight_grad = jnp.einsum(
        "td,tf->df", second_low, grad_hidden, preferred_element_type=jnp.float32
    )
    up_bias_grad = jnp.sum(grad_hidden.astype(jnp.float32), axis=0)
    grad_second = jnp.einsum(
        "tf,df->td", grad_hidden, up_weight, preferred_element_type=jnp.float32
    )
    grad_residual, second_gain_grad, second_shift_grad = norm_back(
        residual, gain_two, shift_two, grad_second
    )
    grad_residual = grad_residual + upstream
    grad_attn = grad_residual.astype(jnp.bfloat16)
    out_bias_grad = jnp.sum(grad_attn.astype(jnp.float32), axis=0)
    out_weight_grad = jnp.einsum(
        "td,te->de", context_low, grad_attn, preferred_element_type=jnp.float32
    )
    grad_context = jnp.einsum(
        "te,de->td", grad_attn, out_weight, preferred_element_type=jnp.float32
    ).astype(jnp.bfloat16)
    grad_heads = grad_context.reshape(rows_dev, head_count, head_dim)
    deltas = jnp.sum(grad_heads.astype(jnp.float32) * context_heads, axis=-1).T

    def query_fold(state, portion, begin_row):
        key_part, value_part = portion
        amount = key_part.shape[0]

        def block_fn(inner, key_blk, value_blk, key_pos):
            grad_query, grad_key, grad_value = pair_grads(
                query_heads,
                grad_heads,
                stats,
                deltas,
                query_pos,
                key_blk,
                value_blk,
                key_pos,
                factor,
            )
            return inner + grad_query

        return over_keys(
            state,
            key_part.reshape(amount, head_count, head_dim),
            value_part.reshape(amount, head_count, head_dim),
            begin_row,
            top_query,
            place,
            block_fn,
        )

    zero_heads = jnp.zeros((rows_dev, head_count, head_dim), jnp.float32)
    key_all, value_all = (
        lax.all_gather(key_rows, "ctx", axis=0, tiled=True),
        lax.all_gather(value_rows, "ctx", axis=0, tiled=True),
    )
    grad_query = query_fold(zero_heads, (key_all, value_all), 0)
    amount = lax.axis_size("ctx") * rows_dev
    stride = math.gcd(amount, 512)
    key_part = key_all.reshape(amount // stride, stride, head_count, head_dim)
    value_part = value_all.reshape(amount // stride, stride, head_count, head_dim)
    offsets = jnp.arange(amount // stride, dtype=jnp.int32) * stride

    def key_step_fn(unused, operands):
        key_blk, value_blk, offset = operands
        key_pos = place(offset + jnp.arange(stride, dtype=jnp.int32))

        def key_compute(blocks_in):
            grad_query_part, grad_key, grad_value = pair_grads(
                query_heads,
                grad_heads,
                stats,
                deltas,
                query_pos,
                blocks_in[0],
                blocks_in[1],
                key_pos,
                factor,
            )
            return jnp.concatenate(
                [grad_key.reshape(stride, width), grad_value.reshape(stride, width)], axis=1
            )

        def nothing(blocks_in):
            return jnp.zeros((stride, 2 * width), jnp.float32)

        return (
            unused,
            lax.cond(jnp.min(key_pos) <= top_query, key_compute, nothing, (key_blk, value_blk)),
        )

    unused, stacked = lax.scan(key_step_fn, 0, (key_part, value_part, offsets))
    grad_pairs = lax.psum_scatter(
        stacked.reshape(amount, 2 * width).astype(jnp.bfloat16),
        "ctx",
        scatter_dimension=0,
        tiled=True,
    ).astype(jnp.float32)
    grad_key = grad_pairs[:, :width]
    grad_value = grad_pairs[:, width:]
    grad_mixture = jnp.concatenate(
        [grad_query.reshape(rows_dev, width), grad_key, grad_value], axis=1
    ).astype(jnp.bfloat16)
    in_weight_grad = jnp.einsum(
        "td,te->de", first_low, grad_mixture, preferred_element_type=jnp.float32
    )
    in_bias_grad = jnp.stack(
        [
            jnp.sum(grad_mixture[:, :width].astype(jnp.float32), axis=0),
            jnp.sum(grad_mixture[:, 2 * width :].astype(jnp.float32), axis=0),
        ]
    )
    grad_first = jnp.einsum(
        "te,de->td", grad_mixture, in_weight, preferred_element_type=jnp.float32
    )
    grad_inputs, first_gain_grad, first_shift_grad = norm_back(
        inputs, gain_one, shift_one, grad_first
    )
    tokens_grad = (grad_inputs + grad_residual).astype(jnp.bfloat16)
    (
        first_gain_grad,
        first_shift_grad,
        in_weight_grad,
        in_bias_grad,
        out_weight_grad,
        out_bias_grad,
        second_gain_grad,
        second_shift_grad,
        up_weight_grad,
        up_bias_grad,
        down_weight_grad,
        down_bias_grad,
    ) = (
        lax.psum_scatter(
            first_gain_grad.astype(jnp.bfloat16), "dp", scatter_dimension=0, tiled=True
        ).astype(jnp.float32),
        lax.psum_scatter(
            first_shift_grad.astype(jnp.bfloat16), "dp", scatter_dimension=0, tiled=True
        ).astype(jnp.float32),
        lax.psum_scatter(
            in_weight_grad.astype(jnp.bfloat16), "dp", scatter_dimension=0, tiled=True
        ).astype(jnp.float32),
        lax.psum_scatter(
            in_bias_grad.astype(jnp.bfloat16), "dp", scatter_dimension=1, tiled=True
        ).astype(jnp.float32),
        lax.psum_scatter(
            out_weight_grad.astype(jnp.bfloat16), "dp", scatter_dimension=0, tiled=True
        ).astype(jnp.float32),
        lax.psum_scatter(
            out_bias_grad.astype(jnp.bfloat16), "dp", scatter_dimension=0, tiled=True
        ).astype(jnp.float32),
        lax.psum_scatter(
            second_gain_grad.astype(jnp.bfloat16), "dp", scatter_dimension=0, tiled=True
        ).astype(jnp.float32),
        lax.psum_scatter(
            second_shift_grad.astype(jnp.bfloat16), "dp", scatter_dimension=0, tiled=True
        ).astype(jnp.float32),
        lax.psum_scatter(
            up_weight_grad.astype(jnp.bfloat16), "dp", scatter_dimension=0, tiled=True
        ).astype(jnp.float32),
        lax.psum_scatter(
            up_bias_grad.astype(jnp.bfloat16), "dp", scatter_dimension=0, tiled=True
        ).astype(jnp.float32),
        lax.psum_scatter(
            down_weight_grad.astype(jnp.bfloat16), "dp", scatter_dimension=0, tiled=True
        ).astype(jnp.float32),
        lax.psum_scatter(
            down_bias_grad.astype(jnp.bfloat16), "dp", scatter_dimension=0, tiled=True
        ).astype(jnp.float32),
    )
    (
        first_gain_grad,
        first_shift_grad,
        in_weight_grad,
        in_bias_grad,
        out_weight_grad,
        out_bias_grad,
        second_gain_grad,
        second_shift_grad,
        up_weight_grad,
        up_bias_grad,
        down_weight_grad,
        down_bias_grad,
    ) = (
        lax.psum(first_gain_grad.astype(jnp.bfloat16), "ctx").astype(jnp.float32),
        lax.psum(first_shift_grad.astype(jnp.bfloat16), "ctx").astype(jnp.float32),
        lax.psum(in_weight_grad.astype(jnp.bfloat16), "ctx").astype(jnp.float32),
        lax.psum(in_bias_grad.astype(jnp.bfloat16), "ctx").astype(jnp.float32),
        lax.psum(out_weight_grad.astype(jnp.bfloat16), "ctx").astype(jnp.float32),
        lax.psum(out_bias_grad.astype(jnp.bfloat16), "ctx").astype(jnp.float32),
        lax.psum(second_gain_grad.astype(jnp.bfloat16), "ctx").astype(jnp.float32),
        lax.psum(second_shift_grad.astype(jnp.bfloat16), "ctx").astype(jnp.float32),
        lax.psum(up_weight_grad.astype(jnp.bfloat16), "ctx").astype(jnp.float32),
        lax.psum(up_bias_grad.astype(jnp.bfloat16), "ctx").astype(jnp.float32),
        lax.psum(down_weight_grad.astype(jnp.bfloat16), "ctx").astype(jnp.float32),
        lax.psum(down_bias_grad.astype(jnp.bfloat16), "ctx").astype(jnp.float32),
    )
    return (
        layer_out,
        tokens_grad,
        first_gain_grad,
        first_shift_grad,
        in_weight_grad,
        in_bias_grad,
        out_weight_grad,
        out_bias_grad,
        second_gain_grad,
        second_shift_grad,
        up_weight_grad,
        up_bias_grad,
        down_weight_grad,
        down_bias_grad,
    )


masks = (0, 2, 1, 3)
dp_masks = (0, 4, 2, 6, 1, 5, 3, 7)
tile = 256
share = 20
lanes = 256
part = 3 * HEAD_DIM
root = math.sqrt(2.0 / math.pi)
low, wide = jnp.bfloat16, jnp.float32


def heads_split(mesh):
    return mesh.shape["ctx"] == 4 and mesh.shape["dp"] == 8


def swap(values, axis, bit):
    count = lax.axis_size(axis)
    return lax.ppermute(values, axis, [(i, i ^ bit) for i in range(count)])


def dp_gather(values, waits):
    index = lax.axis_index("dp")
    for bit in (1, 2, 4):
        if bit > 1:
            values = after(values, waits[bit // 2 - 1])
        other = swap(values, "dp", bit)
        upper = (index // bit) % 2 == 1
        values = jnp.concatenate(
            [jnp.where(upper, other, values), jnp.where(upper, values, other)], axis=0
        )
    return values


def dp_scatter_one(kept, sent):
    values = kept + swap(sent, "dp", 1).astype(wide)
    return values.reshape((2, 2) + values.shape[1:])


def dp_parts(values, axis, bit):
    mine = (lax.axis_index("dp") // bit) % 2
    sent = lax.dynamic_index_in_dim(values, 1 - mine, axis, keepdims=False).astype(low)
    return lax.dynamic_index_in_dim(values, mine, axis, keepdims=False), sent


def after(values, *others):
    return lax.optimization_barrier((values, *others))[0]


def dot_nt(left, right):
    return lax.dot_general(left, right, (((1,), (1,)), ((), ())), preferred_element_type=wide)


def dot_nn(left, right):
    return jnp.dot(left, right, preferred_element_type=wide)


def dot_tn(left, right):
    return lax.dot_general(left, right, (((0,), (0,)), ((), ())), preferred_element_type=wide)


def flip(values):
    return values.astype(wide).T.astype(values.dtype)


def whole(array):
    rank = len(array.shape)
    return pl.BlockSpec(array.shape, lambda *_: (0,) * rank)


def held(array):
    return pl.BlockSpec(memory_space=pltpu.VMEM)


def third(place):
    return lambda array: pl.BlockSpec(
        (array.shape[0], array.shape[1] // 3, array.shape[2]), lambda *_: (0, place, 0)
    )


def kernel_call(
    kernel, name, index, inputs, outputs, flops, exps=0, grid=(1,), scratch=(), plain=None
):
    plain = plain or whole
    arrays = [item[0] if isinstance(item, tuple) else item for item in inputs]
    specs = [
        (item[1](item[0]) if callable(item[1]) else item[1]) if isinstance(item, tuple) else plain(item)
        for item in inputs
    ]
    shapes = [item[0] if isinstance(item, tuple) else item for item in outputs]
    out_specs = [item[1] if isinstance(item, tuple) else plain(item) for item in outputs]
    moved = sum(math.prod(a.shape) * a.dtype.itemsize for a in arrays + shapes)
    return pl.pallas_call(
        kernel,
        grid_spec=pltpu.PrefetchScalarGridSpec(
            num_scalar_prefetch=1,
            grid=grid,
            in_specs=specs,
            out_specs=out_specs,
            scratch_shapes=list(scratch),
        ),
        out_shape=shapes,
        compiler_params=pltpu.CompilerParams(vmem_limit_bytes=(24 if plain is held else 48) * 1024 * 1024),
        cost_estimate=pl.CostEstimate(
            flops=flops // share, bytes_accessed=moved // share, transcendentals=exps // share
        ),
        name=name,
    )(index, *arrays)


def shape_of(shape, kind):
    return jax.ShapeDtypeStruct(shape, kind)


def place_of(index, spot, rows):
    return pl.ds(pl.multiple_of((index ^ masks[spot]) * rows, 128), rows)


def diagonal():
    keys = lax.broadcasted_iota(jnp.int32, (tile, tile), 0)
    queries = lax.broadcasted_iota(jnp.int32, (tile, tile), 1)
    return keys <= queries


def unit_of(values):
    center = values - jnp.mean(values, axis=-1, keepdims=True)
    spread = jnp.mean(center * center, axis=-1, keepdims=True)
    scale = lax.rsqrt(spread + epsilon)
    return center * scale, scale


def norm_pull(unit, scale, gain, upstream):
    scaled = upstream * gain
    return scale * (
        scaled
        - jnp.mean(scaled, axis=-1, keepdims=True)
        - unit * jnp.mean(scaled * unit, axis=-1, keepdims=True)
    )


def column_sum(values):
    return jnp.sum(values, axis=0, keepdims=True)


def pick_in_kernel(index_ref, in_ref, out_ref):
    width = in_ref.shape[1] // 3
    own = width // 4
    for ctx in range(4):

        @pl.when(index_ref[0] == ctx)
        def pick():
            for head in range(own // HEAD_DIM):
                for kind in range(3):
                    begin = kind * width + ctx * own + head * HEAD_DIM
                    target = head * part + kind * HEAD_DIM
                    out_ref[:, target : target + HEAD_DIM] = in_ref[:, begin : begin + HEAD_DIM]


def pick_rest_kernel(index_ref, out_weight_ref, up_ref, down_ref, out_ref):
    shard, width = out_weight_ref.shape
    out_ref[:shard, :] = out_weight_ref[...]
    for ctx in range(4):

        @pl.when(index_ref[0] == ctx)
        def pick():
            for owner in range(width // shard):
                begin = owner * 4 * shard + ctx * shard
                out_ref[shard : 2 * shard, owner * shard : (owner + 1) * shard] = up_ref[
                    :, begin : begin + shard
                ]
            out_ref[2 * shard :, :] = down_ref[ctx * shard : (ctx + 1) * shard, :]


def norm_kernel(
    index_ref,
    own_ref,
    far_ref,
    near_ref,
    last_ref,
    vector_ref,
    first_ref,
    turned_ref,
    unit_ref,
):
    rows = own_ref.shape[0]
    for spot, piece in enumerate((own_ref, far_ref, near_ref, last_ref)):
        here = slice(spot * rows, (spot + 1) * rows)
        unit, scale = unit_of(piece[...].astype(wide))
        unit_ref[:, here] = unit.T.astype(low)
        normed = unit * vector_ref[0:1, :] + vector_ref[1:2, :]
        first_ref[here, :] = normed.astype(low)
        turned_ref[:, here] = normed.T.astype(low)


def attend_kernel(
    index_ref,
    first_ref,
    low_half_ref,
    high_half_ref,
    bias_ref,
    weight_ref,
    mix_ref,
    keep_ref,
    send_ref,
    full_ref,
    stats_ref,
    q_s,
    k_s,
    v_s,
    o_s,
):
    total, width = first_ref.shape
    rows = total // 4
    index = index_ref[0]
    heads = width // lanes

    @pl.when(pl.program_id(0) == 0)
    def begin_all():
        shard = low_half_ref.shape[0] // 4
        for spot in range(8):
            source = low_half_ref if spot < 4 else high_half_ref
            block = source[(spot % 4) * shard : (spot % 4 + 1) * shard, :]
            there = pl.ds(pl.multiple_of((index_ref[1] ^ dp_masks[spot]) * shard, 32), shard)
            for head in range(heads):
                begin = head * lanes
                weight_ref[there, begin : begin + part] = block[:, head * part : (head + 1) * part]
                weight_ref[there, begin + part : begin + lanes] = jnp.zeros(
                    (shard, lanes - part), low
                )

    head = pl.program_id(0)
    slab = pl.ds(pl.multiple_of(head * lanes, lanes), lanes)
    lines = pl.ds(pl.multiple_of(head * HEAD_DIM, HEAD_DIM), HEAD_DIM)
    for spot in range(4):
        here = slice(spot * rows, (spot + 1) * rows)
        there = place_of(index, spot, rows)
        block = (dot_nn(first_ref[here, :], weight_ref[:, slab]) + bias_ref[head]).astype(low)
        mix_ref[here, :] = block
        q_s[there, :] = block[:, 0:64] * jnp.bfloat16(0.125)
        k_s[there, :] = block[:, 64:128]
        v_s[there, :] = block[:, 128:192]
    allowed = diagonal()
    flipped = flip(v_s[...])
    for i in range(total // tile):
        begin, end = i * tile, (i + 1) * tile
        queries = q_s[begin:end, :]
        near = jnp.where(allowed, dot_nt(k_s[begin:end, :], queries), neg_large)
        top = jnp.max(near, axis=0, keepdims=True)
        if i > 0:
            past = dot_nt(k_s[:begin, :], queries)
            top = jnp.maximum(top, jnp.max(past, axis=0, keepdims=True))
        near = jnp.exp(near - top)
        amount = column_sum(near)
        context = dot_nn(flipped[:, begin:end], near.astype(low))
        if i > 0:
            past = jnp.exp(past - top)
            amount = amount + column_sum(past)
            context = context + dot_nn(flipped[:, :begin], past.astype(low))
        o_s[:, begin:end] = context / amount
        stats_ref[0, :, begin:end] = top + jnp.log(amount)
    for spot in range(4):
        block = o_s[:, place_of(index, spot, rows)]
        full_ref[:, spot * rows : (spot + 1) * rows] = block
        target = keep_ref if spot in (0, 2) else send_ref
        target[lines, (spot // 2) * rows : (spot // 2 + 1) * rows] = block.astype(low)


def attend(index, first_low, low_half, high_half, bias):
    total, width = first_low.shape
    rows = total // 4
    heads = width // lanes
    features = heads * HEAD_DIM
    by_head = lambda h, s: (h, 0)
    pairs = heads * total * total // 2
    return kernel_call(
        attend_kernel,
        "attend",
        index,
        [first_low, low_half, high_half, bias],
        [
            (shape_of((width, width), low), whole(first_low[:width])),
            (shape_of((total, width), low), pl.BlockSpec((total, lanes), lambda h, s: (0, h))),
            shape_of((features, 2 * rows), low),
            shape_of((features, 2 * rows), low),
            (shape_of((features, total), wide), pl.BlockSpec((HEAD_DIM, total), by_head)),
            (
                shape_of((heads, 1, total), wide),
                pl.BlockSpec((1, 1, total), lambda h, s: (h, 0, 0)),
            ),
        ],
        pairs * 4 * 256 + 2 * total * width * width,
        pairs,
        (heads,),
        [pltpu.VMEM((total, HEAD_DIM), low)] * 3 + [pltpu.VMEM((HEAD_DIM, total), wide)],
        held,
    )


def project_kernel(
    index_ref,
    keep_ref,
    far_ref,
    near_ref,
    weight_ref,
    tokens_ref,
    vector_ref,
    residual_ref,
    second_ref,
    turned_ref,
):
    rows, width = tokens_ref.shape
    own = width // 4
    pieces = [keep_ref[:, :rows], far_ref[:, :rows], near_ref[:, :rows], near_ref[:, rows:]]
    residual = tokens_ref[...].astype(wide) + vector_ref[4:5, :]
    for spot in range(4):
        turned = flip(pieces[spot])
        group = index_ref[0] ^ masks[spot]
        weights = weight_ref[pl.ds(2 * group, 2)].reshape(own, width)
        residual = residual + dot_nn(turned, weights)
    residual_ref[...] = residual
    unit, scale = unit_of(residual)
    second_ref[...] = (unit * vector_ref[5:6, :] + vector_ref[6:7, :]).astype(low)
    for spot in range(4):
        turned_ref[spot * own : (spot + 1) * own, :] = pieces[spot]


def feed_kernel(
    index_ref,
    one_ref,
    two_ref,
    up_one_ref,
    up_two_ref,
    up_ref,
    down_ref,
    bias_ref,
    active_ref,
    hidden_ref,
    kept_ref,
    sent_ref,
    sum_ref,
):
    rows, width = one_ref.shape
    up = up_ref[...].reshape(width, width)
    down = down_ref[...].reshape(width, width)
    for spot in (1, 0):
        here = slice(spot * rows, (spot + 1) * rows)
        values = two_ref[...] if spot else one_ref[...]
        grads = up_two_ref[...] if spot else up_one_ref[...]
        hidden = dot_nn(values, up) + bias_ref[...]
        square = hidden * hidden
        bend = jnp.tanh(root * hidden * (1.0 + 0.044715 * square))
        active_ref[here, :] = (0.5 * hidden * (1.0 + bend)).astype(low)
        slope = 0.5 * (1.0 + bend) + 0.5 * hidden * (1.0 - bend * bend) * (
            root * (1.0 + 3 * 0.044715 * square)
        )
        grad = (slope * dot_nt(grads, down)).astype(low)
        hidden_ref[here, :] = grad
        sums = column_sum(grad.astype(wide))
        sum_ref[...] = sums if spot else sum_ref[...] + sums
        result = dot_nt(grad, up)
        if spot:
            sent_ref[...] = result.astype(low)
        else:
            kept_ref[...] = result


def halves(index_ref, block, kept_ref, sent_ref, pair):
    upper = index_ref[1] % 2 == 1
    kept_ref[pair] = jnp.where(upper, block[1], block[0])
    sent_ref[pair] = jnp.where(upper, block[0], block[1]).astype(low)


def feed_grad_kernel(
    index_ref,
    own_ref,
    far_ref,
    near_ref,
    last_ref,
    up_own_ref,
    up_far_ref,
    up_near_ref,
    up_last_ref,
    hidden_one_ref,
    hidden_two_ref,
    active_one_ref,
    active_two_ref,
    down_ref,
    out_ref,
    kept_one_ref,
    sent_one_ref,
    kept_two_ref,
    sent_two_ref,
):
    rows, width = own_ref.shape
    count, shard = out_ref.shape[0], out_ref.shape[1] // 2

    def halved(one, two):
        return (one[:rows, :], one[rows:, :], two[:rows, :], two[rows:, :])

    pairs = (
        ((own_ref, near_ref, far_ref, last_ref), halved(hidden_one_ref, hidden_two_ref)),
        (
            halved(active_one_ref, active_two_ref),
            (up_own_ref, up_near_ref, up_far_ref, up_last_ref),
        ),
    )
    for place, (lefts, rights) in enumerate(pairs):
        total = None
        for left, right in zip(lefts, rights):
            update = dot_tn(left[...], right[...])
            total = update if total is None else total + update
        total = total.astype(low).reshape(count, shard, width)
        out_ref[:, place * shard : (place + 1) * shard, :] = total
    down = down_ref[...].reshape(width, width)
    kept_one_ref[...] = dot_nn(active_one_ref[:rows, :], down)
    sent_one_ref[...] = dot_nn(active_one_ref[rows:, :], down).astype(low)
    kept_two_ref[...] = dot_nn(active_two_ref[:rows, :], down)
    sent_two_ref[...] = dot_nn(active_two_ref[rows:, :], down).astype(low)


def in_grad_kernel(
    index_ref,
    turned_ref,
    unit_ref,
    mix_ref,
    weight_ref,
    bias_ref,
    two_ref,
    up_one_ref,
    up_two_ref,
    kept_ref,
    sent_ref,
    rows_s,
):
    pairs, high, columns = kept_ref.shape
    width = mix_ref.shape[1]
    shard = width // (2 * pairs)
    own = columns // 3
    upper = index_ref[1] % 2 == 1
    rows_s[...] = jnp.zeros(rows_s.shape, wide)
    rows_s[4:8, :] = two_ref[...]
    sums = jnp.concatenate([bias_ref[head] for head in range(width // lanes)], axis=1)
    for ctx in range(4):

        @pl.when(index_ref[0] == ctx)
        def put():
            rows_s[8 + ctx : 9 + ctx, :] = up_one_ref[...] + up_two_ref[...]
            for head in range(own // HEAD_DIM):
                begin = ctx * own + head * HEAD_DIM
                for row, kind in ((2, 0), (3, 2)):
                    rows_s[row : row + 1, begin : begin + HEAD_DIM] = bias_ref[
                        head, :, kind * HEAD_DIM : (kind + 1) * HEAD_DIM
                    ]

    column = lax.broadcasted_iota(jnp.int32, (2 * shard, 128), 1)
    for pair in range(pairs):
        here = slice(2 * pair * shard, 2 * (pair + 1) * shard)
        weights = weight_ref[here, :].astype(wide)
        gain = jnp.sum(weights * dot_nn(unit_ref[here, :], mix_ref[...]), axis=1, keepdims=True)
        shift = jnp.sum(weights * sums, axis=1, keepdims=True)
        both = jnp.where(column == 0, gain, jnp.where(column == 1, shift, 0.0)).T
        rows_s[0:2, here] = both[0:2, :]
    for pair in range(pairs):
        begin = 2 * pair * shard
        block = dot_nn(turned_ref[begin : begin + 2 * shard, :], mix_ref[...])
        kept = jnp.where(upper, block[shard:, :], block[:shard, :])
        sent = jnp.where(upper, block[:shard, :], block[shard:, :]).astype(low)
        for head in range(columns // part):
            here = slice(head * part, (head + 1) * part)
            there = slice(head * lanes, head * lanes + part)
            kept_ref[pair, :shard, here] = kept[:, there]
            sent_ref[pair, :shard, here] = sent[:, there]
        one = rows_s[0:12, begin : begin + shard]
        two = rows_s[0:12, begin + shard : begin + 2 * shard]
        kept = jnp.where(upper, two, one)
        sent = jnp.where(upper, one, two)

        def lines(values):
            return jnp.concatenate(
                [
                    jnp.concatenate([values[6 * r + i : 6 * r + i + 1] for i in range(6)], axis=1)
                    for r in range(2)
                ],
                axis=0,
            )

        kept_ref[pair, shard : shard + 2, :] = lines(kept)
        sent_ref[pair, shard:, :] = jnp.concatenate(
            [lines(sent), jnp.zeros((high - shard - 2, columns), wide)], axis=0
        ).astype(low)
        kept_ref[pair, shard + 2 :, :] = jnp.zeros((high - shard - 2, columns), wide)


def turn_kernel(
    index_ref,
    kept_ref,
    core_ref,
    far_ref,
    residual_ref,
    cotangent_ref,
    weight_ref,
    vector_ref,
    grad_ref,
    attn_ref,
    keep_ref,
    send_ref,
    sum_ref,
):
    rows, width = residual_ref.shape
    own = width // 4
    grad = kept_ref[...] + core_ref[...].astype(wide) + far_ref[...].astype(wide)
    unit, scale = unit_of(residual_ref[...])
    upstream = cotangent_ref[...].astype(wide)
    result = upstream + norm_pull(unit, scale, vector_ref[5:6, :], grad)
    grad_ref[...] = result
    attn = result.astype(low)
    attn_ref[...] = attn
    for spot in range(4):
        group = index_ref[0] ^ masks[spot]
        weights = weight_ref[pl.ds(2 * group, 2)].reshape(own, width)
        block = dot_nt(weights, attn).astype(low)
        target = keep_ref if spot in (0, 2) else send_ref
        target[:, (spot // 2) * rows : (spot // 2 + 1) * rows] = block
    sum_ref[0:1, :] = column_sum(grad * unit)
    sum_ref[1:2, :] = column_sum(grad)
    sum_ref[2:3, :] = column_sum(attn.astype(wide))
    sum_ref[3:4, :] = column_sum(upstream)


def out_grad_kernel(index_ref, turned_ref, attn_ref, kept_ref, sent_ref):
    width = turned_ref.shape[0]
    own = width // 4
    for spot in range(4):
        group = index_ref[0] ^ masks[spot]
        block = dot_nn(turned_ref[spot * own : (spot + 1) * own, :], attn_ref[...])
        halves(index_ref, block.reshape(2, own // 2, width), kept_ref, sent_ref, group)


def attend_back_kernel(
    index_ref,
    mix_ref,
    keep_ref,
    far_ref,
    near_ref,
    full_ref,
    stats_ref,
    out_ref,
    sum_ref,
    q_s,
    k_s,
    v_s,
    g_s,
    d_s,
    dq_s,
):
    total = mix_ref.shape[0]
    rows = total // 4
    index = index_ref[0]
    head = pl.program_id(0)
    slab = pl.ds(pl.multiple_of(head * lanes, lanes), lanes)
    lines = pl.ds(pl.multiple_of(head * HEAD_DIM, HEAD_DIM), HEAD_DIM)
    pieces = [keep_ref[lines, :rows], far_ref[lines, :rows]]
    pieces = pieces + [near_ref[lines, :rows], near_ref[lines, rows:]]
    for spot in range(4):
        here = slice(spot * rows, (spot + 1) * rows)
        there = place_of(index, spot, rows)
        block = mix_ref[here, slab]
        q_s[there, :] = block[:, 0:64] * jnp.bfloat16(0.125)
        k_s[there, :] = block[:, 64:128]
        v_s[there, :] = block[:, 128:192]
        block = pieces[spot]
        g_s[:, there] = block
        d_s[:, there] = column_sum(block.astype(wide) * full_ref[lines, here])
    allowed = diagonal()
    turned = flip(g_s[...])
    flipped = flip(k_s[...])
    count = total // tile
    for j in range(count):
        begin, end = j * tile, (j + 1) * tile
        keys, values = k_s[begin:end, :], v_s[begin:end, :]
        probs = jnp.exp(dot_nt(keys, q_s[begin:, :]) - stats_ref[head, :, begin:])
        near = jnp.where(allowed, probs[:, :tile], 0.0)
        probs = near if j == count - 1 else jnp.concatenate([near, probs[:, tile:]], axis=1)
        scores = (probs * (dot_nn(values, g_s[:, begin:]) - d_s[:, begin:])).astype(low)
        grad_value = dot_nn(probs.astype(low), turned[begin:, :])
        grad_key = dot_nn(scores, q_s[begin:, :])
        update = dot_nn(flipped[:, begin:end], scores)
        if j == 0:
            dq_s[...] = update
        else:
            dq_s[:, begin:] = dq_s[:, begin:] + update
        k_s[begin:end, :] = grad_key.astype(low)
        v_s[begin:end, :] = grad_value.astype(low)
    q_s[...] = (dq_s[...] * 0.125).T.astype(low)
    for spot in range(4):
        here = slice(spot * rows, (spot + 1) * rows)
        there = place_of(index, spot, rows)
        block = jnp.concatenate(
            [q_s[there, :], k_s[there, :], v_s[there, :], jnp.zeros((rows, 64), low)], axis=1
        )
        out_ref[here, slab] = block
        sums = column_sum(block.astype(wide))
        sum_ref[head] = sums if spot == 0 else sum_ref[head] + sums


def attend_back(index, mix, keep, far, near, full, stats):
    total, width = mix.shape
    heads = width // lanes
    pairs = heads * total * total // 2
    return kernel_call(
        attend_back_kernel,
        "attend_back",
        index,
        [mix, keep, far, near, full, stats],
        [shape_of((total, width), low), shape_of((heads, 1, lanes), wide)],
        pairs * 10 * 256,
        pairs,
        (heads,),
        [pltpu.VMEM((total, HEAD_DIM), low)] * 3
        + [
            pltpu.VMEM((HEAD_DIM, total), low),
            pltpu.VMEM((1, total), wide),
            pltpu.VMEM((HEAD_DIM, total), wide),
        ],
        held,
    )


def first_back_kernel(
    index_ref, mix_ref, weight_ref, kept_one_ref, sent_one_ref, kept_two_ref, sent_two_ref
):
    rows = kept_one_ref.shape[0]
    targets = (kept_one_ref, kept_two_ref, sent_one_ref, sent_two_ref)
    for spot in range(4):
        grad = dot_nt(mix_ref[spot * rows : (spot + 1) * rows, :], weight_ref[...])
        targets[spot][...] = grad.astype(targets[spot].dtype)


def tokens_kernel(
    index_ref, kept_ref, core_ref, far_ref, tokens_ref, residual_ref, vector_ref, out_ref
):
    rows = tokens_ref.shape[0]
    grad = kept_ref[...] + core_ref[...].astype(wide) + far_ref[...].astype(wide)
    unit, scale = unit_of(tokens_ref[...].astype(wide))
    result = residual_ref[...] + norm_pull(unit, scale, vector_ref[0:1, :], grad)
    out_ref[...] = result.astype(low)


def spread_kernel(index_ref, own_ref, far_ref, near_ref, up_ref, down_ref):
    width = own_ref.shape[1]
    shard = own_ref.shape[0] // 2
    for ctx in range(4):
        for spot in range(4):

            @pl.when((index_ref[0] ^ ctx) == masks[spot])
            def put():
                source = [own_ref, far_ref, near_ref, near_ref][spot]
                base = 2 * shard if spot == 3 else 0
                block = source[base : base + shard, :].astype(wide)
                for owner in range(width // shard):
                    begin = (owner * 4 + ctx) * shard
                    up_ref[:, begin : begin + shard] = block[:, owner * shard : (owner + 1) * shard]
                down_ref[ctx * shard : (ctx + 1) * shard, :] = source[
                    base + shard : base + 2 * shard, :
                ].astype(wide)


def spread_in_kernel(index_ref, own_ref, far_ref, near_ref, in_ref, sum_ref):
    shard, width = in_ref.shape[0], in_ref.shape[1] // 3
    high, own = own_ref.shape[0], width // 4
    for ctx in range(4):
        for spot in range(4):

            @pl.when((index_ref[0] ^ ctx) == masks[spot])
            def put():
                source = [own_ref, far_ref, near_ref, near_ref][spot]
                base = high if spot == 3 else 0
                block = source[base : base + shard, :].astype(wide)
                for head in range(own // HEAD_DIM):
                    for kind in range(3):
                        begin = kind * width + ctx * own + head * HEAD_DIM
                        target = head * part + kind * HEAD_DIM
                        in_ref[:, begin : begin + HEAD_DIM] = block[:, target : target + HEAD_DIM]
                extra = source[base + shard : base + high, :].astype(wide)
                sum_ref[...] = extra if ctx == 0 else sum_ref[...] + extra


def pieces_of(values):
    far = swap(values, "ctx", 2)
    return values, far, swap(jnp.concatenate([values, far], axis=0), "ctx", 1)


def blocks_of(values):
    far = swap(values, "ctx", 2)
    near = swap(values, "ctx", 1)
    return values, far, near, swap(far, "ctx", 1)


def exchange(keep, send):
    rows = keep.shape[1] // 2
    far = swap(send, "ctx", 2)
    near = swap(jnp.concatenate([keep[:, rows:], far[:, rows:]], axis=1), "ctx", 1)
    return far, near


def split_body(
    tokens,
    first_gain,
    first_shift,
    in_weight,
    in_bias,
    out_weight,
    out_bias,
    second_gain,
    second_shift,
    up_weight,
    up_bias,
    down_weight,
    down_bias,
    cotangent,
):
    rows, width = tokens.shape
    total = 4 * rows
    n_dp = lax.axis_size("dp")
    shard = width // n_dp
    ctx = lax.axis_index("ctx")
    owner = lax.axis_index("dp")
    heads = width // HEAD_DIM // 4
    own = heads * HEAD_DIM
    index = jnp.stack([ctx, owner]).astype(jnp.int32)
    big = 2 * total * width * width
    small = 2 * rows * width * width
    row_wide, row_low = shape_of((rows, width), wide), shape_of((rows, width), low)

    (in_own,) = kernel_call(
        pick_in_kernel,
        "pick_in",
        index,
        [in_weight],
        [shape_of((shard, 3 * own), low)],
        0,
        plain=held,
    )
    in_other = swap(in_own, "dp", 4)
    in_two = jnp.concatenate([in_own, in_other], axis=0)
    low_half = jnp.concatenate([in_two, swap(in_two, "dp", 2)], axis=0)
    high_half = swap(low_half, "dp", 1)
    (rest,) = kernel_call(
        pick_rest_kernel,
        "pick_rest",
        index,
        [out_weight, up_weight, after(down_weight, in_other)],
        [shape_of((3 * shard, width), low)],
        0,
    )
    rest = lax.all_gather(rest, "dp", axis=0, tiled=False)
    vectors = jnp.concatenate(
        [first_gain, first_shift, in_bias[0], in_bias[1], out_bias, second_gain, second_shift]
        + [down_bias, up_bias]
    ).reshape(1, 12 * shard)
    vectors = dp_gather(vectors, (in_two, low_half)).reshape(n_dp, 12, shard).transpose(1, 0, 2).reshape(12, width)
    vectors = vectors.astype(wide)
    hidden_bias = lax.dynamic_slice_in_dim(vectors, 8 + ctx, 1, 0)
    zeros = jnp.zeros((heads, HEAD_DIM), wide)
    mine = lax.dynamic_slice(vectors, (2, ctx * own), (2, own)).reshape(2, heads, HEAD_DIM)
    bias_full = jnp.concatenate([mine[0], zeros, mine[1], zeros], axis=1).reshape(heads, 1, lanes)

    token_blocks = blocks_of(tokens)
    first_low, first_turned, unit_turned = kernel_call(
        norm_kernel,
        "norm",
        index,
        [*token_blocks, vectors],
        [shape_of((total, width), low)] + [shape_of((width, total), low)] * 2,
        0,
    )
    upstream = blocks_of(after(cotangent, token_blocks[1]))
    in_full, mix, keep, send, context_full, stats = attend(
        index, first_low, low_half, high_half, bias_full
    )
    far, near = exchange(keep, after(send, upstream[1]))
    out_block = (rest, third(0))
    up_block = (rest, third(1))
    down_block = (rest, third(2))
    residual, second_low, turned = kernel_call(
        project_kernel,
        "project",
        index,
        [keep, far, near, out_block, tokens, vectors],
        [row_wide, row_low, shape_of((width, rows), low)],
        small,
    )

    def feed(name, one, two, up_one, up_two):
        return kernel_call(
            feed_kernel,
            name,
            index,
            [one, two, up_one, up_two, up_block, down_block, hidden_bias],
            [shape_of((total // 2, width), low)] * 2
            + [row_wide, row_low, shape_of((1, width), wide)],
            3 * big // 2,
            total * width // 2,
        )

    far, near = swap(second_low, "ctx", 2), swap(second_low, "ctx", 1)
    active_one, hidden_one, kept_one, sent_one, up_sum_one = feed(
        "feed_one", second_low, near, upstream[0], upstream[2]
    )
    far = after(far, active_one)
    second = (second_low, far, near, swap(far, "ctx", 1))
    active_two, hidden_two, kept_two, sent_two, up_sum_two = feed(
        "feed_two", second[1], second[3], upstream[1], upstream[3]
    )
    core_one = swap(sent_one, "ctx", 1)
    passed = (kept_two + swap(sent_two, "ctx", 1).astype(wide)).astype(low)
    far = swap(passed, "ctx", 2)
    feed_grad, *branch = kernel_call(
        feed_grad_kernel,
        "feed_grad",
        index,
        [after(second[0], passed), *second[1:], *upstream, hidden_one, hidden_two]
        + [active_one, active_two, down_block],
        [shape_of((n_dp, 2 * shard, width), low), row_wide, row_low, row_wide, row_low],
        3 * big,
    )
    far, feed_grad, *branch = lax.optimization_barrier((far, feed_grad, *branch))
    feed_mine = lax.psum_scatter(feed_grad, "dp", scatter_dimension=0, tiled=False)
    grad_residual, grad_attn, keep, send, sums_two = kernel_call(
        turn_kernel,
        "turn",
        index,
        [kept_one, core_one, far, residual, cotangent, out_block, vectors],
        [
            row_wide,
            row_low,
            shape_of((own, 2 * rows), low),
            shape_of((own, 2 * rows), low),
            shape_of((4, width), wide),
        ],
        small,
    )
    out_kept, out_sent = kernel_call(
        out_grad_kernel,
        "out_grad",
        index,
        [turned, grad_attn],
        [shape_of((n_dp // 2, shard, width), wide), shape_of((n_dp // 2, shard, width), low)],
        small,
    )
    far = swap(send, "ctx", 2)
    late = after(far, out_sent)
    near = swap(jnp.concatenate([keep[:, rows:], late[:, rows:]], axis=1), "ctx", 1)
    branch_kept, branch_sent, kept_two, sent_two = branch
    branch_core = swap(branch_sent, "ctx", 1)
    passed = (kept_two + swap(sent_two, "ctx", 1).astype(wide)).astype(low)
    branch_far = swap(passed, "ctx", 2)
    grad_mix, bias_sums = attend_back(
        index, mix, after(keep, passed), far, near, context_full, stats
    )

    high = shard + 16
    out_half = dp_scatter_one(out_kept, out_sent)
    out_next, out_sent = dp_parts(out_half, 1, 2)
    kept_one, sent_one, kept_two, sent_two = kernel_call(
        first_back_kernel,
        "first_back",
        index,
        [after(grad_mix, out_half, branch_far), in_full],
        [row_wide, row_low, row_wide, row_low],
        big,
    )
    core_one = swap(sent_one, "ctx", 1)
    passed = (kept_two + swap(sent_two, "ctx", 1).astype(wide)).astype(low)
    far = swap(passed, "ctx", 2)
    out_sent = after(out_sent, passed)
    out_next = out_next + swap(out_sent, "dp", 2).astype(wide)
    in_kept, in_sent = kernel_call(
        in_grad_kernel,
        "in_grad",
        index,
        [after(first_turned, passed, out_sent), unit_turned, grad_mix, in_full]
        + [bias_sums, sums_two, up_sum_one, up_sum_two],
        [shape_of((n_dp // 2, high, 3 * own), wide), shape_of((n_dp // 2, high, 3 * own), low)],
        2 * big,
        scratch=[pltpu.VMEM((16, width), wide)],
    )
    out_next, out_sent = dp_parts(after(out_next, in_sent), 0, 4)
    (tokens_grad,) = kernel_call(
        tokens_kernel,
        "tokens",
        index,
        [kept_one, core_one, after(far, in_sent, out_sent), tokens, grad_residual, vectors],
        [row_low],
        0,
    )
    in_half = dp_scatter_one(after(in_kept, tokens_grad), in_sent)
    in_next, in_sent = dp_parts(in_half, 1, 2)
    feed_mine = after(feed_mine.reshape(2 * shard, width), in_sent)
    feed_far = swap(feed_mine, "ctx", 2)
    out_mine = (after(out_next, feed_mine) + swap(out_sent, "dp", 4).astype(wide)).astype(low)
    out_far = swap(out_mine, "ctx", 2)
    in_next = after(in_next, out_mine) + swap(in_sent, "dp", 2).astype(wide)
    in_next, in_sent = dp_parts(in_next, 0, 4)
    feed_near = jnp.concatenate([after(feed_mine, in_sent), feed_far], axis=0)
    feed_near = swap(feed_near, "ctx", 1)
    out_mine = (after(out_mine, in_sent).astype(wide) + out_far.astype(wide)).astype(low)
    out_weight_grad = out_mine.astype(wide) + swap(out_mine, "ctx", 1).astype(wide)
    in_mine = (after(in_next, out_mine) + swap(in_sent, "dp", 4).astype(wide)).astype(low)
    branch = branch_kept + branch_core.astype(wide) + branch_far.astype(wide)
    layer_out = (residual + branch + vectors[7]).astype(low)
    up_weight_grad, down_weight_grad = kernel_call(
        spread_kernel,
        "spread",
        index,
        [after(feed_mine, in_mine), feed_far, feed_near],
        [shape_of((shard, 4 * width), wide), shape_of((4 * shard, width), wide)],
        0,
        plain=held,
    )
    in_far = swap(in_mine, "ctx", 2)
    in_near = jnp.concatenate([after(in_mine, up_weight_grad, layer_out), in_far], axis=0)
    in_near = swap(in_near, "ctx", 1)
    in_weight_grad, sums = kernel_call(
        spread_in_kernel,
        "spread_in",
        index,
        [in_mine, in_far, in_near],
        [shape_of((shard, 3 * width), wide), shape_of((high - shard, 3 * own), wide)],
        0,
        plain=held,
    )
    sums = sums[:2].reshape(12, shard)
    return (
        layer_out,
        tokens_grad,
        sums[0],
        sums[1],
        in_weight_grad,
        sums[2:4],
        out_weight_grad,
        sums[6],
        sums[4],
        sums[5],
        up_weight_grad,
        sums[8:12].reshape(4 * shard),
        down_weight_grad,
        sums[7],
    )


def solution(mesh):
    in_specs = (
        P(("dp", "ctx"), None),
        P("dp"),
        P("dp"),
        P("dp", None),
        P(None, "dp"),
        P("dp", None),
        P("dp"),
        P("dp"),
        P("dp"),
        P("dp", None),
        P("dp"),
        P("dp", None),
        P("dp"),
        P(("dp", "ctx"), None),
    )
    out_specs = (
        P(("dp", "ctx"), None),
        P(("dp", "ctx"), None),
        P("dp"),
        P("dp"),
        P("dp", None),
        P(None, "dp"),
        P("dp", None),
        P("dp"),
        P("dp"),
        P("dp"),
        P("dp", None),
        P("dp"),
        P("dp", None),
        P("dp"),
    )
    chosen = split_body if heads_split(mesh) else gathered_body
    return jax.shard_map(chosen, mesh=mesh, in_specs=in_specs, out_specs=out_specs, check_vma=False)
```

```python
import functools
import math

import jax
import jax.numpy as jnp
from jax import lax
from jax.experimental import pallas as pl
from jax.experimental.pallas import tpu as pltpu
from jax.sharding import PartitionSpec as P

HEAD_DIM = 64


epsilon = 1e-05
neg_large = -1e30


def layer_norm(values, gain, shift):
    center = values - jnp.mean(values, axis=-1, keepdims=True)
    spread = jnp.mean(center * center, axis=-1, keepdims=True)
    return center * lax.rsqrt(spread + epsilon) * gain + shift


def norm_back(values, gain, shift, upstream):
    result, pullback = jax.vjp(layer_norm, values, gain, shift)
    return pullback(upstream)


def smooth_gate(values):
    return jax.nn.gelu(values, approximate=True)


def forward_block(state, query_heads, query_pos, key_blk, value_blk, key_pos, factor):
    row_max, row_total, accumulated = state
    scores = (
        jnp.einsum("qhd,khd->hqk", query_heads, key_blk, preferred_element_type=jnp.float32)
        * factor
    )
    allowed = (query_pos[:, None] >= key_pos[None, :])[None]
    scores = jnp.where(allowed, scores, neg_large)
    new_max = jnp.maximum(row_max, jnp.max(scores, axis=-1))
    rescale = jnp.exp(row_max - new_max)
    weights = jnp.where(allowed, jnp.exp(scores - new_max[:, :, None]), 0.0)
    row_total = row_total * rescale + jnp.sum(weights, axis=-1)
    update = jnp.einsum(
        "hqk,khd->qhd", weights.astype(jnp.bfloat16), value_blk, preferred_element_type=jnp.float32
    )
    accumulated = accumulated * rescale.T[:, :, None] + update
    return (new_max, row_total, accumulated)


def pair_grads(
    query_heads, grad_heads, stats, deltas, query_pos, key_blk, value_blk, key_pos, factor
):
    scores = (
        jnp.einsum("qhd,khd->hqk", query_heads, key_blk, preferred_element_type=jnp.float32)
        * factor
    )
    allowed = (query_pos[:, None] >= key_pos[None, :])[None]
    probs = jnp.where(allowed, jnp.exp(scores - stats[:, :, None]), 0.0)
    grad_probs = jnp.einsum(
        "qhd,khd->hqk", grad_heads, value_blk, preferred_element_type=jnp.float32
    )
    grad_scores = (probs * (grad_probs - deltas[:, :, None])).astype(jnp.bfloat16)
    grad_query = (
        jnp.einsum("hqk,khd->qhd", grad_scores, key_blk, preferred_element_type=jnp.float32)
        * factor
    )
    grad_key = (
        jnp.einsum("hqk,qhd->khd", grad_scores, query_heads, preferred_element_type=jnp.float32)
        * factor
    )
    grad_value = jnp.einsum(
        "hqk,qhd->khd", probs.astype(jnp.bfloat16), grad_heads, preferred_element_type=jnp.float32
    )
    return (grad_query, grad_key, grad_value)


def over_keys(state, key_part, value_part, begin_row, top_query, place, block_fn):
    amount, head_count, head_dim = key_part.shape
    stride = math.gcd(amount, 512)
    key_blocks = key_part.reshape(amount // stride, stride, head_count, head_dim)
    value_blocks = value_part.reshape(amount // stride, stride, head_count, head_dim)
    offsets = begin_row + jnp.arange(amount // stride, dtype=jnp.int32) * stride

    def over_step_fn(inner, operands):
        key_blk, value_blk, offset = operands
        key_pos = place(offset + jnp.arange(stride, dtype=jnp.int32))

        def over_compute(current):
            return block_fn(current, key_blk, value_blk, key_pos)

        def keep(current):
            return current

        return (lax.cond(jnp.min(key_pos) <= top_query, over_compute, keep, inner), None)

    state, unused = lax.scan(over_step_fn, state, (key_blocks, value_blocks, offsets))
    return state


def gathered_body(
    tokens,
    first_gain,
    first_shift,
    in_weight,
    in_bias,
    out_weight,
    out_bias,
    second_gain,
    second_shift,
    up_weight,
    up_bias,
    down_weight,
    down_bias,
    cotangent,
):
    (
        first_gain,
        first_shift,
        in_weight,
        in_bias,
        out_weight,
        out_bias,
        second_gain,
        second_shift,
        up_weight,
        up_bias,
        down_weight,
        down_bias,
    ) = (
        lax.all_gather(first_gain, "dp", axis=0, tiled=True),
        lax.all_gather(first_shift, "dp", axis=0, tiled=True),
        lax.all_gather(in_weight, "dp", axis=0, tiled=True),
        lax.all_gather(in_bias, "dp", axis=1, tiled=True),
        lax.all_gather(out_weight, "dp", axis=0, tiled=True),
        lax.all_gather(out_bias, "dp", axis=0, tiled=True),
        lax.all_gather(second_gain, "dp", axis=0, tiled=True),
        lax.all_gather(second_shift, "dp", axis=0, tiled=True),
        lax.all_gather(up_weight, "dp", axis=0, tiled=True),
        lax.all_gather(up_bias, "dp", axis=0, tiled=True),
        lax.all_gather(down_weight, "dp", axis=0, tiled=True),
        lax.all_gather(down_bias, "dp", axis=0, tiled=True),
    )
    rows_dev = tokens.shape[0]
    width = tokens.shape[1]
    head_dim = HEAD_DIM
    head_count = width // head_dim
    factor = 1.0 / math.sqrt(head_dim)
    my_index = lax.axis_index("ctx")

    def place(rows):
        return rows

    query_pos = place(my_index * rows_dev + jnp.arange(rows_dev, dtype=jnp.int32))
    top_query = jnp.max(query_pos)
    inputs = tokens.astype(jnp.float32)
    gain_one = first_gain.astype(jnp.float32)
    shift_one = first_shift.astype(jnp.float32)
    first_low = layer_norm(inputs, gain_one, shift_one).astype(jnp.bfloat16)
    bias_full = jnp.concatenate([in_bias[0], jnp.zeros((width,), jnp.bfloat16), in_bias[1]]).astype(
        jnp.float32
    )
    mixture = (
        jnp.dot(first_low, in_weight, preferred_element_type=jnp.float32) + bias_full
    ).astype(jnp.bfloat16)
    query_rows = mixture[:, :width]
    key_rows = mixture[:, width : 2 * width]
    value_rows = mixture[:, 2 * width :]
    query_heads = query_rows.reshape(rows_dev, head_count, head_dim)

    def forward_fold(state, portion, begin_row):
        key_part, value_part = portion
        amount = key_part.shape[0]

        def block_fn(inner, key_blk, value_blk, key_pos):
            return forward_block(inner, query_heads, query_pos, key_blk, value_blk, key_pos, factor)

        return over_keys(
            state,
            key_part.reshape(amount, head_count, head_dim),
            value_part.reshape(amount, head_count, head_dim),
            begin_row,
            top_query,
            place,
            block_fn,
        )

    start_state = (
        jnp.full((head_count, rows_dev), neg_large, jnp.float32),
        jnp.zeros((head_count, rows_dev), jnp.float32),
        jnp.zeros((rows_dev, head_count, head_dim), jnp.float32),
    )
    row_max, row_total, accumulated = forward_fold(
        start_state,
        (
            lax.all_gather(key_rows, "ctx", axis=0, tiled=True),
            lax.all_gather(value_rows, "ctx", axis=0, tiled=True),
        ),
        jnp.int32(0),
    )
    stats = row_max + jnp.log(row_total)
    context_heads = accumulated / row_total.T[:, :, None]
    context_low = context_heads.reshape(rows_dev, width).astype(jnp.bfloat16)
    residual = (
        inputs
        + jnp.dot(context_low, out_weight, preferred_element_type=jnp.float32)
        + out_bias.astype(jnp.float32)
    )
    gain_two = second_gain.astype(jnp.float32)
    shift_two = second_shift.astype(jnp.float32)
    second_low = layer_norm(residual, gain_two, shift_two).astype(jnp.bfloat16)
    hidden = jnp.dot(second_low, up_weight, preferred_element_type=jnp.float32) + up_bias.astype(
        jnp.float32
    )
    activated, gate_back = jax.vjp(smooth_gate, hidden)
    active_low = activated.astype(jnp.bfloat16)
    layer_out = (
        residual
        + jnp.dot(active_low, down_weight, preferred_element_type=jnp.float32)
        + down_bias.astype(jnp.float32)
    ).astype(jnp.bfloat16)
    upstream = cotangent.astype(jnp.float32)
    down_bias_grad = jnp.sum(upstream, axis=0)
    down_weight_grad = jnp.einsum(
        "tf,td->fd", active_low, cotangent, preferred_element_type=jnp.float32
    )
    (grad_hidden,) = gate_back(
        jnp.einsum("td,fd->tf", cotangent, down_weight, preferred_element_type=jnp.float32)
    )
    grad_hidden = grad_hidden.astype(jnp.bfloat16)
    up_weight_grad = jnp.einsum(
        "td,tf->df", second_low, grad_hidden, preferred_element_type=jnp.float32
    )
    up_bias_grad = jnp.sum(grad_hidden.astype(jnp.float32), axis=0)
    grad_second = jnp.einsum(
        "tf,df->td", grad_hidden, up_weight, preferred_element_type=jnp.float32
    )
    grad_residual, second_gain_grad, second_shift_grad = norm_back(
        residual, gain_two, shift_two, grad_second
    )
    grad_residual = grad_residual + upstream
    grad_attn = grad_residual.astype(jnp.bfloat16)
    out_bias_grad = jnp.sum(grad_attn.astype(jnp.float32), axis=0)
    out_weight_grad = jnp.einsum(
        "td,te->de", context_low, grad_attn, preferred_element_type=jnp.float32
    )
    grad_context = jnp.einsum(
        "te,de->td", grad_attn, out_weight, preferred_element_type=jnp.float32
    ).astype(jnp.bfloat16)
    grad_heads = grad_context.reshape(rows_dev, head_count, head_dim)
    deltas = jnp.sum(grad_heads.astype(jnp.float32) * context_heads, axis=-1).T

    def query_fold(state, portion, begin_row):
        key_part, value_part = portion
        amount = key_part.shape[0]

        def block_fn(inner, key_blk, value_blk, key_pos):
            grad_query, grad_key, grad_value = pair_grads(
                query_heads,
                grad_heads,
                stats,
                deltas,
                query_pos,
                key_blk,
                value_blk,
                key_pos,
                factor,
            )
            return inner + grad_query

        return over_keys(
            state,
            key_part.reshape(amount, head_count, head_dim),
            value_part.reshape(amount, head_count, head_dim),
            begin_row,
            top_query,
            place,
            block_fn,
        )

    zero_heads = jnp.zeros((rows_dev, head_count, head_dim), jnp.float32)
    key_all, value_all = (
        lax.all_gather(key_rows, "ctx", axis=0, tiled=True),
        lax.all_gather(value_rows, "ctx", axis=0, tiled=True),
    )
    grad_query = query_fold(zero_heads, (key_all, value_all), 0)
    amount = lax.axis_size("ctx") * rows_dev
    stride = math.gcd(amount, 512)
    key_part = key_all.reshape(amount // stride, stride, head_count, head_dim)
    value_part = value_all.reshape(amount // stride, stride, head_count, head_dim)
    offsets = jnp.arange(amount // stride, dtype=jnp.int32) * stride

    def key_step_fn(unused, operands):
        key_blk, value_blk, offset = operands
        key_pos = place(offset + jnp.arange(stride, dtype=jnp.int32))

        def key_compute(blocks_in):
            grad_query_part, grad_key, grad_value = pair_grads(
                query_heads,
                grad_heads,
                stats,
                deltas,
                query_pos,
                blocks_in[0],
                blocks_in[1],
                key_pos,
                factor,
            )
            return jnp.concatenate(
                [grad_key.reshape(stride, width), grad_value.reshape(stride, width)], axis=1
            )

        def nothing(blocks_in):
            return jnp.zeros((stride, 2 * width), jnp.float32)

        return (
            unused,
            lax.cond(jnp.min(key_pos) <= top_query, key_compute, nothing, (key_blk, value_blk)),
        )

    unused, stacked = lax.scan(key_step_fn, 0, (key_part, value_part, offsets))
    grad_pairs = lax.psum_scatter(
        stacked.reshape(amount, 2 * width).astype(jnp.bfloat16),
        "ctx",
        scatter_dimension=0,
        tiled=True,
    ).astype(jnp.float32)
    grad_key = grad_pairs[:, :width]
    grad_value = grad_pairs[:, width:]
    grad_mixture = jnp.concatenate(
        [grad_query.reshape(rows_dev, width), grad_key, grad_value], axis=1
    ).astype(jnp.bfloat16)
    in_weight_grad = jnp.einsum(
        "td,te->de", first_low, grad_mixture, preferred_element_type=jnp.float32
    )
    in_bias_grad = jnp.stack(
        [
            jnp.sum(grad_mixture[:, :width].astype(jnp.float32), axis=0),
            jnp.sum(grad_mixture[:, 2 * width :].astype(jnp.float32), axis=0),
        ]
    )
    grad_first = jnp.einsum(
        "te,de->td", grad_mixture, in_weight, preferred_element_type=jnp.float32
    )
    grad_inputs, first_gain_grad, first_shift_grad = norm_back(
        inputs, gain_one, shift_one, grad_first
    )
    tokens_grad = (grad_inputs + grad_residual).astype(jnp.bfloat16)
    (
        first_gain_grad,
        first_shift_grad,
        in_weight_grad,
        in_bias_grad,
        out_weight_grad,
        out_bias_grad,
        second_gain_grad,
        second_shift_grad,
        up_weight_grad,
        up_bias_grad,
        down_weight_grad,
        down_bias_grad,
    ) = (
        lax.psum_scatter(
            first_gain_grad.astype(jnp.bfloat16), "dp", scatter_dimension=0, tiled=True
        ).astype(jnp.float32),
        lax.psum_scatter(
            first_shift_grad.astype(jnp.bfloat16), "dp", scatter_dimension=0, tiled=True
        ).astype(jnp.float32),
        lax.psum_scatter(
            in_weight_grad.astype(jnp.bfloat16), "dp", scatter_dimension=0, tiled=True
        ).astype(jnp.float32),
        lax.psum_scatter(
            in_bias_grad.astype(jnp.bfloat16), "dp", scatter_dimension=1, tiled=True
        ).astype(jnp.float32),
        lax.psum_scatter(
            out_weight_grad.astype(jnp.bfloat16), "dp", scatter_dimension=0, tiled=True
        ).astype(jnp.float32),
        lax.psum_scatter(
            out_bias_grad.astype(jnp.bfloat16), "dp", scatter_dimension=0, tiled=True
        ).astype(jnp.float32),
        lax.psum_scatter(
            second_gain_grad.astype(jnp.bfloat16), "dp", scatter_dimension=0, tiled=True
        ).astype(jnp.float32),
        lax.psum_scatter(
            second_shift_grad.astype(jnp.bfloat16), "dp", scatter_dimension=0, tiled=True
        ).astype(jnp.float32),
        lax.psum_scatter(
            up_weight_grad.astype(jnp.bfloat16), "dp", scatter_dimension=0, tiled=True
        ).astype(jnp.float32),
        lax.psum_scatter(
            up_bias_grad.astype(jnp.bfloat16), "dp", scatter_dimension=0, tiled=True
        ).astype(jnp.float32),
        lax.psum_scatter(
            down_weight_grad.astype(jnp.bfloat16), "dp", scatter_dimension=0, tiled=True
        ).astype(jnp.float32),
        lax.psum_scatter(
            down_bias_grad.astype(jnp.bfloat16), "dp", scatter_dimension=0, tiled=True
        ).astype(jnp.float32),
    )
    (
        first_gain_grad,
        first_shift_grad,
        in_weight_grad,
        in_bias_grad,
        out_weight_grad,
        out_bias_grad,
        second_gain_grad,
        second_shift_grad,
        up_weight_grad,
        up_bias_grad,
        down_weight_grad,
        down_bias_grad,
    ) = (
        lax.psum(first_gain_grad.astype(jnp.bfloat16), "ctx").astype(jnp.float32),
        lax.psum(first_shift_grad.astype(jnp.bfloat16), "ctx").astype(jnp.float32),
        lax.psum(in_weight_grad.astype(jnp.bfloat16), "ctx").astype(jnp.float32),
        lax.psum(in_bias_grad.astype(jnp.bfloat16), "ctx").astype(jnp.float32),
        lax.psum(out_weight_grad.astype(jnp.bfloat16), "ctx").astype(jnp.float32),
        lax.psum(out_bias_grad.astype(jnp.bfloat16), "ctx").astype(jnp.float32),
        lax.psum(second_gain_grad.astype(jnp.bfloat16), "ctx").astype(jnp.float32),
        lax.psum(second_shift_grad.astype(jnp.bfloat16), "ctx").astype(jnp.float32),
        lax.psum(up_weight_grad.astype(jnp.bfloat16), "ctx").astype(jnp.float32),
        lax.psum(up_bias_grad.astype(jnp.bfloat16), "ctx").astype(jnp.float32),
        lax.psum(down_weight_grad.astype(jnp.bfloat16), "ctx").astype(jnp.float32),
        lax.psum(down_bias_grad.astype(jnp.bfloat16), "ctx").astype(jnp.float32),
    )
    return (
        layer_out,
        tokens_grad,
        first_gain_grad,
        first_shift_grad,
        in_weight_grad,
        in_bias_grad,
        out_weight_grad,
        out_bias_grad,
        second_gain_grad,
        second_shift_grad,
        up_weight_grad,
        up_bias_grad,
        down_weight_grad,
        down_bias_grad,
    )


masks = (0, 2, 1, 3)
dp_masks = (0, 4, 2, 6, 1, 5, 3, 7)
tile = 256
share = 20
lanes = 256
part = 3 * HEAD_DIM
root = math.sqrt(2.0 / math.pi)
low, wide = jnp.bfloat16, jnp.float32


def heads_split(mesh):
    return mesh.shape["ctx"] == 4 and mesh.shape["dp"] == 8


def swap(values, axis, bit):
    count = lax.axis_size(axis)
    return lax.ppermute(values, axis, [(i, i ^ bit) for i in range(count)])


def dp_gather(values, waits):
    index = lax.axis_index("dp")
    for bit in (1, 2, 4):
        if bit > 1:
            values = after(values, waits[bit // 2 - 1])
        other = swap(values, "dp", bit)
        upper = (index // bit) % 2 == 1
        values = jnp.concatenate(
            [jnp.where(upper, other, values), jnp.where(upper, values, other)], axis=0
        )
    return values


def dp_scatter_one(kept, sent):
    values = kept + swap(sent, "dp", 1).astype(wide)
    return values.reshape((2, 2) + values.shape[1:])


def dp_parts(values, axis, bit):
    mine = (lax.axis_index("dp") // bit) % 2
    sent = lax.dynamic_index_in_dim(values, 1 - mine, axis, keepdims=False).astype(low)
    return lax.dynamic_index_in_dim(values, mine, axis, keepdims=False), sent


def after(values, *others):
    return lax.optimization_barrier((values, *others))[0]


def dot_nt(left, right):
    return lax.dot_general(left, right, (((1,), (1,)), ((), ())), preferred_element_type=wide)


def dot_nn(left, right):
    return jnp.dot(left, right, preferred_element_type=wide)


def dot_tn(left, right):
    return lax.dot_general(left, right, (((0,), (0,)), ((), ())), preferred_element_type=wide)


def flip(values):
    return values.astype(wide).T.astype(values.dtype)


def whole(array):
    rank = len(array.shape)
    return pl.BlockSpec(array.shape, lambda *_: (0,) * rank)


def held(array):
    return pl.BlockSpec(memory_space=pltpu.VMEM)


def third(place):
    return lambda array: pl.BlockSpec(
        (array.shape[0], array.shape[1] // 3, array.shape[2]), lambda *_: (0, place, 0)
    )


def kernel_call(
    kernel, name, index, inputs, outputs, flops, exps=0, grid=(1,), scratch=(), plain=None
):
    plain = plain or whole
    arrays = [item[0] if isinstance(item, tuple) else item for item in inputs]
    specs = [
        (item[1](item[0]) if callable(item[1]) else item[1]) if isinstance(item, tuple) else plain(item)
        for item in inputs
    ]
    shapes = [item[0] if isinstance(item, tuple) else item for item in outputs]
    out_specs = [item[1] if isinstance(item, tuple) else plain(item) for item in outputs]
    moved = sum(math.prod(a.shape) * a.dtype.itemsize for a in arrays + shapes)
    return pl.pallas_call(
        kernel,
        grid_spec=pltpu.PrefetchScalarGridSpec(
            num_scalar_prefetch=1,
            grid=grid,
            in_specs=specs,
            out_specs=out_specs,
            scratch_shapes=list(scratch),
        ),
        out_shape=shapes,
        compiler_params=pltpu.CompilerParams(vmem_limit_bytes=(24 if plain is held else 48) * 1024 * 1024),
        cost_estimate=pl.CostEstimate(
            flops=flops // share, bytes_accessed=moved // share, transcendentals=exps // share
        ),
        name=name,
    )(index, *arrays)


def shape_of(shape, kind):
    return jax.ShapeDtypeStruct(shape, kind)


def place_of(index, spot, rows):
    return pl.ds(pl.multiple_of((index ^ masks[spot]) * rows, 128), rows)


def diagonal():
    keys = lax.broadcasted_iota(jnp.int32, (tile, tile), 0)
    queries = lax.broadcasted_iota(jnp.int32, (tile, tile), 1)
    return keys <= queries


def unit_of(values):
    center = values - jnp.mean(values, axis=-1, keepdims=True)
    spread = jnp.mean(center * center, axis=-1, keepdims=True)
    scale = lax.rsqrt(spread + epsilon)
    return center * scale, scale


def norm_pull(unit, scale, gain, upstream):
    scaled = upstream * gain
    return scale * (
        scaled
        - jnp.mean(scaled, axis=-1, keepdims=True)
        - unit * jnp.mean(scaled * unit, axis=-1, keepdims=True)
    )


def column_sum(values):
    return jnp.sum(values, axis=0, keepdims=True)


def pick_in_kernel(index_ref, in_ref, out_ref):
    width = in_ref.shape[1] // 3
    own = width // 4
    for ctx in range(4):

        @pl.when(index_ref[0] == ctx)
        def pick():
            for head in range(own // HEAD_DIM):
                for kind in range(3):
                    begin = kind * width + ctx * own + head * HEAD_DIM
                    target = head * part + kind * HEAD_DIM
                    out_ref[:, target : target + HEAD_DIM] = in_ref[:, begin : begin + HEAD_DIM]


def pick_rest_kernel(index_ref, out_weight_ref, up_ref, down_ref, out_ref):
    shard, width = out_weight_ref.shape
    out_ref[:shard, :] = out_weight_ref[...]
    for ctx in range(4):

        @pl.when(index_ref[0] == ctx)
        def pick():
            for owner in range(width // shard):
                begin = owner * 4 * shard + ctx * shard
                out_ref[shard : 2 * shard, owner * shard : (owner + 1) * shard] = up_ref[
                    :, begin : begin + shard
                ]
            out_ref[2 * shard :, :] = down_ref[ctx * shard : (ctx + 1) * shard, :]


def norm_kernel(
    index_ref,
    own_ref,
    far_ref,
    near_ref,
    last_ref,
    vector_ref,
    first_ref,
    turned_ref,
    unit_ref,
):
    rows = own_ref.shape[0]
    for spot, piece in enumerate((own_ref, far_ref, near_ref, last_ref)):
        here = slice(spot * rows, (spot + 1) * rows)
        unit, scale = unit_of(piece[...].astype(wide))
        unit_ref[:, here] = unit.T.astype(low)
        normed = unit * vector_ref[0:1, :] + vector_ref[1:2, :]
        first_ref[here, :] = normed.astype(low)
        turned_ref[:, here] = normed.T.astype(low)


def attend_kernel(
    index_ref,
    first_ref,
    low_half_ref,
    high_half_ref,
    bias_ref,
    weight_ref,
    mix_ref,
    keep_ref,
    send_ref,
    full_ref,
    stats_ref,
    q_s,
    k_s,
    v_s,
    o_s,
):
    total, width = first_ref.shape
    rows = total // 4
    index = index_ref[0]
    heads = width // lanes

    @pl.when(pl.program_id(0) == 0)
    def begin_all():
        shard = low_half_ref.shape[0] // 4
        for spot in range(8):
            source = low_half_ref if spot < 4 else high_half_ref
            block = source[(spot % 4) * shard : (spot % 4 + 1) * shard, :]
            there = pl.ds(pl.multiple_of((index_ref[1] ^ dp_masks[spot]) * shard, 32), shard)
            for head in range(heads):
                begin = head * lanes
                weight_ref[there, begin : begin + part] = block[:, head * part : (head + 1) * part]
                weight_ref[there, begin + part : begin + lanes] = jnp.zeros(
                    (shard, lanes - part), low
                )

    head = pl.program_id(0)
    slab = pl.ds(pl.multiple_of(head * lanes, lanes), lanes)
    lines = pl.ds(pl.multiple_of(head * HEAD_DIM, HEAD_DIM), HEAD_DIM)
    for spot in range(4):
        here = slice(spot * rows, (spot + 1) * rows)
        there = place_of(index, spot, rows)
        block = (dot_nn(first_ref[here, :], weight_ref[:, slab]) + bias_ref[head]).astype(low)
        mix_ref[here, :] = block
        q_s[there, :] = block[:, 0:64] * jnp.bfloat16(0.125)
        k_s[there, :] = block[:, 64:128]
        v_s[there, :] = block[:, 128:192]
    allowed = diagonal()
    flipped = flip(v_s[...])
    for i in range(total // tile):
        begin, end = i * tile, (i + 1) * tile
        queries = q_s[begin:end, :]
        near = jnp.where(allowed, dot_nt(k_s[begin:end, :], queries), neg_large)
        top = jnp.max(near, axis=0, keepdims=True)
        if i > 0:
            past = dot_nt(k_s[:begin, :], queries)
            top = jnp.maximum(top, jnp.max(past, axis=0, keepdims=True))
        near = jnp.exp(near - top)
        amount = column_sum(near)
        context = dot_nn(flipped[:, begin:end], near.astype(low))
        if i > 0:
            past = jnp.exp(past - top)
            amount = amount + column_sum(past)
            context = context + dot_nn(flipped[:, :begin], past.astype(low))
        o_s[:, begin:end] = context / amount
        stats_ref[0, :, begin:end] = top + jnp.log(amount)
    for spot in range(4):
        block = o_s[:, place_of(index, spot, rows)]
        full_ref[:, spot * rows : (spot + 1) * rows] = block
        target = keep_ref if spot in (0, 2) else send_ref
        target[lines, (spot // 2) * rows : (spot // 2 + 1) * rows] = block.astype(low)


def attend(index, first_low, low_half, high_half, bias):
    total, width = first_low.shape
    rows = total // 4
    heads = width // lanes
    features = heads * HEAD_DIM
    by_head = lambda h, s: (h, 0)
    pairs = heads * total * total // 2
    return kernel_call(
        attend_kernel,
        "attend",
        index,
        [first_low, low_half, high_half, bias],
        [
            (shape_of((width, width), low), whole(first_low[:width])),
            (shape_of((total, width), low), pl.BlockSpec((total, lanes), lambda h, s: (0, h))),
            shape_of((features, 2 * rows), low),
            shape_of((features, 2 * rows), low),
            (shape_of((features, total), wide), pl.BlockSpec((HEAD_DIM, total), by_head)),
            (
                shape_of((heads, 1, total), wide),
                pl.BlockSpec((1, 1, total), lambda h, s: (h, 0, 0)),
            ),
        ],
        pairs * 4 * 256 + 2 * total * width * width,
        pairs,
        (heads,),
        [pltpu.VMEM((total, HEAD_DIM), low)] * 3 + [pltpu.VMEM((HEAD_DIM, total), wide)],
        held,
    )


def project_kernel(
    index_ref,
    keep_ref,
    far_ref,
    near_ref,
    weight_ref,
    tokens_ref,
    vector_ref,
    residual_ref,
    second_ref,
    turned_ref,
):
    rows, width = tokens_ref.shape
    own = width // 4
    pieces = [keep_ref[:, :rows], far_ref[:, :rows], near_ref[:, :rows], near_ref[:, rows:]]
    residual = tokens_ref[...].astype(wide) + vector_ref[4:5, :]
    for spot in range(4):
        turned = flip(pieces[spot])
        group = index_ref[0] ^ masks[spot]
        weights = weight_ref[pl.ds(2 * group, 2)].reshape(own, width)
        residual = residual + dot_nn(turned, weights)
    residual_ref[...] = residual
    unit, scale = unit_of(residual)
    second_ref[...] = (unit * vector_ref[5:6, :] + vector_ref[6:7, :]).astype(low)
    for spot in range(4):
        turned_ref[spot * own : (spot + 1) * own, :] = pieces[spot]


def feed_kernel(
    index_ref,
    one_ref,
    two_ref,
    up_one_ref,
    up_two_ref,
    up_ref,
    down_ref,
    bias_ref,
    active_ref,
    hidden_ref,
    kept_ref,
    sent_ref,
    sum_ref,
):
    rows, width = one_ref.shape
    up = up_ref[...].reshape(width, width)
    down = down_ref[...].reshape(width, width)
    for spot in (1, 0):
        here = slice(spot * rows, (spot + 1) * rows)
        values = two_ref[...] if spot else one_ref[...]
        grads = up_two_ref[...] if spot else up_one_ref[...]
        hidden = dot_nn(values, up) + bias_ref[...]
        square = hidden * hidden
        bend = jnp.tanh(root * hidden * (1.0 + 0.044715 * square))
        active_ref[here, :] = (0.5 * hidden * (1.0 + bend)).astype(low)
        slope = 0.5 * (1.0 + bend) + 0.5 * hidden * (1.0 - bend * bend) * (
            root * (1.0 + 3 * 0.044715 * square)
        )
        grad = (slope * dot_nt(grads, down)).astype(low)
        hidden_ref[here, :] = grad
        sums = column_sum(grad.astype(wide))
        sum_ref[...] = sums if spot else sum_ref[...] + sums
        result = dot_nt(grad, up)
        if spot:
            sent_ref[...] = result.astype(low)
        else:
            kept_ref[...] = result


def halves(index_ref, block, kept_ref, sent_ref, pair):
    upper = index_ref[1] % 2 == 1
    kept_ref[pair] = jnp.where(upper, block[1], block[0])
    sent_ref[pair] = jnp.where(upper, block[0], block[1]).astype(low)


def feed_grad_kernel(
    index_ref,
    own_ref,
    far_ref,
    near_ref,
    last_ref,
    up_own_ref,
    up_far_ref,
    up_near_ref,
    up_last_ref,
    hidden_one_ref,
    hidden_two_ref,
    active_one_ref,
    active_two_ref,
    down_ref,
    out_ref,
    kept_one_ref,
    sent_one_ref,
    kept_two_ref,
    sent_two_ref,
):
    rows, width = own_ref.shape
    count, shard = out_ref.shape[0], out_ref.shape[1] // 2

    def halved(one, two):
        return (one[:rows, :], one[rows:, :], two[:rows, :], two[rows:, :])

    pairs = (
        ((own_ref, near_ref, far_ref, last_ref), halved(hidden_one_ref, hidden_two_ref)),
        (
            halved(active_one_ref, active_two_ref),
            (up_own_ref, up_near_ref, up_far_ref, up_last_ref),
        ),
    )
    for place, (lefts, rights) in enumerate(pairs):
        total = None
        for left, right in zip(lefts, rights):
            update = dot_tn(left[...], right[...])
            total = update if total is None else total + update
        total = total.astype(low).reshape(count, shard, width)
        out_ref[:, place * shard : (place + 1) * shard, :] = total
    down = down_ref[...].reshape(width, width)
    kept_one_ref[...] = dot_nn(active_one_ref[:rows, :], down)
    sent_one_ref[...] = dot_nn(active_one_ref[rows:, :], down).astype(low)
    kept_two_ref[...] = dot_nn(active_two_ref[:rows, :], down)
    sent_two_ref[...] = dot_nn(active_two_ref[rows:, :], down).astype(low)


def in_grad_kernel(
    index_ref,
    turned_ref,
    unit_ref,
    mix_ref,
    weight_ref,
    bias_ref,
    two_ref,
    up_one_ref,
    up_two_ref,
    kept_ref,
    sent_ref,
    rows_s,
):
    pairs, high, columns = kept_ref.shape
    width = mix_ref.shape[1]
    shard = width // (2 * pairs)
    own = columns // 3
    upper = index_ref[1] % 2 == 1
    rows_s[...] = jnp.zeros(rows_s.shape, wide)
    rows_s[4:8, :] = two_ref[...]
    sums = jnp.concatenate([bias_ref[head] for head in range(width // lanes)], axis=1)
    for ctx in range(4):

        @pl.when(index_ref[0] == ctx)
        def put():
            rows_s[8 + ctx : 9 + ctx, :] = up_one_ref[...] + up_two_ref[...]
            for head in range(own // HEAD_DIM):
                begin = ctx * own + head * HEAD_DIM
                for row, kind in ((2, 0), (3, 2)):
                    rows_s[row : row + 1, begin : begin + HEAD_DIM] = bias_ref[
                        head, :, kind * HEAD_DIM : (kind + 1) * HEAD_DIM
                    ]

    column = lax.broadcasted_iota(jnp.int32, (2 * shard, 128), 1)
    for pair in range(pairs):
        here = slice(2 * pair * shard, 2 * (pair + 1) * shard)
        weights = weight_ref[here, :].astype(wide)
        gain = jnp.sum(weights * dot_nn(unit_ref[here, :], mix_ref[...]), axis=1, keepdims=True)
        shift = jnp.sum(weights * sums, axis=1, keepdims=True)
        both = jnp.where(column == 0, gain, jnp.where(column == 1, shift, 0.0)).T
        rows_s[0:2, here] = both[0:2, :]
    for pair in range(pairs):
        begin = 2 * pair * shard
        block = dot_nn(turned_ref[begin : begin + 2 * shard, :], mix_ref[...])
        kept = jnp.where(upper, block[shard:, :], block[:shard, :])
        sent = jnp.where(upper, block[:shard, :], block[shard:, :]).astype(low)
        for head in range(columns // part):
            here = slice(head * part, (head + 1) * part)
            there = slice(head * lanes, head * lanes + part)
            kept_ref[pair, :shard, here] = kept[:, there]
            sent_ref[pair, :shard, here] = sent[:, there]
        one = rows_s[0:12, begin : begin + shard]
        two = rows_s[0:12, begin + shard : begin + 2 * shard]
        kept = jnp.where(upper, two, one)
        sent = jnp.where(upper, one, two)

        def lines(values):
            return jnp.concatenate(
                [
                    jnp.concatenate([values[6 * r + i : 6 * r + i + 1] for i in range(6)], axis=1)
                    for r in range(2)
                ],
                axis=0,
            )

        kept_ref[pair, shard : shard + 2, :] = lines(kept)
        sent_ref[pair, shard:, :] = jnp.concatenate(
            [lines(sent), jnp.zeros((high - shard - 2, columns), wide)], axis=0
        ).astype(low)
        kept_ref[pair, shard + 2 :, :] = jnp.zeros((high - shard - 2, columns), wide)


def turn_kernel(
    index_ref,
    kept_ref,
    core_ref,
    far_ref,
    residual_ref,
    cotangent_ref,
    weight_ref,
    vector_ref,
    grad_ref,
    attn_ref,
    keep_ref,
    send_ref,
    sum_ref,
):
    rows, width = residual_ref.shape
    own = width // 4
    grad = kept_ref[...] + core_ref[...].astype(wide) + far_ref[...].astype(wide)
    unit, scale = unit_of(residual_ref[...])
    upstream = cotangent_ref[...].astype(wide)
    result = upstream + norm_pull(unit, scale, vector_ref[5:6, :], grad)
    grad_ref[...] = result
    attn = result.astype(low)
    attn_ref[...] = attn
    for spot in range(4):
        group = index_ref[0] ^ masks[spot]
        weights = weight_ref[pl.ds(2 * group, 2)].reshape(own, width)
        block = dot_nt(weights, attn).astype(low)
        target = keep_ref if spot in (0, 2) else send_ref
        target[:, (spot // 2) * rows : (spot // 2 + 1) * rows] = block
    sum_ref[0:1, :] = column_sum(grad * unit)
    sum_ref[1:2, :] = column_sum(grad)
    sum_ref[2:3, :] = column_sum(attn.astype(wide))
    sum_ref[3:4, :] = column_sum(upstream)


def out_grad_kernel(index_ref, turned_ref, attn_ref, kept_ref, sent_ref):
    width = turned_ref.shape[0]
    own = width // 4
    for spot in range(4):
        group = index_ref[0] ^ masks[spot]
        block = dot_nn(turned_ref[spot * own : (spot + 1) * own, :], attn_ref[...])
        halves(index_ref, block.reshape(2, own // 2, width), kept_ref, sent_ref, group)


def attend_back_kernel(
    index_ref,
    mix_ref,
    keep_ref,
    far_ref,
    near_ref,
    full_ref,
    stats_ref,
    out_ref,
    sum_ref,
    q_s,
    k_s,
    v_s,
    g_s,
    d_s,
    dq_s,
):
    total = mix_ref.shape[0]
    rows = total // 4
    index = index_ref[0]
    head = pl.program_id(0)
    slab = pl.ds(pl.multiple_of(head * lanes, lanes), lanes)
    lines = pl.ds(pl.multiple_of(head * HEAD_DIM, HEAD_DIM), HEAD_DIM)
    pieces = [keep_ref[lines, :rows], far_ref[lines, :rows]]
    pieces = pieces + [near_ref[lines, :rows], near_ref[lines, rows:]]
    for spot in range(4):
        here = slice(spot * rows, (spot + 1) * rows)
        there = place_of(index, spot, rows)
        block = mix_ref[here, slab]
        q_s[there, :] = block[:, 0:64] * jnp.bfloat16(0.125)
        k_s[there, :] = block[:, 64:128]
        v_s[there, :] = block[:, 128:192]
        block = pieces[spot]
        g_s[:, there] = block
        d_s[:, there] = column_sum(block.astype(wide) * full_ref[lines, here])
    allowed = diagonal()
    turned = flip(g_s[...])
    flipped = flip(k_s[...])
    count = total // tile
    for j in range(count):
        begin, end = j * tile, (j + 1) * tile
        keys, values = k_s[begin:end, :], v_s[begin:end, :]
        probs = jnp.exp(dot_nt(keys, q_s[begin:, :]) - stats_ref[head, :, begin:])
        near = jnp.where(allowed, probs[:, :tile], 0.0)
        probs = near if j == count - 1 else jnp.concatenate([near, probs[:, tile:]], axis=1)
        scores = (probs * (dot_nn(values, g_s[:, begin:]) - d_s[:, begin:])).astype(low)
        grad_value = dot_nn(probs.astype(low), turned[begin:, :])
        grad_key = dot_nn(scores, q_s[begin:, :])
        update = dot_nn(flipped[:, begin:end], scores)
        if j == 0:
            dq_s[...] = update
        else:
            dq_s[:, begin:] = dq_s[:, begin:] + update
        k_s[begin:end, :] = grad_key.astype(low)
        v_s[begin:end, :] = grad_value.astype(low)
    q_s[...] = (dq_s[...] * 0.125).T.astype(low)
    for spot in range(4):
        here = slice(spot * rows, (spot + 1) * rows)
        there = place_of(index, spot, rows)
        block = jnp.concatenate(
            [q_s[there, :], k_s[there, :], v_s[there, :], jnp.zeros((rows, 64), low)], axis=1
        )
        out_ref[here, slab] = block
        sums = column_sum(block.astype(wide))
        sum_ref[head] = sums if spot == 0 else sum_ref[head] + sums


def attend_back(index, mix, keep, far, near, full, stats):
    total, width = mix.shape
    heads = width // lanes
    pairs = heads * total * total // 2
    return kernel_call(
        attend_back_kernel,
        "attend_back",
        index,
        [mix, keep, far, near, full, stats],
        [shape_of((total, width), low), shape_of((heads, 1, lanes), wide)],
        pairs * 10 * 256,
        pairs,
        (heads,),
        [pltpu.VMEM((total, HEAD_DIM), low)] * 3
        + [
            pltpu.VMEM((HEAD_DIM, total), low),
            pltpu.VMEM((1, total), wide),
            pltpu.VMEM((HEAD_DIM, total), wide),
        ],
        held,
    )


def first_back_kernel(spots, index_ref, mix_ref, weight_ref, kept_ref, sent_ref):
    rows = kept_ref.shape[0]
    for spot, target in zip(spots, (sent_ref, kept_ref)):
        grad = dot_nt(mix_ref[spot * rows : (spot + 1) * rows, :], weight_ref[...])
        target[...] = grad.astype(target.dtype)


def tokens_kernel(
    index_ref, kept_ref, core_ref, far_ref, tokens_ref, residual_ref, vector_ref, out_ref
):
    rows = tokens_ref.shape[0]
    grad = kept_ref[...] + core_ref[...].astype(wide) + far_ref[...].astype(wide)
    unit, scale = unit_of(tokens_ref[...].astype(wide))
    result = residual_ref[...] + norm_pull(unit, scale, vector_ref[0:1, :], grad)
    out_ref[...] = result.astype(low)


def spread_kernel(index_ref, own_ref, far_ref, near_ref, up_ref, down_ref):
    width = own_ref.shape[1]
    shard = own_ref.shape[0] // 2
    for ctx in range(4):
        for spot in range(4):

            @pl.when((index_ref[0] ^ ctx) == masks[spot])
            def put():
                source = [own_ref, far_ref, near_ref, near_ref][spot]
                base = 2 * shard if spot == 3 else 0
                block = source[base : base + shard, :].astype(wide)
                for owner in range(width // shard):
                    begin = (owner * 4 + ctx) * shard
                    up_ref[:, begin : begin + shard] = block[:, owner * shard : (owner + 1) * shard]
                down_ref[ctx * shard : (ctx + 1) * shard, :] = source[
                    base + shard : base + 2 * shard, :
                ].astype(wide)


def spread_in_kernel(index_ref, own_ref, far_ref, near_ref, in_ref, sum_ref):
    shard, width = in_ref.shape[0], in_ref.shape[1] // 3
    high, own = own_ref.shape[0], width // 4
    for ctx in range(4):
        for spot in range(4):

            @pl.when((index_ref[0] ^ ctx) == masks[spot])
            def put():
                source = [own_ref, far_ref, near_ref, near_ref][spot]
                base = high if spot == 3 else 0
                block = source[base : base + shard, :].astype(wide)
                for head in range(own // HEAD_DIM):
                    for kind in range(3):
                        begin = kind * width + ctx * own + head * HEAD_DIM
                        target = head * part + kind * HEAD_DIM
                        in_ref[:, begin : begin + HEAD_DIM] = block[:, target : target + HEAD_DIM]
                extra = source[base + shard : base + high, :].astype(wide)
                sum_ref[...] = extra if ctx == 0 else sum_ref[...] + extra


def pieces_of(values):
    far = swap(values, "ctx", 2)
    return values, far, swap(jnp.concatenate([values, far], axis=0), "ctx", 1)


def blocks_of(values):
    far = swap(values, "ctx", 2)
    near = swap(values, "ctx", 1)
    return values, far, near, swap(far, "ctx", 1)


def exchange(keep, send):
    rows = keep.shape[1] // 2
    far = swap(send, "ctx", 2)
    near = swap(jnp.concatenate([keep[:, rows:], far[:, rows:]], axis=1), "ctx", 1)
    return far, near


def split_body(
    tokens,
    first_gain,
    first_shift,
    in_weight,
    in_bias,
    out_weight,
    out_bias,
    second_gain,
    second_shift,
    up_weight,
    up_bias,
    down_weight,
    down_bias,
    cotangent,
):
    rows, width = tokens.shape
    total = 4 * rows
    n_dp = lax.axis_size("dp")
    shard = width // n_dp
    ctx = lax.axis_index("ctx")
    owner = lax.axis_index("dp")
    heads = width // HEAD_DIM // 4
    own = heads * HEAD_DIM
    index = jnp.stack([ctx, owner]).astype(jnp.int32)
    big = 2 * total * width * width
    small = 2 * rows * width * width
    row_wide, row_low = shape_of((rows, width), wide), shape_of((rows, width), low)

    (in_own,) = kernel_call(
        pick_in_kernel,
        "pick_in",
        index,
        [in_weight],
        [shape_of((shard, 3 * own), low)],
        0,
        plain=held,
    )
    in_other = swap(in_own, "dp", 4)
    in_two = jnp.concatenate([in_own, in_other], axis=0)
    low_half = jnp.concatenate([in_two, swap(in_two, "dp", 2)], axis=0)
    high_half = swap(low_half, "dp", 1)
    (rest,) = kernel_call(
        pick_rest_kernel,
        "pick_rest",
        index,
        [out_weight, up_weight, after(down_weight, in_other)],
        [shape_of((3 * shard, width), low)],
        0,
    )
    rest = lax.all_gather(rest, "dp", axis=0, tiled=False)
    vectors = jnp.concatenate(
        [first_gain, first_shift, in_bias[0], in_bias[1], out_bias, second_gain, second_shift]
        + [down_bias, up_bias]
    ).reshape(1, 12 * shard)
    vectors = dp_gather(vectors, (in_two, low_half)).reshape(n_dp, 12, shard).transpose(1, 0, 2).reshape(12, width)
    vectors = vectors.astype(wide)
    hidden_bias = lax.dynamic_slice_in_dim(vectors, 8 + ctx, 1, 0)
    zeros = jnp.zeros((heads, HEAD_DIM), wide)
    mine = lax.dynamic_slice(vectors, (2, ctx * own), (2, own)).reshape(2, heads, HEAD_DIM)
    bias_full = jnp.concatenate([mine[0], zeros, mine[1], zeros], axis=1).reshape(heads, 1, lanes)

    token_blocks = blocks_of(tokens)
    first_low, first_turned, unit_turned = kernel_call(
        norm_kernel,
        "norm",
        index,
        [*token_blocks, vectors],
        [shape_of((total, width), low)] + [shape_of((width, total), low)] * 2,
        0,
    )
    upstream = blocks_of(after(cotangent, token_blocks[1]))
    in_full, mix, keep, send, context_full, stats = attend(
        index, first_low, low_half, high_half, bias_full
    )
    far, near = exchange(keep, after(send, upstream[1]))
    out_block = (rest, third(0))
    up_block = (rest, third(1))
    down_block = (rest, third(2))
    residual, second_low, turned = kernel_call(
        project_kernel,
        "project",
        index,
        [keep, far, near, out_block, tokens, vectors],
        [row_wide, row_low, shape_of((width, rows), low)],
        small,
    )

    def feed(name, one, two, up_one, up_two):
        return kernel_call(
            feed_kernel,
            name,
            index,
            [one, two, up_one, up_two, up_block, down_block, hidden_bias],
            [shape_of((total // 2, width), low)] * 2
            + [row_wide, row_low, shape_of((1, width), wide)],
            3 * big // 2,
            total * width // 2,
        )

    far, near = swap(second_low, "ctx", 2), swap(second_low, "ctx", 1)
    active_one, hidden_one, kept_one, sent_one, up_sum_one = feed(
        "feed_one", second_low, near, upstream[0], upstream[2]
    )
    far = after(far, active_one)
    second = (second_low, far, near, swap(far, "ctx", 1))
    active_two, hidden_two, kept_two, sent_two, up_sum_two = feed(
        "feed_two", second[1], second[3], upstream[1], upstream[3]
    )
    core_one = swap(sent_one, "ctx", 1)
    passed = (kept_two + swap(sent_two, "ctx", 1).astype(wide)).astype(low)
    far = swap(passed, "ctx", 2)
    feed_grad, *branch = kernel_call(
        feed_grad_kernel,
        "feed_grad",
        index,
        [after(second[0], passed), *second[1:], *upstream, hidden_one, hidden_two]
        + [active_one, active_two, down_block],
        [shape_of((n_dp, 2 * shard, width), low), row_wide, row_low, row_wide, row_low],
        3 * big,
    )
    far, feed_grad, *branch = lax.optimization_barrier((far, feed_grad, *branch))
    feed_mine = lax.psum_scatter(feed_grad, "dp", scatter_dimension=0, tiled=False)
    grad_residual, grad_attn, keep, send, sums_two = kernel_call(
        turn_kernel,
        "turn",
        index,
        [kept_one, core_one, far, residual, cotangent, out_block, vectors],
        [
            row_wide,
            row_low,
            shape_of((own, 2 * rows), low),
            shape_of((own, 2 * rows), low),
            shape_of((4, width), wide),
        ],
        small,
    )
    out_kept, out_sent = kernel_call(
        out_grad_kernel,
        "out_grad",
        index,
        [turned, grad_attn],
        [shape_of((n_dp // 2, shard, width), wide), shape_of((n_dp // 2, shard, width), low)],
        small,
    )
    far = swap(send, "ctx", 2)
    late = after(far, out_sent)
    near = swap(jnp.concatenate([keep[:, rows:], late[:, rows:]], axis=1), "ctx", 1)
    branch_kept, branch_sent, kept_two, sent_two = branch
    branch_core = swap(branch_sent, "ctx", 1)
    passed = (kept_two + swap(sent_two, "ctx", 1).astype(wide)).astype(low)
    branch_far = swap(passed, "ctx", 2)
    grad_mix, bias_sums = attend_back(
        index, mix, after(keep, passed), far, near, context_full, stats
    )

    high = shard + 16
    out_half = dp_scatter_one(out_kept, out_sent)
    out_next, out_sent = dp_parts(out_half, 1, 2)
    kept_two, sent_two = kernel_call(
        functools.partial(first_back_kernel, (3, 1)),
        "first_back_two",
        index,
        [after(grad_mix, out_half, branch_far), in_full],
        [row_wide, row_low],
        big // 2,
    )
    passed = (kept_two + swap(sent_two, "ctx", 1).astype(wide)).astype(low)
    far = swap(passed, "ctx", 2)
    out_sent = after(out_sent, passed)
    out_arrived = swap(out_sent, "dp", 2)
    in_kept, in_sent = kernel_call(
        in_grad_kernel,
        "in_grad",
        index,
        [after(first_turned, passed, out_sent), unit_turned, grad_mix, in_full]
        + [bias_sums, sums_two, up_sum_one, up_sum_two],
        [shape_of((n_dp // 2, high, 3 * own), wide), shape_of((n_dp // 2, high, 3 * own), low)],
        2 * big,
        scratch=[pltpu.VMEM((16, width), wide)],
    )
    out_next = after(out_next, in_sent) + out_arrived.astype(wide)
    out_next, out_sent = dp_parts(out_next, 0, 4)
    kept_one, sent_one = kernel_call(
        functools.partial(first_back_kernel, (2, 0)),
        "first_back_one",
        index,
        [after(grad_mix, out_sent), in_full],
        [row_wide, row_low],
        big // 2,
    )
    core_one = swap(sent_one, "ctx", 1)
    in_half = dp_scatter_one(after(in_kept, kept_one), in_sent)
    in_next, in_sent = dp_parts(in_half, 1, 2)
    (tokens_grad,) = kernel_call(
        tokens_kernel,
        "tokens",
        index,
        [kept_one, core_one, after(far, in_sent, out_sent), tokens, grad_residual, vectors],
        [row_low],
        0,
    )
    feed_mine = after(feed_mine.reshape(2 * shard, width), in_sent, tokens_grad)
    feed_far = swap(feed_mine, "ctx", 2)
    out_mine = (after(out_next, feed_mine) + swap(out_sent, "dp", 4).astype(wide)).astype(low)
    out_far = swap(out_mine, "ctx", 2)
    in_next = after(in_next, out_mine) + swap(in_sent, "dp", 2).astype(wide)
    in_next, in_sent = dp_parts(in_next, 0, 4)
    feed_near = jnp.concatenate([after(feed_mine, in_sent), feed_far], axis=0)
    feed_near = swap(feed_near, "ctx", 1)
    out_mine = (after(out_mine, in_sent).astype(wide) + out_far.astype(wide)).astype(low)
    out_weight_grad = out_mine.astype(wide) + swap(out_mine, "ctx", 1).astype(wide)
    in_mine = (after(in_next, out_mine) + swap(in_sent, "dp", 4).astype(wide)).astype(low)
    branch = branch_kept + branch_core.astype(wide) + branch_far.astype(wide)
    layer_out = (residual + branch + vectors[7]).astype(low)
    up_weight_grad, down_weight_grad = kernel_call(
        spread_kernel,
        "spread",
        index,
        [after(feed_mine, in_mine), feed_far, feed_near],
        [shape_of((shard, 4 * width), wide), shape_of((4 * shard, width), wide)],
        0,
        plain=held,
    )
    in_far = swap(in_mine, "ctx", 2)
    in_near = jnp.concatenate([after(in_mine, up_weight_grad, layer_out), in_far], axis=0)
    in_near = swap(in_near, "ctx", 1)
    in_weight_grad, sums = kernel_call(
        spread_in_kernel,
        "spread_in",
        index,
        [in_mine, in_far, in_near],
        [shape_of((shard, 3 * width), wide), shape_of((high - shard, 3 * own), wide)],
        0,
        plain=held,
    )
    sums = sums[:2].reshape(12, shard)
    return (
        layer_out,
        tokens_grad,
        sums[0],
        sums[1],
        in_weight_grad,
        sums[2:4],
        out_weight_grad,
        sums[6],
        sums[4],
        sums[5],
        up_weight_grad,
        sums[8:12].reshape(4 * shard),
        down_weight_grad,
        sums[7],
    )


def solution(mesh):
    in_specs = (
        P(("dp", "ctx"), None),
        P("dp"),
        P("dp"),
        P("dp", None),
        P(None, "dp"),
        P("dp", None),
        P("dp"),
        P("dp"),
        P("dp"),
        P("dp", None),
        P("dp"),
        P("dp", None),
        P("dp"),
        P(("dp", "ctx"), None),
    )
    out_specs = (
        P(("dp", "ctx"), None),
        P(("dp", "ctx"), None),
        P("dp"),
        P("dp"),
        P("dp", None),
        P(None, "dp"),
        P("dp", None),
        P("dp"),
        P("dp"),
        P("dp"),
        P("dp", None),
        P("dp"),
        P("dp", None),
        P("dp"),
    )
    chosen = split_body if heads_split(mesh) else gathered_body
    return jax.shard_map(chosen, mesh=mesh, in_specs=in_specs, out_specs=out_specs, check_vma=False)
```

```python
import functools
import math

import jax
import jax.numpy as jnp
from jax import lax
from jax.experimental import pallas as pl
from jax.experimental.pallas import tpu as pltpu
from jax.sharding import PartitionSpec as P

HEAD_DIM = 64


epsilon = 1e-05
neg_large = -1e30


def layer_norm(values, gain, shift):
    center = values - jnp.mean(values, axis=-1, keepdims=True)
    spread = jnp.mean(center * center, axis=-1, keepdims=True)
    return center * lax.rsqrt(spread + epsilon) * gain + shift


def norm_back(values, gain, shift, upstream):
    result, pullback = jax.vjp(layer_norm, values, gain, shift)
    return pullback(upstream)


def smooth_gate(values):
    return jax.nn.gelu(values, approximate=True)


def forward_block(state, query_heads, query_pos, key_blk, value_blk, key_pos, factor):
    row_max, row_total, accumulated = state
    scores = (
        jnp.einsum("qhd,khd->hqk", query_heads, key_blk, preferred_element_type=jnp.float32)
        * factor
    )
    allowed = (query_pos[:, None] >= key_pos[None, :])[None]
    scores = jnp.where(allowed, scores, neg_large)
    new_max = jnp.maximum(row_max, jnp.max(scores, axis=-1))
    rescale = jnp.exp(row_max - new_max)
    weights = jnp.where(allowed, jnp.exp(scores - new_max[:, :, None]), 0.0)
    row_total = row_total * rescale + jnp.sum(weights, axis=-1)
    update = jnp.einsum(
        "hqk,khd->qhd", weights.astype(jnp.bfloat16), value_blk, preferred_element_type=jnp.float32
    )
    accumulated = accumulated * rescale.T[:, :, None] + update
    return (new_max, row_total, accumulated)


def pair_grads(
    query_heads, grad_heads, stats, deltas, query_pos, key_blk, value_blk, key_pos, factor
):
    scores = (
        jnp.einsum("qhd,khd->hqk", query_heads, key_blk, preferred_element_type=jnp.float32)
        * factor
    )
    allowed = (query_pos[:, None] >= key_pos[None, :])[None]
    probs = jnp.where(allowed, jnp.exp(scores - stats[:, :, None]), 0.0)
    grad_probs = jnp.einsum(
        "qhd,khd->hqk", grad_heads, value_blk, preferred_element_type=jnp.float32
    )
    grad_scores = (probs * (grad_probs - deltas[:, :, None])).astype(jnp.bfloat16)
    grad_query = (
        jnp.einsum("hqk,khd->qhd", grad_scores, key_blk, preferred_element_type=jnp.float32)
        * factor
    )
    grad_key = (
        jnp.einsum("hqk,qhd->khd", grad_scores, query_heads, preferred_element_type=jnp.float32)
        * factor
    )
    grad_value = jnp.einsum(
        "hqk,qhd->khd", probs.astype(jnp.bfloat16), grad_heads, preferred_element_type=jnp.float32
    )
    return (grad_query, grad_key, grad_value)


def over_keys(state, key_part, value_part, begin_row, top_query, place, block_fn):
    amount, head_count, head_dim = key_part.shape
    stride = math.gcd(amount, 512)
    key_blocks = key_part.reshape(amount // stride, stride, head_count, head_dim)
    value_blocks = value_part.reshape(amount // stride, stride, head_count, head_dim)
    offsets = begin_row + jnp.arange(amount // stride, dtype=jnp.int32) * stride

    def over_step_fn(inner, operands):
        key_blk, value_blk, offset = operands
        key_pos = place(offset + jnp.arange(stride, dtype=jnp.int32))

        def over_compute(current):
            return block_fn(current, key_blk, value_blk, key_pos)

        def keep(current):
            return current

        return (lax.cond(jnp.min(key_pos) <= top_query, over_compute, keep, inner), None)

    state, unused = lax.scan(over_step_fn, state, (key_blocks, value_blocks, offsets))
    return state


def gathered_body(
    tokens,
    first_gain,
    first_shift,
    in_weight,
    in_bias,
    out_weight,
    out_bias,
    second_gain,
    second_shift,
    up_weight,
    up_bias,
    down_weight,
    down_bias,
    cotangent,
):
    (
        first_gain,
        first_shift,
        in_weight,
        in_bias,
        out_weight,
        out_bias,
        second_gain,
        second_shift,
        up_weight,
        up_bias,
        down_weight,
        down_bias,
    ) = (
        lax.all_gather(first_gain, "dp", axis=0, tiled=True),
        lax.all_gather(first_shift, "dp", axis=0, tiled=True),
        lax.all_gather(in_weight, "dp", axis=0, tiled=True),
        lax.all_gather(in_bias, "dp", axis=1, tiled=True),
        lax.all_gather(out_weight, "dp", axis=0, tiled=True),
        lax.all_gather(out_bias, "dp", axis=0, tiled=True),
        lax.all_gather(second_gain, "dp", axis=0, tiled=True),
        lax.all_gather(second_shift, "dp", axis=0, tiled=True),
        lax.all_gather(up_weight, "dp", axis=0, tiled=True),
        lax.all_gather(up_bias, "dp", axis=0, tiled=True),
        lax.all_gather(down_weight, "dp", axis=0, tiled=True),
        lax.all_gather(down_bias, "dp", axis=0, tiled=True),
    )
    rows_dev = tokens.shape[0]
    width = tokens.shape[1]
    head_dim = HEAD_DIM
    head_count = width // head_dim
    factor = 1.0 / math.sqrt(head_dim)
    my_index = lax.axis_index("ctx")

    def place(rows):
        return rows

    query_pos = place(my_index * rows_dev + jnp.arange(rows_dev, dtype=jnp.int32))
    top_query = jnp.max(query_pos)
    inputs = tokens.astype(jnp.float32)
    gain_one = first_gain.astype(jnp.float32)
    shift_one = first_shift.astype(jnp.float32)
    first_low = layer_norm(inputs, gain_one, shift_one).astype(jnp.bfloat16)
    bias_full = jnp.concatenate([in_bias[0], jnp.zeros((width,), jnp.bfloat16), in_bias[1]]).astype(
        jnp.float32
    )
    mixture = (
        jnp.dot(first_low, in_weight, preferred_element_type=jnp.float32) + bias_full
    ).astype(jnp.bfloat16)
    query_rows = mixture[:, :width]
    key_rows = mixture[:, width : 2 * width]
    value_rows = mixture[:, 2 * width :]
    query_heads = query_rows.reshape(rows_dev, head_count, head_dim)

    def forward_fold(state, portion, begin_row):
        key_part, value_part = portion
        amount = key_part.shape[0]

        def block_fn(inner, key_blk, value_blk, key_pos):
            return forward_block(inner, query_heads, query_pos, key_blk, value_blk, key_pos, factor)

        return over_keys(
            state,
            key_part.reshape(amount, head_count, head_dim),
            value_part.reshape(amount, head_count, head_dim),
            begin_row,
            top_query,
            place,
            block_fn,
        )

    start_state = (
        jnp.full((head_count, rows_dev), neg_large, jnp.float32),
        jnp.zeros((head_count, rows_dev), jnp.float32),
        jnp.zeros((rows_dev, head_count, head_dim), jnp.float32),
    )
    row_max, row_total, accumulated = forward_fold(
        start_state,
        (
            lax.all_gather(key_rows, "ctx", axis=0, tiled=True),
            lax.all_gather(value_rows, "ctx", axis=0, tiled=True),
        ),
        jnp.int32(0),
    )
    stats = row_max + jnp.log(row_total)
    context_heads = accumulated / row_total.T[:, :, None]
    context_low = context_heads.reshape(rows_dev, width).astype(jnp.bfloat16)
    residual = (
        inputs
        + jnp.dot(context_low, out_weight, preferred_element_type=jnp.float32)
        + out_bias.astype(jnp.float32)
    )
    gain_two = second_gain.astype(jnp.float32)
    shift_two = second_shift.astype(jnp.float32)
    second_low = layer_norm(residual, gain_two, shift_two).astype(jnp.bfloat16)
    hidden = jnp.dot(second_low, up_weight, preferred_element_type=jnp.float32) + up_bias.astype(
        jnp.float32
    )
    activated, gate_back = jax.vjp(smooth_gate, hidden)
    active_low = activated.astype(jnp.bfloat16)
    layer_out = (
        residual
        + jnp.dot(active_low, down_weight, preferred_element_type=jnp.float32)
        + down_bias.astype(jnp.float32)
    ).astype(jnp.bfloat16)
    upstream = cotangent.astype(jnp.float32)
    down_bias_grad = jnp.sum(upstream, axis=0)
    down_weight_grad = jnp.einsum(
        "tf,td->fd", active_low, cotangent, preferred_element_type=jnp.float32
    )
    (grad_hidden,) = gate_back(
        jnp.einsum("td,fd->tf", cotangent, down_weight, preferred_element_type=jnp.float32)
    )
    grad_hidden = grad_hidden.astype(jnp.bfloat16)
    up_weight_grad = jnp.einsum(
        "td,tf->df", second_low, grad_hidden, preferred_element_type=jnp.float32
    )
    up_bias_grad = jnp.sum(grad_hidden.astype(jnp.float32), axis=0)
    grad_second = jnp.einsum(
        "tf,df->td", grad_hidden, up_weight, preferred_element_type=jnp.float32
    )
    grad_residual, second_gain_grad, second_shift_grad = norm_back(
        residual, gain_two, shift_two, grad_second
    )
    grad_residual = grad_residual + upstream
    grad_attn = grad_residual.astype(jnp.bfloat16)
    out_bias_grad = jnp.sum(grad_attn.astype(jnp.float32), axis=0)
    out_weight_grad = jnp.einsum(
        "td,te->de", context_low, grad_attn, preferred_element_type=jnp.float32
    )
    grad_context = jnp.einsum(
        "te,de->td", grad_attn, out_weight, preferred_element_type=jnp.float32
    ).astype(jnp.bfloat16)
    grad_heads = grad_context.reshape(rows_dev, head_count, head_dim)
    deltas = jnp.sum(grad_heads.astype(jnp.float32) * context_heads, axis=-1).T

    def query_fold(state, portion, begin_row):
        key_part, value_part = portion
        amount = key_part.shape[0]

        def block_fn(inner, key_blk, value_blk, key_pos):
            grad_query, grad_key, grad_value = pair_grads(
                query_heads,
                grad_heads,
                stats,
                deltas,
                query_pos,
                key_blk,
                value_blk,
                key_pos,
                factor,
            )
            return inner + grad_query

        return over_keys(
            state,
            key_part.reshape(amount, head_count, head_dim),
            value_part.reshape(amount, head_count, head_dim),
            begin_row,
            top_query,
            place,
            block_fn,
        )

    zero_heads = jnp.zeros((rows_dev, head_count, head_dim), jnp.float32)
    key_all, value_all = (
        lax.all_gather(key_rows, "ctx", axis=0, tiled=True),
        lax.all_gather(value_rows, "ctx", axis=0, tiled=True),
    )
    grad_query = query_fold(zero_heads, (key_all, value_all), 0)
    amount = lax.axis_size("ctx") * rows_dev
    stride = math.gcd(amount, 512)
    key_part = key_all.reshape(amount // stride, stride, head_count, head_dim)
    value_part = value_all.reshape(amount // stride, stride, head_count, head_dim)
    offsets = jnp.arange(amount // stride, dtype=jnp.int32) * stride

    def key_step_fn(unused, operands):
        key_blk, value_blk, offset = operands
        key_pos = place(offset + jnp.arange(stride, dtype=jnp.int32))

        def key_compute(blocks_in):
            grad_query_part, grad_key, grad_value = pair_grads(
                query_heads,
                grad_heads,
                stats,
                deltas,
                query_pos,
                blocks_in[0],
                blocks_in[1],
                key_pos,
                factor,
            )
            return jnp.concatenate(
                [grad_key.reshape(stride, width), grad_value.reshape(stride, width)], axis=1
            )

        def nothing(blocks_in):
            return jnp.zeros((stride, 2 * width), jnp.float32)

        return (
            unused,
            lax.cond(jnp.min(key_pos) <= top_query, key_compute, nothing, (key_blk, value_blk)),
        )

    unused, stacked = lax.scan(key_step_fn, 0, (key_part, value_part, offsets))
    grad_pairs = lax.psum_scatter(
        stacked.reshape(amount, 2 * width).astype(jnp.bfloat16),
        "ctx",
        scatter_dimension=0,
        tiled=True,
    ).astype(jnp.float32)
    grad_key = grad_pairs[:, :width]
    grad_value = grad_pairs[:, width:]
    grad_mixture = jnp.concatenate(
        [grad_query.reshape(rows_dev, width), grad_key, grad_value], axis=1
    ).astype(jnp.bfloat16)
    in_weight_grad = jnp.einsum(
        "td,te->de", first_low, grad_mixture, preferred_element_type=jnp.float32
    )
    in_bias_grad = jnp.stack(
        [
            jnp.sum(grad_mixture[:, :width].astype(jnp.float32), axis=0),
            jnp.sum(grad_mixture[:, 2 * width :].astype(jnp.float32), axis=0),
        ]
    )
    grad_first = jnp.einsum(
        "te,de->td", grad_mixture, in_weight, preferred_element_type=jnp.float32
    )
    grad_inputs, first_gain_grad, first_shift_grad = norm_back(
        inputs, gain_one, shift_one, grad_first
    )
    tokens_grad = (grad_inputs + grad_residual).astype(jnp.bfloat16)
    (
        first_gain_grad,
        first_shift_grad,
        in_weight_grad,
        in_bias_grad,
        out_weight_grad,
        out_bias_grad,
        second_gain_grad,
        second_shift_grad,
        up_weight_grad,
        up_bias_grad,
        down_weight_grad,
        down_bias_grad,
    ) = (
        lax.psum_scatter(
            first_gain_grad.astype(jnp.bfloat16), "dp", scatter_dimension=0, tiled=True
        ).astype(jnp.float32),
        lax.psum_scatter(
            first_shift_grad.astype(jnp.bfloat16), "dp", scatter_dimension=0, tiled=True
        ).astype(jnp.float32),
        lax.psum_scatter(
            in_weight_grad.astype(jnp.bfloat16), "dp", scatter_dimension=0, tiled=True
        ).astype(jnp.float32),
        lax.psum_scatter(
            in_bias_grad.astype(jnp.bfloat16), "dp", scatter_dimension=1, tiled=True
        ).astype(jnp.float32),
        lax.psum_scatter(
            out_weight_grad.astype(jnp.bfloat16), "dp", scatter_dimension=0, tiled=True
        ).astype(jnp.float32),
        lax.psum_scatter(
            out_bias_grad.astype(jnp.bfloat16), "dp", scatter_dimension=0, tiled=True
        ).astype(jnp.float32),
        lax.psum_scatter(
            second_gain_grad.astype(jnp.bfloat16), "dp", scatter_dimension=0, tiled=True
        ).astype(jnp.float32),
        lax.psum_scatter(
            second_shift_grad.astype(jnp.bfloat16), "dp", scatter_dimension=0, tiled=True
        ).astype(jnp.float32),
        lax.psum_scatter(
            up_weight_grad.astype(jnp.bfloat16), "dp", scatter_dimension=0, tiled=True
        ).astype(jnp.float32),
        lax.psum_scatter(
            up_bias_grad.astype(jnp.bfloat16), "dp", scatter_dimension=0, tiled=True
        ).astype(jnp.float32),
        lax.psum_scatter(
            down_weight_grad.astype(jnp.bfloat16), "dp", scatter_dimension=0, tiled=True
        ).astype(jnp.float32),
        lax.psum_scatter(
            down_bias_grad.astype(jnp.bfloat16), "dp", scatter_dimension=0, tiled=True
        ).astype(jnp.float32),
    )
    (
        first_gain_grad,
        first_shift_grad,
        in_weight_grad,
        in_bias_grad,
        out_weight_grad,
        out_bias_grad,
        second_gain_grad,
        second_shift_grad,
        up_weight_grad,
        up_bias_grad,
        down_weight_grad,
        down_bias_grad,
    ) = (
        lax.psum(first_gain_grad.astype(jnp.bfloat16), "ctx").astype(jnp.float32),
        lax.psum(first_shift_grad.astype(jnp.bfloat16), "ctx").astype(jnp.float32),
        lax.psum(in_weight_grad.astype(jnp.bfloat16), "ctx").astype(jnp.float32),
        lax.psum(in_bias_grad.astype(jnp.bfloat16), "ctx").astype(jnp.float32),
        lax.psum(out_weight_grad.astype(jnp.bfloat16), "ctx").astype(jnp.float32),
        lax.psum(out_bias_grad.astype(jnp.bfloat16), "ctx").astype(jnp.float32),
        lax.psum(second_gain_grad.astype(jnp.bfloat16), "ctx").astype(jnp.float32),
        lax.psum(second_shift_grad.astype(jnp.bfloat16), "ctx").astype(jnp.float32),
        lax.psum(up_weight_grad.astype(jnp.bfloat16), "ctx").astype(jnp.float32),
        lax.psum(up_bias_grad.astype(jnp.bfloat16), "ctx").astype(jnp.float32),
        lax.psum(down_weight_grad.astype(jnp.bfloat16), "ctx").astype(jnp.float32),
        lax.psum(down_bias_grad.astype(jnp.bfloat16), "ctx").astype(jnp.float32),
    )
    return (
        layer_out,
        tokens_grad,
        first_gain_grad,
        first_shift_grad,
        in_weight_grad,
        in_bias_grad,
        out_weight_grad,
        out_bias_grad,
        second_gain_grad,
        second_shift_grad,
        up_weight_grad,
        up_bias_grad,
        down_weight_grad,
        down_bias_grad,
    )


masks = (0, 2, 1, 3)
dp_masks = (0, 4, 2, 6, 1, 5, 3, 7)
tile = 256
share = 20
lanes = 256
part = 3 * HEAD_DIM
root = math.sqrt(2.0 / math.pi)
low, wide = jnp.bfloat16, jnp.float32


def heads_split(mesh):
    return mesh.shape["ctx"] == 4 and mesh.shape["dp"] == 8


def swap(values, axis, bit):
    count = lax.axis_size(axis)
    return lax.ppermute(values, axis, [(i, i ^ bit) for i in range(count)])


def dp_gather(values, waits):
    index = lax.axis_index("dp")
    for bit in (1, 2, 4):
        if bit > 1:
            values = after(values, waits[bit // 2 - 1])
        other = swap(values, "dp", bit)
        upper = (index // bit) % 2 == 1
        values = jnp.concatenate(
            [jnp.where(upper, other, values), jnp.where(upper, values, other)], axis=0
        )
    return values


def dp_scatter_one(kept, sent):
    values = kept + swap(sent, "dp", 1).astype(wide)
    return values.reshape((2, 2) + values.shape[1:])


def dp_parts(values, axis, bit):
    mine = (lax.axis_index("dp") // bit) % 2
    sent = lax.dynamic_index_in_dim(values, 1 - mine, axis, keepdims=False).astype(low)
    return lax.dynamic_index_in_dim(values, mine, axis, keepdims=False), sent


def after(values, *others):
    return lax.optimization_barrier((values, *others))[0]


def dot_nt(left, right):
    return lax.dot_general(left, right, (((1,), (1,)), ((), ())), preferred_element_type=wide)


def dot_nn(left, right):
    return jnp.dot(left, right, preferred_element_type=wide)


def dot_tn(left, right):
    return lax.dot_general(left, right, (((0,), (0,)), ((), ())), preferred_element_type=wide)


def flip(values):
    return values.astype(wide).T.astype(values.dtype)


def whole(array):
    rank = len(array.shape)
    return pl.BlockSpec(array.shape, lambda *_: (0,) * rank)


def held(array):
    return pl.BlockSpec(memory_space=pltpu.VMEM)


def third(place):
    return lambda array: pl.BlockSpec(
        (array.shape[0], array.shape[1] // 3, array.shape[2]), lambda *_: (0, place, 0)
    )


def kernel_call(
    kernel, name, index, inputs, outputs, flops, exps=0, grid=(1,), scratch=(), plain=None
):
    plain = plain or whole
    arrays = [item[0] if isinstance(item, tuple) else item for item in inputs]
    specs = [
        (item[1](item[0]) if callable(item[1]) else item[1]) if isinstance(item, tuple) else plain(item)
        for item in inputs
    ]
    shapes = [item[0] if isinstance(item, tuple) else item for item in outputs]
    out_specs = [item[1] if isinstance(item, tuple) else plain(item) for item in outputs]
    moved = sum(math.prod(a.shape) * a.dtype.itemsize for a in arrays + shapes)
    return pl.pallas_call(
        kernel,
        grid_spec=pltpu.PrefetchScalarGridSpec(
            num_scalar_prefetch=1,
            grid=grid,
            in_specs=specs,
            out_specs=out_specs,
            scratch_shapes=list(scratch),
        ),
        out_shape=shapes,
        compiler_params=pltpu.CompilerParams(vmem_limit_bytes=(24 if plain is held else 48) * 1024 * 1024),
        cost_estimate=pl.CostEstimate(
            flops=flops // share, bytes_accessed=moved // share, transcendentals=exps // share
        ),
        name=name,
    )(index, *arrays)


def shape_of(shape, kind):
    return jax.ShapeDtypeStruct(shape, kind)


def place_of(index, spot, rows):
    return pl.ds(pl.multiple_of((index ^ masks[spot]) * rows, 128), rows)


def diagonal():
    keys = lax.broadcasted_iota(jnp.int32, (tile, tile), 0)
    queries = lax.broadcasted_iota(jnp.int32, (tile, tile), 1)
    return keys <= queries


def unit_of(values):
    center = values - jnp.mean(values, axis=-1, keepdims=True)
    spread = jnp.mean(center * center, axis=-1, keepdims=True)
    scale = lax.rsqrt(spread + epsilon)
    return center * scale, scale


def norm_pull(unit, scale, gain, upstream):
    scaled = upstream * gain
    return scale * (
        scaled
        - jnp.mean(scaled, axis=-1, keepdims=True)
        - unit * jnp.mean(scaled * unit, axis=-1, keepdims=True)
    )


def column_sum(values):
    return jnp.sum(values, axis=0, keepdims=True)


def pick_in_kernel(index_ref, in_ref, out_ref):
    width = in_ref.shape[1] // 3
    own = width // 4
    for ctx in range(4):

        @pl.when(index_ref[0] == ctx)
        def pick():
            for head in range(own // HEAD_DIM):
                for kind in range(3):
                    begin = kind * width + ctx * own + head * HEAD_DIM
                    target = head * part + kind * HEAD_DIM
                    out_ref[:, target : target + HEAD_DIM] = in_ref[:, begin : begin + HEAD_DIM]


def pick_rest_kernel(index_ref, out_weight_ref, up_ref, down_ref, out_ref):
    shard, width = out_weight_ref.shape
    out_ref[:shard, :] = out_weight_ref[...]
    for ctx in range(4):

        @pl.when(index_ref[0] == ctx)
        def pick():
            for owner in range(width // shard):
                begin = owner * 4 * shard + ctx * shard
                out_ref[shard : 2 * shard, owner * shard : (owner + 1) * shard] = up_ref[
                    :, begin : begin + shard
                ]
            out_ref[2 * shard :, :] = down_ref[ctx * shard : (ctx + 1) * shard, :]


def norm_kernel(
    index_ref,
    own_ref,
    far_ref,
    near_ref,
    last_ref,
    vector_ref,
    first_ref,
    turned_ref,
    unit_ref,
):
    rows = own_ref.shape[0]
    for spot, piece in enumerate((own_ref, far_ref, near_ref, last_ref)):
        here = slice(spot * rows, (spot + 1) * rows)
        unit, scale = unit_of(piece[...].astype(wide))
        unit_ref[:, here] = unit.T.astype(low)
        normed = unit * vector_ref[0:1, :] + vector_ref[1:2, :]
        first_ref[here, :] = normed.astype(low)
        turned_ref[:, here] = normed.T.astype(low)


def attend_kernel(
    index_ref,
    first_ref,
    low_half_ref,
    high_half_ref,
    bias_ref,
    weight_ref,
    mix_ref,
    keep_ref,
    send_ref,
    full_ref,
    stats_ref,
    q_s,
    k_s,
    v_s,
    o_s,
):
    total, width = first_ref.shape
    rows = total // 4
    index = index_ref[0]
    heads = width // lanes

    @pl.when(pl.program_id(0) == 0)
    def begin_all():
        shard = low_half_ref.shape[0] // 4
        for spot in range(8):
            source = low_half_ref if spot < 4 else high_half_ref
            block = source[(spot % 4) * shard : (spot % 4 + 1) * shard, :]
            there = pl.ds(pl.multiple_of((index_ref[1] ^ dp_masks[spot]) * shard, 32), shard)
            for head in range(heads):
                begin = head * lanes
                weight_ref[there, begin : begin + part] = block[:, head * part : (head + 1) * part]
                weight_ref[there, begin + part : begin + lanes] = jnp.zeros(
                    (shard, lanes - part), low
                )

    head = pl.program_id(0)
    slab = pl.ds(pl.multiple_of(head * lanes, lanes), lanes)
    lines = pl.ds(pl.multiple_of(head * HEAD_DIM, HEAD_DIM), HEAD_DIM)
    for spot in range(4):
        here = slice(spot * rows, (spot + 1) * rows)
        there = place_of(index, spot, rows)
        block = (dot_nn(first_ref[here, :], weight_ref[:, slab]) + bias_ref[head]).astype(low)
        mix_ref[here, :] = block
        q_s[there, :] = block[:, 0:64] * jnp.bfloat16(0.125)
        k_s[there, :] = block[:, 64:128]
        v_s[there, :] = block[:, 128:192]
    allowed = diagonal()
    flipped = flip(v_s[...])
    for i in range(total // tile):
        begin, end = i * tile, (i + 1) * tile
        queries = q_s[begin:end, :]
        near = jnp.where(allowed, dot_nt(k_s[begin:end, :], queries), neg_large)
        top = jnp.max(near, axis=0, keepdims=True)
        if i > 0:
            past = dot_nt(k_s[:begin, :], queries)
            top = jnp.maximum(top, jnp.max(past, axis=0, keepdims=True))
        near = jnp.exp(near - top)
        amount = column_sum(near)
        context = dot_nn(flipped[:, begin:end], near.astype(low))
        if i > 0:
            past = jnp.exp(past - top)
            amount = amount + column_sum(past)
            context = context + dot_nn(flipped[:, :begin], past.astype(low))
        o_s[:, begin:end] = context / amount
        stats_ref[0, :, begin:end] = top + jnp.log(amount)
    for spot in range(4):
        block = o_s[:, place_of(index, spot, rows)]
        full_ref[:, spot * rows : (spot + 1) * rows] = block
        target = keep_ref if spot in (0, 2) else send_ref
        target[lines, (spot // 2) * rows : (spot // 2 + 1) * rows] = block.astype(low)


def attend(index, first_low, low_half, high_half, bias):
    total, width = first_low.shape
    rows = total // 4
    heads = width // lanes
    features = heads * HEAD_DIM
    by_head = lambda h, s: (h, 0)
    pairs = heads * total * total // 2
    return kernel_call(
        attend_kernel,
        "attend",
        index,
        [first_low, low_half, high_half, bias],
        [
            (shape_of((width, width), low), whole(first_low[:width])),
            (shape_of((total, width), low), pl.BlockSpec((total, lanes), lambda h, s: (0, h))),
            shape_of((features, 2 * rows), low),
            shape_of((features, 2 * rows), low),
            (shape_of((features, total), wide), pl.BlockSpec((HEAD_DIM, total), by_head)),
            (
                shape_of((heads, 1, total), wide),
                pl.BlockSpec((1, 1, total), lambda h, s: (h, 0, 0)),
            ),
        ],
        pairs * 4 * 256 + 2 * total * width * width,
        pairs,
        (heads,),
        [pltpu.VMEM((total, HEAD_DIM), low)] * 3 + [pltpu.VMEM((HEAD_DIM, total), wide)],
        held,
    )


def project_kernel(
    index_ref,
    keep_ref,
    far_ref,
    near_ref,
    weight_ref,
    tokens_ref,
    vector_ref,
    residual_ref,
    second_ref,
    turned_ref,
):
    rows, width = tokens_ref.shape
    own = width // 4
    pieces = [keep_ref[:, :rows], far_ref[:, :rows], near_ref[:, :rows], near_ref[:, rows:]]
    residual = tokens_ref[...].astype(wide) + vector_ref[4:5, :]
    for spot in range(4):
        turned = flip(pieces[spot])
        group = index_ref[0] ^ masks[spot]
        weights = weight_ref[pl.ds(2 * group, 2)].reshape(own, width)
        residual = residual + dot_nn(turned, weights)
    residual_ref[...] = residual
    unit, scale = unit_of(residual)
    second_ref[...] = (unit * vector_ref[5:6, :] + vector_ref[6:7, :]).astype(low)
    for spot in range(4):
        turned_ref[spot * own : (spot + 1) * own, :] = pieces[spot]


def feed_kernel(
    index_ref,
    one_ref,
    two_ref,
    up_one_ref,
    up_two_ref,
    up_ref,
    down_ref,
    bias_ref,
    active_ref,
    hidden_ref,
    kept_ref,
    sent_ref,
    sum_ref,
):
    rows, width = one_ref.shape
    up = up_ref[...].reshape(width, width)
    down = down_ref[...].reshape(width, width)
    for spot in (1, 0):
        here = slice(spot * rows, (spot + 1) * rows)
        values = two_ref[...] if spot else one_ref[...]
        grads = up_two_ref[...] if spot else up_one_ref[...]
        hidden = dot_nn(values, up) + bias_ref[...]
        square = hidden * hidden
        bend = jnp.tanh(root * hidden * (1.0 + 0.044715 * square))
        active_ref[here, :] = (0.5 * hidden * (1.0 + bend)).astype(low)
        slope = 0.5 * (1.0 + bend) + 0.5 * hidden * (1.0 - bend * bend) * (
            root * (1.0 + 3 * 0.044715 * square)
        )
        grad = (slope * dot_nt(grads, down)).astype(low)
        hidden_ref[here, :] = grad
        sums = column_sum(grad.astype(wide))
        sum_ref[...] = sums if spot else sum_ref[...] + sums
        result = dot_nt(grad, up)
        if spot:
            sent_ref[...] = result.astype(low)
        else:
            kept_ref[...] = result


def halves(index_ref, block, kept_ref, sent_ref, pair):
    upper = index_ref[1] % 2 == 1
    kept_ref[pair] = jnp.where(upper, block[1], block[0])
    sent_ref[pair] = jnp.where(upper, block[0], block[1]).astype(low)


def feed_grad_kernel(
    index_ref,
    own_ref,
    far_ref,
    near_ref,
    last_ref,
    up_own_ref,
    up_far_ref,
    up_near_ref,
    up_last_ref,
    hidden_one_ref,
    hidden_two_ref,
    active_one_ref,
    active_two_ref,
    down_ref,
    out_ref,
    kept_one_ref,
    sent_one_ref,
    kept_two_ref,
    sent_two_ref,
):
    rows, width = own_ref.shape
    count, shard = out_ref.shape[0], out_ref.shape[1] // 2

    def halved(one, two):
        return (one[:rows, :], one[rows:, :], two[:rows, :], two[rows:, :])

    pairs = (
        ((own_ref, near_ref, far_ref, last_ref), halved(hidden_one_ref, hidden_two_ref)),
        (
            halved(active_one_ref, active_two_ref),
            (up_own_ref, up_near_ref, up_far_ref, up_last_ref),
        ),
    )
    for place, (lefts, rights) in enumerate(pairs):
        total = None
        for left, right in zip(lefts, rights):
            update = dot_tn(left[...], right[...])
            total = update if total is None else total + update
        total = total.astype(low).reshape(count, shard, width)
        out_ref[:, place * shard : (place + 1) * shard, :] = total
    down = down_ref[...].reshape(width, width)
    kept_one_ref[...] = dot_nn(active_one_ref[:rows, :], down)
    sent_one_ref[...] = dot_nn(active_one_ref[rows:, :], down).astype(low)
    kept_two_ref[...] = dot_nn(active_two_ref[:rows, :], down)
    sent_two_ref[...] = dot_nn(active_two_ref[rows:, :], down).astype(low)


def in_grad_kernel(
    index_ref,
    turned_ref,
    unit_ref,
    mix_ref,
    weight_ref,
    bias_ref,
    two_ref,
    up_one_ref,
    up_two_ref,
    kept_ref,
    sent_ref,
    rows_s,
):
    pairs, high, columns = kept_ref.shape
    width = mix_ref.shape[1]
    shard = width // (2 * pairs)
    own = columns // 3
    upper = index_ref[1] % 2 == 1
    rows_s[...] = jnp.zeros(rows_s.shape, wide)
    rows_s[4:8, :] = two_ref[...]
    sums = jnp.concatenate([bias_ref[head] for head in range(width // lanes)], axis=1)
    for ctx in range(4):

        @pl.when(index_ref[0] == ctx)
        def put():
            rows_s[8 + ctx : 9 + ctx, :] = up_one_ref[...] + up_two_ref[...]
            for head in range(own // HEAD_DIM):
                begin = ctx * own + head * HEAD_DIM
                for row, kind in ((2, 0), (3, 2)):
                    rows_s[row : row + 1, begin : begin + HEAD_DIM] = bias_ref[
                        head, :, kind * HEAD_DIM : (kind + 1) * HEAD_DIM
                    ]

    column = lax.broadcasted_iota(jnp.int32, (2 * shard, 128), 1)
    for pair in range(pairs):
        here = slice(2 * pair * shard, 2 * (pair + 1) * shard)
        weights = weight_ref[here, :].astype(wide)
        gain = jnp.sum(weights * dot_nn(unit_ref[here, :], mix_ref[...]), axis=1, keepdims=True)
        shift = jnp.sum(weights * sums, axis=1, keepdims=True)
        both = jnp.where(column == 0, gain, jnp.where(column == 1, shift, 0.0)).T
        rows_s[0:2, here] = both[0:2, :]
    for pair in range(pairs):
        begin = 2 * pair * shard
        block = dot_nn(turned_ref[begin : begin + 2 * shard, :], mix_ref[...])
        kept = jnp.where(upper, block[shard:, :], block[:shard, :])
        sent = jnp.where(upper, block[:shard, :], block[shard:, :]).astype(low)
        for head in range(columns // part):
            here = slice(head * part, (head + 1) * part)
            there = slice(head * lanes, head * lanes + part)
            kept_ref[pair, :shard, here] = kept[:, there]
            sent_ref[pair, :shard, here] = sent[:, there]
        one = rows_s[0:12, begin : begin + shard]
        two = rows_s[0:12, begin + shard : begin + 2 * shard]
        kept = jnp.where(upper, two, one)
        sent = jnp.where(upper, one, two)

        def lines(values):
            return jnp.concatenate(
                [
                    jnp.concatenate([values[6 * r + i : 6 * r + i + 1] for i in range(6)], axis=1)
                    for r in range(2)
                ],
                axis=0,
            )

        kept_ref[pair, shard : shard + 2, :] = lines(kept)
        sent_ref[pair, shard:, :] = jnp.concatenate(
            [lines(sent), jnp.zeros((high - shard - 2, columns), wide)], axis=0
        ).astype(low)
        kept_ref[pair, shard + 2 :, :] = jnp.zeros((high - shard - 2, columns), wide)


def turn_kernel(
    index_ref,
    kept_ref,
    core_ref,
    far_ref,
    residual_ref,
    cotangent_ref,
    weight_ref,
    vector_ref,
    grad_ref,
    attn_ref,
    keep_ref,
    send_ref,
    sum_ref,
):
    rows, width = residual_ref.shape
    own = width // 4
    grad = kept_ref[...] + core_ref[...].astype(wide) + far_ref[...].astype(wide)
    unit, scale = unit_of(residual_ref[...])
    upstream = cotangent_ref[...].astype(wide)
    result = upstream + norm_pull(unit, scale, vector_ref[5:6, :], grad)
    grad_ref[...] = result
    attn = result.astype(low)
    attn_ref[...] = attn
    for spot in range(4):
        group = index_ref[0] ^ masks[spot]
        weights = weight_ref[pl.ds(2 * group, 2)].reshape(own, width)
        block = dot_nt(weights, attn).astype(low)
        target = keep_ref if spot in (0, 2) else send_ref
        target[:, (spot // 2) * rows : (spot // 2 + 1) * rows] = block
    sum_ref[0:1, :] = column_sum(grad * unit)
    sum_ref[1:2, :] = column_sum(grad)
    sum_ref[2:3, :] = column_sum(attn.astype(wide))
    sum_ref[3:4, :] = column_sum(upstream)


def out_grad_kernel(index_ref, turned_ref, attn_ref, kept_ref, sent_ref):
    width = turned_ref.shape[0]
    own = width // 4
    for spot in range(4):
        group = index_ref[0] ^ masks[spot]
        block = dot_nn(turned_ref[spot * own : (spot + 1) * own, :], attn_ref[...])
        halves(index_ref, block.reshape(2, own // 2, width), kept_ref, sent_ref, group)


def attend_back_kernel(
    index_ref,
    mix_ref,
    keep_ref,
    far_ref,
    near_ref,
    full_ref,
    stats_ref,
    out_ref,
    sum_ref,
    q_s,
    k_s,
    v_s,
    g_s,
    d_s,
    dq_s,
):
    total = mix_ref.shape[0]
    rows = total // 4
    index = index_ref[0]
    head = pl.program_id(0)
    slab = pl.ds(pl.multiple_of(head * lanes, lanes), lanes)
    lines = pl.ds(pl.multiple_of(head * HEAD_DIM, HEAD_DIM), HEAD_DIM)
    pieces = [keep_ref[lines, :rows], far_ref[lines, :rows]]
    pieces = pieces + [near_ref[lines, :rows], near_ref[lines, rows:]]
    for spot in range(4):
        here = slice(spot * rows, (spot + 1) * rows)
        there = place_of(index, spot, rows)
        block = mix_ref[here, slab]
        q_s[there, :] = block[:, 0:64] * jnp.bfloat16(0.125)
        k_s[there, :] = block[:, 64:128]
        v_s[there, :] = block[:, 128:192]
        block = pieces[spot]
        g_s[:, there] = block
        d_s[:, there] = column_sum(block.astype(wide) * full_ref[lines, here])
    allowed = diagonal()
    turned = flip(g_s[...])
    flipped = flip(k_s[...])
    count = total // tile
    for j in range(count):
        begin, end = j * tile, (j + 1) * tile
        keys, values = k_s[begin:end, :], v_s[begin:end, :]
        probs = jnp.exp(dot_nt(keys, q_s[begin:, :]) - stats_ref[head, :, begin:])
        near = jnp.where(allowed, probs[:, :tile], 0.0)
        probs = near if j == count - 1 else jnp.concatenate([near, probs[:, tile:]], axis=1)
        scores = (probs * (dot_nn(values, g_s[:, begin:]) - d_s[:, begin:])).astype(low)
        grad_value = dot_nn(probs.astype(low), turned[begin:, :])
        grad_key = dot_nn(scores, q_s[begin:, :])
        update = dot_nn(flipped[:, begin:end], scores)
        if j == 0:
            dq_s[...] = update
        else:
            dq_s[:, begin:] = dq_s[:, begin:] + update
        k_s[begin:end, :] = grad_key.astype(low)
        v_s[begin:end, :] = grad_value.astype(low)
    q_s[...] = (dq_s[...] * 0.125).T.astype(low)
    for spot in range(4):
        here = slice(spot * rows, (spot + 1) * rows)
        there = place_of(index, spot, rows)
        block = jnp.concatenate(
            [q_s[there, :], k_s[there, :], v_s[there, :], jnp.zeros((rows, 64), low)], axis=1
        )
        out_ref[here, slab] = block
        sums = column_sum(block.astype(wide))
        sum_ref[head] = sums if spot == 0 else sum_ref[head] + sums


def attend_back(index, mix, keep, far, near, full, stats):
    total, width = mix.shape
    heads = width // lanes
    pairs = heads * total * total // 2
    return kernel_call(
        attend_back_kernel,
        "attend_back",
        index,
        [mix, keep, far, near, full, stats],
        [shape_of((total, width), low), shape_of((heads, 1, lanes), wide)],
        pairs * 10 * 256,
        pairs,
        (heads,),
        [pltpu.VMEM((total, HEAD_DIM), low)] * 3
        + [
            pltpu.VMEM((HEAD_DIM, total), low),
            pltpu.VMEM((1, total), wide),
            pltpu.VMEM((HEAD_DIM, total), wide),
        ],
        held,
    )


def first_back_kernel(spots, index_ref, mix_ref, weight_ref, kept_ref, sent_ref):
    rows = kept_ref.shape[0]
    for spot, target in zip(spots, (sent_ref, kept_ref)):
        grad = dot_nt(mix_ref[spot * rows : (spot + 1) * rows, :], weight_ref[...])
        target[...] = grad.astype(target.dtype)


def tokens_kernel(
    index_ref, kept_ref, core_ref, far_ref, tokens_ref, residual_ref, vector_ref, out_ref
):
    rows = tokens_ref.shape[0]
    grad = kept_ref[...] + core_ref[...].astype(wide) + far_ref[...].astype(wide)
    unit, scale = unit_of(tokens_ref[...].astype(wide))
    result = residual_ref[...] + norm_pull(unit, scale, vector_ref[0:1, :], grad)
    out_ref[...] = result.astype(low)


def spread_kernel(index_ref, own_ref, far_ref, near_ref, up_ref, down_ref):
    width = own_ref.shape[1]
    shard = own_ref.shape[0] // 2
    for ctx in range(4):
        for spot in range(4):

            @pl.when((index_ref[0] ^ ctx) == masks[spot])
            def put():
                source = [own_ref, far_ref, near_ref, near_ref][spot]
                base = 2 * shard if spot == 3 else 0
                block = source[base : base + shard, :].astype(wide)
                for owner in range(width // shard):
                    begin = (owner * 4 + ctx) * shard
                    up_ref[:, begin : begin + shard] = block[:, owner * shard : (owner + 1) * shard]
                down_ref[ctx * shard : (ctx + 1) * shard, :] = source[
                    base + shard : base + 2 * shard, :
                ].astype(wide)


def spread_in_kernel(index_ref, own_ref, far_ref, near_ref, in_ref, sum_ref):
    shard, width = in_ref.shape[0], in_ref.shape[1] // 3
    high, own = own_ref.shape[0], width // 4
    for ctx in range(4):
        for spot in range(4):

            @pl.when((index_ref[0] ^ ctx) == masks[spot])
            def put():
                source = [own_ref, far_ref, near_ref, near_ref][spot]
                base = high if spot == 3 else 0
                block = source[base : base + shard, :].astype(wide)
                for head in range(own // HEAD_DIM):
                    for kind in range(3):
                        begin = kind * width + ctx * own + head * HEAD_DIM
                        target = head * part + kind * HEAD_DIM
                        in_ref[:, begin : begin + HEAD_DIM] = block[:, target : target + HEAD_DIM]
                extra = source[base + shard : base + high, :].astype(wide)
                sum_ref[...] = extra if ctx == 0 else sum_ref[...] + extra


def pieces_of(values):
    far = swap(values, "ctx", 2)
    return values, far, swap(jnp.concatenate([values, far], axis=0), "ctx", 1)


def blocks_of(values):
    far = swap(values, "ctx", 2)
    near = swap(values, "ctx", 1)
    return values, far, near, swap(far, "ctx", 1)


def exchange(keep, send):
    rows = keep.shape[1] // 2
    far = swap(send, "ctx", 2)
    near = swap(jnp.concatenate([keep[:, rows:], far[:, rows:]], axis=1), "ctx", 1)
    return far, near


def split_body(
    tokens,
    first_gain,
    first_shift,
    in_weight,
    in_bias,
    out_weight,
    out_bias,
    second_gain,
    second_shift,
    up_weight,
    up_bias,
    down_weight,
    down_bias,
    cotangent,
):
    rows, width = tokens.shape
    total = 4 * rows
    n_dp = lax.axis_size("dp")
    shard = width // n_dp
    ctx = lax.axis_index("ctx")
    owner = lax.axis_index("dp")
    heads = width // HEAD_DIM // 4
    own = heads * HEAD_DIM
    index = jnp.stack([ctx, owner]).astype(jnp.int32)
    big = 2 * total * width * width
    small = 2 * rows * width * width
    row_wide, row_low = shape_of((rows, width), wide), shape_of((rows, width), low)

    (in_own,) = kernel_call(
        pick_in_kernel,
        "pick_in",
        index,
        [in_weight],
        [shape_of((shard, 3 * own), low)],
        0,
        plain=held,
    )
    in_other = swap(in_own, "dp", 4)
    in_two = jnp.concatenate([in_own, in_other], axis=0)
    low_half = jnp.concatenate([in_two, swap(in_two, "dp", 2)], axis=0)
    high_half = swap(low_half, "dp", 1)
    (rest,) = kernel_call(
        pick_rest_kernel,
        "pick_rest",
        index,
        [out_weight, up_weight, after(down_weight, in_other)],
        [shape_of((3 * shard, width), low)],
        0,
    )
    rest = lax.all_gather(rest, "dp", axis=0, tiled=False)
    vectors = jnp.concatenate(
        [first_gain, first_shift, in_bias[0], in_bias[1], out_bias, second_gain, second_shift]
        + [down_bias, up_bias]
    ).reshape(1, 12 * shard)
    vectors = dp_gather(vectors, (in_two, low_half)).reshape(n_dp, 12, shard).transpose(1, 0, 2).reshape(12, width)
    vectors = vectors.astype(wide)
    hidden_bias = lax.dynamic_slice_in_dim(vectors, 8 + ctx, 1, 0)
    zeros = jnp.zeros((heads, HEAD_DIM), wide)
    mine = lax.dynamic_slice(vectors, (2, ctx * own), (2, own)).reshape(2, heads, HEAD_DIM)
    bias_full = jnp.concatenate([mine[0], zeros, mine[1], zeros], axis=1).reshape(heads, 1, lanes)

    token_blocks = blocks_of(tokens)
    first_low, first_turned, unit_turned = kernel_call(
        norm_kernel,
        "norm",
        index,
        [*token_blocks, vectors],
        [shape_of((total, width), low)] + [shape_of((width, total), low)] * 2,
        0,
    )
    upstream = blocks_of(after(cotangent, token_blocks[1]))
    in_full, mix, keep, send, context_full, stats = attend(
        index, first_low, low_half, high_half, bias_full
    )
    far, near = exchange(keep, after(send, upstream[1]))
    out_block = (rest, third(0))
    up_block = (rest, third(1))
    down_block = (rest, third(2))
    residual, second_low, turned = kernel_call(
        project_kernel,
        "project",
        index,
        [keep, far, near, out_block, tokens, vectors],
        [row_wide, row_low, shape_of((width, rows), low)],
        small,
    )

    def feed(name, one, two, up_one, up_two):
        return kernel_call(
            feed_kernel,
            name,
            index,
            [one, two, up_one, up_two, up_block, down_block, hidden_bias],
            [shape_of((total // 2, width), low)] * 2
            + [row_wide, row_low, shape_of((1, width), wide)],
            3 * big // 2,
            total * width // 2,
        )

    far, near = swap(second_low, "ctx", 2), swap(second_low, "ctx", 1)
    active_one, hidden_one, kept_one, sent_one, up_sum_one = feed(
        "feed_one", second_low, near, upstream[0], upstream[2]
    )
    far = after(far, active_one)
    second = (second_low, far, near, swap(far, "ctx", 1))
    active_two, hidden_two, kept_two, sent_two, up_sum_two = feed(
        "feed_two", second[1], second[3], upstream[1], upstream[3]
    )
    core_one = swap(sent_one, "ctx", 1)
    passed = (kept_two + swap(sent_two, "ctx", 1).astype(wide)).astype(low)
    far = swap(passed, "ctx", 2)
    feed_grad, *branch = kernel_call(
        feed_grad_kernel,
        "feed_grad",
        index,
        [after(second[0], passed), *second[1:], *upstream, hidden_one, hidden_two]
        + [active_one, active_two, down_block],
        [shape_of((n_dp, 2 * shard, width), low), row_wide, row_low, row_wide, row_low],
        3 * big,
    )
    far, feed_grad, *branch = lax.optimization_barrier((far, feed_grad, *branch))
    feed_mine = lax.psum_scatter(feed_grad, "dp", scatter_dimension=0, tiled=False)
    grad_residual, grad_attn, keep, send, sums_two = kernel_call(
        turn_kernel,
        "turn",
        index,
        [kept_one, core_one, far, residual, cotangent, out_block, vectors],
        [
            row_wide,
            row_low,
            shape_of((own, 2 * rows), low),
            shape_of((own, 2 * rows), low),
            shape_of((4, width), wide),
        ],
        small,
    )
    out_kept, out_sent = kernel_call(
        out_grad_kernel,
        "out_grad",
        index,
        [turned, grad_attn],
        [shape_of((n_dp // 2, shard, width), wide), shape_of((n_dp // 2, shard, width), low)],
        small,
    )
    far = swap(send, "ctx", 2)
    late = after(far, out_sent)
    near = swap(jnp.concatenate([keep[:, rows:], late[:, rows:]], axis=1), "ctx", 1)
    branch_kept, branch_sent, kept_two, sent_two = branch
    branch_core = swap(branch_sent, "ctx", 1)
    passed = (kept_two + swap(sent_two, "ctx", 1).astype(wide)).astype(low)
    branch_far = swap(passed, "ctx", 2)
    grad_mix, bias_sums = attend_back(
        index, mix, after(keep, passed), far, near, context_full, stats
    )

    high = shard + 16
    out_half = dp_scatter_one(out_kept, out_sent)
    out_next, out_sent = dp_parts(out_half, 1, 2)
    kept_two, sent_two = kernel_call(
        functools.partial(first_back_kernel, (3, 1)),
        "first_back_two",
        index,
        [after(grad_mix, out_half, branch_far), in_full],
        [row_wide, row_low],
        big // 2,
    )
    passed = (kept_two + swap(sent_two, "ctx", 1).astype(wide)).astype(low)
    far = swap(passed, "ctx", 2)
    out_sent = after(out_sent, passed)
    out_arrived = swap(out_sent, "dp", 2)
    in_kept, in_sent = kernel_call(
        in_grad_kernel,
        "in_grad",
        index,
        [after(first_turned, passed, out_sent), unit_turned, grad_mix, in_full]
        + [bias_sums, sums_two, up_sum_one, up_sum_two],
        [shape_of((n_dp // 2, high, 3 * own), wide), shape_of((n_dp // 2, high, 3 * own), low)],
        2 * big,
        scratch=[pltpu.VMEM((16, width), wide)],
    )
    out_next = after(out_next, in_sent) + out_arrived.astype(wide)
    out_next, out_sent = dp_parts(out_next, 0, 4)
    kept_one, sent_one = kernel_call(
        functools.partial(first_back_kernel, (2, 0)),
        "first_back_one",
        index,
        [after(grad_mix, out_sent), in_full],
        [row_wide, row_low],
        big // 2,
    )
    core_one = swap(sent_one, "ctx", 1)
    in_half = dp_scatter_one(after(in_kept, kept_one), in_sent)
    in_next, in_sent = dp_parts(in_half, 1, 2)
    (tokens_grad,) = kernel_call(
        tokens_kernel,
        "tokens",
        index,
        [kept_one, core_one, after(far, in_sent, out_sent), tokens, grad_residual, vectors],
        [row_low],
        0,
    )
    feed_mine = after(feed_mine.reshape(2 * shard, width), in_sent, tokens_grad)
    feed_far = swap(feed_mine, "ctx", 2)
    branch = branch_kept + branch_core.astype(wide) + branch_far.astype(wide)
    layer_out = (residual + branch + vectors[7]).astype(low)
    out_next = after(out_next, layer_out)
    out_mine = (after(out_next, feed_mine) + swap(out_sent, "dp", 4).astype(wide)).astype(low)
    out_far = swap(out_mine, "ctx", 2)
    in_next = after(in_next, out_mine) + swap(in_sent, "dp", 2).astype(wide)
    in_next, in_sent = dp_parts(in_next, 0, 4)
    feed_near = jnp.concatenate([after(feed_mine, in_sent), feed_far], axis=0)
    feed_near = swap(feed_near, "ctx", 1)
    out_mine = (after(out_mine, in_sent).astype(wide) + out_far.astype(wide)).astype(low)
    out_weight_grad = out_mine.astype(wide) + swap(out_mine, "ctx", 1).astype(wide)
    in_mine = (after(in_next, out_mine) + swap(in_sent, "dp", 4).astype(wide)).astype(low)
    up_weight_grad, down_weight_grad = kernel_call(
        spread_kernel,
        "spread",
        index,
        [after(feed_mine, in_mine), feed_far, feed_near],
        [shape_of((shard, 4 * width), wide), shape_of((4 * shard, width), wide)],
        0,
        plain=held,
    )
    in_far = swap(in_mine, "ctx", 2)
    in_near = jnp.concatenate([after(in_mine, up_weight_grad, layer_out), in_far], axis=0)
    in_near = swap(in_near, "ctx", 1)
    in_weight_grad, sums = kernel_call(
        spread_in_kernel,
        "spread_in",
        index,
        [in_mine, in_far, in_near],
        [shape_of((shard, 3 * width), wide), shape_of((high - shard, 3 * own), wide)],
        0,
        plain=held,
    )
    sums = sums[:2].reshape(12, shard)
    return (
        layer_out,
        tokens_grad,
        sums[0],
        sums[1],
        in_weight_grad,
        sums[2:4],
        out_weight_grad,
        sums[6],
        sums[4],
        sums[5],
        up_weight_grad,
        sums[8:12].reshape(4 * shard),
        down_weight_grad,
        sums[7],
    )


def solution(mesh):
    in_specs = (
        P(("dp", "ctx"), None),
        P("dp"),
        P("dp"),
        P("dp", None),
        P(None, "dp"),
        P("dp", None),
        P("dp"),
        P("dp"),
        P("dp"),
        P("dp", None),
        P("dp"),
        P("dp", None),
        P("dp"),
        P(("dp", "ctx"), None),
    )
    out_specs = (
        P(("dp", "ctx"), None),
        P(("dp", "ctx"), None),
        P("dp"),
        P("dp"),
        P("dp", None),
        P(None, "dp"),
        P("dp", None),
        P("dp"),
        P("dp"),
        P("dp"),
        P("dp", None),
        P("dp"),
        P("dp", None),
        P("dp"),
    )
    chosen = split_body if heads_split(mesh) else gathered_body
    return jax.shard_map(chosen, mesh=mesh, in_specs=in_specs, out_specs=out_specs, check_vma=False)
```
